256 devices in a mesh: query: 8 (over x, y_hi), corpus: 32 (over y_lo, z, core).
Axes of the slice: x: 4, y: 4 (y_hi: 2, y_lo: 2; y = y_hi * 2 + y_lo), z: 8, core: 2. Of those that a mesh axis runs over, the one named last changes fastest.
Arguments:
- teacher_query: bfloat16 [32768, 1024], P('query'), may hold values from -70 to 70
- student_query: bfloat16 [32768, 384], P('query'), may hold values from -110 to 110
- teacher_passages: bfloat16 [16384, 1024], P(('query', 'corpus')), may hold values from -40 to 40
- student_passages: bfloat16 [16384, 384], P(('query', 'corpus')), may hold values from -40 to 40
Outputs:
- divergence: float32 [32768], P(('query', 'corpus'))
- grad_query: float32 [32768, 384], P(('query', 'corpus'))
- grad_passage: float32 [16384, 384], P(('query', 'corpus'))
The draws below stay inside these ranges and needn't reach their ends.
All inputs are finite; a program needn't handle non-finite values.
Results may differ from the reference program's by a relative error of at most 0.0044.
Values may be sent and summed in bfloat16 or wider, within the bound.
A program may use at most 128 MiB of HBM per device.

```python
import math
import jax
import jax.numpy as jnp
from jax import lax

DT = 1024
DS = 384
NQ = 32768
NP = 16384


def passage_scales(key, lowest, highest):
    key = jax.random.fold_in(key, 202)
    return jnp.exp(jax.random.uniform(key, (NP,), jnp.float32, math.log(lowest), math.log(highest)))


def query_scales(key):
    key = jax.random.fold_in(key, 303)
    return jnp.exp(jax.random.uniform(key, (NQ,), jnp.float32, math.log(0.3), math.log(3.0)))


def drawn_dirs(key, stream, height, breadth):
    key = jax.random.fold_in(key, stream)
    return jax.random.truncated_normal(key, -4.0, 4.0, (height, breadth), jnp.float32)


def draw_teacher_query(key, part):
    private = jax.random.fold_in(key, 7)
    scales = query_scales(key)
    return (scales[:, None] * drawn_dirs(private, 13, NQ, DT)).astype(jnp.bfloat16)


def draw_student_query(key, part):
    private = jax.random.fold_in(key, 8)
    scales = query_scales(key)
    return (scales[:, None] * drawn_dirs(private, 14, NQ, DS)).astype(jnp.bfloat16)


def draw_teacher_passages(key, part):
    private = jax.random.fold_in(key, 9)
    scales = passage_scales(key, 0.3, 3.0)
    return (scales[:, None] * drawn_dirs(private, 11, NP, DT)).astype(jnp.bfloat16)


def draw_student_passages(key, part):
    private = jax.random.fold_in(key, 10)
    scales = passage_scales(key, 0.3, 3.0)
    return (scales[:, None] * drawn_dirs(private, 12, NP, DS)).astype(jnp.bfloat16)


def setup_inputs(seed: int = 0) -> dict:
    key_of = jax.random.split(jax.random.key(seed), 5)
    return {
        "teacher_query": draw_teacher_query(jax.random.fold_in(key_of[4], 71), 0),
        "student_query": draw_student_query(jax.random.fold_in(key_of[4], 71), 0),
        "teacher_passages": draw_teacher_passages(jax.random.fold_in(key_of[4], 71), 0),
        "student_passages": draw_student_passages(jax.random.fold_in(key_of[4], 71), 0),
    }


def reference(teacher_query, student_query, teacher_passages, student_passages):
    teacher_scale = teacher_query.shape[1] ** -0.5
    student_scale = student_query.shape[1] ** -0.5
    student_width = student_query.shape[1]
    block_rows = math.gcd(teacher_query.shape[0], 512)
    blocks = teacher_query.shape[0] // block_rows
    teacher_blocks = teacher_query.reshape(blocks, block_rows, teacher_query.shape[1])
    student_blocks = student_query.reshape(blocks, block_rows, student_width)

    def advance(summed, row_block):
        teacher_rows, student_rows = row_block
        teacher_logits = lax.dot_general(teacher_rows, teacher_passages, (((1,), (1,)), ((), ())),
                                         preferred_element_type=jnp.float32) * teacher_scale
        student_logits = lax.dot_general(student_rows, student_passages, (((1,), (1,)), ((), ())),
                                         preferred_element_type=jnp.float32) * student_scale
        teacher_max = jnp.max(teacher_logits, axis=1)
        teacher_weight = jnp.exp(teacher_logits - teacher_max[:, None])
        teacher_sum = jnp.sum(teacher_weight, axis=1)
        teacher_probs = teacher_weight / teacher_sum[:, None]
        student_max = jnp.max(student_logits, axis=1)
        student_weight = jnp.exp(student_logits - student_max[:, None])
        student_sum = jnp.sum(student_weight, axis=1)
        student_probs = student_weight / student_sum[:, None]
        divergence = (jnp.sum(teacher_probs * (teacher_logits - student_logits), axis=1)
                      - (teacher_max + jnp.log(teacher_sum)) + (student_max + jnp.log(student_sum)))
        logit_grad = ((student_probs - teacher_probs) * student_scale).astype(jnp.bfloat16)
        query_grad = jnp.dot(logit_grad, student_passages, preferred_element_type=jnp.float32)
        summed = summed + lax.dot_general(logit_grad, student_rows, (((0,), (0,)), ((), ())),
                                          preferred_element_type=jnp.float32)
        return summed, (divergence, query_grad)

    initial = jnp.zeros(student_passages.shape, jnp.float32)
    grad_passage, outputs = lax.scan(advance, initial, (teacher_blocks, student_blocks))
    divergence, grad_query = outputs
    return divergence.reshape(-1), grad_query.reshape(-1, student_width), grad_passage
```

```python
import functools

import jax
import jax.numpy as jnp
from jax import lax
from jax.experimental import pallas as pl
from jax.experimental.pallas import tpu as pltpu
from jax.sharding import PartitionSpec as P

NX, NYH, NYL, NZ, NCORE = 4, 2, 2, 8, 2
OWN = 64
ROWS = 128
DT, DS = 1024, 384
BATCH = NX * OWN
GROUP = NYL * ROWS
OWNERS = NYL * NZ
HALF = OWN // 2
F32, BF16 = jnp.float32, jnp.bfloat16
MESH = pl.DeviceIdType.MESH

TO_YH, TO_RIGHT, TO_LEFT, ON_RIGHT, ON_LEFT = 0, 1, 2, 3, 4
TO_RIGHT2, TO_LEFT2, ON_RIGHT2, ON_LEFT2 = 5, 6, 7, 8
SIB = 9
RING_R, RING_L = 17, 21
Y_PAIR = 25
GP_SIB, GP_R1, GP_L1, GP_R2, GP_L2, GP_YH = 26, 27, 28, 29, 30, 31
MESSAGES = 32


def nt(a, b):
    return lax.dot_general(a, b, (((1,), (1,)), ((), ())), preferred_element_type=F32)


def nn(a, b):
    return lax.dot_general(a, b, (((1,), (0,)), ((), ())), preferred_element_type=F32)


def kernel(
    tq_hbm, sq_hbm, tp_hbm, sp_hbm,
    gq_out, gp_out, div_out,
    tq, sq, pbuf, spt, tw, sw, gt, stat, gq,
    stat_send, stat_recv, res_recv,
    ring_send_r, ring_recv_r, ring_send_l, ring_recv_l, ring_half, y_send, y_recv,
    gp, gps_send, gps_recv, gp1_recv, gp2_send, gp2_recv, gp3_send, gp3_recv,
    load_sem, send_sem, recv_sem, st_send_sem, st_recv_sem, rs_send_sem, rs_recv_sem,
):
    t_scale = DT ** (-0.5)
    s_scale = DS ** (-0.5)
    q = lax.axis_index("query")
    c = lax.axis_index("corpus")
    x, yh = q // NYH, q % NYH
    yl, z, k = c // (NZ * NCORE), (c // NCORE) % NZ, c % NCORE
    me = yl * NZ + z

    def at(x_, yh_, yl_, z_, k_):
        return (x_ * NYH + yh_, (yl_ * NZ + z_) * NCORE + k_)

    x_r, x_l, x_o = (x + 1) % NX, (x + NX - 1) % NX, (x + 2) % NX
    z_r, z_l = (z + 1) % NZ, (z + NZ - 1) % NZ
    oh, ok = 1 - yh, 1 - k
    right, left = at(x_r, yh, yl, z, k), at(x_l, yh, yl, z, k)
    across = at(x, oh, yl, z, k)
    sibling = at(x, yh, yl, z, ok)
    up, down = at(x, yh, yl, z_r, k), at(x, yh, yl, z_l, k)
    y_mate = at(x, yh, 1 - yl, z, k)

    def owner(m):
        return at(x, yh, m // NZ, m % NZ, k)

    loads = [
        pltpu.make_async_copy(tp_hbm, pbuf.at[k, yh, pl.ds(pl.multiple_of(x * OWN, OWN), OWN), pl.ds(0, DT)], load_sem.at[0]),
        pltpu.make_async_copy(sp_hbm, pbuf.at[k, yh, pl.ds(pl.multiple_of(x * OWN, OWN), OWN), pl.ds(DT, DS)], load_sem.at[1]),
    ]
    for y in range(NYL):
        loads.append(pltpu.make_async_copy(tq_hbm.at[y, :, k], tq.at[:, y], load_sem.at[2 + y]))
        loads.append(pltpu.make_async_copy(sq_hbm.at[y, :, k], sq.at[:, y], load_sem.at[4 + y]))
    for load in loads:
        load.start()

    barrier = pltpu.get_barrier_semaphore()
    for device in (right, left, across, sibling):
        pl.semaphore_signal(barrier, inc=1, device_id=device, device_id_type=MESH)

    def greet(i, carry):
        pl.semaphore_signal(barrier, inc=1, device_id=owner((me + i) % OWNERS), device_id_type=MESH)
        return carry

    lax.fori_loop(1, OWNERS, greet, 0)
    pl.semaphore_wait(barrier, 4 + OWNERS - 1)
    loads[0].wait()
    loads[1].wait()

    sent = []

    def message(src, dst, number, device):
        return pltpu.make_async_remote_copy(
            src_ref=src, dst_ref=dst, send_sem=send_sem.at[number], recv_sem=recv_sem.at[number],
            device_id=device, device_id_type=MESH,
        )

    def send(src, dst, number, device):
        copy = message(src, dst, number, device)
        copy.start()
        sent.append(copy)

    def received(ref, number):
        message(ref, ref, number, sibling).wait_recv()

    def block(k_, h_, x_, part=None):
        start, size = (0, OWN) if part is None else (part * HALF, HALF)
        return pbuf.at[k_, h_, pl.ds(pl.multiple_of(x_ * OWN + start, size), size), :]

    def spread(ref, number, device):
        send(ref, ref, number, device)

    spread(block(k, yh, x), TO_YH, across)
    spread(block(k, yh, x), TO_RIGHT, right)
    spread(block(k, yh, x), TO_LEFT, left)
    spread(block(k, yh, x), SIB, sibling)

    def pass_on(h, to_right, to_left, on_right, on_left, sib):
        received(block(k, h, x_l), to_right)
        spread(block(k, h, x_l, 0), on_right, right)
        spread(block(k, h, x_l), sib, sibling)
        received(block(k, h, x_r), to_left)
        spread(block(k, h, x_r, 1), on_left, left)
        spread(block(k, h, x_r), sib + 1, sibling)

    def last_on(h, on_right, on_left, sib):
        received(block(k, h, x_o, 0), on_right)
        received(block(k, h, x_o, 1), on_left)
        spread(block(k, h, x_o), sib, sibling)

    def from_sibling(h, xs_and_numbers):
        for x_, number in xs_and_numbers:
            received(block(ok, h, x_), number)

    pass_on(yh, TO_RIGHT, TO_LEFT, ON_RIGHT, ON_LEFT, SIB + 1)
    received(block(k, oh, x), TO_YH)
    spread(block(k, oh, x), TO_RIGHT2, right)
    spread(block(k, oh, x), TO_LEFT2, left)
    spread(block(k, oh, x), SIB + 4, sibling)
    last_on(yh, ON_RIGHT, ON_LEFT, SIB + 3)

    for load in loads[2:]:
        load.wait()

    def scores(k_, h_):
        b = k_ * NYH + h_
        spt[b] = pbuf[k_, h_, :, DT:].T

        def tile(n, carry):
            t = nt(pbuf[k_, h_, :, :DT], tq[n].reshape(GROUP, DT)) * t_scale
            s = nt(pbuf[k_, h_, :, DT:], sq[n].reshape(GROUP, DS)) * s_scale
            t_max = jnp.max(t, axis=0, keepdims=True)
            s_max = jnp.max(s, axis=0, keepdims=True)
            t_weight = jnp.exp(t - t_max)
            s_weight = jnp.exp(s - s_max)
            tw[n, b] = t_weight
            sw[n, b] = s_weight
            t_sum = jnp.sum(t_weight, axis=0, keepdims=True)
            s_sum = jnp.sum(s_weight, axis=0, keepdims=True)
            cross = jnp.sum(t_weight * (t - s), axis=0, keepdims=True)
            stat[n, b] = jnp.concatenate([t_max, t_sum, s_max, s_sum, cross, cross, cross, cross], axis=0)
            return carry

        lax.fori_loop(0, NZ, tile, 0)

    scores(k, yh)
    pass_on(oh, TO_RIGHT2, TO_LEFT2, ON_RIGHT2, ON_LEFT2, SIB + 5)
    from_sibling(yh, [(x, SIB), (x_l, SIB + 1), (x_r, SIB + 2), (x_o, SIB + 3)])
    scores(ok, yh)
    last_on(oh, ON_RIGHT2, ON_LEFT2, SIB + 7)
    scores(k, oh)
    from_sibling(oh, [(x, SIB + 4), (x_l, SIB + 5), (x_r, SIB + 6), (x_o, SIB + 7)])
    scores(ok, oh)

    def joined(parts):
        t_max = functools.reduce(jnp.maximum, [p[0:1] for p in parts])
        s_max = functools.reduce(jnp.maximum, [p[2:3] for p in parts])
        t_in = [jnp.exp(p[0:1] - t_max) for p in parts]
        s_in = [jnp.exp(p[2:3] - s_max) for p in parts]
        t_sum = functools.reduce(jnp.add, [p[1:2] * w for p, w in zip(parts, t_in)])
        s_sum = functools.reduce(jnp.add, [p[3:4] * w for p, w in zip(parts, s_in)])
        cross = functools.reduce(jnp.add, [p[4:5] * w for p, w in zip(parts, t_in)])
        return t_max, t_sum, s_max, s_sum, cross

    for n in range(NZ):
        t_max, t_sum, s_max, s_sum, cross = joined([stat[n, b] for b in range(NCORE * NYH)])
        whole = jnp.concatenate([t_max, t_sum, s_max, s_sum, cross, cross, cross, cross], axis=0)
        for y in range(NYL):
            stat_send[y * NZ + n] = whole[:, y * ROWS:(y + 1) * ROWS]
    stat_recv[me] = stat_send[me]

    def stat_copy(m_to, m_slot):
        return pltpu.make_async_remote_copy(
            src_ref=stat_send.at[m_to], dst_ref=stat_recv.at[m_slot],
            send_sem=st_send_sem.at[m_to], recv_sem=st_recv_sem.at[m_slot],
            device_id=owner(m_to), device_id_type=MESH,
        )

    def res_copy(m_to, m_slot):
        return pltpu.make_async_remote_copy(
            src_ref=res_recv.at[m_slot], dst_ref=res_recv.at[m_slot],
            send_sem=rs_send_sem.at[m_to], recv_sem=rs_recv_sem.at[m_slot],
            device_id=owner(m_to), device_id_type=MESH,
        )

    def each_other(step):
        def body(i, carry):
            step((me + i) % OWNERS)
            return carry

        lax.fori_loop(1, OWNERS, body, 0)

    each_other(lambda m: stat_copy(m, me).start())
    each_other(lambda m: stat_copy(m, m).wait_recv())
    t_max, t_sum, s_max, s_sum, cross = joined([stat_recv[m] for m in range(OWNERS)])
    div_out[...] = cross / t_sum - (t_max + jnp.log(t_sum)) + (s_max + jnp.log(s_sum))
    t_in, s_in = s_scale / t_sum, s_scale / s_sum
    res_recv[me] = jnp.concatenate([t_max, t_in, s_max, s_in, t_in, t_in, t_in, t_in], axis=0)
    each_other(lambda m: res_copy(m, me).start())
    each_other(lambda m: res_copy(m, m).wait_recv())

    def query_part(n):
        res = jnp.concatenate([res_recv[n], res_recv[NZ + n]], axis=1)
        total = None
        for b in range(NCORE * NYH):
            st = stat[n, b]
            t_in = jnp.exp(st[0:1] - res[0:1]) * res[1:2]
            s_in = jnp.exp(st[2:3] - res[2:3]) * res[3:4]
            grad = (sw[n, b] * s_in - tw[n, b] * t_in).astype(BF16)
            gt[n, b] = grad
            term = nn(spt[b], grad)
            total = term if total is None else total + term
        return total

    HD = DS // 2
    far = query_part((z + 4) % NZ).astype(BF16)
    ring_half[...] = far
    send(ring_half.at[pl.ds(0, HD)], ring_recv_r.at[0, pl.ds(0, HD)], RING_R, up)
    send(ring_half.at[pl.ds(HD, HD)], ring_recv_l.at[0, pl.ds(HD, HD)], RING_L, down)
    for away in (3, 2, 1):
        gq[(z + away) % NZ] = query_part((z + away) % NZ)
        gq[(z + NZ - away) % NZ] = query_part((z + NZ - away) % NZ)
    gq[z] = query_part(z)

    def ring_step(step):
        n_r, n_l = (z + 4 - step) % NZ, (z + NZ - 4 + step) % NZ
        rows_r, rows_l = (pl.ds(0, HD), pl.ds(HD, HD)) if step == 1 else (pl.ds(0, DS), pl.ds(0, DS))
        received(ring_recv_r.at[step - 1, rows_r], RING_R + step - 1)
        if step == 1:
            ring_send_r[0, 0:HD] = (gq[n_r, 0:HD] + ring_recv_r[0, 0:HD].astype(F32)).astype(BF16)
            ring_send_r[0, HD:] = gq[n_r, HD:].astype(BF16)
        else:
            ring_send_r[step - 1] = (gq[n_r] + ring_recv_r[step - 1].astype(F32)).astype(BF16)
        send(ring_send_r.at[step - 1], ring_recv_r.at[step], RING_R + step, up)
        received(ring_recv_l.at[step - 1, rows_l], RING_L + step - 1)
        if step == 1:
            ring_send_l[0, HD:] = (gq[n_l, HD:] + ring_recv_l[0, HD:].astype(F32)).astype(BF16)
            ring_send_l[0, 0:HD] = gq[n_l, 0:HD].astype(BF16)
        else:
            ring_send_l[step - 1] = (gq[n_l] + ring_recv_l[step - 1].astype(F32)).astype(BF16)
        send(ring_send_l.at[step - 1], ring_recv_l.at[step], RING_L + step, down)

    def passage_part(k_, h_):
        b = k_ * NYH + h_
        total = None
        for n in range(NZ):
            term = nn(gt[n, b], sq[n].reshape(GROUP, DS))
            total = term if total is None else total + term
        return total

    for h in range(NYH):
        gps_send[h] = passage_part(ok, h).astype(gps_send.dtype)
    send(gps_send, gps_recv, GP_SIB, sibling)
    ring_step(1)
    for h in range(NYH):
        gp[h] = passage_part(k, h)
    received(gps_recv, GP_SIB)
    for h in range(NYH):
        gp[h] = gp[h] + gps_recv[h].astype(F32)

    def own_rows(x_):
        return pl.ds(pl.multiple_of(x_ * OWN, OWN), OWN)

    for h in range(NYH):
        gp1_send_h = gp[h, own_rows(x_o)].astype(gp2_send.dtype)
        gp2_send[2, h] = gp1_send_h
    send(gp2_send.at[2, 0], gp1_recv.at[0], GP_R1, right)
    send(gp2_send.at[2, 1], gp1_recv.at[1], GP_L1, left)
    ring_step(2)
    received(gp1_recv.at[0], GP_R1)
    gp2_send[0, 0] = (gp[0, own_rows(x_r)] + gp1_recv[0].astype(F32)).astype(gp2_send.dtype)
    gp2_send[0, 1] = gp[1, own_rows(x_r)].astype(gp2_send.dtype)
    send(gp2_send.at[0], gp2_recv.at[0], GP_R2, right)
    received(gp1_recv.at[1], GP_L1)
    gp2_send[1, 0] = gp[0, own_rows(x_l)].astype(gp2_send.dtype)
    gp2_send[1, 1] = (gp[1, own_rows(x_l)] + gp1_recv[1].astype(F32)).astype(gp2_send.dtype)
    send(gp2_send.at[1], gp2_recv.at[1], GP_L2, left)
    ring_step(3)
    received(gp2_recv.at[0], GP_R2)
    received(gp2_recv.at[1], GP_L2)

    def x_total(h):
        return gp[h, own_rows(x)] + gp2_recv[0, h].astype(F32) + gp2_recv[1, h].astype(F32)

    gp3_send[...] = x_total(oh).astype(gp3_send.dtype)
    send(gp3_send, gp3_recv, GP_YH, across)

    received(ring_recv_r.at[3], RING_R + 3)
    received(ring_recv_l.at[3], RING_L + 3)
    gq[z] = gq[z] + ring_recv_r[3].astype(F32) + ring_recv_l[3].astype(F32)
    y_send[...] = jnp.where(yl == 0, gq[z, :, ROWS:], gq[z, :, :ROWS]).astype(BF16)
    send(y_send, y_recv, Y_PAIR, y_mate)
    received(gp3_recv, GP_YH)
    gp_out[...] = x_total(yh) + gp3_recv[...].astype(F32)
    received(y_recv, Y_PAIR)
    mine = jnp.where(yl == 0, gq[z, :, :ROWS], gq[z, :, ROWS:]) + y_recv[...].astype(F32)
    gq_out[...] = mine.T

    for copy in sent:
        copy.wait_send()
    each_other(lambda m: stat_copy(m, me).wait_send())
    each_other(lambda m: res_copy(m, me).wait_send())


def local(teacher_query, student_query, teacher_passages, student_passages):
    blocks = NYL, NZ, NCORE, ROWS
    gp_type = F32
    hbm = pl.BlockSpec(memory_space=pl.ANY)
    vmem = pl.BlockSpec(memory_space=pltpu.VMEM)
    grad_query, grad_passage, divergence = pl.pallas_call(
        kernel,
        out_shape=(
            jax.ShapeDtypeStruct((ROWS, DS), F32),
            jax.ShapeDtypeStruct((OWN, DS), F32),
            jax.ShapeDtypeStruct((1, ROWS), F32),
        ),
        in_specs=[hbm] * 4,
        out_specs=(vmem,) * 3,
        scratch_shapes=[
            pltpu.VMEM((NZ, NYL, ROWS, DT), BF16),
            pltpu.VMEM((NZ, NYL, ROWS, DS), BF16),
            pltpu.VMEM((NCORE, NYH, BATCH, DT + DS), BF16),
            pltpu.VMEM((NCORE * NYH, DS, BATCH), BF16),
            pltpu.VMEM((NZ, NCORE * NYH, BATCH, GROUP), F32),
            pltpu.VMEM((NZ, NCORE * NYH, BATCH, GROUP), F32),
            pltpu.VMEM((NZ, NCORE * NYH, BATCH, GROUP), BF16),
            pltpu.VMEM((NZ, NCORE * NYH, 8, GROUP), F32),
            pltpu.VMEM((NZ, DS, GROUP), F32),
            pltpu.VMEM((OWNERS, 8, ROWS), F32),
            pltpu.VMEM((OWNERS, 8, ROWS), F32),
            pltpu.VMEM((OWNERS, 8, ROWS), F32),
            pltpu.VMEM((3, DS, GROUP), BF16),
            pltpu.VMEM((4, DS, GROUP), BF16),
            pltpu.VMEM((3, DS, GROUP), BF16),
            pltpu.VMEM((4, DS, GROUP), BF16),
            pltpu.VMEM((DS, GROUP), BF16),
            pltpu.VMEM((DS, ROWS), BF16),
            pltpu.VMEM((DS, ROWS), BF16),
            pltpu.VMEM((NYH, BATCH, DS), F32),
            pltpu.VMEM((NYH, BATCH, DS), gp_type),
            pltpu.VMEM((NYH, BATCH, DS), gp_type),
            pltpu.VMEM((NYH, OWN, DS), gp_type),
            pltpu.VMEM((3, NYH, OWN, DS), gp_type),
            pltpu.VMEM((2, NYH, OWN, DS), gp_type),
            pltpu.VMEM((OWN, DS), gp_type),
            pltpu.VMEM((OWN, DS), gp_type),
            pltpu.SemaphoreType.DMA((6,)),
            pltpu.SemaphoreType.DMA((MESSAGES,)),
            pltpu.SemaphoreType.DMA((MESSAGES,)),
            pltpu.SemaphoreType.DMA((OWNERS,)),
            pltpu.SemaphoreType.DMA((OWNERS,)),
            pltpu.SemaphoreType.DMA((OWNERS,)),
            pltpu.SemaphoreType.DMA((OWNERS,)),
        ],
        compiler_params=pltpu.CompilerParams(
            collective_id=0, has_side_effects=True, vmem_limit_bytes=60 * 1024 * 1024
        ),
    )(
        teacher_query.reshape(*blocks, DT),
        student_query.reshape(*blocks, DS),
        teacher_passages,
        student_passages,
    )
    return divergence.reshape(ROWS), grad_query, grad_passage


def solution(mesh):
    return jax.shard_map(
        local,
        mesh=mesh,
        in_specs=(
            P("query", None),
            P("query", None),
            P(("query", "corpus"), None),
            P(("query", "corpus"), None),
        ),
        out_specs=(
            P(("query", "corpus")),
            P(("query", "corpus"), None),
            P(("query", "corpus"), None),
        ),
        check_vma=False,
    )
```

```python
import functools
import math

import jax
import jax.numpy as jnp
from jax import lax
from jax.experimental import pallas as pl
from jax.experimental.pallas import tpu as pltpu
from jax.sharding import PartitionSpec as P

NX, NYH, NYL, NZ, NCORE = 4, 2, 2, 8, 2
OWN = 64
ROWS = 128
DT, DS = 1024, 384
BATCHES = 4
BATCH = 256
GROUP = NYL * ROWS
OWNERS = NYL * NZ
HALF = OWN // 2
ZF = 192
YF = DS - ZF
LOG2E = math.log2(math.e)
LN2 = math.log(2.0)
F32, BF16 = jnp.float32, jnp.bfloat16
MESH = pl.DeviceIdType.MESH

SELF, LEFT, RIGHT, FAR = 0, 1, 2, 3


def place(h, where, core):
    if where == SELF:
        return 0, core * 2 + h
    if where == FAR:
        return 3, core * 2 + h
    return 1 + h, core * 2 + (where - LEFT)


def nt(a, b):
    return lax.dot_general(a, b, (((1,), (1,)), ((), ())), preferred_element_type=F32)


def nn(a, b):
    return lax.dot_general(a, b, (((1,), (0,)), ((), ())), preferred_element_type=F32)


class Messages:
    def __init__(self):
        self.numbers = {}

    def __call__(self, name):
        return self.numbers.setdefault(name, len(self.numbers))


MESSAGES = 80
VMEM_BYTES = 60 * 1024 * 1024


def kernel(
    tq_hbm, sq_hbm, tp_hbm, sp_hbm,
    gq_out, gp_out, div_out,
    tq, sq, pbuf, spt, tw, sw, gt, stat, gq,
    stat_send, stat_recv, res_recv,
    z_send_r, z_recv_r, z_send_l, z_recv_l, z_pair_send, z_pair_recv,
    y_pair_send, y_pair_recv, y_send_r, y_recv_r, y_send_l, y_recv_l,
    gp, gps_send, gps_recv, gp1_send, gp1_recv, gp2_send, gp2_recv, gp3_send, gp3_recv,
    load_sem, send_sem, recv_sem, st_send_sem, st_recv_sem, rs_send_sem, rs_recv_sem,
):
    t_scale = DT ** (-0.5) * LOG2E
    s_scale = DS ** (-0.5) * LOG2E
    factor = DS ** (-0.5)
    q = lax.axis_index("query")
    c = lax.axis_index("corpus")
    x, yh = q // NYH, q % NYH
    yl, z, k = c // (NZ * NCORE), (c // NCORE) % NZ, c % NCORE
    me = yl * NZ + z

    def at(x_, yh_, yl_, z_, k_):
        return (x_ * NYH + yh_, (yl_ * NZ + z_) * NCORE + k_)

    right, left = at((x + 1) % NX, yh, yl, z, k), at((x + NX - 1) % NX, yh, yl, z, k)
    across = at(x, 1 - yh, yl, z, k)
    sibling = at(x, yh, yl, z, 1 - k)
    up, down = at(x, yh, yl, (z + 1) % NZ, k), at(x, yh, yl, (z + NZ - 1) % NZ, k)
    y_mate = at(x, yh, 1 - yl, z, k)

    def owner(m):
        return at(x, yh, m // NZ, m % NZ, k)

    def slot(h, where, core, half=None):
        b, s = place(h, where, core)
        if half is None:
            return pbuf.at[b, s]
        return pbuf.at[b, s, pl.ds(half * HALF, HALF)]

    loads = [
        pltpu.make_async_copy(tp_hbm, pbuf.at[0, 0, :, pl.ds(0, DT)], load_sem.at[0]),
        pltpu.make_async_copy(sp_hbm, pbuf.at[0, 0, :, pl.ds(DT, DS)], load_sem.at[1]),
    ]
    for y in range(NYL):
        loads.append(pltpu.make_async_copy(tq_hbm.at[y, :, k], tq.at[:, y], load_sem.at[2 + y]))
        loads.append(pltpu.make_async_copy(sq_hbm.at[y, :, k], sq.at[:, y], load_sem.at[4 + y]))
    for load in loads:
        load.start()

    barrier = pltpu.get_barrier_semaphore()
    for device in (right, left, across, sibling):
        pl.semaphore_signal(barrier, inc=1, device_id=device, device_id_type=MESH)

    def greet(i, carry):
        pl.semaphore_signal(barrier, inc=1, device_id=owner((me + i) % OWNERS), device_id_type=MESH)
        return carry

    lax.fori_loop(1, OWNERS, greet, 0)
    pl.semaphore_wait(barrier, 4 + OWNERS - 1)
    loads[0].wait()
    loads[1].wait()

    number = Messages()
    sent = []

    def message(src, dst, name, device):
        i = number(name)
        return pltpu.make_async_remote_copy(
            src_ref=src, dst_ref=dst, send_sem=send_sem.at[i], recv_sem=recv_sem.at[i],
            device_id=device, device_id_type=MESH,
        )

    def send(src, dst, name, device):
        copy = message(src, dst, name, device)
        copy.start()
        sent.append(copy)

    def received(ref, name):
        message(ref, ref, name, sibling).wait_recv()

    def to_sides(h):
        for first in (0, 1):
            half = first
            send(slot(h, SELF, 0, half), slot(h, LEFT, 0, half), ("p", h, LEFT, half), right)
            half = 1 - first
            send(slot(h, SELF, 0, half), slot(h, RIGHT, 0, half), ("p", h, RIGHT, half), left)

    def to_sibling(h, where):
        send(slot(h, where, 0), slot(h, where, 1), ("sib", h, where), sibling)

    def side_halves_on(h):
        received(slot(h, LEFT, 0, 0), ("p", h, LEFT, 0))
        send(slot(h, LEFT, 0, 0), slot(h, FAR, 0, 0), ("p", h, FAR, 0), right)
        received(slot(h, RIGHT, 0, 1), ("p", h, RIGHT, 1))
        send(slot(h, RIGHT, 0, 1), slot(h, FAR, 0, 1), ("p", h, FAR, 1), left)

    def sides_to_sibling(h):
        received(slot(h, LEFT, 0, 1), ("p", h, LEFT, 1))
        to_sibling(h, LEFT)
        received(slot(h, RIGHT, 0, 0), ("p", h, RIGHT, 0))
        to_sibling(h, RIGHT)

    def far_to_sibling(h):
        received(slot(h, FAR, 0, 0), ("p", h, FAR, 0))
        received(slot(h, FAR, 0, 1), ("p", h, FAR, 1))
        to_sibling(h, FAR)

    def from_sibling(h, where):
        received(slot(h, where, 1), ("sib", h, where))

    for half in (0, 1):
        send(slot(0, SELF, 0, half), slot(1, SELF, 0, half), ("p", 1, SELF, half), across)
    to_sides(0)
    to_sibling(0, SELF)

    def scores(b, first, count):
        def tile(n, carry):
            passages = pbuf[b].reshape(BATCH, DT + DS)
            t = nt(passages[:, :DT], tq[n].reshape(GROUP, DT)) * t_scale
            s = nt(passages[:, DT:], sq[n].reshape(GROUP, DS)) * s_scale
            t_max = jnp.max(t, axis=0, keepdims=True)
            s_max = jnp.max(s, axis=0, keepdims=True)
            t_weight = jnp.exp2(t - t_max)
            s_weight = jnp.exp2(s - s_max)
            tw[n, b] = t_weight
            sw[n, b] = s_weight
            t_sum = jnp.sum(t_weight, axis=0, keepdims=True)
            s_sum = jnp.sum(s_weight, axis=0, keepdims=True)
            cross = jnp.sum(t_weight * (t - s), axis=0, keepdims=True)
            stat[n, b] = jnp.concatenate([t_max, t_sum, s_max, s_sum, cross, cross, cross, cross], axis=0)
            return carry

        lax.fori_loop(first, first + count, tile, 0, unroll=2)

    def turn(b):
        spt[b] = pbuf[b].reshape(BATCH, DT + DS)[:, DT:].T

    side_halves_on(0)
    sides_to_sibling(0)
    for half in (0, 1):
        received(slot(1, SELF, 0, half), ("p", 1, SELF, half))
    to_sides(1)
    to_sibling(1, SELF)
    for load in loads[2:]:
        load.wait()
    from_sibling(0, LEFT)
    from_sibling(0, RIGHT)
    scores(1, 0, 4)
    far_to_sibling(0)
    scores(1, 4, 4)
    side_halves_on(1)
    from_sibling(0, SELF)
    from_sibling(1, SELF)
    scores(0, 0, 4)
    sides_to_sibling(1)
    scores(0, 4, 4)
    from_sibling(1, LEFT)
    from_sibling(1, RIGHT)
    scores(2, 0, 4)
    far_to_sibling(1)
    scores(2, 4, 4)
    from_sibling(0, FAR)
    from_sibling(1, FAR)

    def joined(parts):
        t_max = functools.reduce(jnp.maximum, [p[0:1] for p in parts])
        s_max = functools.reduce(jnp.maximum, [p[2:3] for p in parts])
        t_in = [jnp.exp2(p[0:1] - t_max) for p in parts]
        s_in = [jnp.exp2(p[2:3] - s_max) for p in parts]
        t_sum = functools.reduce(jnp.add, [p[1:2] * w for p, w in zip(parts, t_in)])
        s_sum = functools.reduce(jnp.add, [p[3:4] * w for p, w in zip(parts, s_in)])
        cross = functools.reduce(jnp.add, [p[4:5] * w for p, w in zip(parts, t_in)])
        return t_max, t_sum, s_max, s_sum, cross

    def stat_copy(m_to, m_slot):
        return pltpu.make_async_remote_copy(
            src_ref=stat_send.at[m_to], dst_ref=stat_recv.at[m_slot],
            send_sem=st_send_sem.at[m_to], recv_sem=st_recv_sem.at[m_slot],
            device_id=owner(m_to), device_id_type=MESH,
        )

    def res_copy(m_to, m_slot):
        return pltpu.make_async_remote_copy(
            src_ref=res_recv.at[m_slot], dst_ref=res_recv.at[m_slot],
            send_sem=rs_send_sem.at[m_to], recv_sem=rs_recv_sem.at[m_slot],
            device_id=owner(m_to), device_id_type=MESH,
        )

    def each_other(step):
        def body(i, carry):
            step((me + i) % OWNERS)
            return carry

        lax.fori_loop(1, OWNERS, body, 0)

    for first in (0, 4):
        scores(3, first, 4)
        for n in range(first, first + 4):
            t_max, t_sum, s_max, s_sum, cross = joined([stat[n, b] for b in range(BATCHES)])
            whole = jnp.concatenate([t_max, t_sum, s_max, s_sum, cross, cross, cross, cross], axis=0)
            for y in range(NYL):
                stat_send[y * NZ + n] = whole[:, y * ROWS:(y + 1) * ROWS]

        def leave(i, carry):
            m = (i // 4) * NZ + first + i % 4

            @pl.when(m != me)
            def _():
                stat_copy(m, me).start()

            return carry

        lax.fori_loop(0, 8, leave, 0)
    stat_recv[me] = stat_send[me]
    for b in range(BATCHES):
        turn(b)

    each_other(lambda m: stat_copy(m, m).wait_recv())
    t_max, t_sum, s_max, s_sum, cross = joined([stat_recv[m] for m in range(OWNERS)])
    t_in, s_in = factor / t_sum, factor / s_sum
    res_recv[me] = jnp.concatenate([t_max, t_in, s_max, s_in, t_in, t_in, t_in, t_in], axis=0)
    each_other(lambda m: res_copy(m, me).start())
    div_out[...] = cross * LN2 / t_sum - (t_max * LN2 + jnp.log(t_sum)) + (s_max * LN2 + jnp.log(s_sum))
    each_other(lambda m: res_copy(m, m).wait_recv())

    def group(away):
        return (z + NZ + away) % NZ

    def query_part(away):
        n = group(away)
        res = jnp.concatenate([res_recv[n], res_recv[NZ + n]], axis=1)
        total = None
        for b in range(BATCHES):
            st = stat[n, b]
            t_in = jnp.exp2(st[0:1] - res[0:1]) * res[1:2]
            s_in = jnp.exp2(st[2:3] - res[2:3]) * res[3:4]
            grad = (sw[n, b] * s_in - tw[n, b] * t_in).astype(BF16)
            lanes = pl.ds(pl.multiple_of(n * GROUP, GROUP), GROUP)
            gt[0, b, :, lanes] = grad[:BATCH // 2]
            gt[1, b, :, lanes] = grad[BATCH // 2:]
            term = nn(spt[b], grad)
            total = term if total is None else total + term
        gq[n, 0] = total[:, :ROWS]
        gq[n, 1] = total[:, ROWS:]
        i = away + 3
        y_pair_send[i] = gq[n, 1 - yl, ZF:].astype(BF16)
        send(y_pair_send.at[i], y_pair_recv.at[i], ("y pair", i), y_mate)

    def z_part(away):
        return gq[group(away), :, :ZF]

    def y_part(away):
        i = away + 3
        received(y_pair_recv.at[i], ("y pair", i))
        return gq[group(away), yl, ZF:] + y_pair_recv[i].astype(F32)

    ZH, YH = ZF // 2, YF // 2

    def z_start():
        far = z_part(4).astype(BF16)
        z_send_r[0] = far
        send(z_send_r.at[0, :, pl.ds(0, ZH)], z_recv_r.at[0, :, pl.ds(0, ZH)], ("zr", 0), up)
        send(z_send_r.at[0, :, pl.ds(ZH, ZH)], z_recv_l.at[0, :, pl.ds(ZH, ZH)], ("zl", 0), down)

    def y_start():
        y_send_r[0] = y_part(4).astype(BF16)
        send(y_send_r.at[0, pl.ds(0, YH)], y_recv_r.at[0, pl.ds(0, YH)], ("yr", 0), up)
        send(y_send_r.at[0, pl.ds(YH, YH)], y_recv_l.at[0, pl.ds(YH, YH)], ("yl", 0), down)

    def z_step(step):
        if step == 1:
            mine = z_part(3)
            received(z_recv_r.at[0, :, pl.ds(0, ZH)], ("zr", 0))
            z_send_r[1, :, :ZH] = (mine[:, :ZH] + z_recv_r[0, :, :ZH].astype(F32)).astype(BF16)
            z_send_r[1, :, ZH:] = mine[:, ZH:].astype(BF16)
        else:
            received(z_recv_r.at[step - 1], ("zr", step - 1))
            z_send_r[step] = (z_part(4 - step) + z_recv_r[step - 1].astype(F32)).astype(BF16)
        send(z_send_r.at[step], z_recv_r.at[step], ("zr", step), up)
        if step == 1:
            mine = z_part(-3)
            received(z_recv_l.at[0, :, pl.ds(ZH, ZH)], ("zl", 0))
            z_send_l[1, :, :ZH] = mine[:, :ZH].astype(BF16)
            z_send_l[1, :, ZH:] = (mine[:, ZH:] + z_recv_l[0, :, ZH:].astype(F32)).astype(BF16)
        else:
            received(z_recv_l.at[step - 1], ("zl", step - 1))
            z_send_l[step] = (z_part(step - 4) + z_recv_l[step - 1].astype(F32)).astype(BF16)
        send(z_send_l.at[step], z_recv_l.at[step], ("zl", step), down)

    def y_step(step):
        mine = y_part(4 - step)
        if step == 1:
            received(y_recv_r.at[0, pl.ds(0, YH)], ("yr", 0))
            y_send_r[1, :YH] = (mine[:YH] + y_recv_r[0, :YH].astype(F32)).astype(BF16)
            y_send_r[1, YH:] = mine[YH:].astype(BF16)
        else:
            received(y_recv_r.at[step - 1], ("yr", step - 1))
            y_send_r[step] = (mine + y_recv_r[step - 1].astype(F32)).astype(BF16)
        send(y_send_r.at[step], y_recv_r.at[step], ("yr", step), up)
        mine = y_part(step - 4)
        if step == 1:
            received(y_recv_l.at[0, pl.ds(YH, YH)], ("yl", 0))
            y_send_l[1, :YH] = mine[:YH].astype(BF16)
            y_send_l[1, YH:] = (mine[YH:] + y_recv_l[0, YH:].astype(F32)).astype(BF16)
        else:
            received(y_recv_l.at[step - 1], ("yl", step - 1))
            y_send_l[step] = (mine + y_recv_l[step - 1].astype(F32)).astype(BF16)
        send(y_send_l.at[step], y_recv_l.at[step], ("yl", step), down)

    def passage_part(core):
        grads = gt[core].reshape(BATCHES * BATCH // 2, NZ * GROUP)
        return nn(grads, sq[...].reshape(NZ * GROUP, DS)).reshape(BATCHES, 2, OWN, DS)

    def gp_of(h, where):
        b, s = place(h, where, 0)
        return gp[b, s]

    query_part(4)
    z_start()
    query_part(3)
    query_part(-3)
    z_step(1)
    y_start()
    query_part(2)
    query_part(-2)
    query_part(1)
    query_part(-1)
    query_part(0)
    gps_send[...] = passage_part(1).astype(BF16)
    send(gps_send, gps_recv, "gp sibling", sibling)
    z_step(2)
    y_step(1)
    gp[...] = passage_part(0)
    z_step(3)
    received(gps_recv, "gp sibling")
    gp[...] = gp[...] + gps_recv[...].astype(F32)
    for h in range(NYH):
        gp1_send[h] = gp_of(h, FAR).astype(BF16)
    send(gp1_send.at[0], gp1_recv.at[0], ("gp", RIGHT, 1), right)
    send(gp1_send.at[1], gp1_recv.at[1], ("gp", LEFT, 1), left)
    y_step(2)
    received(gp1_recv.at[0], ("gp", RIGHT, 1))
    gp2_send[0, 0] = (gp_of(0, RIGHT) + gp1_recv[0].astype(F32)).astype(BF16)
    gp2_send[0, 1] = gp_of(1, RIGHT).astype(BF16)
    send(gp2_send.at[0], gp2_recv.at[0], ("gp", RIGHT, 2), right)
    received(gp1_recv.at[1], ("gp", LEFT, 1))
    gp2_send[1, 0] = gp_of(0, LEFT).astype(BF16)
    gp2_send[1, 1] = (gp_of(1, LEFT) + gp1_recv[1].astype(F32)).astype(BF16)
    send(gp2_send.at[1], gp2_recv.at[1], ("gp", LEFT, 2), left)
    y_step(3)
    received(z_recv_r.at[3], ("zr", 3))
    received(z_recv_l.at[3], ("zl", 3))
    for y in range(NYL):
        gq[z, y, :ZF] = gq[z, y, :ZF] + z_recv_r[3, y].astype(F32) + z_recv_l[3, y].astype(F32)
    z_pair_send[...] = gq[z, 1 - yl, :ZF].astype(BF16)
    send(z_pair_send, z_pair_recv, "z pair", y_mate)
    received(gp2_recv.at[0], ("gp", RIGHT, 2))
    received(gp2_recv.at[1], ("gp", LEFT, 2))

    def x_total(h):
        return gp_of(h, SELF) + gp2_recv[0, h].astype(F32) + gp2_recv[1, h].astype(F32)

    gp3_send[...] = x_total(1).astype(BF16)
    send(gp3_send, gp3_recv, "gp across", across)

    mine = y_part(0)
    received(y_recv_r.at[3], ("yr", 3))
    received(y_recv_l.at[3], ("yl", 3))
    gq_out[:, ZF:] = (mine + y_recv_r[3].astype(F32) + y_recv_l[3].astype(F32)).T
    received(z_pair_recv, "z pair")
    gq_out[:, :ZF] = (gq[z, yl, :ZF] + z_pair_recv[...].astype(F32)).T
    received(gp3_recv, "gp across")
    gp_out[...] = x_total(0) + gp3_recv[...].astype(F32)

    for copy in sent:
        copy.wait_send()
    each_other(lambda m: stat_copy(m, me).wait_send())
    each_other(lambda m: res_copy(m, me).wait_send())


def deliver(gq_in, gp_in, div_in, gq_out, gp_out, div_out, sem):
    pairs = ((gq_in, gq_out), (gp_in, gp_out), (div_in, div_out))
    copies = [pltpu.make_async_copy(src, dst, sem.at[i]) for i, (src, dst) in enumerate(pairs)]
    for copy in copies:
        copy.start()
    for copy in copies:
        copy.wait()


def local(teacher_query, student_query, teacher_passages, student_passages):
    blocks = NYL, NZ, NCORE, ROWS
    hbm = pl.BlockSpec(memory_space=pl.ANY)
    vmem = pl.BlockSpec(memory_space=pltpu.VMEM)
    outs = (
        jax.ShapeDtypeStruct((ROWS, DS), F32),
        jax.ShapeDtypeStruct((OWN, DS), F32),
        jax.ShapeDtypeStruct((1, ROWS), F32),
    )
    results = pl.pallas_call(
        kernel,
        out_shape=outs,
        in_specs=[hbm] * 4,
        out_specs=(vmem,) * 3,
        scratch_shapes=[
            pltpu.VMEM((NZ, NYL, ROWS, DT), BF16),
            pltpu.VMEM((NZ, NYL, ROWS, DS), BF16),
            pltpu.VMEM((BATCHES, BATCH // OWN, OWN, DT + DS), BF16),
            pltpu.VMEM((BATCHES, DS, BATCH), BF16),
            pltpu.VMEM((NZ, BATCHES, BATCH, GROUP), F32),
            pltpu.VMEM((NZ, BATCHES, BATCH, GROUP), F32),
            pltpu.VMEM((NCORE, BATCHES, BATCH // 2, NZ * GROUP), BF16),
            pltpu.VMEM((NZ, BATCHES, 8, GROUP), F32),
            pltpu.VMEM((NZ, NYL, DS, ROWS), F32),
            pltpu.VMEM((OWNERS, 8, ROWS), F32),
            pltpu.VMEM((OWNERS, 8, ROWS), F32),
            pltpu.VMEM((OWNERS, 8, ROWS), F32),
            pltpu.VMEM((4, NYL, ZF, ROWS), BF16),
            pltpu.VMEM((4, NYL, ZF, ROWS), BF16),
            pltpu.VMEM((4, NYL, ZF, ROWS), BF16),
            pltpu.VMEM((4, NYL, ZF, ROWS), BF16),
            pltpu.VMEM((ZF, ROWS), BF16),
            pltpu.VMEM((ZF, ROWS), BF16),
            pltpu.VMEM((NZ, YF, ROWS), BF16),
            pltpu.VMEM((NZ, YF, ROWS), BF16),
            pltpu.VMEM((4, YF, ROWS), BF16),
            pltpu.VMEM((4, YF, ROWS), BF16),
            pltpu.VMEM((4, YF, ROWS), BF16),
            pltpu.VMEM((4, YF, ROWS), BF16),
            pltpu.VMEM((BATCHES, 2, OWN, DS), F32),
            pltpu.VMEM((BATCHES, 2, OWN, DS), BF16),
            pltpu.VMEM((BATCHES, 2, OWN, DS), BF16),
            pltpu.VMEM((NYH, OWN, DS), BF16),
            pltpu.VMEM((NYH, OWN, DS), BF16),
            pltpu.VMEM((2, NYH, OWN, DS), BF16),
            pltpu.VMEM((2, NYH, OWN, DS), BF16),
            pltpu.VMEM((OWN, DS), BF16),
            pltpu.VMEM((OWN, DS), BF16),
            pltpu.SemaphoreType.DMA((6,)),
            pltpu.SemaphoreType.DMA((MESSAGES,)),
            pltpu.SemaphoreType.DMA((MESSAGES,)),
            pltpu.SemaphoreType.DMA((OWNERS,)),
            pltpu.SemaphoreType.DMA((OWNERS,)),
            pltpu.SemaphoreType.DMA((OWNERS,)),
            pltpu.SemaphoreType.DMA((OWNERS,)),
        ],
        compiler_params=pltpu.CompilerParams(
            collective_id=0, has_side_effects=True, vmem_limit_bytes=VMEM_BYTES
        ),
    )(
        teacher_query.reshape(*blocks, DT),
        student_query.reshape(*blocks, DS),
        teacher_passages,
        student_passages,
    )
    grad_query, grad_passage, divergence = pl.pallas_call(
        deliver,
        out_shape=outs,
        in_specs=[hbm] * 3,
        out_specs=(hbm,) * 3,
        scratch_shapes=[pltpu.SemaphoreType.DMA((3,))],
        compiler_params=pltpu.CompilerParams(vmem_limit_bytes=VMEM_BYTES),
    )(*results)
    return divergence.reshape(ROWS), grad_query, grad_passage


def solution(mesh):
    return jax.shard_map(
        local,
        mesh=mesh,
        in_specs=(
            P("query", None),
            P("query", None),
            P(("query", "corpus"), None),
            P(("query", "corpus"), None),
        ),
        out_specs=(
            P(("query", "corpus")),
            P(("query", "corpus"), None),
            P(("query", "corpus"), None),
        ),
        check_vma=False,
    )
```

```python
import functools
import math

import jax
import jax.numpy as jnp
from jax import lax
from jax.experimental import pallas as pl
from jax.experimental.pallas import tpu as pltpu
from jax.sharding import PartitionSpec as P

NX, NYH, NYL, NZ, NCORE = 4, 2, 2, 8, 2
OWN = 64
ROWS = 128
DT, DS = 1024, 384
BATCHES = 4
BATCH = 256
GROUP = NYL * ROWS
OWNERS = NYL * NZ
HALF = OWN // 2
ZF = 192
YF = DS - ZF
LOG2E = math.log2(math.e)
LN2 = math.log(2.0)
F32, BF16 = jnp.float32, jnp.bfloat16
MESH = pl.DeviceIdType.MESH

SELF, LEFT, RIGHT, FAR = 0, 1, 2, 3


def place(h, where, core):
    if where == SELF:
        return 0, core * 2 + h
    if where == FAR:
        return 3, core * 2 + h
    return 1 + h, core * 2 + (where - LEFT)


def nn(a, b):
    return lax.dot_general(a, b, (((1,), (0,)), ((), ())), preferred_element_type=F32)


class Messages:
    def __init__(self):
        self.numbers = {}

    def __call__(self, name):
        return self.numbers.setdefault(name, len(self.numbers))


MESSAGES = 80
VMEM_BYTES = 60 * 1024 * 1024


def kernel(
    tq_hbm, sq_hbm, tp_hbm, sp_hbm,
    gq_out, gp_out, div_out,
    tq, sq, tqt, sqt, pbuf, spt, tw, sw, gt, stat, gq,
    stat_send, stat_recv, res_recv,
    z_send_r, z_recv_r, z_send_l, z_recv_l, z_pair_send, z_pair_recv,
    y_pair_send, y_pair_recv, y_send_r, y_recv_r, y_send_l, y_recv_l,
    gp, gps_send, gps_recv, gp1_send, gp1_recv, gp2_send, gp2_recv, gp3_send, gp3_recv,
    load_sem, send_sem, recv_sem, st_send_sem, st_recv_sem, rs_send_sem, rs_recv_sem,
):
    t_scale = DT ** (-0.5) * LOG2E
    s_scale = DS ** (-0.5) * LOG2E
    factor = DS ** (-0.5)
    q = lax.axis_index("query")
    c = lax.axis_index("corpus")
    x, yh = q // NYH, q % NYH
    yl, z, k = c // (NZ * NCORE), (c // NCORE) % NZ, c % NCORE
    me = yl * NZ + z

    def at(x_, yh_, yl_, z_, k_):
        return (x_ * NYH + yh_, (yl_ * NZ + z_) * NCORE + k_)

    right, left = at((x + 1) % NX, yh, yl, z, k), at((x + NX - 1) % NX, yh, yl, z, k)
    across = at(x, 1 - yh, yl, z, k)
    sibling = at(x, yh, yl, z, 1 - k)
    up, down = at(x, yh, yl, (z + 1) % NZ, k), at(x, yh, yl, (z + NZ - 1) % NZ, k)
    y_mate = at(x, yh, 1 - yl, z, k)

    def owner(m):
        return at(x, yh, m // NZ, m % NZ, k)

    def slot(h, where, core, half=None):
        b, s = place(h, where, core)
        if half is None:
            return pbuf.at[b, s]
        return pbuf.at[b, s, pl.ds(half * HALF, HALF)]

    loads = [
        pltpu.make_async_copy(tp_hbm, pbuf.at[0, 0, :, pl.ds(0, DT)], load_sem.at[0]),
        pltpu.make_async_copy(sp_hbm, pbuf.at[0, 0, :, pl.ds(DT, DS)], load_sem.at[1]),
    ]
    for y in range(NYL):
        loads.append(pltpu.make_async_copy(tq_hbm.at[y, :, k], tq.at[:, y], load_sem.at[2 + y]))
        loads.append(pltpu.make_async_copy(sq_hbm.at[y, :, k], sq.at[:, y], load_sem.at[4 + y]))
    for load in loads:
        load.start()

    barrier = pltpu.get_barrier_semaphore()
    for device in (right, left, across, sibling):
        pl.semaphore_signal(barrier, inc=1, device_id=device, device_id_type=MESH)

    def greet(i, carry):
        pl.semaphore_signal(barrier, inc=1, device_id=owner((me + i) % OWNERS), device_id_type=MESH)
        return carry

    lax.fori_loop(1, OWNERS, greet, 0)
    pl.semaphore_wait(barrier, 4 + OWNERS - 1)
    loads[0].wait()
    loads[1].wait()

    number = Messages()
    sent = []

    def message(src, dst, name, device):
        i = number(name)
        return pltpu.make_async_remote_copy(
            src_ref=src, dst_ref=dst, send_sem=send_sem.at[i], recv_sem=recv_sem.at[i],
            device_id=device, device_id_type=MESH,
        )

    def send(src, dst, name, device):
        copy = message(src, dst, name, device)
        copy.start()
        sent.append(copy)

    def received(ref, name):
        message(ref, ref, name, sibling).wait_recv()

    def to_sides(h):
        for first in (0, 1):
            half = first
            send(slot(h, SELF, 0, half), slot(h, LEFT, 0, half), ("p", h, LEFT, half), right)
            half = 1 - first
            send(slot(h, SELF, 0, half), slot(h, RIGHT, 0, half), ("p", h, RIGHT, half), left)

    def to_sibling(h, where):
        send(slot(h, where, 0), slot(h, where, 1), ("sib", h, where), sibling)

    def side_halves_on(h):
        received(slot(h, LEFT, 0, 0), ("p", h, LEFT, 0))
        send(slot(h, LEFT, 0, 0), slot(h, FAR, 0, 0), ("p", h, FAR, 0), right)
        received(slot(h, RIGHT, 0, 1), ("p", h, RIGHT, 1))
        send(slot(h, RIGHT, 0, 1), slot(h, FAR, 0, 1), ("p", h, FAR, 1), left)

    def sides_to_sibling(h):
        received(slot(h, LEFT, 0, 1), ("p", h, LEFT, 1))
        to_sibling(h, LEFT)
        received(slot(h, RIGHT, 0, 0), ("p", h, RIGHT, 0))
        to_sibling(h, RIGHT)

    def far_to_sibling(h):
        received(slot(h, FAR, 0, 0), ("p", h, FAR, 0))
        received(slot(h, FAR, 0, 1), ("p", h, FAR, 1))
        to_sibling(h, FAR)

    def from_sibling(h, where):
        received(slot(h, where, 1), ("sib", h, where))

    for half in (0, 1):
        send(slot(0, SELF, 0, half), slot(1, SELF, 0, half), ("p", 1, SELF, half), across)
    to_sides(0)
    to_sibling(0, SELF)

    def scores(b, first, count):
        def tile(n, carry):
            passages = pbuf[b].reshape(BATCH, DT + DS)
            t = nn(passages[:, :DT], tqt[n]) * t_scale
            s = nn(passages[:, DT:], sqt[n]) * s_scale
            t_max = jnp.max(t, axis=0, keepdims=True)
            s_max = jnp.max(s, axis=0, keepdims=True)
            t_weight = jnp.exp2(t - t_max)
            s_weight = jnp.exp2(s - s_max)
            tw[n, b] = t_weight
            sw[n, b] = s_weight
            t_sum = jnp.sum(t_weight, axis=0, keepdims=True)
            s_sum = jnp.sum(s_weight, axis=0, keepdims=True)
            cross = jnp.sum(t_weight * (t - s), axis=0, keepdims=True)
            stat[n, b] = jnp.concatenate([t_max, t_sum, s_max, s_sum, cross, cross, cross, cross], axis=0)
            return carry

        lax.fori_loop(first, first + count, tile, 0, unroll=2)

    def turn(b):
        spt[b] = pbuf[b].reshape(BATCH, DT + DS)[:, DT:].T

    def turn_queries(first, count):
        def body(n, carry):
            tqt[n] = tq[n].reshape(GROUP, DT).T
            sqt[n] = sq[n].reshape(GROUP, DS).T
            return carry

        lax.fori_loop(first, first + count, body, 0)

    for load in loads[2:]:
        load.wait()
    turn_queries(0, 4)
    side_halves_on(0)
    turn_queries(4, 4)
    sides_to_sibling(0)
    for half in (0, 1):
        received(slot(1, SELF, 0, half), ("p", 1, SELF, half))
    to_sides(1)
    to_sibling(1, SELF)
    from_sibling(0, LEFT)
    from_sibling(0, RIGHT)
    scores(1, 0, 4)
    far_to_sibling(0)
    scores(1, 4, 4)
    side_halves_on(1)
    from_sibling(0, SELF)
    from_sibling(1, SELF)
    scores(0, 0, 4)
    sides_to_sibling(1)
    scores(0, 4, 4)
    from_sibling(1, LEFT)
    from_sibling(1, RIGHT)
    scores(2, 0, 4)
    far_to_sibling(1)
    scores(2, 4, 4)
    from_sibling(0, FAR)
    from_sibling(1, FAR)

    def joined(parts):
        t_max = functools.reduce(jnp.maximum, [p[0:1] for p in parts])
        s_max = functools.reduce(jnp.maximum, [p[2:3] for p in parts])
        t_in = [jnp.exp2(p[0:1] - t_max) for p in parts]
        s_in = [jnp.exp2(p[2:3] - s_max) for p in parts]
        t_sum = functools.reduce(jnp.add, [p[1:2] * w for p, w in zip(parts, t_in)])
        s_sum = functools.reduce(jnp.add, [p[3:4] * w for p, w in zip(parts, s_in)])
        cross = functools.reduce(jnp.add, [p[4:5] * w for p, w in zip(parts, t_in)])
        return t_max, t_sum, s_max, s_sum, cross

    def stat_copy(m_to, m_slot):
        return pltpu.make_async_remote_copy(
            src_ref=stat_send.at[m_to], dst_ref=stat_recv.at[m_slot],
            send_sem=st_send_sem.at[m_to], recv_sem=st_recv_sem.at[m_slot],
            device_id=owner(m_to), device_id_type=MESH,
        )

    def res_copy(m_to, m_slot):
        return pltpu.make_async_remote_copy(
            src_ref=res_recv.at[m_slot], dst_ref=res_recv.at[m_slot],
            send_sem=rs_send_sem.at[m_to], recv_sem=rs_recv_sem.at[m_slot],
            device_id=owner(m_to), device_id_type=MESH,
        )

    def each_other(step):
        def body(i, carry):
            step((me + i) % OWNERS)
            return carry

        lax.fori_loop(1, OWNERS, body, 0)

    for first in (0, 4):
        scores(3, first, 4)
        for n in range(first, first + 4):
            t_max, t_sum, s_max, s_sum, cross = joined([stat[n, b] for b in range(BATCHES)])
            whole = jnp.concatenate([t_max, t_sum, s_max, s_sum, cross, cross, cross, cross], axis=0)
            for y in range(NYL):
                stat_send[y * NZ + n] = whole[:, y * ROWS:(y + 1) * ROWS]

        def leave(i, carry):
            m = (i // 4) * NZ + first + i % 4

            @pl.when(m != me)
            def _():
                stat_copy(m, me).start()

            return carry

        lax.fori_loop(0, 8, leave, 0)
    stat_recv[me] = stat_send[me]
    for b in range(BATCHES):
        turn(b)

    each_other(lambda m: stat_copy(m, m).wait_recv())
    t_max, t_sum, s_max, s_sum, cross = joined([stat_recv[m] for m in range(OWNERS)])
    t_in, s_in = factor / t_sum, factor / s_sum
    res_recv[me] = jnp.concatenate([t_max, t_in, s_max, s_in, t_in, t_in, t_in, t_in], axis=0)
    each_other(lambda m: res_copy(m, me).start())
    div_out[...] = cross * LN2 / t_sum - (t_max * LN2 + jnp.log(t_sum)) + (s_max * LN2 + jnp.log(s_sum))
    each_other(lambda m: res_copy(m, m).wait_recv())

    def group(away):
        return (z + NZ + away) % NZ

    def query_part(away):
        n = group(away)
        res = jnp.concatenate([res_recv[n], res_recv[NZ + n]], axis=1)
        total = None
        for b in range(BATCHES):
            st = stat[n, b]
            t_in = jnp.exp2(st[0:1] - res[0:1]) * res[1:2]
            s_in = jnp.exp2(st[2:3] - res[2:3]) * res[3:4]
            grad = (sw[n, b] * s_in - tw[n, b] * t_in).astype(BF16)
            lanes = pl.ds(pl.multiple_of(n * GROUP, GROUP), GROUP)
            gt[0, b, :, lanes] = grad[:BATCH // 2]
            gt[1, b, :, lanes] = grad[BATCH // 2:]
            term = nn(spt[b], grad)
            total = term if total is None else total + term
        gq[n, 0] = total[:, :ROWS]
        gq[n, 1] = total[:, ROWS:]
        i = away + 3
        y_pair_send[i] = gq[n, 1 - yl, ZF:].astype(BF16)
        send(y_pair_send.at[i], y_pair_recv.at[i], ("y pair", i), y_mate)

    def z_part(away):
        return gq[group(away), :, :ZF]

    def y_part(away):
        i = away + 3
        received(y_pair_recv.at[i], ("y pair", i))
        return gq[group(away), yl, ZF:] + y_pair_recv[i].astype(F32)

    ZH, YH = ZF // 2, YF // 2

    def z_start():
        far = z_part(4).astype(BF16)
        z_send_r[0] = far
        send(z_send_r.at[0, :, pl.ds(0, ZH)], z_recv_r.at[0, :, pl.ds(0, ZH)], ("zr", 0), up)
        send(z_send_r.at[0, :, pl.ds(ZH, ZH)], z_recv_l.at[0, :, pl.ds(ZH, ZH)], ("zl", 0), down)

    def y_start():
        y_send_r[0] = y_part(4).astype(BF16)
        send(y_send_r.at[0, pl.ds(0, YH)], y_recv_r.at[0, pl.ds(0, YH)], ("yr", 0), up)
        send(y_send_r.at[0, pl.ds(YH, YH)], y_recv_l.at[0, pl.ds(YH, YH)], ("yl", 0), down)

    def z_step(step):
        if step == 1:
            mine = z_part(3)
            received(z_recv_r.at[0, :, pl.ds(0, ZH)], ("zr", 0))
            z_send_r[1, :, :ZH] = (mine[:, :ZH] + z_recv_r[0, :, :ZH].astype(F32)).astype(BF16)
            z_send_r[1, :, ZH:] = mine[:, ZH:].astype(BF16)
        else:
            received(z_recv_r.at[step - 1], ("zr", step - 1))
            z_send_r[step] = (z_part(4 - step) + z_recv_r[step - 1].astype(F32)).astype(BF16)
        send(z_send_r.at[step], z_recv_r.at[step], ("zr", step), up)
        if step == 1:
            mine = z_part(-3)
            received(z_recv_l.at[0, :, pl.ds(ZH, ZH)], ("zl", 0))
            z_send_l[1, :, :ZH] = mine[:, :ZH].astype(BF16)
            z_send_l[1, :, ZH:] = (mine[:, ZH:] + z_recv_l[0, :, ZH:].astype(F32)).astype(BF16)
        else:
            received(z_recv_l.at[step - 1], ("zl", step - 1))
            z_send_l[step] = (z_part(step - 4) + z_recv_l[step - 1].astype(F32)).astype(BF16)
        send(z_send_l.at[step], z_recv_l.at[step], ("zl", step), down)

    def y_step(step):
        mine = y_part(4 - step)
        if step == 1:
            received(y_recv_r.at[0, pl.ds(0, YH)], ("yr", 0))
            y_send_r[1, :YH] = (mine[:YH] + y_recv_r[0, :YH].astype(F32)).astype(BF16)
            y_send_r[1, YH:] = mine[YH:].astype(BF16)
        else:
            received(y_recv_r.at[step - 1], ("yr", step - 1))
            y_send_r[step] = (mine + y_recv_r[step - 1].astype(F32)).astype(BF16)
        send(y_send_r.at[step], y_recv_r.at[step], ("yr", step), up)
        mine = y_part(step - 4)
        if step == 1:
            received(y_recv_l.at[0, pl.ds(YH, YH)], ("yl", 0))
            y_send_l[1, :YH] = mine[:YH].astype(BF16)
            y_send_l[1, YH:] = (mine[YH:] + y_recv_l[0, YH:].astype(F32)).astype(BF16)
        else:
            received(y_recv_l.at[step - 1], ("yl", step - 1))
            y_send_l[step] = (mine + y_recv_l[step - 1].astype(F32)).astype(BF16)
        send(y_send_l.at[step], y_recv_l.at[step], ("yl", step), down)

    def passage_part(core):
        grads = gt[core].reshape(BATCHES * BATCH // 2, NZ * GROUP)
        return nn(grads, sq[...].reshape(NZ * GROUP, DS)).reshape(BATCHES, 2, OWN, DS)

    def gp_of(h, where):
        b, s = place(h, where, 0)
        return gp[b, s]

    query_part(4)
    z_start()
    query_part(3)
    query_part(-3)
    z_step(1)
    y_start()
    query_part(2)
    query_part(-2)
    query_part(1)
    query_part(-1)
    query_part(0)
    gps_send[...] = passage_part(1).astype(BF16)
    send(gps_send, gps_recv, "gp sibling", sibling)
    z_step(2)
    y_step(1)
    gp[...] = passage_part(0)
    z_step(3)
    received(gps_recv, "gp sibling")
    gp[...] = gp[...] + gps_recv[...].astype(F32)
    for h in range(NYH):
        gp1_send[h] = gp_of(h, FAR).astype(BF16)
    send(gp1_send.at[0], gp1_recv.at[0], ("gp", RIGHT, 1), right)
    send(gp1_send.at[1], gp1_recv.at[1], ("gp", LEFT, 1), left)
    y_step(2)
    received(gp1_recv.at[0], ("gp", RIGHT, 1))
    gp2_send[0, 0] = (gp_of(0, RIGHT) + gp1_recv[0].astype(F32)).astype(BF16)
    gp2_send[0, 1] = gp_of(1, RIGHT).astype(BF16)
    send(gp2_send.at[0], gp2_recv.at[0], ("gp", RIGHT, 2), right)
    received(gp1_recv.at[1], ("gp", LEFT, 1))
    gp2_send[1, 0] = gp_of(0, LEFT).astype(BF16)
    gp2_send[1, 1] = (gp_of(1, LEFT) + gp1_recv[1].astype(F32)).astype(BF16)
    send(gp2_send.at[1], gp2_recv.at[1], ("gp", LEFT, 2), left)
    y_step(3)
    received(z_recv_r.at[3], ("zr", 3))
    received(z_recv_l.at[3], ("zl", 3))
    for y in range(NYL):
        gq[z, y, :ZF] = gq[z, y, :ZF] + z_recv_r[3, y].astype(F32) + z_recv_l[3, y].astype(F32)
    z_pair_send[...] = gq[z, 1 - yl, :ZF].astype(BF16)
    send(z_pair_send, z_pair_recv, "z pair", y_mate)
    received(gp2_recv.at[0], ("gp", RIGHT, 2))
    received(gp2_recv.at[1], ("gp", LEFT, 2))

    def x_total(h):
        return gp_of(h, SELF) + gp2_recv[0, h].astype(F32) + gp2_recv[1, h].astype(F32)

    gp3_send[...] = x_total(1).astype(BF16)
    send(gp3_send, gp3_recv, "gp across", across)

    mine = y_part(0)
    received(y_recv_r.at[3], ("yr", 3))
    received(y_recv_l.at[3], ("yl", 3))
    gq_out[:, ZF:] = (mine + y_recv_r[3].astype(F32) + y_recv_l[3].astype(F32)).T
    received(z_pair_recv, "z pair")
    gq_out[:, :ZF] = (gq[z, yl, :ZF] + z_pair_recv[...].astype(F32)).T
    received(gp3_recv, "gp across")
    gp_out[...] = x_total(0) + gp3_recv[...].astype(F32)

    for copy in sent:
        copy.wait_send()
    each_other(lambda m: stat_copy(m, me).wait_send())
    each_other(lambda m: res_copy(m, me).wait_send())


def deliver(gq_in, gp_in, div_in, gq_out, gp_out, div_out, gq, gp, div, in_sem, out_sem):
    parts = ((gq_in, gq, gq_out), (gp_in, gp, gp_out), (div_in, div, div_out))
    ins = [pltpu.make_async_copy(src, mid, in_sem.at[i]) for i, (src, mid, _) in enumerate(parts)]
    outs = [pltpu.make_async_copy(mid, dst, out_sem.at[i]) for i, (_, mid, dst) in enumerate(parts)]
    for copy in ins:
        copy.start()
    for arrive, leave in zip(ins, outs):
        arrive.wait()
        leave.start()
    for copy in outs:
        copy.wait()


def local(teacher_query, student_query, teacher_passages, student_passages):
    blocks = NYL, NZ, NCORE, ROWS
    hbm = pl.BlockSpec(memory_space=pl.ANY)
    vmem = pl.BlockSpec(memory_space=pltpu.VMEM)
    outs = (
        jax.ShapeDtypeStruct((ROWS, DS), F32),
        jax.ShapeDtypeStruct((OWN, DS), F32),
        jax.ShapeDtypeStruct((1, ROWS), F32),
    )
    results = pl.pallas_call(
        kernel,
        out_shape=outs,
        in_specs=[hbm] * 4,
        out_specs=(vmem,) * 3,
        scratch_shapes=[
            pltpu.VMEM((NZ, NYL, ROWS, DT), BF16),
            pltpu.VMEM((NZ, NYL, ROWS, DS), BF16),
            pltpu.VMEM((NZ, DT, GROUP), BF16),
            pltpu.VMEM((NZ, DS, GROUP), BF16),
            pltpu.VMEM((BATCHES, BATCH // OWN, OWN, DT + DS), BF16),
            pltpu.VMEM((BATCHES, DS, BATCH), BF16),
            pltpu.VMEM((NZ, BATCHES, BATCH, GROUP), F32),
            pltpu.VMEM((NZ, BATCHES, BATCH, GROUP), F32),
            pltpu.VMEM((NCORE, BATCHES, BATCH // 2, NZ * GROUP), BF16),
            pltpu.VMEM((NZ, BATCHES, 8, GROUP), F32),
            pltpu.VMEM((NZ, NYL, DS, ROWS), F32),
            pltpu.VMEM((OWNERS, 8, ROWS), F32),
            pltpu.VMEM((OWNERS, 8, ROWS), F32),
            pltpu.VMEM((OWNERS, 8, ROWS), F32),
            pltpu.VMEM((4, NYL, ZF, ROWS), BF16),
            pltpu.VMEM((4, NYL, ZF, ROWS), BF16),
            pltpu.VMEM((4, NYL, ZF, ROWS), BF16),
            pltpu.VMEM((4, NYL, ZF, ROWS), BF16),
            pltpu.VMEM((ZF, ROWS), BF16),
            pltpu.VMEM((ZF, ROWS), BF16),
            pltpu.VMEM((NZ, YF, ROWS), BF16),
            pltpu.VMEM((NZ, YF, ROWS), BF16),
            pltpu.VMEM((4, YF, ROWS), BF16),
            pltpu.VMEM((4, YF, ROWS), BF16),
            pltpu.VMEM((4, YF, ROWS), BF16),
            pltpu.VMEM((4, YF, ROWS), BF16),
            pltpu.VMEM((BATCHES, 2, OWN, DS), F32),
            pltpu.VMEM((BATCHES, 2, OWN, DS), BF16),
            pltpu.VMEM((BATCHES, 2, OWN, DS), BF16),
            pltpu.VMEM((NYH, OWN, DS), BF16),
            pltpu.VMEM((NYH, OWN, DS), BF16),
            pltpu.VMEM((2, NYH, OWN, DS), BF16),
            pltpu.VMEM((2, NYH, OWN, DS), BF16),
            pltpu.VMEM((OWN, DS), BF16),
            pltpu.VMEM((OWN, DS), BF16),
            pltpu.SemaphoreType.DMA((6,)),
            pltpu.SemaphoreType.DMA((MESSAGES,)),
            pltpu.SemaphoreType.DMA((MESSAGES,)),
            pltpu.SemaphoreType.DMA((OWNERS,)),
            pltpu.SemaphoreType.DMA((OWNERS,)),
            pltpu.SemaphoreType.DMA((OWNERS,)),
            pltpu.SemaphoreType.DMA((OWNERS,)),
        ],
        compiler_params=pltpu.CompilerParams(
            collective_id=0, has_side_effects=True, vmem_limit_bytes=VMEM_BYTES
        ),
    )(
        teacher_query.reshape(*blocks, DT),
        student_query.reshape(*blocks, DS),
        teacher_passages,
        student_passages,
    )
    grad_query, grad_passage, divergence = pl.pallas_call(
        deliver,
        out_shape=outs,
        in_specs=[hbm] * 3,
        out_specs=(hbm,) * 3,
        scratch_shapes=[
            *(pltpu.VMEM(out.shape, out.dtype) for out in outs),
            pltpu.SemaphoreType.DMA((3,)),
            pltpu.SemaphoreType.DMA((3,)),
        ],
        compiler_params=pltpu.CompilerParams(vmem_limit_bytes=VMEM_BYTES),
    )(*results)
    return divergence.reshape(ROWS), grad_query, grad_passage


def solution(mesh):
    return jax.shard_map(
        local,
        mesh=mesh,
        in_specs=(
            P("query", None),
            P("query", None),
            P(("query", "corpus"), None),
            P(("query", "corpus"), None),
        ),
        out_specs=(
            P(("query", "corpus")),
            P(("query", "corpus"), None),
            P(("query", "corpus"), None),
        ),
        check_vma=False,
    )
```

```python
import functools
import math

import jax
import jax.numpy as jnp
from jax import lax
from jax.experimental import pallas as pl
from jax.experimental.pallas import tpu as pltpu
from jax.sharding import PartitionSpec as P

NX, NYH, NYL, NZ, NCORE = 4, 2, 2, 8, 2
OWN = 64
ROWS = 128
DT, DS = 1024, 384
BATCHES = 4
BATCH = 256
GROUP = NYL * ROWS
OWNERS = NYL * NZ
HALF = OWN // 2
ZF = 192
YF = DS - ZF
LOG2E = math.log2(math.e)
LN2 = math.log(2.0)
F32, BF16 = jnp.float32, jnp.bfloat16
MESH = pl.DeviceIdType.MESH

SELF, LEFT, RIGHT, FAR = 0, 1, 2, 3


def place(h, where, core):
    if where == SELF:
        return 0, core * 2 + h
    if where == FAR:
        return 3, core * 2 + h
    return 1 + h, core * 2 + (where - LEFT)


def nn(a, b):
    return lax.dot_general(a, b, (((1,), (0,)), ((), ())), preferred_element_type=F32)


class Messages:
    def __init__(self):
        self.numbers = {}

    def __call__(self, name):
        return self.numbers.setdefault(name, len(self.numbers))


MESSAGES = 80
VMEM_BYTES = 60 * 1024 * 1024


def kernel(
    tq_hbm, sq_hbm, tp_hbm, sp_hbm,
    gq_out, gp_out, div_out,
    tq, sq, tqt, sqt, pbuf, spt, tw, sw, gt, stat, gq,
    stat_send, stat_recv, res_recv,
    z_send_r, z_recv_r, z_send_l, z_recv_l, z_pair_send, z_pair_recv,
    y_pair_send, y_pair_recv, y_send_r, y_recv_r, y_send_l, y_recv_l,
    gp, gps_send, gps_recv, gp1_send, gp1_recv, gp2_send, gp2_recv, gp3_send, gp3_recv,
    load_sem, send_sem, recv_sem, st_send_sem, st_recv_sem, rs_send_sem, rs_recv_sem,
):
    t_scale = DT ** (-0.5) * LOG2E
    s_scale = DS ** (-0.5) * LOG2E
    factor = DS ** (-0.5)
    q = lax.axis_index("query")
    c = lax.axis_index("corpus")
    x, yh = q // NYH, q % NYH
    yl, z, k = c // (NZ * NCORE), (c // NCORE) % NZ, c % NCORE
    me = yl * NZ + z

    def at(x_, yh_, yl_, z_, k_):
        return (x_ * NYH + yh_, (yl_ * NZ + z_) * NCORE + k_)

    right, left = at((x + 1) % NX, yh, yl, z, k), at((x + NX - 1) % NX, yh, yl, z, k)
    across = at(x, 1 - yh, 1 - yl, z, k)
    sibling = at(x, yh, yl, z, 1 - k)
    up, down = at(x, yh, yl, (z + 1) % NZ, k), at(x, yh, yl, (z + NZ - 1) % NZ, k)
    y_mate = at(x, yh, 1 - yl, z, k)

    def owner(m):
        return at(x, yh, m // NZ, m % NZ, k)

    def slot(h, where, core, half=None):
        b, s = place(h, where, core)
        if half is None:
            return pbuf.at[b, s]
        return pbuf.at[b, s, pl.ds(half * HALF, HALF)]

    loads = [
        pltpu.make_async_copy(tp_hbm, pbuf.at[0, 0, :, pl.ds(0, DT)], load_sem.at[0]),
        pltpu.make_async_copy(sp_hbm, pbuf.at[0, 0, :, pl.ds(DT, DS)], load_sem.at[1]),
    ]
    for y in range(NYL):
        loads.append(pltpu.make_async_copy(tq_hbm.at[y, :, k], tq.at[:, y], load_sem.at[2 + y]))
        loads.append(pltpu.make_async_copy(sq_hbm.at[y, :, k], sq.at[:, y], load_sem.at[4 + y]))
    for load in loads:
        load.start()

    barrier = pltpu.get_barrier_semaphore()
    for device in (right, left, across, sibling):
        pl.semaphore_signal(barrier, inc=1, device_id=device, device_id_type=MESH)

    def greet(i, carry):
        pl.semaphore_signal(barrier, inc=1, device_id=owner((me + i) % OWNERS), device_id_type=MESH)
        return carry

    lax.fori_loop(1, OWNERS, greet, 0)
    pl.semaphore_wait(barrier, 4 + OWNERS - 1)
    loads[0].wait()
    loads[1].wait()

    number = Messages()
    sent = []

    def message(src, dst, name, device):
        i = number(name)
        return pltpu.make_async_remote_copy(
            src_ref=src, dst_ref=dst, send_sem=send_sem.at[i], recv_sem=recv_sem.at[i],
            device_id=device, device_id_type=MESH,
        )

    def send(src, dst, name, device):
        copy = message(src, dst, name, device)
        copy.start()
        sent.append(copy)

    def flush():
        for copy in sent:
            copy.wait_send()
        sent.clear()

    def received(ref, name):
        message(ref, ref, name, sibling).wait_recv()

    def to_sides(h):
        for first in (0, 1):
            half = first
            send(slot(h, SELF, 0, half), slot(h, LEFT, 0, half), ("p", h, LEFT, half), right)
            half = 1 - first
            send(slot(h, SELF, 0, half), slot(h, RIGHT, 0, half), ("p", h, RIGHT, half), left)

    def to_sibling(h, where):
        send(slot(h, where, 0), slot(h, where, 1), ("sib", h, where), sibling)

    def side_halves_on():
        received(slot(0, LEFT, 0, 0), ("p", 0, LEFT, 0))
        send(slot(0, LEFT, 0, 0), slot(0, FAR, 0, 0), ("p", 0, FAR, 0), right)
        received(slot(0, RIGHT, 0, 1), ("p", 0, RIGHT, 1))
        send(slot(0, RIGHT, 0, 1), slot(0, FAR, 0, 1), ("p", 0, FAR, 1), left)

    def sides_to_sibling(h, rest):
        for half in rest:
            received(slot(h, LEFT, 0, half), ("p", h, LEFT, half))
        to_sibling(h, LEFT)
        for half in rest:
            received(slot(h, RIGHT, 0, 1 - half), ("p", h, RIGHT, 1 - half))
        to_sibling(h, RIGHT)

    def far_across():
        for half in (0, 1):
            received(slot(0, FAR, 0, half), ("p", 0, FAR, half))
            send(slot(0, FAR, 0, half), slot(1, FAR, 0, half), ("p", 1, FAR, half), across)
        to_sibling(0, FAR)

    def far_from_across():
        for half in (0, 1):
            received(slot(1, FAR, 0, half), ("p", 1, FAR, half))
        to_sibling(1, FAR)

    def from_sibling(h, where):
        received(slot(h, where, 1), ("sib", h, where))

    for half in (0, 1):
        send(slot(0, SELF, 0, half), slot(1, SELF, 0, half), ("p", 1, SELF, half), across)
    to_sides(0)
    to_sibling(0, SELF)

    def scores(b, first, count):
        def tile(n, carry):
            passages = pbuf[b].reshape(BATCH, DT + DS)
            t = nn(passages[:, :DT], tqt[n]) * t_scale
            s = nn(passages[:, DT:], sqt[n]) * s_scale
            t_max = jnp.max(t, axis=0, keepdims=True)
            s_max = jnp.max(s, axis=0, keepdims=True)
            t_weight = jnp.exp2(t - t_max)
            s_weight = jnp.exp2(s - s_max)
            tw[n, b] = t_weight
            sw[n, b] = s_weight
            t_sum = jnp.sum(t_weight, axis=0, keepdims=True)
            s_sum = jnp.sum(s_weight, axis=0, keepdims=True)
            cross = jnp.sum(t_weight * (t - s), axis=0, keepdims=True)
            stat[n, b] = jnp.concatenate([t_max, t_sum, s_max, s_sum, cross, cross, cross, cross], axis=0)
            return carry

        lax.fori_loop(first, first + count, tile, 0, unroll=2)

    def turn(b):
        turned = pbuf[b].reshape(BATCH, DT + DS)[:, DT:].T
        part = BATCH // NCORE
        for core in range(NCORE):
            start = (core * BATCHES + b) * part
            spt[:, start:start + part] = turned[:, core * part:(core + 1) * part]

    def turn_queries(first, count):
        def body(n, carry):
            tqt[n] = tq[n].reshape(GROUP, DT).T
            sqt[n] = sq[n].reshape(GROUP, DS).T
            return carry

        lax.fori_loop(first, first + count, body, 0)

    for load in loads[2:]:
        load.wait()
    turn_queries(0, 4)
    side_halves_on()
    turn_queries(4, 4)
    for half in (0, 1):
        received(slot(1, SELF, 0, half), ("p", 1, SELF, half))
    to_sides(1)
    to_sibling(1, SELF)
    sides_to_sibling(0, (1,))
    from_sibling(0, LEFT)
    from_sibling(0, RIGHT)
    scores(1, 0, 2)
    far_across()
    scores(1, 2, 6)
    from_sibling(0, SELF)
    from_sibling(1, SELF)
    scores(0, 0, 4)
    sides_to_sibling(1, (0, 1))
    scores(0, 4, 4)
    far_from_across()
    from_sibling(1, LEFT)
    from_sibling(1, RIGHT)
    scores(2, 0, 8)
    from_sibling(0, FAR)
    from_sibling(1, FAR)

    def joined(parts):
        t_max = functools.reduce(jnp.maximum, [p[0:1] for p in parts])
        s_max = functools.reduce(jnp.maximum, [p[2:3] for p in parts])
        t_in = [jnp.exp2(p[0:1] - t_max) for p in parts]
        s_in = [jnp.exp2(p[2:3] - s_max) for p in parts]
        t_sum = functools.reduce(jnp.add, [p[1:2] * w for p, w in zip(parts, t_in)])
        s_sum = functools.reduce(jnp.add, [p[3:4] * w for p, w in zip(parts, s_in)])
        cross = functools.reduce(jnp.add, [p[4:5] * w for p, w in zip(parts, t_in)])
        return t_max, t_sum, s_max, s_sum, cross

    def stat_copy(m_to, m_slot):
        return pltpu.make_async_remote_copy(
            src_ref=stat_send.at[m_to], dst_ref=stat_recv.at[m_slot],
            send_sem=st_send_sem.at[m_to], recv_sem=st_recv_sem.at[m_slot],
            device_id=owner(m_to), device_id_type=MESH,
        )

    def res_copy(m_to, m_slot):
        return pltpu.make_async_remote_copy(
            src_ref=res_recv.at[m_slot], dst_ref=res_recv.at[m_slot],
            send_sem=rs_send_sem.at[m_to], recv_sem=rs_recv_sem.at[m_slot],
            device_id=owner(m_to), device_id_type=MESH,
        )

    def each_other(step):
        def body(i, carry):
            step((me + i) % OWNERS)
            return carry

        lax.fori_loop(1, OWNERS, body, 0)

    for first in (0, 4):
        scores(3, first, 4)
        for n in range(first, first + 4):
            t_max, t_sum, s_max, s_sum, cross = joined([stat[n, b] for b in range(BATCHES)])
            whole = jnp.concatenate([t_max, t_sum, s_max, s_sum, cross, cross, cross, cross], axis=0)
            for y in range(NYL):
                stat_send[y * NZ + n] = whole[:, y * ROWS:(y + 1) * ROWS]

        def leave(i, carry):
            m = (i // 4) * NZ + first + i % 4

            @pl.when(m != me)
            def _():
                stat_copy(m, me).start()

            return carry

        lax.fori_loop(0, 8, leave, 0)
    stat_recv[me] = stat_send[me]
    for b in range(BATCHES):
        turn(b)
    flush()
    each_other(lambda m: stat_copy(m, m).wait_recv())
    t_max, t_sum, s_max, s_sum, cross = joined([stat_recv[m] for m in range(OWNERS)])
    t_in, s_in = factor / t_sum, factor / s_sum
    res_recv[me] = jnp.concatenate([t_max, t_in, s_max, s_in, t_in, t_in, t_in, t_in], axis=0)
    each_other(lambda m: res_copy(m, me).start())
    div_out[...] = cross * LN2 / t_sum - (t_max * LN2 + jnp.log(t_sum)) + (s_max * LN2 + jnp.log(s_sum))
    each_other(lambda m: stat_copy(m, me).wait_send())
    each_other(lambda m: res_copy(m, m).wait_recv())

    def group(away):
        return (z + NZ + away) % NZ

    def lanes(away):
        return pl.ds(pl.multiple_of(group(away) * GROUP, GROUP), GROUP)

    def form(away):
        n = group(away)
        res = jnp.concatenate([res_recv[n], res_recv[NZ + n]], axis=1)
        for b in range(BATCHES):
            st = stat[n, b]
            t_in = jnp.exp2(st[0:1] - res[0:1]) * res[1:2]
            s_in = jnp.exp2(st[2:3] - res[2:3]) * res[3:4]
            grad = (sw[n, b] * s_in - tw[n, b] * t_in).astype(BF16)
            gt[0, b, :, lanes(away)] = grad[:BATCH // 2]
            gt[1, b, :, lanes(away)] = grad[BATCH // 2:]

    def query_part(away):
        n = group(away)
        total = nn(spt[...], gt[:, :, :, lanes(away)].reshape(NCORE * BATCHES * BATCH // 2, GROUP))
        gq[n, 0] = total[:, :ROWS]
        gq[n, 1] = total[:, ROWS:]
        i = away + 3
        y_pair_send[i] = gq[n, 1 - yl, ZF:].astype(BF16)
        send(y_pair_send.at[i], y_pair_recv.at[i], ("y pair", i), y_mate)

    def z_part(away):
        return gq[group(away), :, :ZF]

    def y_part(away):
        i = away + 3
        received(y_pair_recv.at[i], ("y pair", i))
        return gq[group(away), yl, ZF:] + y_pair_recv[i].astype(F32)

    ZH, YH = ZF // 2, YF // 2

    def z_start():
        far = z_part(4).astype(BF16)
        z_send_r[0] = far
        send(z_send_r.at[0, :, pl.ds(0, ZH)], z_recv_r.at[0, :, pl.ds(0, ZH)], ("zr", 0), up)
        send(z_send_r.at[0, :, pl.ds(ZH, ZH)], z_recv_l.at[0, :, pl.ds(ZH, ZH)], ("zl", 0), down)

    def y_start():
        y_send_r[0] = y_part(4).astype(BF16)
        send(y_send_r.at[0, pl.ds(0, YH)], y_recv_r.at[0, pl.ds(0, YH)], ("yr", 0), up)
        send(y_send_r.at[0, pl.ds(YH, YH)], y_recv_l.at[0, pl.ds(YH, YH)], ("yl", 0), down)

    def z_step(step):
        if step == 1:
            mine = z_part(3)
            received(z_recv_r.at[0, :, pl.ds(0, ZH)], ("zr", 0))
            z_send_r[1, :, :ZH] = (mine[:, :ZH] + z_recv_r[0, :, :ZH].astype(F32)).astype(BF16)
            z_send_r[1, :, ZH:] = mine[:, ZH:].astype(BF16)
        else:
            received(z_recv_r.at[step - 1], ("zr", step - 1))
            z_send_r[step] = (z_part(4 - step) + z_recv_r[step - 1].astype(F32)).astype(BF16)
        send(z_send_r.at[step], z_recv_r.at[step], ("zr", step), up)
        if step == 1:
            mine = z_part(-3)
            received(z_recv_l.at[0, :, pl.ds(ZH, ZH)], ("zl", 0))
            z_send_l[1, :, :ZH] = mine[:, :ZH].astype(BF16)
            z_send_l[1, :, ZH:] = (mine[:, ZH:] + z_recv_l[0, :, ZH:].astype(F32)).astype(BF16)
        else:
            received(z_recv_l.at[step - 1], ("zl", step - 1))
            z_send_l[step] = (z_part(step - 4) + z_recv_l[step - 1].astype(F32)).astype(BF16)
        send(z_send_l.at[step], z_recv_l.at[step], ("zl", step), down)

    def y_step(step):
        mine = y_part(4 - step)
        if step == 1:
            received(y_recv_r.at[0, pl.ds(0, YH)], ("yr", 0))
            y_send_r[1, :YH] = (mine[:YH] + y_recv_r[0, :YH].astype(F32)).astype(BF16)
            y_send_r[1, YH:] = mine[YH:].astype(BF16)
        else:
            received(y_recv_r.at[step - 1], ("yr", step - 1))
            y_send_r[step] = (mine + y_recv_r[step - 1].astype(F32)).astype(BF16)
        send(y_send_r.at[step], y_recv_r.at[step], ("yr", step), up)
        mine = y_part(step - 4)
        if step == 1:
            received(y_recv_l.at[0, pl.ds(YH, YH)], ("yl", 0))
            y_send_l[1, :YH] = mine[:YH].astype(BF16)
            y_send_l[1, YH:] = (mine[YH:] + y_recv_l[0, YH:].astype(F32)).astype(BF16)
        else:
            received(y_recv_l.at[step - 1], ("yl", step - 1))
            y_send_l[step] = (mine + y_recv_l[step - 1].astype(F32)).astype(BF16)
        send(y_send_l.at[step], y_recv_l.at[step], ("yl", step), down)

    def passage_part(core):
        grads = gt[core].reshape(BATCHES * BATCH // 2, NZ * GROUP)
        return nn(grads, sq[...].reshape(NZ * GROUP, DS)).reshape(BATCHES, 2, OWN, DS)

    def gp_of(h, where):
        b, s = place(h, where, 0)
        return gp[b, s]

    def gp_first():
        received(gps_recv, "gp sibling")
        gp[...] = gp[...] + gps_recv[...].astype(F32)
        for h in range(NYH):
            gp1_send[h] = gp_of(h, FAR).astype(BF16)
        send(gp1_send.at[0], gp1_recv.at[0], ("gp", RIGHT, 1), right)
        send(gp1_send.at[1], gp1_recv.at[1], ("gp", LEFT, 1), left)

    def gp_second():
        received(gp1_recv.at[0], ("gp", RIGHT, 1))
        gp2_send[0, 0] = (gp_of(0, RIGHT) + gp1_recv[0].astype(F32)).astype(BF16)
        gp2_send[0, 1] = gp_of(1, RIGHT).astype(BF16)
        send(gp2_send.at[0], gp2_recv.at[0], ("gp", RIGHT, 2), right)
        received(gp1_recv.at[1], ("gp", LEFT, 1))
        gp2_send[1, 0] = gp_of(0, LEFT).astype(BF16)
        gp2_send[1, 1] = (gp_of(1, LEFT) + gp1_recv[1].astype(F32)).astype(BF16)
        send(gp2_send.at[1], gp2_recv.at[1], ("gp", LEFT, 2), left)

    def gp_third():
        received(gp2_recv.at[0], ("gp", RIGHT, 2))
        received(gp2_recv.at[1], ("gp", LEFT, 2))
        gp3_send[...] = x_total(1).astype(BF16)
        send(gp3_send, gp3_recv, "gp across", across)

    def x_total(h):
        return gp_of(h, SELF) + gp2_recv[0, h].astype(F32) + gp2_recv[1, h].astype(F32)

    def z_last():
        received(z_recv_r.at[3], ("zr", 3))
        received(z_recv_l.at[3], ("zl", 3))
        for y in range(NYL):
            gq[z, y, :ZF] = gq[z, y, :ZF] + z_recv_r[3, y].astype(F32) + z_recv_l[3, y].astype(F32)
        z_pair_send[...] = gq[z, 1 - yl, :ZF].astype(BF16)
        send(z_pair_send, z_pair_recv, "z pair", y_mate)

    form(4)
    query_part(4)
    z_start()
    form(3)
    query_part(3)
    form(-3)
    query_part(-3)
    form(2)
    form(-2)
    z_step(1)
    y_start()
    form(1)
    form(-1)
    form(0)
    gps_send[...] = passage_part(1).astype(BF16)
    send(gps_send, gps_recv, "gp sibling", sibling)
    query_part(2)
    query_part(-2)
    z_step(2)
    y_step(1)
    gp[...] = passage_part(0)
    gp_first()
    query_part(1)
    query_part(-1)
    z_step(3)
    y_step(2)
    gp_second()
    query_part(0)
    each_other(lambda m: res_copy(m, me).wait_send())
    z_last()
    y_step(3)
    gp_third()
    flush()

    mine = y_part(0)
    received(y_recv_r.at[3], ("yr", 3))
    received(y_recv_l.at[3], ("yl", 3))
    gq_out[:, ZF:] = (mine + y_recv_r[3].astype(F32) + y_recv_l[3].astype(F32)).T
    received(z_pair_recv, "z pair")
    gq_out[:, :ZF] = (gq[z, yl, :ZF] + z_pair_recv[...].astype(F32)).T
    received(gp3_recv, "gp across")
    gp_out[...] = x_total(0) + gp3_recv[...].astype(F32)


def deliver(gq_in, gp_in, div_in, gq_out, gp_out, div_out, gq, gp, div, in_sem, out_sem):
    parts = ((gq_in, gq, gq_out), (gp_in, gp, gp_out), (div_in, div, div_out))
    ins = [pltpu.make_async_copy(src, mid, in_sem.at[i]) for i, (src, mid, _) in enumerate(parts)]
    outs = [pltpu.make_async_copy(mid, dst, out_sem.at[i]) for i, (_, mid, dst) in enumerate(parts)]
    for copy in ins:
        copy.start()
    for arrive, leave in zip(ins, outs):
        arrive.wait()
        leave.start()
    for copy in outs:
        copy.wait()


def local(teacher_query, student_query, teacher_passages, student_passages):
    blocks = NYL, NZ, NCORE, ROWS
    hbm = pl.BlockSpec(memory_space=pl.ANY)
    vmem = pl.BlockSpec(memory_space=pltpu.VMEM)
    outs = (
        jax.ShapeDtypeStruct((ROWS, DS), F32),
        jax.ShapeDtypeStruct((OWN, DS), F32),
        jax.ShapeDtypeStruct((1, ROWS), F32),
    )
    results = pl.pallas_call(
        kernel,
        out_shape=outs,
        in_specs=[hbm] * 4,
        out_specs=(vmem,) * 3,
        scratch_shapes=[
            pltpu.VMEM((NZ, NYL, ROWS, DT), BF16),
            pltpu.VMEM((NZ, NYL, ROWS, DS), BF16),
            pltpu.VMEM((NZ, DT, GROUP), BF16),
            pltpu.VMEM((NZ, DS, GROUP), BF16),
            pltpu.VMEM((BATCHES, BATCH // OWN, OWN, DT + DS), BF16),
            pltpu.VMEM((DS, BATCHES * BATCH), BF16),
            pltpu.VMEM((NZ, BATCHES, BATCH, GROUP), F32),
            pltpu.VMEM((NZ, BATCHES, BATCH, GROUP), F32),
            pltpu.VMEM((NCORE, BATCHES, BATCH // 2, NZ * GROUP), BF16),
            pltpu.VMEM((NZ, BATCHES, 8, GROUP), F32),
            pltpu.VMEM((NZ, NYL, DS, ROWS), F32),
            pltpu.VMEM((OWNERS, 8, ROWS), F32),
            pltpu.VMEM((OWNERS, 8, ROWS), F32),
            pltpu.VMEM((OWNERS, 8, ROWS), F32),
            pltpu.VMEM((4, NYL, ZF, ROWS), BF16),
            pltpu.VMEM((4, NYL, ZF, ROWS), BF16),
            pltpu.VMEM((4, NYL, ZF, ROWS), BF16),
            pltpu.VMEM((4, NYL, ZF, ROWS), BF16),
            pltpu.VMEM((ZF, ROWS), BF16),
            pltpu.VMEM((ZF, ROWS), BF16),
            pltpu.VMEM((NZ, YF, ROWS), BF16),
            pltpu.VMEM((NZ, YF, ROWS), BF16),
            pltpu.VMEM((4, YF, ROWS), BF16),
            pltpu.VMEM((4, YF, ROWS), BF16),
            pltpu.VMEM((4, YF, ROWS), BF16),
            pltpu.VMEM((4, YF, ROWS), BF16),
            pltpu.VMEM((BATCHES, 2, OWN, DS), F32),
            pltpu.VMEM((BATCHES, 2, OWN, DS), BF16),
            pltpu.VMEM((BATCHES, 2, OWN, DS), BF16),
            pltpu.VMEM((NYH, OWN, DS), BF16),
            pltpu.VMEM((NYH, OWN, DS), BF16),
            pltpu.VMEM((2, NYH, OWN, DS), BF16),
            pltpu.VMEM((2, NYH, OWN, DS), BF16),
            pltpu.VMEM((OWN, DS), BF16),
            pltpu.VMEM((OWN, DS), BF16),
            pltpu.SemaphoreType.DMA((6,)),
            pltpu.SemaphoreType.DMA((MESSAGES,)),
            pltpu.SemaphoreType.DMA((MESSAGES,)),
            pltpu.SemaphoreType.DMA((OWNERS,)),
            pltpu.SemaphoreType.DMA((OWNERS,)),
            pltpu.SemaphoreType.DMA((OWNERS,)),
            pltpu.SemaphoreType.DMA((OWNERS,)),
        ],
        compiler_params=pltpu.CompilerParams(
            collective_id=0, has_side_effects=True, vmem_limit_bytes=VMEM_BYTES
        ),
    )(
        teacher_query.reshape(*blocks, DT),
        student_query.reshape(*blocks, DS),
        teacher_passages,
        student_passages,
    )
    grad_query, grad_passage, divergence = pl.pallas_call(
        deliver,
        out_shape=outs,
        in_specs=[hbm] * 3,
        out_specs=(hbm,) * 3,
        scratch_shapes=[
            *(pltpu.VMEM(out.shape, out.dtype) for out in outs),
            pltpu.SemaphoreType.DMA((3,)),
            pltpu.SemaphoreType.DMA((3,)),
        ],
        compiler_params=pltpu.CompilerParams(vmem_limit_bytes=VMEM_BYTES),
    )(*results)
    return divergence.reshape(ROWS), grad_query, grad_passage


def solution(mesh):
    return jax.shard_map(
        local,
        mesh=mesh,
        in_specs=(
            P("query", None),
            P("query", None),
            P(("query", "corpus"), None),
            P(("query", "corpus"), None),
        ),
        out_specs=(
            P(("query", "corpus")),
            P(("query", "corpus"), None),
            P(("query", "corpus"), None),
        ),
        check_vma=False,
    )
```

```python
import functools
import math

import jax
import jax.numpy as jnp
from jax import lax
from jax.experimental import pallas as pl
from jax.experimental.pallas import tpu as pltpu
from jax.sharding import PartitionSpec as P

NX, NYH, NYL, NZ, NCORE = 4, 2, 2, 8, 2
OWN = 64
ROWS = 128
DT, DS = 1024, 384
BATCHES = 4
BATCH = 256
GROUP = NYL * ROWS
OWNERS = NYL * NZ
HALF = OWN // 2
ZF = 192
YF = DS - ZF
LOG2E = math.log2(math.e)
LN2 = math.log(2.0)
F32, BF16 = jnp.float32, jnp.bfloat16
MESH = pl.DeviceIdType.MESH

SELF, LEFT, RIGHT, FAR = 0, 1, 2, 3


def place(h, where, core):
    if where == SELF:
        return 1, core * 2 + h
    if where == FAR:
        return 3, core * 2 + h
    return 2 * h, core * 2 + (where - LEFT)


def nn(a, b):
    return lax.dot_general(a, b, (((1,), (0,)), ((), ())), preferred_element_type=F32)


class Messages:
    def __init__(self):
        self.numbers = {}

    def __call__(self, name):
        return self.numbers.setdefault(name, len(self.numbers))


MESSAGES = 80
VMEM_BYTES = 60 * 1024 * 1024


def kernel(
    tq_hbm, sq_hbm, tp_hbm, sp_hbm,
    gq_out, gp_out, div_out,
    tq, sq, tqt, sqt, pbuf, spt, tw, sw, raw_a, raw_b, gt, stat, gq,
    stat_send, stat_recv, res_recv,
    z_send_r, z_recv_r, z_send_l, z_recv_l, z_pair_send, z_pair_recv,
    y_pair_send, y_pair_recv, y_send_r, y_recv_r, y_send_l, y_recv_l,
    gp, gps_send, gps_recv, gp1_send, gp1_recv, gp2_send, gp2_recv, gp3_send, gp3_recv,
    load_sem, send_sem, recv_sem, yp_send_sem, yp_recv_sem, st_send_sem, st_recv_sem, rs_send_sem, rs_recv_sem,
):
    t_scale = DT ** (-0.5) * LOG2E
    s_scale = DS ** (-0.5) * LOG2E
    factor = DS ** (-0.5)
    q = lax.axis_index("query")
    c = lax.axis_index("corpus")
    x, yh = q // NYH, q % NYH
    yl, z, k = c // (NZ * NCORE), (c // NCORE) % NZ, c % NCORE
    me = yl * NZ + z

    def at(x_, yh_, yl_, z_, k_):
        return (x_ * NYH + yh_, (yl_ * NZ + z_) * NCORE + k_)

    right, left = at((x + 1) % NX, yh, yl, z, k), at((x + NX - 1) % NX, yh, yl, z, k)
    across = at(x, 1 - yh, 1 - yl, z, k)
    sibling = at(x, yh, yl, z, 1 - k)
    up, down = at(x, yh, yl, (z + 1) % NZ, k), at(x, yh, yl, (z + NZ - 1) % NZ, k)
    y_mate = at(x, yh, 1 - yl, z, k)

    def owner(m):
        return at(x, yh, m // NZ, m % NZ, k)

    def slot(h, where, core, half=None):
        b, s = place(h, where, core)
        if half is None:
            return pbuf.at[b, s]
        return pbuf.at[b, s, pl.ds(half * HALF, HALF)]

    loads = [
        pltpu.make_async_copy(tp_hbm, pbuf.at[1, 0, :, pl.ds(0, DT)], load_sem.at[0]),
        pltpu.make_async_copy(sp_hbm, pbuf.at[1, 0, :, pl.ds(DT, DS)], load_sem.at[1]),
    ]
    for y in range(NYL):
        loads.append(pltpu.make_async_copy(tq_hbm.at[y, :, k], tq.at[:, y], load_sem.at[2 + y]))
        loads.append(pltpu.make_async_copy(sq_hbm.at[y, :, k], sq.at[:, y], load_sem.at[4 + y]))
    for load in loads:
        load.start()

    barrier = pltpu.get_barrier_semaphore()
    for device in (right, left, across, sibling):
        pl.semaphore_signal(barrier, inc=1, device_id=device, device_id_type=MESH)

    def greet(i, carry):
        pl.semaphore_signal(barrier, inc=1, device_id=owner((me + i) % OWNERS), device_id_type=MESH)
        return carry

    lax.fori_loop(1, OWNERS, greet, 0)
    pl.semaphore_wait(barrier, 4 + OWNERS - 1)
    loads[0].wait()
    loads[1].wait()

    number = Messages()
    sent = []

    def message(refs, name, device):
        i = number(name)
        src, dst = refs()
        return pltpu.make_async_remote_copy(
            src_ref=src, dst_ref=dst, send_sem=send_sem.at[i], recv_sem=recv_sem.at[i],
            device_id=device, device_id_type=MESH,
        )

    def send(refs, name, device):
        message(refs, name, device).start()
        sent.append((refs, name, device))

    def flush():
        for args in sent:
            message(*args).wait_send()
        sent.clear()

    def received(ref, name):
        message(lambda: (ref, ref), name, sibling).wait_recv()

    def to_sides(h):
        for first in (0, 1):
            half = first
            send(lambda half=half, h=h: (slot(h, SELF, 0, half), slot(h, LEFT, 0, half)), ("p", h, LEFT, half), right)
            half = 1 - first
            send(lambda half=half, h=h: (slot(h, SELF, 0, half), slot(h, RIGHT, 0, half)), ("p", h, RIGHT, half), left)

    def to_sibling(h, where):
        send(lambda h=h, where=where: (slot(h, where, 0), slot(h, where, 1)), ("sib", h, where), sibling)

    def side_halves_on():
        received(slot(0, LEFT, 0, 0), ("p", 0, LEFT, 0))
        send(lambda: (slot(0, LEFT, 0, 0), slot(0, FAR, 0, 0)), ("p", 0, FAR, 0), right)
        received(slot(0, RIGHT, 0, 1), ("p", 0, RIGHT, 1))
        send(lambda: (slot(0, RIGHT, 0, 1), slot(0, FAR, 0, 1)), ("p", 0, FAR, 1), left)

    def sides_to_sibling(h, rest):
        for half in rest:
            received(slot(h, LEFT, 0, half), ("p", h, LEFT, half))
        to_sibling(h, LEFT)
        for half in rest:
            received(slot(h, RIGHT, 0, 1 - half), ("p", h, RIGHT, 1 - half))
        to_sibling(h, RIGHT)

    def far_across():
        for half in (0, 1):
            received(slot(0, FAR, 0, half), ("p", 0, FAR, half))
            send(lambda half=half: (slot(0, FAR, 0, half), slot(1, FAR, 0, half)), ("p", 1, FAR, half), across)
        to_sibling(0, FAR)

    def far_from_across():
        for half in (0, 1):
            received(slot(1, FAR, 0, half), ("p", 1, FAR, half))
        to_sibling(1, FAR)

    def from_sibling(h, where):
        received(slot(h, where, 1), ("sib", h, where))

    for half in (0, 1):
        send(lambda half=half: (slot(0, SELF, 0, half), slot(1, SELF, 0, half)), ("p", 1, SELF, half), across)
    to_sides(0)
    to_sibling(0, SELF)

    def product(i, raw):
        b, n = i // NZ, i % NZ
        passages = pbuf[b].reshape(BATCH, DT + DS)
        raw[0] = nn(passages[:, :DT], tqt[n])
        raw[1] = nn(passages[:, DT:], sqt[n])

    def weights(i, raw):
        b, n = i // NZ, i % NZ
        t = raw[0] * t_scale
        s = raw[1] * s_scale
        t_max = jnp.max(t, axis=0, keepdims=True)
        s_max = jnp.max(s, axis=0, keepdims=True)
        t_weight = jnp.exp2(t - t_max)
        s_weight = jnp.exp2(s - s_max)
        tw[n, b] = t_weight
        sw[n, b] = s_weight
        t_sum = jnp.sum(t_weight, axis=0, keepdims=True)
        s_sum = jnp.sum(s_weight, axis=0, keepdims=True)
        cross = jnp.sum(t_weight * (t - s), axis=0, keepdims=True)
        stat[n, b] = jnp.concatenate([t_max, t_sum, s_max, s_sum, cross, cross, cross, cross], axis=0)

    def turn(b):
        turned = pbuf[b].reshape(BATCH, DT + DS)[:, DT:].T
        part = BATCH // NCORE
        for core in range(NCORE):
            start = (core * BATCHES + b) * part
            spt[:, start:start + part] = turned[:, core * part:(core + 1) * part]

    def turn_queries(first, count):
        def body(n, carry):
            tqt[n] = tq[n].reshape(GROUP, DT).T
            sqt[n] = sq[n].reshape(GROUP, DS).T
            return carry

        lax.fori_loop(first, first + count, body, 0)

    for load in loads[2:]:
        load.wait()
    turn_queries(0, 4)
    side_halves_on()
    turn_queries(4, 4)
    for half in (0, 1):
        received(slot(1, SELF, 0, half), ("p", 1, SELF, half))
    to_sides(1)
    to_sibling(1, SELF)
    sides_to_sibling(0, (1,))
    def joined(parts):
        t_max = functools.reduce(jnp.maximum, [p[0:1] for p in parts])
        s_max = functools.reduce(jnp.maximum, [p[2:3] for p in parts])
        t_in = [jnp.exp2(p[0:1] - t_max) for p in parts]
        s_in = [jnp.exp2(p[2:3] - s_max) for p in parts]
        t_sum = functools.reduce(jnp.add, [p[1:2] * w for p, w in zip(parts, t_in)])
        s_sum = functools.reduce(jnp.add, [p[3:4] * w for p, w in zip(parts, s_in)])
        cross = functools.reduce(jnp.add, [p[4:5] * w for p, w in zip(parts, t_in)])
        return t_max, t_sum, s_max, s_sum, cross

    def stat_copy(m_to, m_slot):
        return pltpu.make_async_remote_copy(
            src_ref=stat_send.at[m_to], dst_ref=stat_recv.at[m_slot],
            send_sem=st_send_sem.at[m_to], recv_sem=st_recv_sem.at[m_slot],
            device_id=owner(m_to), device_id_type=MESH,
        )

    def res_copy(m_to, m_slot):
        return pltpu.make_async_remote_copy(
            src_ref=res_recv.at[m_slot], dst_ref=res_recv.at[m_slot],
            send_sem=rs_send_sem.at[m_to], recv_sem=rs_recv_sem.at[m_slot],
            device_id=owner(m_to), device_id_type=MESH,
        )

    def each_other(step):
        def body(i, carry):
            step((me + i) % OWNERS)
            return carry

        lax.fori_loop(1, OWNERS, body, 0)

    def leave(first):
        for n in range(first, first + 4):
            t_max, t_sum, s_max, s_sum, cross = joined([stat[n, b] for b in range(BATCHES)])
            whole = jnp.concatenate([t_max, t_sum, s_max, s_sum, cross, cross, cross, cross], axis=0)
            for y in range(NYL):
                stat_send[y * NZ + n] = whole[:, y * ROWS:(y + 1) * ROWS]

        def body(i, carry):
            m = (i // 4) * NZ + first + i % 4

            @pl.when(m != me)
            def _():
                stat_copy(m, me).start()

            return carry

        lax.fori_loop(0, 8, body, 0)

    from_sibling(0, LEFT)
    from_sibling(0, RIGHT)
    product(0, raw_a)

    def score_step(j, carry):
        @pl.when(j == 1)
        def _():
            far_across()

        @pl.when(j == 3)
        def _():
            from_sibling(0, SELF)
            from_sibling(1, SELF)

        @pl.when(j == 6)
        def _():
            sides_to_sibling(1, (0, 1))

        @pl.when(j == 7)
        def _():
            from_sibling(1, LEFT)
            from_sibling(1, RIGHT)

        @pl.when(j == 9)
        def _():
            far_from_across()

        @pl.when(j == 11)
        def _():
            from_sibling(0, FAR)
            from_sibling(1, FAR)

        @pl.when(j == 14)
        def _():
            leave(0)

        product(2 * j + 1, raw_b)
        weights(2 * j, raw_a)
        product(jnp.minimum(2 * j + 2, BATCHES * NZ - 1), raw_a)
        weights(2 * j + 1, raw_b)
        return carry

    lax.fori_loop(0, BATCHES * NZ // 2, score_step, 0)
    leave(4)
    stat_recv[me] = stat_send[me]
    for b in range(BATCHES):
        turn(b)
    flush()
    each_other(lambda m: stat_copy(m, m).wait_recv())
    t_max, t_sum, s_max, s_sum, cross = joined([stat_recv[m] for m in range(OWNERS)])
    t_in, s_in = factor / t_sum, factor / s_sum
    res_recv[me] = jnp.concatenate([t_max, t_in, s_max, s_in, t_in, t_in, t_in, t_in], axis=0)
    each_other(lambda m: res_copy(m, me).start())
    div_out[...] = cross * LN2 / t_sum - (t_max * LN2 + jnp.log(t_sum)) + (s_max * LN2 + jnp.log(s_sum))
    each_other(lambda m: stat_copy(m, me).wait_send())
    each_other(lambda m: res_copy(m, m).wait_recv())

    def group(away):
        return (z + NZ + away) % NZ

    def sequence(i):
        size = 4 - (i + 1) // 2
        return group(size * (2 * (i % 2) - 1))

    def lanes(n):
        return pl.ds(pl.multiple_of(n * GROUP, GROUP), GROUP)

    def form(i):
        n = sequence(i)
        res = jnp.concatenate([res_recv[n], res_recv[NZ + n]], axis=1)
        for b in range(BATCHES):
            st = stat[n, b]
            t_in = jnp.exp2(st[0:1] - res[0:1]) * res[1:2]
            s_in = jnp.exp2(st[2:3] - res[2:3]) * res[3:4]
            grad = (sw[n, b] * s_in - tw[n, b] * t_in).astype(BF16)
            gt[0, b, :, lanes(n)] = grad[:BATCH // 2]
            gt[1, b, :, lanes(n)] = grad[BATCH // 2:]

    def pair_copy(i):
        return pltpu.make_async_remote_copy(
            src_ref=y_pair_send.at[i], dst_ref=y_pair_recv.at[i],
            send_sem=yp_send_sem.at[i], recv_sem=yp_recv_sem.at[i],
            device_id=y_mate, device_id_type=MESH,
        )

    def query_part(i):
        n = sequence(i)
        total = nn(spt[...], gt[:, :, :, lanes(n)].reshape(NCORE * BATCHES * BATCH // 2, GROUP))
        gq[n, 0] = total[:, :ROWS]
        gq[n, 1] = total[:, ROWS:]
        y_pair_send[i] = gq[n, 1 - yl, ZF:].astype(BF16)

    def z_part(away):
        return gq[group(away), :, :ZF]

    def y_part(away):
        i = (4, 3, -3, 2, -2, 1, -1, 0).index(away)
        pair_copy(i).wait_recv()
        return gq[group(away), yl, ZF:] + y_pair_recv[i].astype(F32)

    ZH, YH = ZF // 2, YF // 2

    def z_start():
        far = z_part(4).astype(BF16)
        z_send_r[0] = far
        send(lambda: (z_send_r.at[0, :, pl.ds(0, ZH)], z_recv_r.at[0, :, pl.ds(0, ZH)]), ("zr", 0), up)
        send(lambda: (z_send_r.at[0, :, pl.ds(ZH, ZH)], z_recv_l.at[0, :, pl.ds(ZH, ZH)]), ("zl", 0), down)

    def y_start():
        y_send_r[0] = y_part(4).astype(BF16)
        send(lambda: (y_send_r.at[0, pl.ds(0, YH)], y_recv_r.at[0, pl.ds(0, YH)]), ("yr", 0), up)
        send(lambda: (y_send_r.at[0, pl.ds(YH, YH)], y_recv_l.at[0, pl.ds(YH, YH)]), ("yl", 0), down)

    def z_step(step):
        if step == 1:
            mine = z_part(3)
            received(z_recv_r.at[0, :, pl.ds(0, ZH)], ("zr", 0))
            z_send_r[1, :, :ZH] = (mine[:, :ZH] + z_recv_r[0, :, :ZH].astype(F32)).astype(BF16)
            z_send_r[1, :, ZH:] = mine[:, ZH:].astype(BF16)
        else:
            received(z_recv_r.at[step - 1], ("zr", step - 1))
            z_send_r[step] = (z_part(4 - step) + z_recv_r[step - 1].astype(F32)).astype(BF16)
        send(lambda step=step: (z_send_r.at[step], z_recv_r.at[step]), ("zr", step), up)
        if step == 1:
            mine = z_part(-3)
            received(z_recv_l.at[0, :, pl.ds(ZH, ZH)], ("zl", 0))
            z_send_l[1, :, :ZH] = mine[:, :ZH].astype(BF16)
            z_send_l[1, :, ZH:] = (mine[:, ZH:] + z_recv_l[0, :, ZH:].astype(F32)).astype(BF16)
        else:
            received(z_recv_l.at[step - 1], ("zl", step - 1))
            z_send_l[step] = (z_part(step - 4) + z_recv_l[step - 1].astype(F32)).astype(BF16)
        send(lambda step=step: (z_send_l.at[step], z_recv_l.at[step]), ("zl", step), down)

    def y_step(step):
        mine = y_part(4 - step)
        if step == 1:
            received(y_recv_r.at[0, pl.ds(0, YH)], ("yr", 0))
            y_send_r[1, :YH] = (mine[:YH] + y_recv_r[0, :YH].astype(F32)).astype(BF16)
            y_send_r[1, YH:] = mine[YH:].astype(BF16)
        else:
            received(y_recv_r.at[step - 1], ("yr", step - 1))
            y_send_r[step] = (mine + y_recv_r[step - 1].astype(F32)).astype(BF16)
        send(lambda step=step: (y_send_r.at[step], y_recv_r.at[step]), ("yr", step), up)
        mine = y_part(step - 4)
        if step == 1:
            received(y_recv_l.at[0, pl.ds(YH, YH)], ("yl", 0))
            y_send_l[1, :YH] = mine[:YH].astype(BF16)
            y_send_l[1, YH:] = (mine[YH:] + y_recv_l[0, YH:].astype(F32)).astype(BF16)
        else:
            received(y_recv_l.at[step - 1], ("yl", step - 1))
            y_send_l[step] = (mine + y_recv_l[step - 1].astype(F32)).astype(BF16)
        send(lambda step=step: (y_send_l.at[step], y_recv_l.at[step]), ("yl", step), down)

    def passage_part(core, to):
        to[...] = jnp.zeros_like(to)

        def body(n, carry):
            grads = gt[core, :, :, lanes(n)].reshape(BATCHES * BATCH // 2, GROUP)
            term = nn(grads, sq[n].reshape(GROUP, DS))
            to[...] = to[...] + term.reshape(BATCHES, 2, OWN, DS)
            return carry

        lax.fori_loop(0, NZ, body, 0)

    def gp_of(h, where):
        b, s = place(h, where, 0)
        return gp[b, s]

    def gp_first():
        received(gps_recv, "gp sibling")
        gp[...] = gp[...] + gps_recv[...].astype(F32)
        for h in range(NYH):
            gp1_send[h] = gp_of(h, FAR).astype(BF16)
        send(lambda: (gp1_send.at[0], gp1_recv.at[0]), ("gp", RIGHT, 1), right)
        send(lambda: (gp1_send.at[1], gp1_recv.at[1]), ("gp", LEFT, 1), left)

    def gp_second():
        received(gp1_recv.at[0], ("gp", RIGHT, 1))
        gp2_send[0, 0] = (gp_of(0, RIGHT) + gp1_recv[0].astype(F32)).astype(BF16)
        gp2_send[0, 1] = gp_of(1, RIGHT).astype(BF16)
        send(lambda: (gp2_send.at[0], gp2_recv.at[0]), ("gp", RIGHT, 2), right)
        received(gp1_recv.at[1], ("gp", LEFT, 1))
        gp2_send[1, 0] = gp_of(0, LEFT).astype(BF16)
        gp2_send[1, 1] = (gp_of(1, LEFT) + gp1_recv[1].astype(F32)).astype(BF16)
        send(lambda: (gp2_send.at[1], gp2_recv.at[1]), ("gp", LEFT, 2), left)

    def gp_third():
        received(gp2_recv.at[0], ("gp", RIGHT, 2))
        received(gp2_recv.at[1], ("gp", LEFT, 2))
        gp3_send[...] = x_total(1).astype(BF16)
        send(lambda: (gp3_send, gp3_recv), "gp across", across)

    def x_total(h):
        return gp_of(h, SELF) + gp2_recv[0, h].astype(F32) + gp2_recv[1, h].astype(F32)

    def z_last():
        received(z_recv_r.at[3], ("zr", 3))
        received(z_recv_l.at[3], ("zl", 3))
        for y in range(NYL):
            gq[z, y, :ZF] = gq[z, y, :ZF] + z_recv_r[3, y].astype(F32) + z_recv_l[3, y].astype(F32)
        z_pair_send[...] = gq[z, 1 - yl, :ZF].astype(BF16)
        send(lambda: (z_pair_send, z_pair_recv), "z pair", y_mate)

    form(0)

    def gradient_step(i, carry):
        query_part(i)
        form(i + 1)
        pair_copy(i).start()

        @pl.when(i == 0)
        def _():
            z_start()

        @pl.when(i == 5)
        def _():
            z_step(1)
            y_start()

        return carry

    lax.fori_loop(0, NZ - 1, gradient_step, 0)
    query_part(NZ - 1)
    pair_copy(NZ - 1).start()
    passage_part(1, gp)
    gps_send[...] = gp[...].astype(BF16)
    send(lambda: (gps_send, gps_recv), "gp sibling", sibling)
    z_step(2)
    y_step(1)
    passage_part(0, gp)
    gp_first()
    z_step(3)
    y_step(2)
    gp_second()
    each_other(lambda m: res_copy(m, me).wait_send())
    lax.fori_loop(0, NZ, lambda i, carry: (pair_copy(i).wait_send(), carry)[1], 0)
    z_last()
    y_step(3)
    gp_third()
    flush()

    mine = y_part(0)
    received(y_recv_r.at[3], ("yr", 3))
    received(y_recv_l.at[3], ("yl", 3))
    gq_out[:, ZF:] = (mine + y_recv_r[3].astype(F32) + y_recv_l[3].astype(F32)).T
    received(z_pair_recv, "z pair")
    gq_out[:, :ZF] = (gq[z, yl, :ZF] + z_pair_recv[...].astype(F32)).T
    received(gp3_recv, "gp across")
    gp_out[...] = x_total(0) + gp3_recv[...].astype(F32)


def deliver(gq_in, gp_in, div_in, gq_out, gp_out, div_out, gq, gp, div, in_sem, out_sem):
    parts = ((gq_in, gq, gq_out), (gp_in, gp, gp_out), (div_in, div, div_out))
    ins = [pltpu.make_async_copy(src, mid, in_sem.at[i]) for i, (src, mid, _) in enumerate(parts)]
    outs = [pltpu.make_async_copy(mid, dst, out_sem.at[i]) for i, (_, mid, dst) in enumerate(parts)]
    for copy in ins:
        copy.start()
    for arrive, leave in zip(ins, outs):
        arrive.wait()
        leave.start()
    for copy in outs:
        copy.wait()


def local(teacher_query, student_query, teacher_passages, student_passages):
    blocks = NYL, NZ, NCORE, ROWS
    hbm = pl.BlockSpec(memory_space=pl.ANY)
    vmem = pl.BlockSpec(memory_space=pltpu.VMEM)
    outs = (
        jax.ShapeDtypeStruct((ROWS, DS), F32),
        jax.ShapeDtypeStruct((OWN, DS), F32),
        jax.ShapeDtypeStruct((1, ROWS), F32),
    )
    results = pl.pallas_call(
        kernel,
        out_shape=outs,
        in_specs=[hbm] * 4,
        out_specs=(vmem,) * 3,
        scratch_shapes=[
            pltpu.VMEM((NZ, NYL, ROWS, DT), BF16),
            pltpu.VMEM((NZ, NYL, ROWS, DS), BF16),
            pltpu.VMEM((NZ, DT, GROUP), BF16),
            pltpu.VMEM((NZ, DS, GROUP), BF16),
            pltpu.VMEM((BATCHES, BATCH // OWN, OWN, DT + DS), BF16),
            pltpu.VMEM((DS, BATCHES * BATCH), BF16),
            pltpu.VMEM((NZ, BATCHES, BATCH, GROUP), F32),
            pltpu.VMEM((NZ, BATCHES, BATCH, GROUP), F32),
            pltpu.VMEM((2, BATCH, GROUP), F32),
            pltpu.VMEM((2, BATCH, GROUP), F32),
            pltpu.VMEM((NCORE, BATCHES, BATCH // 2, NZ * GROUP), BF16),
            pltpu.VMEM((NZ, BATCHES, 8, GROUP), F32),
            pltpu.VMEM((NZ, NYL, DS, ROWS), F32),
            pltpu.VMEM((OWNERS, 8, ROWS), F32),
            pltpu.VMEM((OWNERS, 8, ROWS), F32),
            pltpu.VMEM((OWNERS, 8, ROWS), F32),
            pltpu.VMEM((4, NYL, ZF, ROWS), BF16),
            pltpu.VMEM((4, NYL, ZF, ROWS), BF16),
            pltpu.VMEM((4, NYL, ZF, ROWS), BF16),
            pltpu.VMEM((4, NYL, ZF, ROWS), BF16),
            pltpu.VMEM((ZF, ROWS), BF16),
            pltpu.VMEM((ZF, ROWS), BF16),
            pltpu.VMEM((NZ, YF, ROWS), BF16),
            pltpu.VMEM((NZ, YF, ROWS), BF16),
            pltpu.VMEM((4, YF, ROWS), BF16),
            pltpu.VMEM((4, YF, ROWS), BF16),
            pltpu.VMEM((4, YF, ROWS), BF16),
            pltpu.VMEM((4, YF, ROWS), BF16),
            pltpu.VMEM((BATCHES, 2, OWN, DS), F32),
            pltpu.VMEM((BATCHES, 2, OWN, DS), BF16),
            pltpu.VMEM((BATCHES, 2, OWN, DS), BF16),
            pltpu.VMEM((NYH, OWN, DS), BF16),
            pltpu.VMEM((NYH, OWN, DS), BF16),
            pltpu.VMEM((2, NYH, OWN, DS), BF16),
            pltpu.VMEM((2, NYH, OWN, DS), BF16),
            pltpu.VMEM((OWN, DS), BF16),
            pltpu.VMEM((OWN, DS), BF16),
            pltpu.SemaphoreType.DMA((6,)),
            pltpu.SemaphoreType.DMA((MESSAGES,)),
            pltpu.SemaphoreType.DMA((MESSAGES,)),
            pltpu.SemaphoreType.DMA((NZ,)),
            pltpu.SemaphoreType.DMA((NZ,)),
            pltpu.SemaphoreType.DMA((OWNERS,)),
            pltpu.SemaphoreType.DMA((OWNERS,)),
            pltpu.SemaphoreType.DMA((OWNERS,)),
            pltpu.SemaphoreType.DMA((OWNERS,)),
        ],
        compiler_params=pltpu.CompilerParams(
            collective_id=0, has_side_effects=True, vmem_limit_bytes=VMEM_BYTES
        ),
    )(
        teacher_query.reshape(*blocks, DT),
        student_query.reshape(*blocks, DS),
        teacher_passages,
        student_passages,
    )
    grad_query, grad_passage, divergence = pl.pallas_call(
        deliver,
        out_shape=outs,
        in_specs=[hbm] * 3,
        out_specs=(hbm,) * 3,
        scratch_shapes=[
            *(pltpu.VMEM(out.shape, out.dtype) for out in outs),
            pltpu.SemaphoreType.DMA((3,)),
            pltpu.SemaphoreType.DMA((3,)),
        ],
        compiler_params=pltpu.CompilerParams(vmem_limit_bytes=VMEM_BYTES),
    )(*results)
    return divergence.reshape(ROWS), grad_query, grad_passage


def solution(mesh):
    return jax.shard_map(
        local,
        mesh=mesh,
        in_specs=(
            P("query", None),
            P("query", None),
            P(("query", "corpus"), None),
            P(("query", "corpus"), None),
        ),
        out_specs=(
            P(("query", "corpus")),
            P(("query", "corpus"), None),
            P(("query", "corpus"), None),
        ),
        check_vma=False,
    )
```

```python
import functools
import math

import jax
import jax.numpy as jnp
from jax import lax
from jax.experimental import pallas as pl
from jax.experimental.pallas import tpu as pltpu
from jax.sharding import PartitionSpec as P

NX, NYH, NYL, NZ, NCORE = 4, 2, 2, 8, 2
OWN = 64
ROWS = 128
DT, DS = 1024, 384
BATCHES = 4
BATCH = 256
GROUP = NYL * ROWS
OWNERS = NYL * NZ
PIECE = OWN // 4
ZF = 192
YF = DS - ZF
LOG2E = math.log2(math.e)
LN2 = math.log(2.0)
F32, BF16 = jnp.float32, jnp.bfloat16
MESH = pl.DeviceIdType.MESH

SELF, LEFT, RIGHT, FAR = 0, 1, 2, 3


def place(h, where, core):
    if where == SELF:
        return 1, core * 2 + h
    if where == FAR:
        return 3, core * 2 + h
    return 2 * h, core * 2 + (where - LEFT)


def nn(a, b):
    return lax.dot_general(a, b, (((1,), (0,)), ((), ())), preferred_element_type=F32)


class Messages:
    def __init__(self):
        self.numbers = {}

    def __call__(self, name):
        return self.numbers.setdefault(name, len(self.numbers))


MESSAGES = 96
VMEM_BYTES = 60 * 1024 * 1024


def kernel(
    tq_hbm, sq_hbm, tp_hbm, sp_hbm,
    gq_out, gp_out, div_out,
    tq, sq, tqt, sqt, pbuf, spt, tw, sw, raw_a, raw_b, gt, stat, gq,
    stat_send, stat_recv, res_recv,
    z_send, z_recv, z_pair_send, z_pair_recv,
    y_pair_send, y_pair_recv, y_send, y_recv,
    gp, gps_send, gps_recv, gp1_send, gp1_recv, gp2_send, gp2_recv, gp3_send, gp3_recv,
    load_sem, send_sem, recv_sem, yp_send_sem, yp_recv_sem, st_send_sem, st_recv_sem, rs_send_sem, rs_recv_sem,
):
    t_scale = DT ** (-0.5) * LOG2E
    s_scale = DS ** (-0.5) * LOG2E
    factor = DS ** (-0.5)
    q = lax.axis_index("query")
    c = lax.axis_index("corpus")
    x, yh = q // NYH, q % NYH
    yl, z, k = c // (NZ * NCORE), (c // NCORE) % NZ, c % NCORE
    me = yl * NZ + z

    def at(x_, yh_, yl_, z_, k_):
        return (x_ * NYH + yh_, (yl_ * NZ + z_) * NCORE + k_)

    right, left = at((x + 1) % NX, yh, yl, z, k), at((x + NX - 1) % NX, yh, yl, z, k)
    across = at(x, 1 - yh, 1 - yl, z, k)
    sibling = at(x, yh, yl, z, 1 - k)
    up, down = at(x, yh, yl, (z + 1) % NZ, k), at(x, yh, yl, (z + NZ - 1) % NZ, k)
    y_mate = at(x, yh, 1 - yl, z, k)

    def owner(m):
        return at(x, yh, m // NZ, m % NZ, k)

    def slot(h, where, core, first=0, count=4):
        b, s = place(h, where, core)
        return pbuf.at[b, s, pl.ds(first * PIECE, count * PIECE)]

    loads = [
        pltpu.make_async_copy(tp_hbm, pbuf.at[1, 0, :, pl.ds(0, DT)], load_sem.at[0]),
        pltpu.make_async_copy(sp_hbm, pbuf.at[1, 0, :, pl.ds(DT, DS)], load_sem.at[1]),
    ]
    for y in range(NYL):
        loads.append(pltpu.make_async_copy(tq_hbm.at[y, :, k], tq.at[:, y], load_sem.at[2 + y]))
        loads.append(pltpu.make_async_copy(sq_hbm.at[y, :, k], sq.at[:, y], load_sem.at[4 + y]))
    for load in loads:
        load.start()

    barrier = pltpu.get_barrier_semaphore()
    for device in (right, left, across, sibling):
        pl.semaphore_signal(barrier, inc=1, device_id=device, device_id_type=MESH)

    def greet(i, carry):
        pl.semaphore_signal(barrier, inc=1, device_id=owner((me + i) % OWNERS), device_id_type=MESH)
        return carry

    lax.fori_loop(1, OWNERS, greet, 0)
    pl.semaphore_wait(barrier, 4 + OWNERS - 1)
    loads[0].wait()
    loads[1].wait()

    number = Messages()
    sent = []

    def message(refs, name, device):
        i = number(name)
        src, dst = refs()
        return pltpu.make_async_remote_copy(
            src_ref=src, dst_ref=dst, send_sem=send_sem.at[i], recv_sem=recv_sem.at[i],
            device_id=device, device_id_type=MESH,
        )

    def send(refs, name, device):
        message(refs, name, device).start()
        sent.append((refs, name, device))

    def flush():
        for args in sent:
            message(*args).wait_send()
        sent.clear()

    def received(ref, name):
        message(lambda: (ref, ref), name, sibling).wait_recv()

    def passages(h, where, to_h, to_where, first, count, device):
        send(
            lambda: (slot(h, where, 0, first, count), slot(to_h, to_where, 0, first, count)),
            ("p", to_h, to_where, first, count), device,
        )

    def arrived(h, where, first, count):
        received(slot(h, where, 0, first, count), ("p", h, where, first, count))

    def to_sibling(h, where):
        send(lambda: (slot(h, where, 0), slot(h, where, 1)), ("sib", h, where), sibling)

    def far_on(i):
        arrived(0, LEFT, i, 1)
        passages(0, LEFT, 0, FAR, i, 1, right)
        arrived(0, RIGHT, 2 + i, 1)
        passages(0, RIGHT, 0, FAR, 2 + i, 1, left)

    def far_across():
        for i in (0, 2, 1, 3):
            arrived(0, FAR, i, 1)
            passages(0, FAR, 1, FAR, i, 1, across)
        to_sibling(0, FAR)

    def far_from_across():
        for i in (0, 2, 1, 3):
            arrived(1, FAR, i, 1)
        to_sibling(1, FAR)

    def across_to_sides(first):
        arrived(1, SELF, first, 2)
        passages(1, SELF, 1, LEFT, first, 2, right)
        passages(1, SELF, 1, RIGHT, first, 2, left)

    def sides_to_sibling(h):
        for where in (LEFT, RIGHT):
            if h == 0:
                arrived(0, where, 2 if where == LEFT else 0, 2)
            else:
                arrived(1, where, 0, 2)
                arrived(1, where, 2, 2)
            to_sibling(h, where)

    def from_sibling(h, where):
        received(slot(h, where, 1), ("sib", h, where))

    passages(0, SELF, 0, LEFT, 0, 1, right)
    passages(0, SELF, 0, RIGHT, 2, 1, left)
    passages(0, SELF, 1, SELF, 0, 2, across)
    passages(0, SELF, 0, LEFT, 1, 1, right)
    passages(0, SELF, 0, RIGHT, 3, 1, left)
    passages(0, SELF, 0, LEFT, 2, 2, right)
    passages(0, SELF, 0, RIGHT, 0, 2, left)
    passages(0, SELF, 1, SELF, 2, 2, across)
    to_sibling(0, SELF)

    def product(i, raw):
        b, n = i // NZ, i % NZ
        batch = pbuf[b].reshape(BATCH, DT + DS)
        raw[0] = nn(batch[:, :DT], tqt[n])
        raw[1] = nn(batch[:, DT:], sqt[n])

    def weights(i, raw):
        b, n = i // NZ, i % NZ
        t = raw[0] * t_scale
        s = raw[1] * s_scale
        t_max = jnp.max(t, axis=0, keepdims=True)
        s_max = jnp.max(s, axis=0, keepdims=True)
        t_weight = jnp.exp2(t - t_max)
        s_weight = jnp.exp2(s - s_max)
        tw[n, b] = t_weight
        sw[n, b] = s_weight
        t_sum = jnp.sum(t_weight, axis=0, keepdims=True)
        s_sum = jnp.sum(s_weight, axis=0, keepdims=True)
        cross = jnp.sum(t_weight * (t - s), axis=0, keepdims=True)
        stat[n, b] = jnp.concatenate([t_max, t_sum, s_max, s_sum, cross, cross, cross, cross], axis=0)

    def turn(b):
        turned = pbuf[b].reshape(BATCH, DT + DS)[:, DT:].T
        part = BATCH // NCORE
        for core in range(NCORE):
            start = (core * BATCHES + b) * part
            spt[:, start:start + part] = turned[:, core * part:(core + 1) * part]

    def turn_queries(first, count):
        def body(n, carry):
            tqt[n] = tq[n].reshape(GROUP, DT).T
            sqt[n] = sq[n].reshape(GROUP, DS).T
            return carry

        lax.fori_loop(first, first + count, body, 0)

    for load in loads[2:]:
        load.wait()
    turn_queries(0, 4)
    far_on(0)
    turn_queries(4, 2)
    far_on(1)
    across_to_sides(0)
    turn_queries(6, 2)
    sides_to_sibling(0)
    across_to_sides(2)
    to_sibling(1, SELF)
    far_across()

    def joined(parts):
        t_max = functools.reduce(jnp.maximum, [p[0:1] for p in parts])
        s_max = functools.reduce(jnp.maximum, [p[2:3] for p in parts])
        t_in = [jnp.exp2(p[0:1] - t_max) for p in parts]
        s_in = [jnp.exp2(p[2:3] - s_max) for p in parts]
        t_sum = functools.reduce(jnp.add, [p[1:2] * w for p, w in zip(parts, t_in)])
        s_sum = functools.reduce(jnp.add, [p[3:4] * w for p, w in zip(parts, s_in)])
        cross = functools.reduce(jnp.add, [p[4:5] * w for p, w in zip(parts, t_in)])
        return t_max, t_sum, s_max, s_sum, cross

    def stat_copy(m_to, m_slot):
        return pltpu.make_async_remote_copy(
            src_ref=stat_send.at[m_to], dst_ref=stat_recv.at[m_slot],
            send_sem=st_send_sem.at[m_to], recv_sem=st_recv_sem.at[m_slot],
            device_id=owner(m_to), device_id_type=MESH,
        )

    def res_copy(m_to, m_slot):
        return pltpu.make_async_remote_copy(
            src_ref=res_recv.at[m_slot], dst_ref=res_recv.at[m_slot],
            send_sem=rs_send_sem.at[m_to], recv_sem=rs_recv_sem.at[m_slot],
            device_id=owner(m_to), device_id_type=MESH,
        )

    def each_other(step):
        def body(i, carry):
            step((me + i) % OWNERS)
            return carry

        lax.fori_loop(1, OWNERS, body, 0)

    def leave(first):
        for n in range(first, first + 4):
            t_max, t_sum, s_max, s_sum, cross = joined([stat[n, b] for b in range(BATCHES)])
            whole = jnp.concatenate([t_max, t_sum, s_max, s_sum, cross, cross, cross, cross], axis=0)
            for y in range(NYL):
                stat_send[y * NZ + n] = whole[:, y * ROWS:(y + 1) * ROWS]

        def body(i, carry):
            m = (i // 4) * NZ + first + i % 4

            @pl.when(m != me)
            def _():
                stat_copy(m, me).start()

            return carry

        lax.fori_loop(0, 8, body, 0)

    from_sibling(0, LEFT)
    from_sibling(0, RIGHT)
    product(0, raw_a)

    def score_step(j, carry):
        @pl.when(j == 3)
        def _():
            from_sibling(0, SELF)
            from_sibling(1, SELF)

        @pl.when(j == 5)
        def _():
            sides_to_sibling(1)

        @pl.when(j == 6)
        def _():
            far_from_across()

        @pl.when(j == 7)
        def _():
            from_sibling(1, LEFT)
            from_sibling(1, RIGHT)

        @pl.when(j == 11)
        def _():
            from_sibling(0, FAR)
            from_sibling(1, FAR)

        @pl.when(j == 14)
        def _():
            leave(0)

        product(2 * j + 1, raw_b)
        weights(2 * j, raw_a)
        product(jnp.minimum(2 * j + 2, BATCHES * NZ - 1), raw_a)
        weights(2 * j + 1, raw_b)
        return carry

    lax.fori_loop(0, BATCHES * NZ // 2, score_step, 0)
    leave(4)
    stat_recv[me] = stat_send[me]
    for b in range(BATCHES):
        turn(b)
    flush()
    each_other(lambda m: stat_copy(m, m).wait_recv())
    t_max, t_sum, s_max, s_sum, cross = joined([stat_recv[m] for m in range(OWNERS)])
    t_in, s_in = factor / t_sum, factor / s_sum
    res_recv[me] = jnp.concatenate([t_max, t_in, s_max, s_in, t_in, t_in, t_in, t_in], axis=0)
    each_other(lambda m: res_copy(m, me).start())
    div_out[...] = cross * LN2 / t_sum - (t_max * LN2 + jnp.log(t_sum)) + (s_max * LN2 + jnp.log(s_sum))
    each_other(lambda m: stat_copy(m, me).wait_send())
    each_other(lambda m: res_copy(m, m).wait_recv())

    def group(away):
        return (z + NZ + away) % NZ

    def sequence(i):
        size = 4 - (i + 1) // 2
        return group(size * (2 * (i % 2) - 1))

    def lanes(n):
        return pl.ds(pl.multiple_of(n * GROUP, GROUP), GROUP)

    def form(i):
        n = sequence(i)
        res = jnp.concatenate([res_recv[n], res_recv[NZ + n]], axis=1)
        for b in range(BATCHES):
            st = stat[n, b]
            t_in = jnp.exp2(st[0:1] - res[0:1]) * res[1:2]
            s_in = jnp.exp2(st[2:3] - res[2:3]) * res[3:4]
            grad = (sw[n, b] * s_in - tw[n, b] * t_in).astype(BF16)
            gt[0, b, :, lanes(n)] = grad[:BATCH // 2]
            gt[1, b, :, lanes(n)] = grad[BATCH // 2:]

    def pair_copy(i):
        return pltpu.make_async_remote_copy(
            src_ref=y_pair_send.at[i], dst_ref=y_pair_recv.at[i],
            send_sem=yp_send_sem.at[i], recv_sem=yp_recv_sem.at[i],
            device_id=y_mate, device_id_type=MESH,
        )

    def query_part(i):
        n = sequence(i)
        total = nn(spt[...], gt[:, :, :, lanes(n)].reshape(NCORE * BATCHES * BATCH // 2, GROUP))
        gq[n, 0] = total[:, :ROWS]
        gq[n, 1] = total[:, ROWS:]
        y_pair_send[i] = gq[n, 1 - yl, ZF:].astype(BF16)

    def order(away):
        return (4, 3, -3, 2, -2, 1, -1, 0).index(4 if away == -4 else away)

    def pair_arrived(away):
        pair_copy(order(away)).wait_recv()

    def part(chain, away):
        n = group(away)
        if chain < 2:
            return gq[n, chain, :ZF]
        i = order(away)
        start = (chain - 2) * YF // 2
        pair = y_pair_recv[i, start:start + YF // 2].astype(F32)
        return gq[n, yl, ZF + start:ZF + start + YF // 2] + pair

    rings = (z_send, z_recv), (y_send, y_recv)

    def slots(chain, way, step):
        sends, recvs = rings[chain // 2]
        return sends.at[chain % 2, way, step], recvs.at[chain % 2, way, step]

    def come(chain, way, step):
        received(slots(chain, way, step)[1], ("ring", chain, way, step))
        return rings[chain // 2][1][chain % 2, way, step].astype(F32)

    def ring_step(chain, way, step):
        total = part(chain, 4 - step if way == 0 else step - 4)
        if step > 1 or (step == 1 and chain % 2 == way):
            total = total + come(chain, way, step - 1)
        rings[chain // 2][0][chain % 2, way, step] = total.astype(BF16)
        send(lambda: slots(chain, way, step), ("ring", chain, way, step), down if way else up)

    def ring_steps(chains, step):
        for chain in chains:
            for way in (chain % 2, 1 - chain % 2):
                ring_step(chain, way, step)

    def ring_total(chain):
        return part(chain, 0) + come(chain, 0, 3) + come(chain, 1, 3)

    def passage_part(core, to):
        to[...] = jnp.zeros_like(to)

        def body(n, carry):
            grads = gt[core, :, :, lanes(n)].reshape(BATCHES * BATCH // 2, GROUP)
            term = nn(grads, sq[n].reshape(GROUP, DS))
            to[...] = to[...] + term.reshape(BATCHES, 2, OWN, DS)
            return carry

        lax.fori_loop(0, NZ, body, 0)

    def gp_of(h, where):
        b, s = place(h, where, 0)
        return gp[b, s]

    def gp_first():
        received(gps_recv, "gp sibling")
        gp[...] = gp[...] + gps_recv[...].astype(F32)
        for h in range(NYH):
            gp1_send[h] = gp_of(h, FAR).astype(BF16)
        send(lambda: (gp1_send.at[0], gp1_recv.at[0]), ("gp", RIGHT, 1), right)
        send(lambda: (gp1_send.at[1], gp1_recv.at[1]), ("gp", LEFT, 1), left)

    def gp_second():
        received(gp1_recv.at[0], ("gp", RIGHT, 1))
        gp2_send[0, 0] = (gp_of(0, RIGHT) + gp1_recv[0].astype(F32)).astype(BF16)
        gp2_send[0, 1] = gp_of(1, RIGHT).astype(BF16)
        send(lambda: (gp2_send.at[0], gp2_recv.at[0]), ("gp", RIGHT, 2), right)
        received(gp1_recv.at[1], ("gp", LEFT, 1))
        gp2_send[1, 0] = gp_of(0, LEFT).astype(BF16)
        gp2_send[1, 1] = (gp_of(1, LEFT) + gp1_recv[1].astype(F32)).astype(BF16)
        send(lambda: (gp2_send.at[1], gp2_recv.at[1]), ("gp", LEFT, 2), left)

    def gp_third():
        received(gp2_recv.at[0], ("gp", RIGHT, 2))
        received(gp2_recv.at[1], ("gp", LEFT, 2))
        gp3_send[...] = x_total(1).astype(BF16)
        send(lambda: (gp3_send, gp3_recv), "gp across", across)

    def x_total(h):
        return gp_of(h, SELF) + gp2_recv[0, h].astype(F32) + gp2_recv[1, h].astype(F32)

    form(0)

    def gradient_step(i, carry):
        query_part(i)
        form(i + 1)
        pair_copy(i).start()

        @pl.when(i == 0)
        def _():
            ring_step(0, 0, 0)
            ring_step(1, 1, 0)

        @pl.when(i == 2)
        def _():
            ring_step(1, 0, 1)
            ring_step(0, 1, 1)

        @pl.when(i == 5)
        def _():
            ring_step(0, 0, 1)
            ring_step(1, 1, 1)

        @pl.when(i == 6)
        def _():
            pair_arrived(4)
            ring_step(2, 0, 0)
            ring_step(3, 1, 0)
            pair_arrived(3)
            ring_step(3, 0, 1)
            pair_arrived(-3)
            ring_step(2, 1, 1)

        return carry

    lax.fori_loop(0, NZ - 1, gradient_step, 0)
    query_part(NZ - 1)
    pair_copy(NZ - 1).start()
    ring_steps((0, 1), 2)
    passage_part(1, gp)
    gps_send[...] = gp[...].astype(BF16)
    send(lambda: (gps_send, gps_recv), "gp sibling", sibling)
    ring_step(2, 0, 1)
    ring_step(3, 1, 1)
    passage_part(0, gp)
    gp_first()
    ring_steps((0, 1), 3)
    pair_arrived(2)
    pair_arrived(-2)
    ring_steps((2, 3), 2)
    gp_second()
    each_other(lambda m: res_copy(m, me).wait_send())
    lax.fori_loop(0, NZ, lambda i, carry: (pair_copy(i).wait_send(), carry)[1], 0)
    pair_arrived(1)
    pair_arrived(-1)
    for y in range(NYL):
        gq[z, y, :ZF] = ring_total(y)
    z_pair_send[...] = gq[z, 1 - yl, :ZF].astype(BF16)
    send(lambda: (z_pair_send, z_pair_recv), "z pair", y_mate)
    ring_steps((2, 3), 3)
    gp_third()
    flush()
    pair_arrived(0)
    for chain in (2, 3):
        start = ZF + (chain - 2) * YF // 2
        gq[z, yl, start:start + YF // 2] = ring_total(chain)
    gq_out[:, ZF:] = gq[z, yl, ZF:].T
    received(z_pair_recv, "z pair")
    gq_out[:, :ZF] = (gq[z, yl, :ZF] + z_pair_recv[...].astype(F32)).T
    received(gp3_recv, "gp across")
    gp_out[...] = x_total(0) + gp3_recv[...].astype(F32)


def deliver(gq_in, gp_in, div_in, gq_out, gp_out, div_out, gq, gp, div, in_sem, out_sem):
    parts = ((gq_in, gq, gq_out), (gp_in, gp, gp_out), (div_in, div, div_out))
    ins = [pltpu.make_async_copy(src, mid, in_sem.at[i]) for i, (src, mid, _) in enumerate(parts)]
    outs = [pltpu.make_async_copy(mid, dst, out_sem.at[i]) for i, (_, mid, dst) in enumerate(parts)]
    for copy in ins:
        copy.start()
    for arrive, leave in zip(ins, outs):
        arrive.wait()
        leave.start()
    for copy in outs:
        copy.wait()


def local(teacher_query, student_query, teacher_passages, student_passages):
    blocks = NYL, NZ, NCORE, ROWS
    hbm = pl.BlockSpec(memory_space=pl.ANY)
    vmem = pl.BlockSpec(memory_space=pltpu.VMEM)
    outs = (
        jax.ShapeDtypeStruct((ROWS, DS), F32),
        jax.ShapeDtypeStruct((OWN, DS), F32),
        jax.ShapeDtypeStruct((1, ROWS), F32),
    )
    results = pl.pallas_call(
        kernel,
        out_shape=outs,
        in_specs=[hbm] * 4,
        out_specs=(vmem,) * 3,
        scratch_shapes=[
            pltpu.VMEM((NZ, NYL, ROWS, DT), BF16),
            pltpu.VMEM((NZ, NYL, ROWS, DS), BF16),
            pltpu.VMEM((NZ, DT, GROUP), BF16),
            pltpu.VMEM((NZ, DS, GROUP), BF16),
            pltpu.VMEM((BATCHES, BATCH // OWN, OWN, DT + DS), BF16),
            pltpu.VMEM((DS, BATCHES * BATCH), BF16),
            pltpu.VMEM((NZ, BATCHES, BATCH, GROUP), F32),
            pltpu.VMEM((NZ, BATCHES, BATCH, GROUP), F32),
            pltpu.VMEM((2, BATCH, GROUP), F32),
            pltpu.VMEM((2, BATCH, GROUP), F32),
            pltpu.VMEM((NCORE, BATCHES, BATCH // 2, NZ * GROUP), BF16),
            pltpu.VMEM((NZ, BATCHES, 8, GROUP), F32),
            pltpu.VMEM((NZ, NYL, DS, ROWS), F32),
            pltpu.VMEM((OWNERS, 8, ROWS), F32),
            pltpu.VMEM((OWNERS, 8, ROWS), F32),
            pltpu.VMEM((OWNERS, 8, ROWS), F32),
            pltpu.VMEM((2, 2, 4, ZF, ROWS), BF16),
            pltpu.VMEM((2, 2, 4, ZF, ROWS), BF16),
            pltpu.VMEM((ZF, ROWS), BF16),
            pltpu.VMEM((ZF, ROWS), BF16),
            pltpu.VMEM((NZ, YF, ROWS), BF16),
            pltpu.VMEM((NZ, YF, ROWS), BF16),
            pltpu.VMEM((2, 2, 4, YF // 2, ROWS), BF16),
            pltpu.VMEM((2, 2, 4, YF // 2, ROWS), BF16),
            pltpu.VMEM((BATCHES, 2, OWN, DS), F32),
            pltpu.VMEM((BATCHES, 2, OWN, DS), BF16),
            pltpu.VMEM((BATCHES, 2, OWN, DS), BF16),
            pltpu.VMEM((NYH, OWN, DS), BF16),
            pltpu.VMEM((NYH, OWN, DS), BF16),
            pltpu.VMEM((2, NYH, OWN, DS), BF16),
            pltpu.VMEM((2, NYH, OWN, DS), BF16),
            pltpu.VMEM((OWN, DS), BF16),
            pltpu.VMEM((OWN, DS), BF16),
            pltpu.SemaphoreType.DMA((6,)),
            pltpu.SemaphoreType.DMA((MESSAGES,)),
            pltpu.SemaphoreType.DMA((MESSAGES,)),
            pltpu.SemaphoreType.DMA((NZ,)),
            pltpu.SemaphoreType.DMA((NZ,)),
            pltpu.SemaphoreType.DMA((OWNERS,)),
            pltpu.SemaphoreType.DMA((OWNERS,)),
            pltpu.SemaphoreType.DMA((OWNERS,)),
            pltpu.SemaphoreType.DMA((OWNERS,)),
        ],
        compiler_params=pltpu.CompilerParams(
            collective_id=0, has_side_effects=True, vmem_limit_bytes=VMEM_BYTES
        ),
    )(
        teacher_query.reshape(*blocks, DT),
        student_query.reshape(*blocks, DS),
        teacher_passages,
        student_passages,
    )
    grad_query, grad_passage, divergence = pl.pallas_call(
        deliver,
        out_shape=outs,
        in_specs=[hbm] * 3,
        out_specs=(hbm,) * 3,
        scratch_shapes=[
            *(pltpu.VMEM(out.shape, out.dtype) for out in outs),
            pltpu.SemaphoreType.DMA((3,)),
            pltpu.SemaphoreType.DMA((3,)),
        ],
        compiler_params=pltpu.CompilerParams(vmem_limit_bytes=VMEM_BYTES),
    )(*results)
    return divergence.reshape(ROWS), grad_query, grad_passage


def solution(mesh):
    return jax.shard_map(
        local,
        mesh=mesh,
        in_specs=(
            P("query", None),
            P("query", None),
            P(("query", "corpus"), None),
            P(("query", "corpus"), None),
        ),
        out_specs=(
            P(("query", "corpus")),
            P(("query", "corpus"), None),
            P(("query", "corpus"), None),
        ),
        check_vma=False,
    )
```

```python
import functools
import math

import jax
import jax.numpy as jnp
from jax import lax
from jax.experimental import pallas as pl
from jax.experimental.pallas import tpu as pltpu
from jax.sharding import PartitionSpec as P

NX, NYH, NYL, NZ, NCORE = 4, 2, 2, 8, 2
OWN = 64
ROWS = 128
DT, DS = 1024, 384
BATCHES = 4
SLOTS = 4
BATCH = 256
GROUP = NYL * ROWS
OWNERS = NYL * NZ
HALF = OWN // 2
ZF = 192
YF = DS - ZF
LOG2E = math.log2(math.e)
LN2 = math.log(2.0)
F32, BF16 = jnp.float32, jnp.bfloat16
MESH = pl.DeviceIdType.MESH

SELF, LEFT, RIGHT, FAR = 0, 1, 2, 3


def place(h, where, core):
    if where == SELF:
        return 1, core * 2 + h
    if where == FAR:
        return 3, core * 2 + h
    return 2 * h, core * 2 + (where - LEFT)


def div(a, b):
    return lax.div(a, jnp.int32(b))


def rem(a, b):
    return lax.rem(a, jnp.int32(b))


def nt(a, b):
    return lax.dot_general(a, b, (((1,), (1,)), ((), ())), preferred_element_type=F32)


def nn(a, b):
    return lax.dot_general(a, b, (((1,), (0,)), ((), ())), preferred_element_type=F32)


class Messages:
    def __init__(self):
        self.numbers = {}

    def __call__(self, name):
        return self.numbers.setdefault(name, len(self.numbers))


MESSAGES = 80
VMEM_BYTES = 60 * 1024 * 1024


def kernel(
    tq_hbm, sq_hbm, tp_hbm, sp_hbm,
    gq_out, gp_out, div_out,
    tq, sq, pbuf, spt, tw, sw, raw_a, raw_b, gt, stat, gq,
    stat_send, stat_recv, res_recv,
    z_send, z_recv_r, z_recv_l, z_pair_send, z_pair_recv,
    y_pair_send, y_pair_recv, y_send, y_recv_r, y_recv_l,
    gp, gps_send, gps_recv, gp1_send, gp1_recv, gp2_send, gp2_recv, gp3_send, gp3_recv,
    load_sem, gather_sem, ring_sem, send_sem, recv_sem, yp_recv_sem, st_sem,
):
    t_scale = DT ** (-0.5) * LOG2E
    s_scale = DS ** (-0.5) * LOG2E
    factor = DS ** (-0.5)
    q = lax.axis_index("query")
    c = lax.axis_index("corpus")
    x, yh = div(q, NYH), rem(q, NYH)
    yl, z, k = div(c, NZ * NCORE), rem(div(c, NCORE), NZ), rem(c, NCORE)
    me = yl * NZ + z

    def at(x_, yh_, yl_, z_, k_):
        return (x_ * NYH + yh_, (yl_ * NZ + z_) * NCORE + k_)

    right, left = at(rem(x + 1, NX), yh, yl, z, k), at(rem(x + NX - 1, NX), yh, yl, z, k)
    across = at(x, 1 - yh, 1 - yl, z, k)
    sibling = at(x, yh, yl, z, 1 - k)
    up, down = at(x, yh, yl, rem(z + 1, NZ), k), at(x, yh, yl, rem(z + NZ - 1, NZ), k)
    y_mate = at(x, yh, 1 - yl, z, k)

    offsets = [(dy, dz) for dy in range(NYL) for dz in range(NZ) if (dy, dz) != (0, 0)]
    y_of = [yl, 1 - yl]
    z_of = [rem(z + dz, NZ) for dz in range(NZ)]

    def offset_device(dy, dz):
        return at(x, yh, y_of[dy], z_of[dz], k)

    def slot(h, where, core, half=None):
        b, s = place(h, where, core)
        if half is None:
            return pbuf.at[b * SLOTS + s]
        return pbuf.at[b * SLOTS + s, pl.ds(half * HALF, HALF)]

    def both(b, core):
        return pbuf.at[pl.ds(b * SLOTS + core * 2, 2)]

    loads = [
        pltpu.make_async_copy(tp_hbm, pbuf.at[SLOTS, :, pl.ds(0, DT)], load_sem.at[0]),
        pltpu.make_async_copy(sp_hbm, pbuf.at[SLOTS, :, pl.ds(DT, DS)], load_sem.at[1]),
    ]
    for y in range(NYL):
        loads.append(pltpu.make_async_copy(tq_hbm.at[y, :, k], tq.at[:, y], load_sem.at[2 + y]))
        loads.append(pltpu.make_async_copy(sq_hbm.at[y, :, k], sq.at[:, y], load_sem.at[4 + y]))
    for load in loads:
        load.start()

    barrier = pltpu.get_barrier_semaphore()
    for device in (right, left, across, sibling):
        pl.semaphore_signal(barrier, inc=1, device_id=device, device_id_type=MESH)

    for offset in offsets:
        pl.semaphore_signal(barrier, inc=1, device_id=offset_device(*offset), device_id_type=MESH)
    pl.semaphore_wait(barrier, 4 + OWNERS - 1)
    loads[0].wait()
    loads[1].wait()

    number = Messages()
    sent = []

    def message(refs, name, device, out=None):
        i = number(name)
        src, dst = refs()
        return pltpu.make_async_remote_copy(
            src_ref=src, dst_ref=dst, send_sem=send_sem.at[i] if out is None else out, recv_sem=recv_sem.at[i],
            device_id=device, device_id_type=MESH,
        )

    def send(refs, name, device):
        message(refs, name, device).start()
        sent.append((refs, name, device))

    def flush():
        for args in sent:
            message(*args).wait_send()
        sent.clear()

    def received(ref, name):
        message(lambda: (ref, ref), name, sibling).wait_recv()

    def spread(refs, name, device):
        message(refs, name, device, gather_sem).start()

    def spread_wait():
        everything = pbuf.at[pl.ds(0, BATCHES * SLOTS - 1)]
        message(lambda: (everything, everything), "gather", sibling, gather_sem).wait_send()

    def half_to(where, half, device):
        spread(lambda: (slot(0, SELF, 0, half), slot(0, where, 0, half)), ("p", where, half), device)

    def sides_to_sibling(h):
        if h == 0:
            received(slot(0, LEFT, 0, 1), ("p", LEFT, 1))
            received(slot(0, RIGHT, 0, 0), ("p", RIGHT, 0))
        else:
            received(slot(1, LEFT, 0), ("p1", LEFT))
            received(slot(1, RIGHT, 0), ("p1", RIGHT))
        to_sibling(2 * h)

    def to_sibling(b):
        spread(lambda: (both(b, 0), both(b, 1)), ("sib", b), sibling)

    def from_sibling(b):
        received(both(b, 1), ("sib", b))

    def far_on():
        received(slot(0, LEFT, 0, 0), ("p", LEFT, 0))
        spread(lambda: (slot(0, LEFT, 0, 0), slot(0, FAR, 0, 0)), ("far",), right)
        received(slot(0, RIGHT, 0, 1), ("p", RIGHT, 1))
        spread(lambda: (slot(0, RIGHT, 0, 1), slot(0, FAR, 0, 1)), ("far",), left)

    def across_on():
        received(slot(1, SELF, 0), ("across",))
        spread(lambda: (slot(1, SELF, 0), slot(1, LEFT, 0)), ("p1", LEFT), right)
        spread(lambda: (slot(1, SELF, 0), slot(1, RIGHT, 0)), ("p1", RIGHT), left)
        to_sibling(1)

    def far_across():
        received(slot(0, FAR, 0), ("far",))
        spread(lambda: (slot(0, FAR, 0), slot(1, FAR, 0)), ("far across",), across)

    def far_from_across():
        received(slot(1, FAR, 0), ("far across",))
        to_sibling(3)

    half_to(LEFT, 0, right)
    half_to(RIGHT, 1, left)
    spread(lambda: (slot(0, SELF, 0), slot(1, SELF, 0)), ("across",), across)
    half_to(LEFT, 1, right)
    half_to(RIGHT, 0, left)

    def product(i, raw):
        b, n = div(i, NZ), rem(i, NZ)
        batch = pbuf[pl.ds(b * SLOTS, SLOTS)].reshape(BATCH, DT + DS)
        raw[0] = nt(batch[:, :DT], tq[n].reshape(GROUP, DT))
        raw[1] = nt(batch[:, DT:], sq[n].reshape(GROUP, DS))

    def weights(i, raw):
        b, n = div(i, NZ), rem(i, NZ)
        t = raw[0] * t_scale
        s = raw[1] * s_scale
        t_max = jnp.max(t, axis=0, keepdims=True)
        s_max = jnp.max(s, axis=0, keepdims=True)
        t_weight = jnp.exp2(t - t_max)
        s_weight = jnp.exp2(s - s_max)
        tw[n, b] = t_weight
        sw[n, b] = s_weight
        t_sum = jnp.sum(t_weight, axis=0, keepdims=True)
        s_sum = jnp.sum(s_weight, axis=0, keepdims=True)
        cross = jnp.sum(t_weight * (t - s), axis=0, keepdims=True)
        stat[n, b] = jnp.concatenate([t_max, t_sum, s_max, s_sum, cross, cross, cross, cross], axis=0)

    def turn(b):
        turned = pbuf[b * SLOTS:(b + 1) * SLOTS].reshape(BATCH, DT + DS)[:, DT:].T
        part = BATCH // NCORE
        for core in range(NCORE):
            start = (core * BATCHES + b) * part
            spt[:, start:start + part] = turned[:, core * part:(core + 1) * part]

    far_on()
    across_on()
    sides_to_sibling(0)
    far_across()
    for load in loads[2:]:
        load.wait()

    def joined(parts):
        t_max = functools.reduce(jnp.maximum, [p[0:1] for p in parts])
        s_max = functools.reduce(jnp.maximum, [p[2:3] for p in parts])
        t_in = [jnp.exp2(p[0:1] - t_max) for p in parts]
        s_in = [jnp.exp2(p[2:3] - s_max) for p in parts]
        t_sum = functools.reduce(jnp.add, [p[1:2] * w for p, w in zip(parts, t_in)])
        s_sum = functools.reduce(jnp.add, [p[3:4] * w for p, w in zip(parts, s_in)])
        cross = functools.reduce(jnp.add, [p[4:5] * w for p, w in zip(parts, t_in)])
        return t_max, t_sum, s_max, s_sum, cross

    def stat_copy(dy, dz):
        return pltpu.make_async_remote_copy(
            src_ref=stat_send.at[y_of[dy] * NZ + z_of[dz]], dst_ref=stat_recv.at[dy * NZ + (NZ - dz) % NZ],
            send_sem=st_sem.at[0], recv_sem=st_sem.at[1],
            device_id=offset_device(dy, dz), device_id_type=MESH,
        )

    def res_copy(dy, dz):
        return pltpu.make_async_remote_copy(
            src_ref=res_recv.at[me], dst_ref=res_recv.at[me],
            send_sem=st_sem.at[2], recv_sem=st_sem.at[3],
            device_id=offset_device(dy, dz), device_id_type=MESH,
        )

    def all_copies(ref, first):
        others = ref.at[pl.ds(0, OWNERS - 1)]
        return pltpu.make_async_remote_copy(
            src_ref=others, dst_ref=others, send_sem=st_sem.at[first], recv_sem=st_sem.at[first + 1],
            device_id=sibling, device_id_type=MESH,
        )

    def leave(first):
        for n in range(first, first + 4):
            t_max, t_sum, s_max, s_sum, cross = joined([stat[n, b] for b in range(BATCHES)])
            whole = jnp.concatenate([t_max, t_sum, s_max, s_sum, cross, cross, cross, cross], axis=0)
            for y in range(NYL):
                stat_send[y * NZ + n] = whole[:, y * ROWS:(y + 1) * ROWS]

    from_sibling(0)
    product(0, raw_a)

    def score_step(j, carry):
        @pl.when(j == 3)
        def _():
            from_sibling(1)

        @pl.when(j == 5)
        def _():
            sides_to_sibling(1)

        @pl.when(j == 7)
        def _():
            far_from_across()
            from_sibling(2)

        @pl.when(j == 11)
        def _():
            from_sibling(3)

        @pl.when(j == 14)
        def _():
            leave(0)

        product(2 * j + 1, raw_b)
        weights(2 * j, raw_a)
        product(jnp.minimum(2 * j + 2, BATCHES * NZ - 1), raw_a)
        weights(2 * j + 1, raw_b)
        return carry

    lax.fori_loop(0, BATCHES * NZ // 2, score_step, 0)
    leave(4)
    for offset in offsets:
        stat_copy(*offset).start()
    stat_recv[0] = stat_send[me]
    for b in range(BATCHES):
        turn(b)
    spread_wait()
    all_copies(stat_recv, 0).wait_recv()
    t_max, t_sum, s_max, s_sum, cross = joined([stat_recv[m] for m in range(OWNERS)])
    t_in, s_in = factor / t_sum, factor / s_sum
    res_recv[me] = jnp.concatenate([t_max, t_in, s_max, s_in, t_in, t_in, t_in, t_in], axis=0)
    for offset in offsets:
        res_copy(*offset).start()
    div_out[...] = cross * LN2 / t_sum - (t_max * LN2 + jnp.log(t_sum)) + (s_max * LN2 + jnp.log(s_sum))
    all_copies(stat_send, 0).wait_send()
    all_copies(res_recv, 2).wait_recv()

    def group(away):
        return rem(z + NZ + away, NZ)

    def sequence(i):
        size = 4 - div(i + 1, 2)
        return group(size * (2 * rem(i, 2) - 1))

    def lanes(n):
        return pl.ds(pl.multiple_of(n * GROUP, GROUP), GROUP)

    def form(i):
        n = sequence(i)
        res = jnp.concatenate([res_recv[n], res_recv[NZ + n]], axis=1)
        for b in range(BATCHES):
            st = stat[n, b]
            t_in = jnp.exp2(st[0:1] - res[0:1]) * res[1:2]
            s_in = jnp.exp2(st[2:3] - res[2:3]) * res[3:4]
            grad = (sw[n, b] * s_in - tw[n, b] * t_in).astype(BF16)
            gt[0, b, :, lanes(n)] = grad[:BATCH // 2]
            gt[1, b, :, lanes(n)] = grad[BATCH // 2:]

    def pair_copy(i):
        return pltpu.make_async_remote_copy(
            src_ref=y_pair_send.at[i], dst_ref=y_pair_recv.at[i],
            send_sem=ring_sem.at[2], recv_sem=yp_recv_sem.at[i],
            device_id=y_mate, device_id_type=MESH,
        )

    def query_part(i):
        n = sequence(i)
        total = nn(spt[...], gt[:, :, :, lanes(n)].reshape(NCORE * BATCHES * BATCH // 2, GROUP))
        gq[n, 0] = total[:, :ROWS]
        gq[n, 1] = total[:, ROWS:]
        y_pair_send[i] = gq[n, 1 - yl, ZF:].astype(BF16)

    def z_part(away):
        return gq[group(away), :, :ZF]

    def y_part(away):
        i = (4, 3, -3, 2, -2, 1, -1, 0).index(away)
        pair_copy(i).wait_recv()
        return gq[group(away), yl, ZF:] + y_pair_recv[i].astype(F32)

    ZH, YH = ZF // 2, YF // 2

    def z_start():
        far = z_part(4).astype(BF16)
        z_send[0] = far
        message(lambda: (z_send.at[0, :, pl.ds(0, ZH)], z_recv_r.at[0, :, pl.ds(0, ZH)]), ("zr", 0), up, ring_sem.at[0]).start()
        message(lambda: (z_send.at[0, :, pl.ds(ZH, ZH)], z_recv_l.at[0, :, pl.ds(ZH, ZH)]), ("zl", 0), down, ring_sem.at[0]).start()

    def y_start():
        y_send[0] = y_part(4).astype(BF16)
        message(lambda: (y_send.at[0, pl.ds(0, YH)], y_recv_r.at[0, pl.ds(0, YH)]), ("yr", 0), up, ring_sem.at[1]).start()
        message(lambda: (y_send.at[0, pl.ds(YH, YH)], y_recv_l.at[0, pl.ds(YH, YH)]), ("yl", 0), down, ring_sem.at[1]).start()

    def z_step(step):
        if step == 1:
            mine = z_part(3)
            received(z_recv_r.at[0, :, pl.ds(0, ZH)], ("zr", 0))
            z_send[1, :, :ZH] = (mine[:, :ZH] + z_recv_r[0, :, :ZH].astype(F32)).astype(BF16)
            z_send[1, :, ZH:] = mine[:, ZH:].astype(BF16)
        else:
            received(z_recv_r.at[step - 1], ("zr", step - 1))
            z_send[step] = (z_part(4 - step) + z_recv_r[step - 1].astype(F32)).astype(BF16)
        message(lambda step=step: (z_send.at[step], z_recv_r.at[step]), ("zr", step), up, ring_sem.at[0]).start()
        if step == 1:
            mine = z_part(-3)
            received(z_recv_l.at[0, :, pl.ds(ZH, ZH)], ("zl", 0))
            z_send[5, :, :ZH] = mine[:, :ZH].astype(BF16)
            z_send[5, :, ZH:] = (mine[:, ZH:] + z_recv_l[0, :, ZH:].astype(F32)).astype(BF16)
        else:
            received(z_recv_l.at[step - 1], ("zl", step - 1))
            z_send[4 + step] = (z_part(step - 4) + z_recv_l[step - 1].astype(F32)).astype(BF16)
        message(lambda step=step: (z_send.at[4 + step], z_recv_l.at[step]), ("zl", step), down, ring_sem.at[0]).start()

    def y_step(step):
        mine = y_part(4 - step)
        if step == 1:
            received(y_recv_r.at[0, pl.ds(0, YH)], ("yr", 0))
            y_send[1, :YH] = (mine[:YH] + y_recv_r[0, :YH].astype(F32)).astype(BF16)
            y_send[1, YH:] = mine[YH:].astype(BF16)
        else:
            received(y_recv_r.at[step - 1], ("yr", step - 1))
            y_send[step] = (mine + y_recv_r[step - 1].astype(F32)).astype(BF16)
        message(lambda step=step: (y_send.at[step], y_recv_r.at[step]), ("yr", step), up, ring_sem.at[1]).start()
        mine = y_part(step - 4)
        if step == 1:
            received(y_recv_l.at[0, pl.ds(YH, YH)], ("yl", 0))
            y_send[5, :YH] = mine[:YH].astype(BF16)
            y_send[5, YH:] = (mine[YH:] + y_recv_l[0, YH:].astype(F32)).astype(BF16)
        else:
            received(y_recv_l.at[step - 1], ("yl", step - 1))
            y_send[4 + step] = (mine + y_recv_l[step - 1].astype(F32)).astype(BF16)
        message(lambda step=step: (y_send.at[4 + step], y_recv_l.at[step]), ("yl", step), down, ring_sem.at[1]).start()

    def passage_part(core, to):
        to[...] = jnp.zeros_like(to)

        def body(n, carry):
            grads = gt[core, :, :, lanes(n)].reshape(BATCHES * BATCH // 2, GROUP)
            term = nn(grads, sq[n].reshape(GROUP, DS))
            to[...] = to[...] + term.reshape(BATCHES, 2, OWN, DS)
            return carry

        lax.fori_loop(0, NZ, body, 0)

    def gp_of(h, where):
        b, s = place(h, where, 0)
        return gp[b, s]

    def gp_first():
        received(gps_recv, "gp sibling")
        gp[...] = gp[...] + gps_recv[...].astype(F32)
        for h in range(NYH):
            gp1_send[h] = gp_of(h, FAR).astype(BF16)
        send(lambda: (gp1_send.at[0], gp1_recv.at[0]), ("gp", RIGHT, 1), right)
        send(lambda: (gp1_send.at[1], gp1_recv.at[1]), ("gp", LEFT, 1), left)

    def gp_second():
        received(gp1_recv.at[0], ("gp", RIGHT, 1))
        gp2_send[0, 0] = (gp_of(0, RIGHT) + gp1_recv[0].astype(F32)).astype(BF16)
        gp2_send[0, 1] = gp_of(1, RIGHT).astype(BF16)
        send(lambda: (gp2_send.at[0], gp2_recv.at[0]), ("gp", RIGHT, 2), right)
        received(gp1_recv.at[1], ("gp", LEFT, 1))
        gp2_send[1, 0] = gp_of(0, LEFT).astype(BF16)
        gp2_send[1, 1] = (gp_of(1, LEFT) + gp1_recv[1].astype(F32)).astype(BF16)
        send(lambda: (gp2_send.at[1], gp2_recv.at[1]), ("gp", LEFT, 2), left)

    def gp_third():
        received(gp2_recv.at[0], ("gp", RIGHT, 2))
        received(gp2_recv.at[1], ("gp", LEFT, 2))
        gp3_send[...] = x_total(1).astype(BF16)
        send(lambda: (gp3_send, gp3_recv), "gp across", across)

    def x_total(h):
        return gp_of(h, SELF) + gp2_recv[0, h].astype(F32) + gp2_recv[1, h].astype(F32)

    def z_last():
        received(z_recv_r.at[3], ("zr", 3))
        received(z_recv_l.at[3], ("zl", 3))
        for y in range(NYL):
            gq[z, y, :ZF] = gq[z, y, :ZF] + z_recv_r[3, y].astype(F32) + z_recv_l[3, y].astype(F32)
        z_pair_send[...] = gq[z, 1 - yl, :ZF].astype(BF16)
        send(lambda: (z_pair_send, z_pair_recv), "z pair", y_mate)

    form(0)

    def gradient_step(i, carry):
        query_part(i)
        form(i + 1)
        pair_copy(i).start()

        @pl.when(i == 0)
        def _():
            z_start()

        @pl.when(i == 5)
        def _():
            z_step(1)
            y_start()

        return carry

    lax.fori_loop(0, NZ - 1, gradient_step, 0)
    query_part(NZ - 1)
    pair_copy(NZ - 1).start()
    passage_part(1, gp)
    gps_send[...] = gp[...].astype(BF16)
    send(lambda: (gps_send, gps_recv), "gp sibling", sibling)
    z_step(2)
    y_step(1)
    passage_part(0, gp)
    gp_first()
    z_step(3)
    y_step(2)
    gp_second()
    all_copies(res_recv, 2).wait_send()
    z_last()
    y_step(3)
    gp_third()
    for i, ref in enumerate((z_send.at[pl.ds(0, 7)], y_send.at[pl.ds(0, 7)], y_pair_send)):
        message(lambda: (ref, ref), "ring", sibling, ring_sem.at[i]).wait_send()
    flush()

    mine = y_part(0)
    received(y_recv_r.at[3], ("yr", 3))
    received(y_recv_l.at[3], ("yl", 3))
    gq_out[:, ZF:] = (mine + y_recv_r[3].astype(F32) + y_recv_l[3].astype(F32)).T
    received(z_pair_recv, "z pair")
    gq_out[:, :ZF] = (gq[z, yl, :ZF] + z_pair_recv[...].astype(F32)).T
    received(gp3_recv, "gp across")
    gp_out[...] = x_total(0) + gp3_recv[...].astype(F32)


def deliver(gq_in, gp_in, div_in, gq_out, gp_out, div_out, gq, gp, div, in_sem, out_sem):
    parts = ((gq_in, gq, gq_out), (gp_in, gp, gp_out), (div_in, div, div_out))
    ins = [pltpu.make_async_copy(src, mid, in_sem.at[i]) for i, (src, mid, _) in enumerate(parts)]
    outs = [pltpu.make_async_copy(mid, dst, out_sem.at[i]) for i, (_, mid, dst) in enumerate(parts)]
    for copy in ins:
        copy.start()
    for arrive, leave in zip(ins, outs):
        arrive.wait()
        leave.start()
    for copy in outs:
        copy.wait()


def local(teacher_query, student_query, teacher_passages, student_passages):
    blocks = NYL, NZ, NCORE, ROWS
    hbm = pl.BlockSpec(memory_space=pl.ANY)
    vmem = pl.BlockSpec(memory_space=pltpu.VMEM)
    outs = (
        jax.ShapeDtypeStruct((ROWS, DS), F32),
        jax.ShapeDtypeStruct((OWN, DS), F32),
        jax.ShapeDtypeStruct((1, ROWS), F32),
    )
    results = pl.pallas_call(
        kernel,
        out_shape=outs,
        in_specs=[hbm] * 4,
        out_specs=(vmem,) * 3,
        scratch_shapes=[
            pltpu.VMEM((NZ, NYL, ROWS, DT), BF16),
            pltpu.VMEM((NZ, NYL, ROWS, DS), BF16),
            pltpu.VMEM((BATCHES * SLOTS, OWN, DT + DS), BF16),
            pltpu.VMEM((DS, BATCHES * BATCH), BF16),
            pltpu.VMEM((NZ, BATCHES, BATCH, GROUP), F32),
            pltpu.VMEM((NZ, BATCHES, BATCH, GROUP), F32),
            pltpu.VMEM((2, BATCH, GROUP), F32),
            pltpu.VMEM((2, BATCH, GROUP), F32),
            pltpu.VMEM((NCORE, BATCHES, BATCH // 2, NZ * GROUP), BF16),
            pltpu.VMEM((NZ, BATCHES, 8, GROUP), F32),
            pltpu.VMEM((NZ, NYL, DS, ROWS), F32),
            pltpu.VMEM((OWNERS, 8, ROWS), F32),
            pltpu.VMEM((OWNERS, 8, ROWS), F32),
            pltpu.VMEM((OWNERS, 8, ROWS), F32),
            pltpu.VMEM((8, NYL, ZF, ROWS), BF16),
            pltpu.VMEM((4, NYL, ZF, ROWS), BF16),
            pltpu.VMEM((4, NYL, ZF, ROWS), BF16),
            pltpu.VMEM((ZF, ROWS), BF16),
            pltpu.VMEM((ZF, ROWS), BF16),
            pltpu.VMEM((NZ, YF, ROWS), BF16),
            pltpu.VMEM((NZ, YF, ROWS), BF16),
            pltpu.VMEM((8, YF, ROWS), BF16),
            pltpu.VMEM((4, YF, ROWS), BF16),
            pltpu.VMEM((4, YF, ROWS), BF16),
            pltpu.VMEM((BATCHES, 2, OWN, DS), F32),
            pltpu.VMEM((BATCHES, 2, OWN, DS), BF16),
            pltpu.VMEM((BATCHES, 2, OWN, DS), BF16),
            pltpu.VMEM((NYH, OWN, DS), BF16),
            pltpu.VMEM((NYH, OWN, DS), BF16),
            pltpu.VMEM((2, NYH, OWN, DS), BF16),
            pltpu.VMEM((2, NYH, OWN, DS), BF16),
            pltpu.VMEM((OWN, DS), BF16),
            pltpu.VMEM((OWN, DS), BF16),
            pltpu.SemaphoreType.DMA((6,)),
            pltpu.SemaphoreType.DMA,
            pltpu.SemaphoreType.DMA((3,)),
            pltpu.SemaphoreType.DMA((MESSAGES,)),
            pltpu.SemaphoreType.DMA((MESSAGES,)),
            pltpu.SemaphoreType.DMA((NZ,)),
            pltpu.SemaphoreType.DMA((4,)),
        ],
        compiler_params=pltpu.CompilerParams(
            collective_id=0, has_side_effects=True, vmem_limit_bytes=VMEM_BYTES
        ),
    )(
        teacher_query.reshape(*blocks, DT),
        student_query.reshape(*blocks, DS),
        teacher_passages,
        student_passages,
    )
    grad_query, grad_passage, divergence = pl.pallas_call(
        deliver,
        out_shape=outs,
        in_specs=[hbm] * 3,
        out_specs=(hbm,) * 3,
        scratch_shapes=[
            *(pltpu.VMEM(out.shape, out.dtype) for out in outs),
            pltpu.SemaphoreType.DMA((3,)),
            pltpu.SemaphoreType.DMA((3,)),
        ],
        compiler_params=pltpu.CompilerParams(vmem_limit_bytes=VMEM_BYTES),
    )(*results)
    return divergence.reshape(ROWS), grad_query, grad_passage


def solution(mesh):
    return jax.shard_map(
        local,
        mesh=mesh,
        in_specs=(
            P("query", None),
            P("query", None),
            P(("query", "corpus"), None),
            P(("query", "corpus"), None),
        ),
        out_specs=(
            P(("query", "corpus")),
            P(("query", "corpus"), None),
            P(("query", "corpus"), None),
        ),
        check_vma=False,
    )
```

```python
import functools
import math

import jax
import jax.numpy as jnp
from jax import lax
from jax.experimental import pallas as pl
from jax.experimental.pallas import tpu as pltpu
from jax.sharding import PartitionSpec as P

NX, NYH, NYL, NZ, NCORE = 4, 2, 2, 8, 2
OWN = 64
ROWS = 128
DT, DS = 1024, 384
BATCHES = 4
SLOTS = 4
BATCH = 256
GROUP = NYL * ROWS
OWNERS = NYL * NZ
HALF = OWN // 2
ZF = 160
YF = DS - ZF
LOG2E = math.log2(math.e)
LN2 = math.log(2.0)
F32, BF16 = jnp.float32, jnp.bfloat16
MESH = pl.DeviceIdType.MESH

SELF, LEFT, RIGHT, FAR = 0, 1, 2, 3


def place(h, where, core):
    if where == SELF:
        return 1, core * 2 + h
    if where == FAR:
        return 3, core * 2 + h
    return 2 * h, core * 2 + (where - LEFT)


def div(a, b):
    return lax.div(a, jnp.int32(b))


def rem(a, b):
    return lax.rem(a, jnp.int32(b))


def nt(a, b):
    return lax.dot_general(a, b, (((1,), (1,)), ((), ())), preferred_element_type=F32)


def nn(a, b):
    return lax.dot_general(a, b, (((1,), (0,)), ((), ())), preferred_element_type=F32)


class Messages:
    def __init__(self):
        self.numbers = {}

    def __call__(self, name):
        return self.numbers.setdefault(name, len(self.numbers))


MESSAGES = 80
VMEM_BYTES = 60 * 1024 * 1024


def kernel(
    tq_hbm, sq_hbm, tp_hbm, sp_hbm,
    gq_out, gp_out, div_out,
    tq, sq, pbuf, spt, tw, sw, raw_a, raw_b, gt, stat, gq,
    stat_send, stat_recv, res_recv,
    z_send, z_recv, z_pair_send, z_pair_recv,
    y_pair_send, y_pair_recv, y_send, y_recv,
    gp, gps_send, gps_recv, gp1_send, gp1_recv, gp2_send, gp2_recv, gp3_send, gp3_recv,
    load_sem, gather_sem, ring_sem, send_sem, recv_sem, yp_recv_sem, st_sem,
):
    t_scale = DT ** (-0.5) * LOG2E
    s_scale = DS ** (-0.5) * LOG2E
    factor = DS ** (-0.5)
    q = lax.axis_index("query")
    c = lax.axis_index("corpus")
    x, yh = div(q, NYH), rem(q, NYH)
    yl, z, k = div(c, NZ * NCORE), rem(div(c, NCORE), NZ), rem(c, NCORE)
    me = yl * NZ + z

    def at(x_, yh_, yl_, z_, k_):
        return (x_ * NYH + yh_, (yl_ * NZ + z_) * NCORE + k_)

    right, left = at(rem(x + 1, NX), yh, yl, z, k), at(rem(x + NX - 1, NX), yh, yl, z, k)
    across = at(x, 1 - yh, 1 - yl, z, k)
    sibling = at(x, yh, yl, z, 1 - k)
    up, down = at(x, yh, yl, rem(z + 1, NZ), k), at(x, yh, yl, rem(z + NZ - 1, NZ), k)
    y_mate = at(x, yh, 1 - yl, z, k)

    offsets = [(dy, dz) for dy in range(NYL) for dz in range(NZ) if (dy, dz) != (0, 0)]
    y_of = [yl, 1 - yl]
    z_of = [rem(z + dz, NZ) for dz in range(NZ)]

    def offset_device(dy, dz):
        return at(x, yh, y_of[dy], z_of[dz], k)

    def slot(h, where, core, half=None):
        b, s = place(h, where, core)
        if half is None:
            return pbuf.at[b * SLOTS + s]
        return pbuf.at[b * SLOTS + s, pl.ds(half * HALF, HALF)]

    def both(b, core):
        return pbuf.at[pl.ds(b * SLOTS + core * 2, 2)]

    loads = [
        pltpu.make_async_copy(tp_hbm, pbuf.at[SLOTS, :, pl.ds(0, DT)], load_sem.at[0]),
        pltpu.make_async_copy(sp_hbm, pbuf.at[SLOTS, :, pl.ds(DT, DS)], load_sem.at[1]),
    ]
    for y in range(NYL):
        loads.append(pltpu.make_async_copy(tq_hbm.at[y, :, k], tq.at[:, y], load_sem.at[2 + y]))
        loads.append(pltpu.make_async_copy(sq_hbm.at[y, :, k], sq.at[:, y], load_sem.at[4 + y]))
    for load in loads:
        load.start()

    barrier = pltpu.get_barrier_semaphore()
    for device in (right, left, across, sibling):
        pl.semaphore_signal(barrier, inc=1, device_id=device, device_id_type=MESH)

    for offset in offsets:
        pl.semaphore_signal(barrier, inc=1, device_id=offset_device(*offset), device_id_type=MESH)
    pl.semaphore_wait(barrier, 4 + OWNERS - 1)
    loads[0].wait()
    loads[1].wait()

    number = Messages()
    sent = []

    def message(refs, name, device, out=None):
        i = number(name)
        src, dst = refs()
        return pltpu.make_async_remote_copy(
            src_ref=src, dst_ref=dst, send_sem=send_sem.at[i] if out is None else out, recv_sem=recv_sem.at[i],
            device_id=device, device_id_type=MESH,
        )

    def send(refs, name, device):
        message(refs, name, device).start()
        sent.append((refs, name, device))

    def flush():
        for args in sent:
            message(*args).wait_send()
        sent.clear()

    def received(ref, name):
        message(lambda: (ref, ref), name, sibling).wait_recv()

    def spread(refs, name, device):
        message(refs, name, device, gather_sem).start()

    def spread_wait():
        everything = pbuf.at[pl.ds(0, BATCHES * SLOTS - 1)]
        message(lambda: (everything, everything), "gather", sibling, gather_sem).wait_send()

    def half_to(where, half, device):
        spread(lambda: (slot(0, SELF, 0, half), slot(0, where, 0, half)), ("p", where, half), device)

    def sides_to_sibling(h):
        if h == 0:
            received(slot(0, LEFT, 0, 1), ("p", LEFT, 1))
            received(slot(0, RIGHT, 0, 0), ("p", RIGHT, 0))
        else:
            received(slot(1, LEFT, 0), ("p1", LEFT))
            received(slot(1, RIGHT, 0), ("p1", RIGHT))
        to_sibling(2 * h)

    def to_sibling(b):
        spread(lambda: (both(b, 0), both(b, 1)), ("sib", b), sibling)

    def from_sibling(b):
        received(both(b, 1), ("sib", b))

    def far_on():
        received(slot(0, LEFT, 0, 0), ("p", LEFT, 0))
        spread(lambda: (slot(0, LEFT, 0, 0), slot(0, FAR, 0, 0)), ("far",), right)
        received(slot(0, RIGHT, 0, 1), ("p", RIGHT, 1))
        spread(lambda: (slot(0, RIGHT, 0, 1), slot(0, FAR, 0, 1)), ("far",), left)

    def across_on(half):
        received(slot(1, SELF, 0, half), ("across", half))
        spread(lambda: (slot(1, SELF, 0, half), slot(1, LEFT, 0, half)), ("p1", LEFT), right)
        spread(lambda: (slot(1, SELF, 0, half), slot(1, RIGHT, 0, half)), ("p1", RIGHT), left)

    def far_across():
        received(slot(0, FAR, 0), ("far",))
        spread(lambda: (slot(0, FAR, 0), slot(1, FAR, 0)), ("far across",), across)

    def far_from_across():
        received(slot(1, FAR, 0), ("far across",))
        to_sibling(3)

    half_to(LEFT, 0, right)
    half_to(RIGHT, 1, left)
    spread(lambda: (slot(0, SELF, 0, 0), slot(1, SELF, 0, 0)), ("across", 0), across)
    half_to(LEFT, 1, right)
    half_to(RIGHT, 0, left)
    spread(lambda: (slot(0, SELF, 0, 1), slot(1, SELF, 0, 1)), ("across", 1), across)

    def product(i, raw):
        b, n = div(i, NZ), rem(i, NZ)
        batch = pbuf[pl.ds(b * SLOTS, SLOTS)].reshape(BATCH, DT + DS)
        raw[0] = nt(batch[:, :DT], tq[n].reshape(GROUP, DT))
        raw[1] = nt(batch[:, DT:], sq[n].reshape(GROUP, DS))

    def weights(i, raw):
        b, n = div(i, NZ), rem(i, NZ)
        t = raw[0] * t_scale
        s = raw[1] * s_scale
        t_max = jnp.max(t, axis=0, keepdims=True)
        s_max = jnp.max(s, axis=0, keepdims=True)
        t_weight = jnp.exp2(t - t_max)
        s_weight = jnp.exp2(s - s_max)
        tw[n, b] = t_weight
        sw[n, b] = s_weight
        t_sum = jnp.sum(t_weight, axis=0, keepdims=True)
        s_sum = jnp.sum(s_weight, axis=0, keepdims=True)
        cross = jnp.sum(t_weight * (t - s), axis=0, keepdims=True)
        stat[n, b] = jnp.concatenate([t_max, t_sum, s_max, s_sum, cross, cross, cross, cross], axis=0)

    def turn(b):
        turned = pbuf[b * SLOTS:(b + 1) * SLOTS].reshape(BATCH, DT + DS)[:, DT:].T
        part = BATCH // NCORE
        for core in range(NCORE):
            start = (core * BATCHES + b) * part
            spt[:, start:start + part] = turned[:, core * part:(core + 1) * part]

    far_on()
    across_on(0)
    across_on(1)
    to_sibling(1)
    sides_to_sibling(0)
    far_across()
    for load in loads[2:]:
        load.wait()

    def joined(parts):
        t_max = functools.reduce(jnp.maximum, [p[0:1] for p in parts])
        s_max = functools.reduce(jnp.maximum, [p[2:3] for p in parts])
        t_in = [jnp.exp2(p[0:1] - t_max) for p in parts]
        s_in = [jnp.exp2(p[2:3] - s_max) for p in parts]
        t_sum = functools.reduce(jnp.add, [p[1:2] * w for p, w in zip(parts, t_in)])
        s_sum = functools.reduce(jnp.add, [p[3:4] * w for p, w in zip(parts, s_in)])
        cross = functools.reduce(jnp.add, [p[4:5] * w for p, w in zip(parts, t_in)])
        return t_max, t_sum, s_max, s_sum, cross

    def stat_copy(dy, dz):
        return pltpu.make_async_remote_copy(
            src_ref=stat_send.at[y_of[dy] * NZ + z_of[dz]], dst_ref=stat_recv.at[dy * NZ + (NZ - dz) % NZ],
            send_sem=st_sem.at[0], recv_sem=st_sem.at[1],
            device_id=offset_device(dy, dz), device_id_type=MESH,
        )

    def res_copy(dy, dz):
        return pltpu.make_async_remote_copy(
            src_ref=res_recv.at[me], dst_ref=res_recv.at[me],
            send_sem=st_sem.at[2], recv_sem=st_sem.at[3],
            device_id=offset_device(dy, dz), device_id_type=MESH,
        )

    def all_copies(ref, first):
        others = ref.at[pl.ds(0, OWNERS - 1)]
        return pltpu.make_async_remote_copy(
            src_ref=others, dst_ref=others, send_sem=st_sem.at[first], recv_sem=st_sem.at[first + 1],
            device_id=sibling, device_id_type=MESH,
        )

    def leave(first):
        for n in range(first, first + 4):
            t_max, t_sum, s_max, s_sum, cross = joined([stat[n, b] for b in range(BATCHES)])
            whole = jnp.concatenate([t_max, t_sum, s_max, s_sum, cross, cross, cross, cross], axis=0)
            for y in range(NYL):
                stat_send[y * NZ + n] = whole[:, y * ROWS:(y + 1) * ROWS]

    from_sibling(0)
    product(0, raw_a)

    def score_step(j, carry):
        @pl.when(j == 3)
        def _():
            from_sibling(1)

        @pl.when(j == 5)
        def _():
            sides_to_sibling(1)

        @pl.when(j == 7)
        def _():
            far_from_across()
            from_sibling(2)

        @pl.when(j == 11)
        def _():
            from_sibling(3)

        @pl.when(j == 14)
        def _():
            leave(0)

        product(2 * j + 1, raw_b)
        weights(2 * j, raw_a)
        product(jnp.minimum(2 * j + 2, BATCHES * NZ - 1), raw_a)
        weights(2 * j + 1, raw_b)
        return carry

    lax.fori_loop(0, BATCHES * NZ // 2, score_step, 0)
    leave(4)
    for offset in offsets:
        stat_copy(*offset).start()
    stat_recv[0] = stat_send[me]
    for b in range(BATCHES):
        turn(b)
    spread_wait()
    all_copies(stat_recv, 0).wait_recv()
    t_max, t_sum, s_max, s_sum, cross = joined([stat_recv[m] for m in range(OWNERS)])
    t_in, s_in = factor / t_sum, factor / s_sum
    res_recv[me] = jnp.concatenate([t_max, t_in, s_max, s_in, t_in, t_in, t_in, t_in], axis=0)
    for offset in offsets:
        res_copy(*offset).start()
    div_out[...] = cross * LN2 / t_sum - (t_max * LN2 + jnp.log(t_sum)) + (s_max * LN2 + jnp.log(s_sum))
    all_copies(stat_send, 0).wait_send()
    all_copies(res_recv, 2).wait_recv()

    def group(away):
        return rem(z + NZ + away, NZ)

    def sequence(i):
        size = 4 - div(i + 1, 2)
        return group(size * (2 * rem(i, 2) - 1))

    def lanes(n):
        return pl.ds(pl.multiple_of(n * GROUP, GROUP), GROUP)

    def form(i):
        n = sequence(i)
        res = jnp.concatenate([res_recv[n], res_recv[NZ + n]], axis=1)
        for b in range(BATCHES):
            st = stat[n, b]
            t_in = jnp.exp2(st[0:1] - res[0:1]) * res[1:2]
            s_in = jnp.exp2(st[2:3] - res[2:3]) * res[3:4]
            grad = (sw[n, b] * s_in - tw[n, b] * t_in).astype(BF16)
            gt[0, b, :, lanes(n)] = grad[:BATCH // 2]
            gt[1, b, :, lanes(n)] = grad[BATCH // 2:]

    def pair_copy(i):
        return pltpu.make_async_remote_copy(
            src_ref=y_pair_send.at[i], dst_ref=y_pair_recv.at[i],
            send_sem=ring_sem.at[2], recv_sem=yp_recv_sem.at[i],
            device_id=y_mate, device_id_type=MESH,
        )

    def query_part(i):
        n = sequence(i)
        total = nn(spt[...], gt[:, :, :, lanes(n)].reshape(NCORE * BATCHES * BATCH // 2, GROUP))
        gq[n, 0] = total[:, :ROWS]
        gq[n, 1] = total[:, ROWS:]
        y_pair_send[i] = gq[n, 1 - yl, ZF:].astype(BF16)

    ORDER = (4, 3, -3, 2, -2, 1, -1, 0)

    def pair_arrived(away):
        pair_copy(ORDER.index(away)).wait_recv()

    def part(kind, away):
        n = group(away)
        if kind == 0:
            return gq[n, :, :ZF]
        return gq[n, yl, ZF:] + y_pair_recv[ORDER.index(away)].astype(F32)

    sends, recvs = (z_send, y_send), (z_recv, y_recv)
    far_devices = at(x, yh, yl, z_of[2], k), at(x, yh, yl, z_of[6], k)
    near_devices = up, down

    def far_half(refs, kind, way):
        if kind == 0:
            return refs[0].at[0, way]
        return refs[1].at[0, pl.ds(way * (YF // 2), YF // 2)]

    def leave_far(kind):
        sends[kind][0] = part(kind, 4).astype(BF16)
        for way in (0, 1):
            message(
                lambda: (far_half(sends, kind, way), far_half(recvs, kind, way)),
                ("tree", kind, 4, way), far_devices[way], ring_sem.at[kind],
            ).start()

    def leave_to(kind, away, way, total, device):
        i = ORDER.index(away)
        sends[kind][i] = total.astype(BF16)
        message(
            lambda: (sends[kind].at[i], recvs[kind].at[i]), ("tree", kind, i), device, ring_sem.at[kind]
        ).start()

    def leave_near(kind, away):
        way = 0 if away > 0 else 1
        leave_to(kind, away, way, part(kind, away), near_devices[way])

    def come(kind, away):
        i = ORDER.index(away)
        received(recvs[kind].at[i], ("tree", kind, i))
        return recvs[kind][i].astype(F32)

    def leave_joined(kind, away):
        way = 0 if away > 0 else 1
        i = ORDER.index(away)
        total = part(kind, away) + come(kind, 3 if way == 0 else -3)
        received(far_half(recvs, kind, way), ("tree", kind, 4, way))
        far = far_half(recvs, kind, way)[...].astype(F32)
        if kind == 0:
            parts = [total[0], total[1]]
            parts[way] = parts[way] + far
            sends[0][i, 0] = parts[0].astype(BF16)
            sends[0][i, 1] = parts[1].astype(BF16)
        else:
            parts = [total[:YF // 2], total[YF // 2:]]
            parts[way] = parts[way] + far
            sends[1][i, :YF // 2] = parts[0].astype(BF16)
            sends[1][i, YF // 2:] = parts[1].astype(BF16)
        message(
            lambda: (sends[kind].at[i], recvs[kind].at[i]), ("tree", kind, i), far_devices[way], ring_sem.at[kind]
        ).start()

    def tree_total(kind):
        total = part(kind, 0)
        for away in (1, -1, 2, -2):
            total = total + come(kind, away)
        return total

    def passage_part(core, to):
        to[...] = jnp.zeros_like(to)

        def body(n, carry):
            grads = gt[core, :, :, lanes(n)].reshape(BATCHES * BATCH // 2, GROUP)
            term = nn(grads, sq[n].reshape(GROUP, DS))
            to[...] = to[...] + term.reshape(BATCHES, 2, OWN, DS)
            return carry

        lax.fori_loop(0, NZ, body, 0)

    def gp_of(h, where):
        b, s = place(h, where, 0)
        return gp[b, s]

    def gp_first():
        received(gps_recv, "gp sibling")
        gp[...] = gp[...] + gps_recv[...].astype(F32)
        for h in range(NYH):
            gp1_send[h] = gp_of(h, FAR).astype(BF16)
        send(lambda: (gp1_send.at[0], gp1_recv.at[0]), ("gp", RIGHT, 1), right)
        send(lambda: (gp1_send.at[1], gp1_recv.at[1]), ("gp", LEFT, 1), left)

    def gp_second():
        received(gp1_recv.at[0], ("gp", RIGHT, 1))
        gp2_send[0, 0] = (gp_of(0, RIGHT) + gp1_recv[0].astype(F32)).astype(BF16)
        gp2_send[0, 1] = gp_of(1, RIGHT).astype(BF16)
        send(lambda: (gp2_send.at[0], gp2_recv.at[0]), ("gp", RIGHT, 2), right)
        received(gp1_recv.at[1], ("gp", LEFT, 1))
        gp2_send[1, 0] = gp_of(0, LEFT).astype(BF16)
        gp2_send[1, 1] = (gp_of(1, LEFT) + gp1_recv[1].astype(F32)).astype(BF16)
        send(lambda: (gp2_send.at[1], gp2_recv.at[1]), ("gp", LEFT, 2), left)

    def gp_third():
        received(gp2_recv.at[0], ("gp", RIGHT, 2))
        received(gp2_recv.at[1], ("gp", LEFT, 2))
        gp3_send[...] = x_total(1).astype(BF16)
        send(lambda: (gp3_send, gp3_recv), "gp across", across)

    def x_total(h):
        return gp_of(h, SELF) + gp2_recv[0, h].astype(F32) + gp2_recv[1, h].astype(F32)

    form(0)

    def gradient_step(i, carry):
        query_part(i)
        form(i + 1)
        pair_copy(i).start()

        @pl.when(i == 0)
        def _():
            leave_far(0)

        for place_, away in ((1, 3), (2, -3), (5, 1), (6, -1)):
            @pl.when(i == place_)
            def _():
                leave_near(0, away)

        @pl.when(i == 5)
        def _():
            pair_arrived(4)
            leave_far(1)

        return carry

    lax.fori_loop(0, NZ - 1, gradient_step, 0)
    query_part(NZ - 1)
    pair_copy(NZ - 1).start()
    for away in (3, -3):
        pair_arrived(away)
        leave_near(1, away)
    leave_joined(0, 2)
    leave_joined(0, -2)
    passage_part(1, gp)
    gps_send[...] = gp[...].astype(BF16)
    send(lambda: (gps_send, gps_recv), "gp sibling", sibling)
    for away in (2, -2):
        pair_arrived(away)
        leave_joined(1, away)
    for away in (1, -1):
        pair_arrived(away)
        leave_near(1, away)
    passage_part(0, gp)
    gp_first()
    all_copies(res_recv, 2).wait_send()
    whole = tree_total(0)
    for y in range(NYL):
        gq[z, y, :ZF] = whole[y]
    z_pair_send[...] = gq[z, 1 - yl, :ZF].astype(BF16)
    send(lambda: (z_pair_send, z_pair_recv), "z pair", y_mate)
    gp_second()
    pair_arrived(0)
    gq_out[:, ZF:] = tree_total(1).T
    gp_third()
    for i, ref in enumerate((z_send.at[pl.ds(0, 7)], y_send.at[pl.ds(0, 7)], y_pair_send)):
        message(lambda: (ref, ref), "ring", sibling, ring_sem.at[i]).wait_send()
    flush()
    received(z_pair_recv, "z pair")
    gq_out[:, :ZF] = (gq[z, yl, :ZF] + z_pair_recv[...].astype(F32)).T
    received(gp3_recv, "gp across")
    gp_out[...] = x_total(0) + gp3_recv[...].astype(F32)


def deliver(gq_in, gp_in, div_in, gq_out, gp_out, div_out, gq, gp, div, in_sem, out_sem):
    parts = ((gq_in, gq, gq_out), (gp_in, gp, gp_out), (div_in, div, div_out))
    ins = [pltpu.make_async_copy(src, mid, in_sem.at[i]) for i, (src, mid, _) in enumerate(parts)]
    outs = [pltpu.make_async_copy(mid, dst, out_sem.at[i]) for i, (_, mid, dst) in enumerate(parts)]
    for copy in ins:
        copy.start()
    for arrive, leave in zip(ins, outs):
        arrive.wait()
        leave.start()
    for copy in outs:
        copy.wait()


def local(teacher_query, student_query, teacher_passages, student_passages):
    blocks = NYL, NZ, NCORE, ROWS
    hbm = pl.BlockSpec(memory_space=pl.ANY)
    vmem = pl.BlockSpec(memory_space=pltpu.VMEM)
    outs = (
        jax.ShapeDtypeStruct((ROWS, DS), F32),
        jax.ShapeDtypeStruct((OWN, DS), F32),
        jax.ShapeDtypeStruct((1, ROWS), F32),
    )
    results = pl.pallas_call(
        kernel,
        out_shape=outs,
        in_specs=[hbm] * 4,
        out_specs=(vmem,) * 3,
        scratch_shapes=[
            pltpu.VMEM((NZ, NYL, ROWS, DT), BF16),
            pltpu.VMEM((NZ, NYL, ROWS, DS), BF16),
            pltpu.VMEM((BATCHES * SLOTS, OWN, DT + DS), BF16),
            pltpu.VMEM((DS, BATCHES * BATCH), BF16),
            pltpu.VMEM((NZ, BATCHES, BATCH, GROUP), F32),
            pltpu.VMEM((NZ, BATCHES, BATCH, GROUP), F32),
            pltpu.VMEM((2, BATCH, GROUP), F32),
            pltpu.VMEM((2, BATCH, GROUP), F32),
            pltpu.VMEM((NCORE, BATCHES, BATCH // 2, NZ * GROUP), BF16),
            pltpu.VMEM((NZ, BATCHES, 8, GROUP), F32),
            pltpu.VMEM((NZ, NYL, DS, ROWS), F32),
            pltpu.VMEM((OWNERS, 8, ROWS), F32),
            pltpu.VMEM((OWNERS, 8, ROWS), F32),
            pltpu.VMEM((OWNERS, 8, ROWS), F32),
            pltpu.VMEM((7, NYL, ZF, ROWS), BF16),
            pltpu.VMEM((7, NYL, ZF, ROWS), BF16),
            pltpu.VMEM((ZF, ROWS), BF16),
            pltpu.VMEM((ZF, ROWS), BF16),
            pltpu.VMEM((NZ, YF, ROWS), BF16),
            pltpu.VMEM((NZ, YF, ROWS), BF16),
            pltpu.VMEM((7, YF, ROWS), BF16),
            pltpu.VMEM((7, YF, ROWS), BF16),
            pltpu.VMEM((BATCHES, 2, OWN, DS), F32),
            pltpu.VMEM((BATCHES, 2, OWN, DS), BF16),
            pltpu.VMEM((BATCHES, 2, OWN, DS), BF16),
            pltpu.VMEM((NYH, OWN, DS), BF16),
            pltpu.VMEM((NYH, OWN, DS), BF16),
            pltpu.VMEM((2, NYH, OWN, DS), BF16),
            pltpu.VMEM((2, NYH, OWN, DS), BF16),
            pltpu.VMEM((OWN, DS), BF16),
            pltpu.VMEM((OWN, DS), BF16),
            pltpu.SemaphoreType.DMA((6,)),
            pltpu.SemaphoreType.DMA,
            pltpu.SemaphoreType.DMA((3,)),
            pltpu.SemaphoreType.DMA((MESSAGES,)),
            pltpu.SemaphoreType.DMA((MESSAGES,)),
            pltpu.SemaphoreType.DMA((NZ,)),
            pltpu.SemaphoreType.DMA((4,)),
        ],
        compiler_params=pltpu.CompilerParams(
            collective_id=0, has_side_effects=True, vmem_limit_bytes=VMEM_BYTES
        ),
    )(
        teacher_query.reshape(*blocks, DT),
        student_query.reshape(*blocks, DS),
        teacher_passages,
        student_passages,
    )
    grad_query, grad_passage, divergence = pl.pallas_call(
        deliver,
        out_shape=outs,
        in_specs=[hbm] * 3,
        out_specs=(hbm,) * 3,
        scratch_shapes=[
            *(pltpu.VMEM(out.shape, out.dtype) for out in outs),
            pltpu.SemaphoreType.DMA((3,)),
            pltpu.SemaphoreType.DMA((3,)),
        ],
        compiler_params=pltpu.CompilerParams(vmem_limit_bytes=VMEM_BYTES),
    )(*results)
    return divergence.reshape(ROWS), grad_query, grad_passage


def solution(mesh):
    return jax.shard_map(
        local,
        mesh=mesh,
        in_specs=(
            P("query", None),
            P("query", None),
            P(("query", "corpus"), None),
            P(("query", "corpus"), None),
        ),
        out_specs=(
            P(("query", "corpus")),
            P(("query", "corpus"), None),
            P(("query", "corpus"), None),
        ),
        check_vma=False,
    )
```

```python
import functools
import math

import jax
import jax.numpy as jnp
from jax import lax
from jax.experimental import pallas as pl
from jax.experimental.pallas import tpu as pltpu
from jax.sharding import PartitionSpec as P

NX, NYH, NYL, NZ, NCORE = 4, 2, 2, 8, 2
OWN = 64
ROWS = 128
DT, DS = 1024, 384
BATCHES = 4
SLOTS = 4
BATCH = 256
GROUP = NYL * ROWS
OWNERS = NYL * NZ
HALF = OWN // 2
ZF = 192
YF = DS - ZF
LOG2E = math.log2(math.e)
LN2 = math.log(2.0)
F32, BF16 = jnp.float32, jnp.bfloat16
MESH = pl.DeviceIdType.MESH

SELF, LEFT, RIGHT, FAR = 0, 1, 2, 3


def place(h, where, core):
    if where == SELF:
        return 1, core * 2 + h
    if where == FAR:
        return 3, core * 2 + h
    return 2 * h, core * 2 + (where - LEFT)


def div(a, b):
    return lax.div(a, jnp.int32(b))


def rem(a, b):
    return lax.rem(a, jnp.int32(b))


def nt(a, b):
    return lax.dot_general(a, b, (((1,), (1,)), ((), ())), preferred_element_type=F32)


def nn(a, b):
    return lax.dot_general(a, b, (((1,), (0,)), ((), ())), preferred_element_type=F32)


class Messages:
    def __init__(self):
        self.numbers = {}

    def __call__(self, name):
        return self.numbers.setdefault(name, len(self.numbers))


MESSAGES = 80
VMEM_BYTES = 60 * 1024 * 1024


def kernel(
    tq_hbm, sq_hbm, tp_hbm, sp_hbm,
    gq_out, gp_out, div_out,
    tq, sq, pbuf, spt, tw, sw, raw_a, raw_b, gt, stat, gq,
    stat_send, stat_recv, res_recv,
    z_send, z_recv_r, z_recv_l, z_pair_send, z_pair_recv,
    y_pair_send, y_pair_recv, y_send, y_recv_r, y_recv_l,
    gp, gps_send, gps_recv, gp1_send, gp1_recv, gp2_send, gp2_recv, gp3_send, gp3_recv,
    load_sem, known_sem, gather_sem, ring_sem, send_sem, recv_sem, yp_recv_sem, st_sem,
):
    t_scale = DT ** (-0.5) * LOG2E
    s_scale = DS ** (-0.5) * LOG2E
    factor = DS ** (-0.5)
    q = lax.axis_index("query")
    c = lax.axis_index("corpus")
    x, yh = div(q, NYH), rem(q, NYH)
    yl, z, k = div(c, NZ * NCORE), rem(div(c, NCORE), NZ), rem(c, NCORE)
    me = yl * NZ + z

    def at(x_, yh_, yl_, z_, k_):
        return (x_ * NYH + yh_, (yl_ * NZ + z_) * NCORE + k_)

    right, left = at(rem(x + 1, NX), yh, yl, z, k), at(rem(x + NX - 1, NX), yh, yl, z, k)
    across = at(x, 1 - yh, 1 - yl, z, k)
    sibling = at(x, yh, yl, z, 1 - k)
    up, down = at(x, yh, yl, rem(z + 1, NZ), k), at(x, yh, yl, rem(z + NZ - 1, NZ), k)
    y_mate = at(x, yh, 1 - yl, z, k)

    offsets = [(dy, dz) for dy in range(NYL) for dz in range(NZ) if (dy, dz) != (0, 0)]
    y_of = [yl, 1 - yl]
    z_of = [rem(z + dz, NZ) for dz in range(NZ)]

    def offset_device(dy, dz):
        return at(x, yh, y_of[dy], z_of[dz], k)

    def slot(h, where, core, half=None):
        b, s = place(h, where, core)
        if half is None:
            return pbuf.at[b * SLOTS + s]
        return pbuf.at[b * SLOTS + s, pl.ds(half * HALF, HALF)]

    def both(b, core):
        return pbuf.at[pl.ds(b * SLOTS + core * 2, 2)]

    loads = [
        pltpu.make_async_copy(tp_hbm, pbuf.at[SLOTS, :, pl.ds(0, DT)], load_sem.at[0]),
        pltpu.make_async_copy(sp_hbm, pbuf.at[SLOTS, :, pl.ds(DT, DS)], load_sem.at[1]),
    ]
    for y in range(NYL):
        loads.append(pltpu.make_async_copy(tq_hbm.at[y, :, k], tq.at[:, y], load_sem.at[2 + y]))
        loads.append(pltpu.make_async_copy(sq_hbm.at[y, :, k], sq.at[:, y], load_sem.at[4 + y]))
    for load in loads:
        load.start()

    barrier = pltpu.get_barrier_semaphore()
    for device in (right, left, across, sibling, up, down, y_mate):
        pl.semaphore_signal(barrier, inc=1, device_id=device, device_id_type=MESH)
    pl.semaphore_wait(barrier, 7)
    loads[0].wait()
    loads[1].wait()

    number = Messages()
    sent = []

    def message(refs, name, device, out=None):
        i = number(name)
        src, dst = refs()
        return pltpu.make_async_remote_copy(
            src_ref=src, dst_ref=dst, send_sem=send_sem.at[i] if out is None else out, recv_sem=recv_sem.at[i],
            device_id=device, device_id_type=MESH,
        )

    def send(refs, name, device):
        message(refs, name, device).start()
        sent.append((refs, name, device))

    def flush():
        for args in sent:
            message(*args).wait_send()
        sent.clear()

    def received(ref, name):
        message(lambda: (ref, ref), name, sibling).wait_recv()

    def spread(refs, name, device):
        message(refs, name, device, gather_sem).start()

    def spread_wait():
        everything = pbuf.at[pl.ds(0, BATCHES * SLOTS - 1)]
        message(lambda: (everything, everything), "gather", sibling, gather_sem).wait_send()

    def half_to(where, half, device):
        spread(lambda: (slot(0, SELF, 0, half), slot(0, where, 0, half)), ("p", where, half), device)

    def sides_to_sibling(h):
        if h == 0:
            received(slot(0, LEFT, 0, 1), ("p", LEFT, 1))
            received(slot(0, RIGHT, 0, 0), ("p", RIGHT, 0))
        else:
            received(slot(1, LEFT, 0), ("p1", LEFT))
            received(slot(1, RIGHT, 0), ("p1", RIGHT))
        to_sibling(2 * h)

    def to_sibling(b):
        spread(lambda: (both(b, 0), both(b, 1)), ("sib", b), sibling)

    def from_sibling(b):
        received(both(b, 1), ("sib", b))

    def far_on():
        received(slot(0, LEFT, 0, 0), ("p", LEFT, 0))
        spread(lambda: (slot(0, LEFT, 0, 0), slot(0, FAR, 0, 0)), ("far",), right)
        received(slot(0, RIGHT, 0, 1), ("p", RIGHT, 1))
        spread(lambda: (slot(0, RIGHT, 0, 1), slot(0, FAR, 0, 1)), ("far",), left)

    def across_on(half):
        received(slot(1, SELF, 0, half), ("across", half))
        spread(lambda: (slot(1, SELF, 0, half), slot(1, LEFT, 0, half)), ("p1", LEFT), right)
        spread(lambda: (slot(1, SELF, 0, half), slot(1, RIGHT, 0, half)), ("p1", RIGHT), left)

    def far_across():
        received(slot(0, FAR, 0), ("far",))
        spread(lambda: (slot(0, FAR, 0), slot(1, FAR, 0)), ("far across",), across)

    def far_from_across():
        received(slot(1, FAR, 0), ("far across",))
        to_sibling(3)

    half_to(LEFT, 0, right)
    half_to(RIGHT, 1, left)
    spread(lambda: (slot(0, SELF, 0, 0), slot(1, SELF, 0, 0)), ("across", 0), across)
    half_to(LEFT, 1, right)
    half_to(RIGHT, 0, left)
    spread(lambda: (slot(0, SELF, 0, 1), slot(1, SELF, 0, 1)), ("across", 1), across)

    def product(i, raw):
        b, n = div(i, NZ), rem(i, NZ)
        batch = pbuf[pl.ds(b * SLOTS, SLOTS)].reshape(BATCH, DT + DS)
        raw[0] = nt(batch[:, :DT], tq[n].reshape(GROUP, DT))
        raw[1] = nt(batch[:, DT:], sq[n].reshape(GROUP, DS))

    def weights(i, raw):
        b, n = div(i, NZ), rem(i, NZ)
        t = raw[0] * t_scale
        s = raw[1] * s_scale
        t_max = jnp.max(t, axis=0, keepdims=True)
        s_max = jnp.max(s, axis=0, keepdims=True)
        t_weight = jnp.exp2(t - t_max)
        s_weight = jnp.exp2(s - s_max)
        tw[n, b] = t_weight
        sw[n, b] = s_weight
        t_sum = jnp.sum(t_weight, axis=0, keepdims=True)
        s_sum = jnp.sum(s_weight, axis=0, keepdims=True)
        cross = jnp.sum(t_weight * (t - s), axis=0, keepdims=True)
        stat[n, b] = jnp.concatenate([t_max, t_sum, s_max, s_sum, cross, cross, cross, cross], axis=0)

    def turn(b):
        turned = pbuf[b * SLOTS:(b + 1) * SLOTS].reshape(BATCH, DT + DS)[:, DT:].T
        part = BATCH // NCORE
        for core in range(NCORE):
            start = (core * BATCHES + b) * part
            spt[:, start:start + part] = turned[:, core * part:(core + 1) * part]

    def know(i):
        for device in (up, down, y_mate):
            pl.semaphore_signal(known_sem.at[i], inc=1, device_id=device, device_id_type=MESH)
        pl.semaphore_wait(known_sem.at[i], 3)

    know(0)
    far_on()
    across_on(0)
    across_on(1)
    to_sibling(1)
    know(1)
    sides_to_sibling(0)
    know(2)
    far_across()
    know(3)
    for load in loads[2:]:
        load.wait()

    def joined(parts):
        t_max = functools.reduce(jnp.maximum, [p[0:1] for p in parts])
        s_max = functools.reduce(jnp.maximum, [p[2:3] for p in parts])
        t_in = [jnp.exp2(p[0:1] - t_max) for p in parts]
        s_in = [jnp.exp2(p[2:3] - s_max) for p in parts]
        t_sum = functools.reduce(jnp.add, [p[1:2] * w for p, w in zip(parts, t_in)])
        s_sum = functools.reduce(jnp.add, [p[3:4] * w for p, w in zip(parts, s_in)])
        cross = functools.reduce(jnp.add, [p[4:5] * w for p, w in zip(parts, t_in)])
        return t_max, t_sum, s_max, s_sum, cross

    def stat_copy(dy, dz):
        return pltpu.make_async_remote_copy(
            src_ref=stat_send.at[y_of[dy] * NZ + z_of[dz]], dst_ref=stat_recv.at[dy * NZ + (NZ - dz) % NZ],
            send_sem=st_sem.at[0], recv_sem=st_sem.at[1],
            device_id=offset_device(dy, dz), device_id_type=MESH,
        )

    def res_copy(dy, dz):
        return pltpu.make_async_remote_copy(
            src_ref=res_recv.at[me], dst_ref=res_recv.at[me],
            send_sem=st_sem.at[2], recv_sem=st_sem.at[3],
            device_id=offset_device(dy, dz), device_id_type=MESH,
        )

    def all_copies(ref, first):
        others = ref.at[pl.ds(0, OWNERS - 1)]
        return pltpu.make_async_remote_copy(
            src_ref=others, dst_ref=others, send_sem=st_sem.at[first], recv_sem=st_sem.at[first + 1],
            device_id=sibling, device_id_type=MESH,
        )

    def leave(first):
        for n in range(first, first + 4):
            t_max, t_sum, s_max, s_sum, cross = joined([stat[n, b] for b in range(BATCHES)])
            whole = jnp.concatenate([t_max, t_sum, s_max, s_sum, cross, cross, cross, cross], axis=0)
            for y in range(NYL):
                stat_send[y * NZ + n, 0] = whole[:, y * ROWS:(y + 1) * ROWS]
            four = jnp.concatenate([whole[0:4, :ROWS], whole[0:4, ROWS:]], axis=0)
            for y in range(NYL):
                stat_send[y * NZ + (n + 4) % NZ, 1] = four

    from_sibling(0)
    product(0, raw_a)

    def score_step(j, carry):
        @pl.when(j == 3)
        def _():
            from_sibling(1)

        @pl.when(j == 5)
        def _():
            sides_to_sibling(1)

        @pl.when(j == 7)
        def _():
            far_from_across()
            from_sibling(2)

        @pl.when(j == 11)
        def _():
            from_sibling(3)

        @pl.when(j == 14)
        def _():
            leave(0)

        product(2 * j + 1, raw_b)
        weights(2 * j, raw_a)
        product(jnp.minimum(2 * j + 2, BATCHES * NZ - 1), raw_a)
        weights(2 * j + 1, raw_b)
        return carry

    lax.fori_loop(0, BATCHES * NZ // 2, score_step, 0)
    leave(4)
    for offset in offsets:
        stat_copy(*offset).start()
    stat_recv[0] = stat_send[me]
    for b in range(BATCHES):
        turn(b)
    spread_wait()
    all_copies(stat_recv, 0).wait_recv()
    def totals(parts):
        t_max, t_sum, s_max, s_sum, cross = joined(parts)
        t_in, s_in = factor / t_sum, factor / s_sum
        result = jnp.concatenate([t_max, t_in, s_max, s_in, t_in, t_in, t_in, t_in], axis=0)
        return result, (t_max, t_sum, s_max, s_sum, cross)

    result, (t_max, t_sum, s_max, s_sum, cross) = totals([stat_recv[m, 0] for m in range(OWNERS)])
    res_recv[me] = result
    for offset in offsets:
        res_copy(*offset).start()
    far = []
    for y in range(NYL):
        parts = [stat_recv[m, 1, 4 * y:4 * y + 4] for m in range(OWNERS)]
        far.append(totals([jnp.concatenate([p, p], axis=0) for p in parts])[0])
    far = jnp.concatenate(far, axis=1)

    def group(away):
        return rem(z + NZ + away, NZ)

    def sequence(i):
        size = 4 - div(i + 1, 2)
        return group(size * (2 * rem(i, 2) - 1))

    def lanes(n):
        return pl.ds(pl.multiple_of(n * GROUP, GROUP), GROUP)

    def form(i, res=None):
        n = sequence(i)
        if res is None:
            res = jnp.concatenate([res_recv[n], res_recv[NZ + n]], axis=1)
        for b in range(BATCHES):
            st = stat[n, b]
            t_in = jnp.exp2(st[0:1] - res[0:1]) * res[1:2]
            s_in = jnp.exp2(st[2:3] - res[2:3]) * res[3:4]
            grad = (sw[n, b] * s_in - tw[n, b] * t_in).astype(BF16)
            gt[0, b, :, lanes(n)] = grad[:BATCH // 2]
            gt[1, b, :, lanes(n)] = grad[BATCH // 2:]

    def pair_copy(i):
        return pltpu.make_async_remote_copy(
            src_ref=y_pair_send.at[i], dst_ref=y_pair_recv.at[i],
            send_sem=ring_sem.at[2], recv_sem=yp_recv_sem.at[i],
            device_id=y_mate, device_id_type=MESH,
        )

    def query_part(i):
        n = sequence(i)
        total = nn(spt[...], gt[:, :, :, lanes(n)].reshape(NCORE * BATCHES * BATCH // 2, GROUP))
        gq[n, 0] = total[:, :ROWS]
        gq[n, 1] = total[:, ROWS:]
        y_pair_send[i] = gq[n, 1 - yl, ZF:].astype(BF16)

    def z_part(away):
        return gq[group(away), :, :ZF]

    def y_part(away):
        i = (4, 3, -3, 2, -2, 1, -1, 0).index(away)
        pair_copy(i).wait_recv()
        return gq[group(away), yl, ZF:] + y_pair_recv[i].astype(F32)

    ZH, YH = ZF // 2, YF // 2

    def z_start():
        far = z_part(4).astype(BF16)
        z_send[0] = far
        message(lambda: (z_send.at[0, :, pl.ds(0, ZH)], z_recv_r.at[0, :, pl.ds(0, ZH)]), ("zr", 0), up, ring_sem.at[0]).start()
        message(lambda: (z_send.at[0, :, pl.ds(ZH, ZH)], z_recv_l.at[0, :, pl.ds(ZH, ZH)]), ("zl", 0), down, ring_sem.at[0]).start()

    def y_start():
        y_send[0] = y_part(4).astype(BF16)
        message(lambda: (y_send.at[0, pl.ds(0, YH)], y_recv_r.at[0, pl.ds(0, YH)]), ("yr", 0), up, ring_sem.at[1]).start()
        message(lambda: (y_send.at[0, pl.ds(YH, YH)], y_recv_l.at[0, pl.ds(YH, YH)]), ("yl", 0), down, ring_sem.at[1]).start()

    def z_step(step):
        if step == 1:
            mine = z_part(3)
            received(z_recv_r.at[0, :, pl.ds(0, ZH)], ("zr", 0))
            z_send[1, :, :ZH] = (mine[:, :ZH] + z_recv_r[0, :, :ZH].astype(F32)).astype(BF16)
            z_send[1, :, ZH:] = mine[:, ZH:].astype(BF16)
        else:
            received(z_recv_r.at[step - 1], ("zr", step - 1))
            z_send[step] = (z_part(4 - step) + z_recv_r[step - 1].astype(F32)).astype(BF16)
        message(lambda step=step: (z_send.at[step], z_recv_r.at[step]), ("zr", step), up, ring_sem.at[0]).start()
        if step == 1:
            mine = z_part(-3)
            received(z_recv_l.at[0, :, pl.ds(ZH, ZH)], ("zl", 0))
            z_send[5, :, :ZH] = mine[:, :ZH].astype(BF16)
            z_send[5, :, ZH:] = (mine[:, ZH:] + z_recv_l[0, :, ZH:].astype(F32)).astype(BF16)
        else:
            received(z_recv_l.at[step - 1], ("zl", step - 1))
            z_send[4 + step] = (z_part(step - 4) + z_recv_l[step - 1].astype(F32)).astype(BF16)
        message(lambda step=step: (z_send.at[4 + step], z_recv_l.at[step]), ("zl", step), down, ring_sem.at[0]).start()

    def y_step(step):
        mine = y_part(4 - step)
        if step == 1:
            received(y_recv_r.at[0, pl.ds(0, YH)], ("yr", 0))
            y_send[1, :YH] = (mine[:YH] + y_recv_r[0, :YH].astype(F32)).astype(BF16)
            y_send[1, YH:] = mine[YH:].astype(BF16)
        else:
            received(y_recv_r.at[step - 1], ("yr", step - 1))
            y_send[step] = (mine + y_recv_r[step - 1].astype(F32)).astype(BF16)
        message(lambda step=step: (y_send.at[step], y_recv_r.at[step]), ("yr", step), up, ring_sem.at[1]).start()
        mine = y_part(step - 4)
        if step == 1:
            received(y_recv_l.at[0, pl.ds(YH, YH)], ("yl", 0))
            y_send[5, :YH] = mine[:YH].astype(BF16)
            y_send[5, YH:] = (mine[YH:] + y_recv_l[0, YH:].astype(F32)).astype(BF16)
        else:
            received(y_recv_l.at[step - 1], ("yl", step - 1))
            y_send[4 + step] = (mine + y_recv_l[step - 1].astype(F32)).astype(BF16)
        message(lambda step=step: (y_send.at[4 + step], y_recv_l.at[step]), ("yl", step), down, ring_sem.at[1]).start()

    def passage_part(core, to):
        to[...] = jnp.zeros_like(to)

        def body(n, carry):
            grads = gt[core, :, :, lanes(n)].reshape(BATCHES * BATCH // 2, GROUP)
            term = nn(grads, sq[n].reshape(GROUP, DS))
            to[...] = to[...] + term.reshape(BATCHES, 2, OWN, DS)
            return carry

        lax.fori_loop(0, NZ, body, 0)

    def gp_of(h, where):
        b, s = place(h, where, 0)
        return gp[b, s]

    def gp_first():
        received(gps_recv, "gp sibling")
        gp[...] = gp[...] + gps_recv[...].astype(F32)
        for h in range(NYH):
            gp1_send[h] = gp_of(h, FAR).astype(BF16)
        send(lambda: (gp1_send.at[0], gp1_recv.at[0]), ("gp", RIGHT, 1), right)
        send(lambda: (gp1_send.at[1], gp1_recv.at[1]), ("gp", LEFT, 1), left)

    def gp_second():
        received(gp1_recv.at[0], ("gp", RIGHT, 1))
        gp2_send[0, 0] = (gp_of(0, RIGHT) + gp1_recv[0].astype(F32)).astype(BF16)
        gp2_send[0, 1] = gp_of(1, RIGHT).astype(BF16)
        send(lambda: (gp2_send.at[0], gp2_recv.at[0]), ("gp", RIGHT, 2), right)
        received(gp1_recv.at[1], ("gp", LEFT, 1))
        gp2_send[1, 0] = gp_of(0, LEFT).astype(BF16)
        gp2_send[1, 1] = (gp_of(1, LEFT) + gp1_recv[1].astype(F32)).astype(BF16)
        send(lambda: (gp2_send.at[1], gp2_recv.at[1]), ("gp", LEFT, 2), left)

    def gp_third():
        received(gp2_recv.at[0], ("gp", RIGHT, 2))
        received(gp2_recv.at[1], ("gp", LEFT, 2))
        gp3_send[...] = x_total(1).astype(BF16)
        send(lambda: (gp3_send, gp3_recv), "gp across", across)

    def x_total(h):
        return gp_of(h, SELF) + gp2_recv[0, h].astype(F32) + gp2_recv[1, h].astype(F32)

    def z_last():
        received(z_recv_r.at[3], ("zr", 3))
        received(z_recv_l.at[3], ("zl", 3))
        for y in range(NYL):
            gq[z, y, :ZF] = gq[z, y, :ZF] + z_recv_r[3, y].astype(F32) + z_recv_l[3, y].astype(F32)
        z_pair_send[...] = gq[z, 1 - yl, :ZF].astype(BF16)
        send(lambda: (z_pair_send, z_pair_recv), "z pair", y_mate)

    form(0, far)
    query_part(0)
    pair_copy(0).start()
    z_start()
    div_out[...] = cross * LN2 / t_sum - (t_max * LN2 + jnp.log(t_sum)) + (s_max * LN2 + jnp.log(s_sum))
    all_copies(stat_send, 0).wait_send()
    all_copies(res_recv, 2).wait_recv()
    form(1)

    def gradient_step(i, carry):
        query_part(i)
        form(i + 1)
        pair_copy(i).start()

        @pl.when(i == 3)
        def _():
            z_step(1)

        @pl.when(i == 4)
        def _():
            y_start()

        return carry

    lax.fori_loop(1, NZ - 1, gradient_step, 0)
    query_part(NZ - 1)
    pair_copy(NZ - 1).start()
    passage_part(1, gp)
    gps_send[...] = gp[...].astype(BF16)
    send(lambda: (gps_send, gps_recv), "gp sibling", sibling)
    z_step(2)
    y_step(1)
    passage_part(0, gp)
    gp_first()
    z_step(3)
    y_step(2)
    gp_second()
    all_copies(res_recv, 2).wait_send()
    z_last()
    y_step(3)
    gp_third()
    for i, ref in enumerate((z_send.at[pl.ds(0, 7)], y_send.at[pl.ds(0, 7)], y_pair_send)):
        message(lambda: (ref, ref), "ring", sibling, ring_sem.at[i]).wait_send()
    flush()

    mine = y_part(0)
    received(y_recv_r.at[3], ("yr", 3))
    received(y_recv_l.at[3], ("yl", 3))
    gq_out[:, ZF:] = (mine + y_recv_r[3].astype(F32) + y_recv_l[3].astype(F32)).T
    received(z_pair_recv, "z pair")
    gq_out[:, :ZF] = (gq[z, yl, :ZF] + z_pair_recv[...].astype(F32)).T
    received(gp3_recv, "gp across")
    gp_out[...] = x_total(0) + gp3_recv[...].astype(F32)


def deliver(gq_in, gp_in, div_in, gq_out, gp_out, div_out, gq, gp, div, in_sem, out_sem):
    parts = ((gq_in, gq, gq_out), (gp_in, gp, gp_out), (div_in, div, div_out))
    ins = [pltpu.make_async_copy(src, mid, in_sem.at[i]) for i, (src, mid, _) in enumerate(parts)]
    outs = [pltpu.make_async_copy(mid, dst, out_sem.at[i]) for i, (_, mid, dst) in enumerate(parts)]
    for copy in ins:
        copy.start()
    for arrive, leave in zip(ins, outs):
        arrive.wait()
        leave.start()
    for copy in outs:
        copy.wait()


def local(teacher_query, student_query, teacher_passages, student_passages):
    blocks = NYL, NZ, NCORE, ROWS
    hbm = pl.BlockSpec(memory_space=pl.ANY)
    vmem = pl.BlockSpec(memory_space=pltpu.VMEM)
    outs = (
        jax.ShapeDtypeStruct((ROWS, DS), F32),
        jax.ShapeDtypeStruct((OWN, DS), F32),
        jax.ShapeDtypeStruct((1, ROWS), F32),
    )
    results = pl.pallas_call(
        kernel,
        out_shape=outs,
        in_specs=[hbm] * 4,
        out_specs=(vmem,) * 3,
        scratch_shapes=[
            pltpu.VMEM((NZ, NYL, ROWS, DT), BF16),
            pltpu.VMEM((NZ, NYL, ROWS, DS), BF16),
            pltpu.VMEM((BATCHES * SLOTS, OWN, DT + DS), BF16),
            pltpu.VMEM((DS, BATCHES * BATCH), BF16),
            pltpu.VMEM((NZ, BATCHES, BATCH, GROUP), F32),
            pltpu.VMEM((NZ, BATCHES, BATCH, GROUP), F32),
            pltpu.VMEM((2, BATCH, GROUP), F32),
            pltpu.VMEM((2, BATCH, GROUP), F32),
            pltpu.VMEM((NCORE, BATCHES, BATCH // 2, NZ * GROUP), BF16),
            pltpu.VMEM((NZ, BATCHES, 8, GROUP), F32),
            pltpu.VMEM((NZ, NYL, DS, ROWS), F32),
            pltpu.VMEM((OWNERS, 2, 8, ROWS), F32),
            pltpu.VMEM((OWNERS, 2, 8, ROWS), F32),
            pltpu.VMEM((OWNERS, 8, ROWS), F32),
            pltpu.VMEM((8, NYL, ZF, ROWS), BF16),
            pltpu.VMEM((4, NYL, ZF, ROWS), BF16),
            pltpu.VMEM((4, NYL, ZF, ROWS), BF16),
            pltpu.VMEM((ZF, ROWS), BF16),
            pltpu.VMEM((ZF, ROWS), BF16),
            pltpu.VMEM((NZ, YF, ROWS), BF16),
            pltpu.VMEM((NZ, YF, ROWS), BF16),
            pltpu.VMEM((8, YF, ROWS), BF16),
            pltpu.VMEM((4, YF, ROWS), BF16),
            pltpu.VMEM((4, YF, ROWS), BF16),
            pltpu.VMEM((BATCHES, 2, OWN, DS), F32),
            pltpu.VMEM((BATCHES, 2, OWN, DS), BF16),
            pltpu.VMEM((BATCHES, 2, OWN, DS), BF16),
            pltpu.VMEM((NYH, OWN, DS), BF16),
            pltpu.VMEM((NYH, OWN, DS), BF16),
            pltpu.VMEM((2, NYH, OWN, DS), BF16),
            pltpu.VMEM((2, NYH, OWN, DS), BF16),
            pltpu.VMEM((OWN, DS), BF16),
            pltpu.VMEM((OWN, DS), BF16),
            pltpu.SemaphoreType.DMA((6,)),
            pltpu.SemaphoreType.REGULAR((4,)),
            pltpu.SemaphoreType.DMA,
            pltpu.SemaphoreType.DMA((3,)),
            pltpu.SemaphoreType.DMA((MESSAGES,)),
            pltpu.SemaphoreType.DMA((MESSAGES,)),
            pltpu.SemaphoreType.DMA((NZ,)),
            pltpu.SemaphoreType.DMA((4,)),
        ],
        compiler_params=pltpu.CompilerParams(
            collective_id=0, has_side_effects=True, vmem_limit_bytes=VMEM_BYTES
        ),
    )(
        teacher_query.reshape(*blocks, DT),
        student_query.reshape(*blocks, DS),
        teacher_passages,
        student_passages,
    )
    grad_query, grad_passage, divergence = pl.pallas_call(
        deliver,
        out_shape=outs,
        in_specs=[hbm] * 3,
        out_specs=(hbm,) * 3,
        scratch_shapes=[
            *(pltpu.VMEM(out.shape, out.dtype) for out in outs),
            pltpu.SemaphoreType.DMA((3,)),
            pltpu.SemaphoreType.DMA((3,)),
        ],
        compiler_params=pltpu.CompilerParams(vmem_limit_bytes=VMEM_BYTES),
    )(*results)
    return divergence.reshape(ROWS), grad_query, grad_passage


def solution(mesh):
    return jax.shard_map(
        local,
        mesh=mesh,
        in_specs=(
            P("query", None),
            P("query", None),
            P(("query", "corpus"), None),
            P(("query", "corpus"), None),
        ),
        out_specs=(
            P(("query", "corpus")),
            P(("query", "corpus"), None),
            P(("query", "corpus"), None),
        ),
        check_vma=False,
    )
```

```python
import functools
import math

import jax
import jax.numpy as jnp
from jax import lax
from jax.experimental import pallas as pl
from jax.experimental.pallas import tpu as pltpu
from jax.sharding import PartitionSpec as P

NX, NYH, NYL, NZ, NCORE = 4, 2, 2, 8, 2
OWN = 64
ROWS = 128
DT, DS = 1024, 384
BATCH = 256
GROUP = NYL * ROWS
OWNERS = NYL * NZ
HALF = OWN // 2
ZF = 192
YF = DS - ZF
LOG2E = math.log2(math.e)
LN2 = math.log(2.0)
F32, BF16 = jnp.float32, jnp.bfloat16
MESH = pl.DeviceIdType.MESH

SELF, LEFT, RIGHT, FAR = 0, 1, 2, 3


BATCH_SLOTS = (0, 2), (2, 4), (6, 4), (10, 4), (14, 2)
BATCHES = len(BATCH_SLOTS)
SLOTS = 16
PLACES = 8


def place(h, where):
    if h == 0:
        return {SELF: 0, LEFT: 1, RIGHT: 2, FAR: 4}[where]
    return {SELF: 3, LEFT: 5, RIGHT: 6, FAR: 7}[where]


def slot_of(h, where, core):
    p = place(h, where)
    for first, count in BATCH_SLOTS:
        if p < count // 2:
            return first + p + core * (count // 2)
        p -= count // 2


def div(a, b):
    return lax.div(a, jnp.int32(b))


def rem(a, b):
    return lax.rem(a, jnp.int32(b))


def nt(a, b):
    return lax.dot_general(a, b, (((1,), (1,)), ((), ())), preferred_element_type=F32)


def nn(a, b):
    return lax.dot_general(a, b, (((1,), (0,)), ((), ())), preferred_element_type=F32)


class Messages:
    def __init__(self):
        self.numbers = {}

    def __call__(self, name):
        return self.numbers.setdefault(name, len(self.numbers))


MESSAGES = 80
VMEM_BYTES = 60 * 1024 * 1024


def kernel(
    tq_hbm, sq_hbm, tp_hbm, sp_hbm,
    gq_out, gp_out, div_out,
    tq, sq, pbuf, spt, tw, sw, raw_a, raw_b, gt, stat, gq,
    stat_send, stat_recv, res_recv,
    z_send, z_recv_r, z_recv_l, z_pair_send, z_pair_recv,
    y_pair_send, y_pair_recv, y_send, y_recv_r, y_recv_l,
    gp, gps_send, gps_recv, gp1_send, gp1_recv, gp2_send, gp2_recv, gp3_send, gp3_recv,
    load_sem, known_sem, gather_sem, ring_sem, send_sem, recv_sem, yp_recv_sem, st_sem,
):
    t_scale = DT ** (-0.5) * LOG2E
    s_scale = DS ** (-0.5) * LOG2E
    factor = DS ** (-0.5)
    q = lax.axis_index("query")
    c = lax.axis_index("corpus")
    x, yh = div(q, NYH), rem(q, NYH)
    yl, z, k = div(c, NZ * NCORE), rem(div(c, NCORE), NZ), rem(c, NCORE)
    me = yl * NZ + z

    def at(x_, yh_, yl_, z_, k_):
        return (x_ * NYH + yh_, (yl_ * NZ + z_) * NCORE + k_)

    right, left = at(rem(x + 1, NX), yh, yl, z, k), at(rem(x + NX - 1, NX), yh, yl, z, k)
    across = at(x, 1 - yh, 1 - yl, z, k)
    sibling = at(x, yh, yl, z, 1 - k)
    up, down = at(x, yh, yl, rem(z + 1, NZ), k), at(x, yh, yl, rem(z + NZ - 1, NZ), k)
    y_mate = at(x, yh, 1 - yl, z, k)

    offsets = [(dy, dz) for dy in range(NYL) for dz in range(NZ) if (dy, dz) != (0, 0)]
    y_of = [yl, 1 - yl]
    z_of = [rem(z + dz, NZ) for dz in range(NZ)]

    def offset_device(dy, dz):
        return at(x, yh, y_of[dy], z_of[dz], k)

    def slot(h, where, core, half=None):
        i = slot_of(h, where, core)
        if half is None:
            return pbuf.at[i]
        return pbuf.at[i, pl.ds(half * HALF, HALF)]

    def both(b, core):
        first, count = BATCH_SLOTS[b]
        return pbuf.at[pl.ds(first + core * (count // 2), count // 2)]

    loads = [
        pltpu.make_async_copy(tp_hbm, pbuf.at[0, :, pl.ds(0, DT)], load_sem.at[0]),
        pltpu.make_async_copy(sp_hbm, pbuf.at[0, :, pl.ds(DT, DS)], load_sem.at[1]),
    ]
    for y in range(NYL):
        loads.append(pltpu.make_async_copy(tq_hbm.at[y, :, k], tq.at[:, y], load_sem.at[2 + y]))
        loads.append(pltpu.make_async_copy(sq_hbm.at[y, :, k], sq.at[:, y], load_sem.at[4 + y]))
    for load in loads:
        load.start()

    barrier = pltpu.get_barrier_semaphore()
    for device in (right, left, across, sibling, up, down, y_mate):
        pl.semaphore_signal(barrier, inc=1, device_id=device, device_id_type=MESH)
    pl.semaphore_wait(barrier, 7)
    loads[0].wait()
    loads[1].wait()

    number = Messages()
    sent = []

    def message(refs, name, device, out=None):
        i = number(name)
        src, dst = refs()
        return pltpu.make_async_remote_copy(
            src_ref=src, dst_ref=dst, send_sem=send_sem.at[i] if out is None else out, recv_sem=recv_sem.at[i],
            device_id=device, device_id_type=MESH,
        )

    def send(refs, name, device):
        message(refs, name, device).start()
        sent.append((refs, name, device))

    def flush():
        for args in sent:
            message(*args).wait_send()
        sent.clear()

    def received(ref, name):
        message(lambda: (ref, ref), name, sibling).wait_recv()

    def spread(refs, name, device):
        message(refs, name, device, gather_sem).start()

    def spread_wait():
        everything = pbuf.at[pl.ds(0, SLOTS - 1)]
        message(lambda: (everything, everything), "gather", sibling, gather_sem).wait_send()

    def half_to(where, half, device):
        spread(lambda: (slot(0, SELF, 0, half), slot(0, where, 0, half)), ("p", where, half), device)

    def sides_to_sibling(h):
        if h == 0:
            received(slot(0, LEFT, 0, 1), ("p", LEFT, 1))
            received(slot(0, RIGHT, 0, 0), ("p", RIGHT, 0))
        else:
            received(slot(1, LEFT, 0), ("p1", LEFT))
            received(slot(1, RIGHT, 0), ("p1", RIGHT))
        to_sibling(3 if h else 1)

    def to_sibling(b):
        spread(lambda: (both(b, 0), both(b, 1)), ("sib", b), sibling)

    def from_sibling(b):
        received(both(b, 1), ("sib", b))

    def far_on():
        received(slot(0, LEFT, 0, 0), ("p", LEFT, 0))
        spread(lambda: (slot(0, LEFT, 0, 0), slot(0, FAR, 0, 0)), ("far",), right)
        received(slot(0, RIGHT, 0, 1), ("p", RIGHT, 1))
        spread(lambda: (slot(0, RIGHT, 0, 1), slot(0, FAR, 0, 1)), ("far",), left)

    def across_on(half):
        received(slot(1, SELF, 0, half), ("across", half))
        spread(lambda: (slot(1, SELF, 0, half), slot(1, LEFT, 0, half)), ("p1", LEFT), right)
        spread(lambda: (slot(1, SELF, 0, half), slot(1, RIGHT, 0, half)), ("p1", RIGHT), left)

    def far_across():
        received(slot(0, FAR, 0), ("far",))
        spread(lambda: (slot(0, FAR, 0), slot(1, FAR, 0)), ("far across",), across)
        to_sibling(2)

    def far_from_across():
        received(slot(1, FAR, 0), ("far across",))
        to_sibling(4)

    half_to(LEFT, 0, right)
    half_to(RIGHT, 1, left)
    spread(lambda: (slot(0, SELF, 0, 0), slot(1, SELF, 0, 0)), ("across", 0), across)
    half_to(LEFT, 1, right)
    half_to(RIGHT, 0, left)
    spread(lambda: (slot(0, SELF, 0, 1), slot(1, SELF, 0, 1)), ("across", 1), across)
    to_sibling(0)

    def product(slots, n, raw):
        first, count = slots
        batch = pbuf[pl.ds(first, count)].reshape(count * OWN, DT + DS)
        raw[0] = nt(batch[:, :DT], tq[n].reshape(GROUP, DT))
        raw[1] = nt(batch[:, DT:], sq[n].reshape(GROUP, DS))

    def weights(b, row, n, raw, size):
        t = raw[0] * t_scale
        s = raw[1] * s_scale
        t_max = jnp.max(t, axis=0, keepdims=True)
        s_max = jnp.max(s, axis=0, keepdims=True)
        t_weight = jnp.exp2(t - t_max)
        s_weight = jnp.exp2(s - s_max)
        tw[n, pl.ds(row, size)] = t_weight
        sw[n, pl.ds(row, size)] = s_weight
        t_sum = jnp.sum(t_weight, axis=0, keepdims=True)
        s_sum = jnp.sum(s_weight, axis=0, keepdims=True)
        cross = jnp.sum(t_weight * (t - s), axis=0, keepdims=True)
        stat[n, b] = jnp.concatenate([t_max, t_sum, s_max, s_sum, cross, cross, cross, cross], axis=0)

    def small_scores(b, first):
        slots = BATCH_SLOTS[b]
        row, size = slots[0] * OWN, slots[1] * OWN
        half_a, half_b = raw_a.at[:, pl.ds(0, size)], raw_b.at[:, pl.ds(0, size)]

        def body(i, carry):
            n = first + 2 * i
            product(slots, n, half_a)
            product(slots, n + 1, half_b)
            weights(b, row, n, half_a, size)
            weights(b, row, n + 1, half_b, size)
            return carry

        lax.fori_loop(0, 2, body, 0)

    def turn():
        for core in range(NCORE):
            rows = [
                pbuf[first + core * (count // 2):first + (core + 1) * (count // 2)].reshape(-1, DT + DS)[:, DT:]
                for first, count in BATCH_SLOTS
            ]
            size = PLACES * OWN
            spt[:, core * size:(core + 1) * size] = jnp.concatenate(rows, axis=0).T

    def know(i):
        for device in (up, down, y_mate):
            pl.semaphore_signal(known_sem.at[i], inc=1, device_id=device, device_id_type=MESH)
        pl.semaphore_wait(known_sem.at[i], 3)

    know(0)
    for load in loads[2:]:
        load.wait()
    from_sibling(0)
    small_scores(0, 0)
    far_on()
    across_on(0)
    know(1)
    small_scores(0, 4)
    across_on(1)
    sides_to_sibling(0)
    know(2)
    know(3)

    def joined(parts):
        t_max = functools.reduce(jnp.maximum, [p[0:1] for p in parts])
        s_max = functools.reduce(jnp.maximum, [p[2:3] for p in parts])
        t_in = [jnp.exp2(p[0:1] - t_max) for p in parts]
        s_in = [jnp.exp2(p[2:3] - s_max) for p in parts]
        t_sum = functools.reduce(jnp.add, [p[1:2] * w for p, w in zip(parts, t_in)])
        s_sum = functools.reduce(jnp.add, [p[3:4] * w for p, w in zip(parts, s_in)])
        cross = functools.reduce(jnp.add, [p[4:5] * w for p, w in zip(parts, t_in)])
        return t_max, t_sum, s_max, s_sum, cross

    def stat_copy(dy, dz):
        return pltpu.make_async_remote_copy(
            src_ref=stat_send.at[y_of[dy] * NZ + z_of[dz]], dst_ref=stat_recv.at[dy * NZ + (NZ - dz) % NZ],
            send_sem=st_sem.at[0], recv_sem=st_sem.at[1],
            device_id=offset_device(dy, dz), device_id_type=MESH,
        )

    def res_copy(dy, dz):
        return pltpu.make_async_remote_copy(
            src_ref=res_recv.at[me], dst_ref=res_recv.at[me],
            send_sem=st_sem.at[2], recv_sem=st_sem.at[3],
            device_id=offset_device(dy, dz), device_id_type=MESH,
        )

    def all_copies(ref, first):
        others = ref.at[pl.ds(0, OWNERS - 1)]
        return pltpu.make_async_remote_copy(
            src_ref=others, dst_ref=others, send_sem=st_sem.at[first], recv_sem=st_sem.at[first + 1],
            device_id=sibling, device_id_type=MESH,
        )

    def leave(first):
        for n in range(first, first + 4):
            t_max, t_sum, s_max, s_sum, cross = joined([stat[n, b] for b in range(BATCHES)])
            whole = jnp.concatenate([t_max, t_sum, s_max, s_sum, cross, cross, cross, cross], axis=0)
            for y in range(NYL):
                stat_send[y * NZ + n, 0] = whole[:, y * ROWS:(y + 1) * ROWS]
            four = jnp.concatenate([whole[0:4, :ROWS], whole[0:4, ROWS:]], axis=0)
            for y in range(NYL):
                stat_send[y * NZ + (n + 4) % NZ, 1] = four

    large = 3 * NZ
    size = 4 * OWN

    def large_product(i, raw):
        product((2 + 4 * div(i, NZ), 4), rem(i, NZ), raw)

    def large_weights(i, raw):
        b = div(i, NZ)
        weights(1 + b, pl.multiple_of(2 * OWN + b * size, 2 * OWN), rem(i, NZ), raw, size)

    from_sibling(1)
    large_product(0, raw_a)

    def score_step(j, carry):
        @pl.when(j == 1)
        def _():
            far_across()

        @pl.when(j == 3)
        def _():
            from_sibling(2)

        @pl.when(j == 6)
        def _():
            sides_to_sibling(1)

        @pl.when(j == 7)
        def _():
            from_sibling(3)

        @pl.when(j == 10)
        def _():
            far_from_across()

        large_product(2 * j + 1, raw_b)
        large_weights(2 * j, raw_a)
        large_product(jnp.minimum(2 * j + 2, large - 1), raw_a)
        large_weights(2 * j + 1, raw_b)
        return carry

    lax.fori_loop(0, large // 2, score_step, 0)
    from_sibling(4)
    for first in (0, 4):
        small_scores(4, first)
        leave(first)
    for offset in offsets:
        stat_copy(*offset).start()
    stat_recv[0] = stat_send[me]
    turn()
    spread_wait()
    all_copies(stat_recv, 0).wait_recv()
    def totals(parts):
        t_max, t_sum, s_max, s_sum, cross = joined(parts)
        t_in, s_in = factor / t_sum, factor / s_sum
        result = jnp.concatenate([t_max, t_in, s_max, s_in, t_in, t_in, t_in, t_in], axis=0)
        return result, (t_max, t_sum, s_max, s_sum, cross)

    result, (t_max, t_sum, s_max, s_sum, cross) = totals([stat_recv[m, 0] for m in range(OWNERS)])
    res_recv[me] = result
    for offset in offsets:
        res_copy(*offset).start()
    far = []
    for y in range(NYL):
        parts = [stat_recv[m, 1, 4 * y:4 * y + 4] for m in range(OWNERS)]
        far.append(totals([jnp.concatenate([p, p], axis=0) for p in parts])[0])
    far = jnp.concatenate(far, axis=1)

    def group(away):
        return rem(z + NZ + away, NZ)

    def sequence(i):
        size = 4 - div(i + 1, 2)
        return group(size * (2 * rem(i, 2) - 1))

    def lanes(n):
        return pl.ds(pl.multiple_of(n * GROUP, GROUP), GROUP)

    def form(i, res=None):
        n = sequence(i)
        if res is None:
            res = jnp.concatenate([res_recv[n], res_recv[NZ + n]], axis=1)
        for b, (first, count) in enumerate(BATCH_SLOTS):
            st = stat[n, b]
            t_in = jnp.exp2(st[0:1] - res[0:1]) * res[1:2]
            s_in = jnp.exp2(st[2:3] - res[2:3]) * res[3:4]
            rows = pl.ds(first * OWN, count * OWN)
            grad = (sw[n, rows] * s_in - tw[n, rows] * t_in).astype(BF16)
            half = count * OWN // 2
            rows = pl.ds(first * OWN // 2, half)
            gt[0, rows, lanes(n)] = grad[:half]
            gt[1, rows, lanes(n)] = grad[half:]

    def pair_copy(i):
        return pltpu.make_async_remote_copy(
            src_ref=y_pair_send.at[i], dst_ref=y_pair_recv.at[i],
            send_sem=ring_sem.at[2], recv_sem=yp_recv_sem.at[i],
            device_id=y_mate, device_id_type=MESH,
        )

    def query_part(i):
        n = sequence(i)
        total = nn(spt[...], gt[:, :, lanes(n)].reshape(NCORE * PLACES * OWN, GROUP))
        gq[n, 0] = total[:, :ROWS]
        gq[n, 1] = total[:, ROWS:]
        y_pair_send[i] = gq[n, 1 - yl, ZF:].astype(BF16)

    def z_part(away):
        return gq[group(away), :, :ZF]

    def y_part(away):
        i = (4, 3, -3, 2, -2, 1, -1, 0).index(away)
        pair_copy(i).wait_recv()
        return gq[group(away), yl, ZF:] + y_pair_recv[i].astype(F32)

    ZH, YH = ZF // 2, YF // 2

    def z_start():
        far = z_part(4).astype(BF16)
        z_send[0] = far
        message(lambda: (z_send.at[0, :, pl.ds(0, ZH)], z_recv_r.at[0, :, pl.ds(0, ZH)]), ("zr", 0), up, ring_sem.at[0]).start()
        message(lambda: (z_send.at[0, :, pl.ds(ZH, ZH)], z_recv_l.at[0, :, pl.ds(ZH, ZH)]), ("zl", 0), down, ring_sem.at[0]).start()

    def y_start():
        y_send[0] = y_part(4).astype(BF16)
        message(lambda: (y_send.at[0, pl.ds(0, YH)], y_recv_r.at[0, pl.ds(0, YH)]), ("yr", 0), up, ring_sem.at[1]).start()
        message(lambda: (y_send.at[0, pl.ds(YH, YH)], y_recv_l.at[0, pl.ds(YH, YH)]), ("yl", 0), down, ring_sem.at[1]).start()

    def z_step(step):
        if step == 1:
            mine = z_part(3)
            received(z_recv_r.at[0, :, pl.ds(0, ZH)], ("zr", 0))
            z_send[1, :, :ZH] = (mine[:, :ZH] + z_recv_r[0, :, :ZH].astype(F32)).astype(BF16)
            z_send[1, :, ZH:] = mine[:, ZH:].astype(BF16)
        else:
            received(z_recv_r.at[step - 1], ("zr", step - 1))
            z_send[step] = (z_part(4 - step) + z_recv_r[step - 1].astype(F32)).astype(BF16)
        message(lambda step=step: (z_send.at[step], z_recv_r.at[step]), ("zr", step), up, ring_sem.at[0]).start()
        if step == 1:
            mine = z_part(-3)
            received(z_recv_l.at[0, :, pl.ds(ZH, ZH)], ("zl", 0))
            z_send[5, :, :ZH] = mine[:, :ZH].astype(BF16)
            z_send[5, :, ZH:] = (mine[:, ZH:] + z_recv_l[0, :, ZH:].astype(F32)).astype(BF16)
        else:
            received(z_recv_l.at[step - 1], ("zl", step - 1))
            z_send[4 + step] = (z_part(step - 4) + z_recv_l[step - 1].astype(F32)).astype(BF16)
        message(lambda step=step: (z_send.at[4 + step], z_recv_l.at[step]), ("zl", step), down, ring_sem.at[0]).start()

    def y_step(step):
        mine = y_part(4 - step)
        if step == 1:
            received(y_recv_r.at[0, pl.ds(0, YH)], ("yr", 0))
            y_send[1, :YH] = (mine[:YH] + y_recv_r[0, :YH].astype(F32)).astype(BF16)
            y_send[1, YH:] = mine[YH:].astype(BF16)
        else:
            received(y_recv_r.at[step - 1], ("yr", step - 1))
            y_send[step] = (mine + y_recv_r[step - 1].astype(F32)).astype(BF16)
        message(lambda step=step: (y_send.at[step], y_recv_r.at[step]), ("yr", step), up, ring_sem.at[1]).start()
        mine = y_part(step - 4)
        if step == 1:
            received(y_recv_l.at[0, pl.ds(YH, YH)], ("yl", 0))
            y_send[5, :YH] = mine[:YH].astype(BF16)
            y_send[5, YH:] = (mine[YH:] + y_recv_l[0, YH:].astype(F32)).astype(BF16)
        else:
            received(y_recv_l.at[step - 1], ("yl", step - 1))
            y_send[4 + step] = (mine + y_recv_l[step - 1].astype(F32)).astype(BF16)
        message(lambda step=step: (y_send.at[4 + step], y_recv_l.at[step]), ("yl", step), down, ring_sem.at[1]).start()

    def passage_part(core, to):
        to[...] = jnp.zeros_like(to)

        def body(n, carry):
            term = nn(gt[core, :, lanes(n)], sq[n].reshape(GROUP, DS))
            to[...] = to[...] + term.reshape(PLACES, OWN, DS)
            return carry

        lax.fori_loop(0, NZ, body, 0)

    def gp_of(h, where):
        return gp[place(h, where)]

    def gp_first():
        received(gps_recv, "gp sibling")
        gp[...] = gp[...] + gps_recv[...].astype(F32)
        for h in range(NYH):
            gp1_send[h] = gp_of(h, FAR).astype(BF16)
        send(lambda: (gp1_send.at[0], gp1_recv.at[0]), ("gp", RIGHT, 1), right)
        send(lambda: (gp1_send.at[1], gp1_recv.at[1]), ("gp", LEFT, 1), left)

    def gp_second():
        received(gp1_recv.at[0], ("gp", RIGHT, 1))
        gp2_send[0, 0] = (gp_of(0, RIGHT) + gp1_recv[0].astype(F32)).astype(BF16)
        gp2_send[0, 1] = gp_of(1, RIGHT).astype(BF16)
        send(lambda: (gp2_send.at[0], gp2_recv.at[0]), ("gp", RIGHT, 2), right)
        received(gp1_recv.at[1], ("gp", LEFT, 1))
        gp2_send[1, 0] = gp_of(0, LEFT).astype(BF16)
        gp2_send[1, 1] = (gp_of(1, LEFT) + gp1_recv[1].astype(F32)).astype(BF16)
        send(lambda: (gp2_send.at[1], gp2_recv.at[1]), ("gp", LEFT, 2), left)

    def gp_third():
        received(gp2_recv.at[0], ("gp", RIGHT, 2))
        received(gp2_recv.at[1], ("gp", LEFT, 2))
        gp3_send[...] = x_total(1).astype(BF16)
        send(lambda: (gp3_send, gp3_recv), "gp across", across)

    def x_total(h):
        return gp_of(h, SELF) + gp2_recv[0, h].astype(F32) + gp2_recv[1, h].astype(F32)

    def z_last():
        received(z_recv_r.at[3], ("zr", 3))
        received(z_recv_l.at[3], ("zl", 3))
        for y in range(NYL):
            gq[z, y, :ZF] = gq[z, y, :ZF] + z_recv_r[3, y].astype(F32) + z_recv_l[3, y].astype(F32)
        z_pair_send[...] = gq[z, 1 - yl, :ZF].astype(BF16)
        send(lambda: (z_pair_send, z_pair_recv), "z pair", y_mate)

    form(0, far)
    query_part(0)
    pair_copy(0).start()
    z_start()
    div_out[...] = cross * LN2 / t_sum - (t_max * LN2 + jnp.log(t_sum)) + (s_max * LN2 + jnp.log(s_sum))
    all_copies(stat_send, 0).wait_send()
    all_copies(res_recv, 2).wait_recv()
    form(1)

    def gradient_step(i, carry):
        query_part(i)
        form(i + 1)
        pair_copy(i).start()

        @pl.when(i == 3)
        def _():
            z_step(1)

        @pl.when(i == 4)
        def _():
            y_start()

        return carry

    lax.fori_loop(1, NZ - 1, gradient_step, 0)
    query_part(NZ - 1)
    pair_copy(NZ - 1).start()
    passage_part(1, gp)
    gps_send[...] = gp[...].astype(BF16)
    send(lambda: (gps_send, gps_recv), "gp sibling", sibling)
    z_step(2)
    y_step(1)
    passage_part(0, gp)
    gp_first()
    z_step(3)
    y_step(2)
    gp_second()
    all_copies(res_recv, 2).wait_send()
    z_last()
    y_step(3)
    gp_third()
    for i, ref in enumerate((z_send.at[pl.ds(0, 7)], y_send.at[pl.ds(0, 7)], y_pair_send)):
        message(lambda: (ref, ref), "ring", sibling, ring_sem.at[i]).wait_send()
    flush()

    mine = y_part(0)
    received(y_recv_r.at[3], ("yr", 3))
    received(y_recv_l.at[3], ("yl", 3))
    gq_out[:, ZF:] = (mine + y_recv_r[3].astype(F32) + y_recv_l[3].astype(F32)).T
    received(z_pair_recv, "z pair")
    gq_out[:, :ZF] = (gq[z, yl, :ZF] + z_pair_recv[...].astype(F32)).T
    received(gp3_recv, "gp across")
    gp_out[...] = x_total(0) + gp3_recv[...].astype(F32)


def deliver(gq_in, gp_in, div_in, gq_out, gp_out, div_out, gq, gp, div, in_sem, out_sem):
    parts = ((gq_in, gq, gq_out), (gp_in, gp, gp_out), (div_in, div, div_out))
    ins = [pltpu.make_async_copy(src, mid, in_sem.at[i]) for i, (src, mid, _) in enumerate(parts)]
    outs = [pltpu.make_async_copy(mid, dst, out_sem.at[i]) for i, (_, mid, dst) in enumerate(parts)]
    for copy in ins:
        copy.start()
    for arrive, leave in zip(ins, outs):
        arrive.wait()
        leave.start()
    for copy in outs:
        copy.wait()


def local(teacher_query, student_query, teacher_passages, student_passages):
    blocks = NYL, NZ, NCORE, ROWS
    hbm = pl.BlockSpec(memory_space=pl.ANY)
    vmem = pl.BlockSpec(memory_space=pltpu.VMEM)
    outs = (
        jax.ShapeDtypeStruct((ROWS, DS), F32),
        jax.ShapeDtypeStruct((OWN, DS), F32),
        jax.ShapeDtypeStruct((1, ROWS), F32),
    )
    results = pl.pallas_call(
        kernel,
        out_shape=outs,
        in_specs=[hbm] * 4,
        out_specs=(vmem,) * 3,
        scratch_shapes=[
            pltpu.VMEM((NZ, NYL, ROWS, DT), BF16),
            pltpu.VMEM((NZ, NYL, ROWS, DS), BF16),
            pltpu.VMEM((SLOTS, OWN, DT + DS), BF16),
            pltpu.VMEM((DS, SLOTS * OWN), BF16),
            pltpu.VMEM((NZ, SLOTS * OWN, GROUP), F32),
            pltpu.VMEM((NZ, SLOTS * OWN, GROUP), F32),
            pltpu.VMEM((2, BATCH, GROUP), F32),
            pltpu.VMEM((2, BATCH, GROUP), F32),
            pltpu.VMEM((NCORE, PLACES * OWN, NZ * GROUP), BF16),
            pltpu.VMEM((NZ, BATCHES, 8, GROUP), F32),
            pltpu.VMEM((NZ, NYL, DS, ROWS), F32),
            pltpu.VMEM((OWNERS, 2, 8, ROWS), F32),
            pltpu.VMEM((OWNERS, 2, 8, ROWS), F32),
            pltpu.VMEM((OWNERS, 8, ROWS), F32),
            pltpu.VMEM((8, NYL, ZF, ROWS), BF16),
            pltpu.VMEM((4, NYL, ZF, ROWS), BF16),
            pltpu.VMEM((4, NYL, ZF, ROWS), BF16),
            pltpu.VMEM((ZF, ROWS), BF16),
            pltpu.VMEM((ZF, ROWS), BF16),
            pltpu.VMEM((NZ, YF, ROWS), BF16),
            pltpu.VMEM((NZ, YF, ROWS), BF16),
            pltpu.VMEM((8, YF, ROWS), BF16),
            pltpu.VMEM((4, YF, ROWS), BF16),
            pltpu.VMEM((4, YF, ROWS), BF16),
            pltpu.VMEM((PLACES, OWN, DS), F32),
            pltpu.VMEM((PLACES, OWN, DS), BF16),
            pltpu.VMEM((PLACES, OWN, DS), BF16),
            pltpu.VMEM((NYH, OWN, DS), BF16),
            pltpu.VMEM((NYH, OWN, DS), BF16),
            pltpu.VMEM((2, NYH, OWN, DS), BF16),
            pltpu.VMEM((2, NYH, OWN, DS), BF16),
            pltpu.VMEM((OWN, DS), BF16),
            pltpu.VMEM((OWN, DS), BF16),
            pltpu.SemaphoreType.DMA((6,)),
            pltpu.SemaphoreType.REGULAR((4,)),
            pltpu.SemaphoreType.DMA,
            pltpu.SemaphoreType.DMA((3,)),
            pltpu.SemaphoreType.DMA((MESSAGES,)),
            pltpu.SemaphoreType.DMA((MESSAGES,)),
            pltpu.SemaphoreType.DMA((NZ,)),
            pltpu.SemaphoreType.DMA((4,)),
        ],
        compiler_params=pltpu.CompilerParams(
            collective_id=0, has_side_effects=True, vmem_limit_bytes=VMEM_BYTES
        ),
    )(
        teacher_query.reshape(*blocks, DT),
        student_query.reshape(*blocks, DS),
        teacher_passages,
        student_passages,
    )
    grad_query, grad_passage, divergence = pl.pallas_call(
        deliver,
        out_shape=outs,
        in_specs=[hbm] * 3,
        out_specs=(hbm,) * 3,
        scratch_shapes=[
            *(pltpu.VMEM(out.shape, out.dtype) for out in outs),
            pltpu.SemaphoreType.DMA((3,)),
            pltpu.SemaphoreType.DMA((3,)),
        ],
        compiler_params=pltpu.CompilerParams(vmem_limit_bytes=VMEM_BYTES),
    )(*results)
    return divergence.reshape(ROWS), grad_query, grad_passage


def solution(mesh):
    return jax.shard_map(
        local,
        mesh=mesh,
        in_specs=(
            P("query", None),
            P("query", None),
            P(("query", "corpus"), None),
            P(("query", "corpus"), None),
        ),
        out_specs=(
            P(("query", "corpus")),
            P(("query", "corpus"), None),
            P(("query", "corpus"), None),
        ),
        check_vma=False,
    )
```

```python
import functools
import math

import jax
import jax.numpy as jnp
from jax import lax
from jax.experimental import pallas as pl
from jax.experimental.pallas import tpu as pltpu
from jax.sharding import PartitionSpec as P

NX, NYH, NYL, NZ, NCORE = 4, 2, 2, 8, 2
OWN = 64
ROWS = 128
DT, DS = 1024, 384
BATCH = 256
GROUP = NYL * ROWS
OWNERS = NYL * NZ
HALF = OWN // 2
ZF = 192
YF = DS - ZF
LOG2E = math.log2(math.e)
LN2 = math.log(2.0)
F32, BF16 = jnp.float32, jnp.bfloat16
MESH = pl.DeviceIdType.MESH

SELF, LEFT, RIGHT, FAR = 0, 1, 2, 3


BATCH_SLOTS = (0, 2), (2, 4), (6, 4), (10, 4), (14, 2)
BATCHES = len(BATCH_SLOTS)
SLOTS = 16
PLACES = 8


def place(h, where):
    if h == 0:
        return {SELF: 0, LEFT: 1, RIGHT: 2, FAR: 4}[where]
    return {SELF: 3, LEFT: 5, RIGHT: 6, FAR: 7}[where]


def slot_of(h, where, core):
    p = place(h, where)
    for first, count in BATCH_SLOTS:
        if p < count // 2:
            return first + p + core * (count // 2)
        p -= count // 2


def div(a, b):
    return lax.div(a, jnp.int32(b))


def rem(a, b):
    return lax.rem(a, jnp.int32(b))


def nt(a, b):
    return lax.dot_general(a, b, (((1,), (1,)), ((), ())), preferred_element_type=F32)


def nn(a, b):
    return lax.dot_general(a, b, (((1,), (0,)), ((), ())), preferred_element_type=F32)


class Messages:
    def __init__(self):
        self.numbers = {}

    def __call__(self, name):
        return self.numbers.setdefault(name, len(self.numbers))


MESSAGES = 80
VMEM_BYTES = 60 * 1024 * 1024


def kernel(
    tq_hbm, sq_hbm, tp_hbm, sp_hbm,
    gq_out, gp_out, div_out,
    tq, sq, pbuf, spt, tw, sw, raw_a, raw_b, gt, stat, gq,
    stat_send, stat_recv, res_recv,
    z_send, z_recv, z_pair_send, z_pair_recv,
    y_pair_send, y_pair_recv, y_send, y_recv,
    gp, gps_send, gps_recv, gp1_send, gp1_recv, gp2_send, gp2_recv, gp3_send, gp3_recv,
    load_sem, known_sem, gather_sem, ring_sem, send_sem, recv_sem, yp_recv_sem, st_sem,
):
    t_scale = DT ** (-0.5) * LOG2E
    s_scale = DS ** (-0.5) * LOG2E
    factor = DS ** (-0.5)
    q = lax.axis_index("query")
    c = lax.axis_index("corpus")
    x, yh = div(q, NYH), rem(q, NYH)
    yl, z, k = div(c, NZ * NCORE), rem(div(c, NCORE), NZ), rem(c, NCORE)
    me = yl * NZ + z

    def at(x_, yh_, yl_, z_, k_):
        return (x_ * NYH + yh_, (yl_ * NZ + z_) * NCORE + k_)

    right, left = at(rem(x + 1, NX), yh, yl, z, k), at(rem(x + NX - 1, NX), yh, yl, z, k)
    across = at(x, 1 - yh, 1 - yl, z, k)
    sibling = at(x, yh, yl, z, 1 - k)
    up, down = at(x, yh, yl, rem(z + 1, NZ), k), at(x, yh, yl, rem(z + NZ - 1, NZ), k)
    y_mate = at(x, yh, 1 - yl, z, k)

    offsets = [(dy, dz) for dy in range(NYL) for dz in range(NZ) if (dy, dz) != (0, 0)]
    y_of = [yl, 1 - yl]
    z_of = [rem(z + dz, NZ) for dz in range(NZ)]

    def offset_device(dy, dz):
        return at(x, yh, y_of[dy], z_of[dz], k)

    def slot(h, where, core, half=None):
        i = slot_of(h, where, core)
        if half is None:
            return pbuf.at[i]
        return pbuf.at[i, pl.ds(half * HALF, HALF)]

    def both(b, core):
        first, count = BATCH_SLOTS[b]
        return pbuf.at[pl.ds(first + core * (count // 2), count // 2)]

    loads = [
        pltpu.make_async_copy(tp_hbm, pbuf.at[0, :, pl.ds(0, DT)], load_sem.at[0]),
        pltpu.make_async_copy(sp_hbm, pbuf.at[0, :, pl.ds(DT, DS)], load_sem.at[1]),
    ]
    for y in range(NYL):
        loads.append(pltpu.make_async_copy(tq_hbm.at[y, :, k], tq.at[:, y], load_sem.at[2 + y]))
        loads.append(pltpu.make_async_copy(sq_hbm.at[y, :, k], sq.at[:, y], load_sem.at[4 + y]))
    for load in loads:
        load.start()

    barrier = pltpu.get_barrier_semaphore()
    for device in (right, left, across, sibling, up, down, y_mate):
        pl.semaphore_signal(barrier, inc=1, device_id=device, device_id_type=MESH)
    pl.semaphore_wait(barrier, 7)
    loads[0].wait()
    loads[1].wait()

    number = Messages()
    sent = []

    def message(refs, name, device, out=None):
        i = number(name)
        src, dst = refs()
        return pltpu.make_async_remote_copy(
            src_ref=src, dst_ref=dst, send_sem=send_sem.at[i] if out is None else out, recv_sem=recv_sem.at[i],
            device_id=device, device_id_type=MESH,
        )

    def send(refs, name, device):
        message(refs, name, device).start()
        sent.append((refs, name, device))

    def flush():
        for args in sent:
            message(*args).wait_send()
        sent.clear()

    def received(ref, name):
        message(lambda: (ref, ref), name, sibling).wait_recv()

    def spread(refs, name, device):
        message(refs, name, device, gather_sem).start()

    def spread_wait():
        everything = pbuf.at[pl.ds(0, SLOTS - 1)]
        message(lambda: (everything, everything), "gather", sibling, gather_sem).wait_send()

    def half_to(where, half, device):
        spread(lambda: (slot(0, SELF, 0, half), slot(0, where, 0, half)), ("p", where, half), device)

    def sides_to_sibling(h):
        if h == 0:
            received(slot(0, LEFT, 0, 1), ("p", LEFT, 1))
            received(slot(0, RIGHT, 0, 0), ("p", RIGHT, 0))
        else:
            received(slot(1, LEFT, 0), ("p1", LEFT))
            received(slot(1, RIGHT, 0), ("p1", RIGHT))
        to_sibling(3 if h else 1)

    def to_sibling(b):
        spread(lambda: (both(b, 0), both(b, 1)), ("sib", b), sibling)

    def from_sibling(b):
        received(both(b, 1), ("sib", b))

    def far_on():
        received(slot(0, LEFT, 0, 0), ("p", LEFT, 0))
        spread(lambda: (slot(0, LEFT, 0, 0), slot(0, FAR, 0, 0)), ("far",), right)
        received(slot(0, RIGHT, 0, 1), ("p", RIGHT, 1))
        spread(lambda: (slot(0, RIGHT, 0, 1), slot(0, FAR, 0, 1)), ("far",), left)

    def across_on(half):
        received(slot(1, SELF, 0, half), ("across", half))
        spread(lambda: (slot(1, SELF, 0, half), slot(1, LEFT, 0, half)), ("p1", LEFT), right)
        spread(lambda: (slot(1, SELF, 0, half), slot(1, RIGHT, 0, half)), ("p1", RIGHT), left)

    def far_across():
        received(slot(0, FAR, 0), ("far",))
        spread(lambda: (slot(0, FAR, 0), slot(1, FAR, 0)), ("far across",), across)
        to_sibling(2)

    def far_from_across():
        received(slot(1, FAR, 0), ("far across",))
        to_sibling(4)

    half_to(LEFT, 0, right)
    half_to(RIGHT, 1, left)
    spread(lambda: (slot(0, SELF, 0, 0), slot(1, SELF, 0, 0)), ("across", 0), across)
    half_to(LEFT, 1, right)
    half_to(RIGHT, 0, left)
    spread(lambda: (slot(0, SELF, 0, 1), slot(1, SELF, 0, 1)), ("across", 1), across)
    to_sibling(0)

    def product(slots, n, raw):
        first, count = slots
        batch = pbuf[pl.ds(first, count)].reshape(count * OWN, DT + DS)
        raw[0] = nt(batch[:, :DT], tq[n].reshape(GROUP, DT))
        raw[1] = nt(batch[:, DT:], sq[n].reshape(GROUP, DS))

    def weights(b, row, n, raw, size):
        t = raw[0] * t_scale
        s = raw[1] * s_scale
        t_max = jnp.max(t, axis=0, keepdims=True)
        s_max = jnp.max(s, axis=0, keepdims=True)
        t_weight = jnp.exp2(t - t_max)
        s_weight = jnp.exp2(s - s_max)
        tw[n, pl.ds(row, size)] = t_weight
        sw[n, pl.ds(row, size)] = s_weight
        t_sum = jnp.sum(t_weight, axis=0, keepdims=True)
        s_sum = jnp.sum(s_weight, axis=0, keepdims=True)
        cross = jnp.sum(t_weight * (t - s), axis=0, keepdims=True)
        stat[n, b] = jnp.concatenate([t_max, t_sum, s_max, s_sum, cross, cross, cross, cross], axis=0)

    def small_scores(b, first):
        slots = BATCH_SLOTS[b]
        row, size = slots[0] * OWN, slots[1] * OWN
        half_a, half_b = raw_a.at[:, pl.ds(0, size)], raw_b.at[:, pl.ds(0, size)]

        def body(i, carry):
            n = first + 2 * i
            product(slots, n, half_a)
            product(slots, n + 1, half_b)
            weights(b, row, n, half_a, size)
            weights(b, row, n + 1, half_b, size)
            return carry

        lax.fori_loop(0, 2, body, 0)

    def turn():
        for core in range(NCORE):
            rows = [
                pbuf[first + core * (count // 2):first + (core + 1) * (count // 2)].reshape(-1, DT + DS)[:, DT:]
                for first, count in BATCH_SLOTS
            ]
            size = PLACES * OWN
            spt[:, core * size:(core + 1) * size] = jnp.concatenate(rows, axis=0).T

    def know(i):
        for device in (up, down, y_mate):
            pl.semaphore_signal(known_sem.at[i], inc=1, device_id=device, device_id_type=MESH)
        pl.semaphore_wait(known_sem.at[i], 3)

    know(0)
    far_on()
    across_on(0)
    know(1)
    for load in loads[2:]:
        load.wait()
    from_sibling(0)
    small_scores(0, 0)
    across_on(1)
    know(2)
    small_scores(0, 4)
    sides_to_sibling(0)
    know(3)

    def joined(parts):
        t_max = functools.reduce(jnp.maximum, [p[0:1] for p in parts])
        s_max = functools.reduce(jnp.maximum, [p[2:3] for p in parts])
        t_in = [jnp.exp2(p[0:1] - t_max) for p in parts]
        s_in = [jnp.exp2(p[2:3] - s_max) for p in parts]
        t_sum = functools.reduce(jnp.add, [p[1:2] * w for p, w in zip(parts, t_in)])
        s_sum = functools.reduce(jnp.add, [p[3:4] * w for p, w in zip(parts, s_in)])
        cross = functools.reduce(jnp.add, [p[4:5] * w for p, w in zip(parts, t_in)])
        return t_max, t_sum, s_max, s_sum, cross

    def stat_copy(dy, dz):
        return pltpu.make_async_remote_copy(
            src_ref=stat_send.at[y_of[dy] * NZ + z_of[dz]], dst_ref=stat_recv.at[dy * NZ + (NZ - dz) % NZ],
            send_sem=st_sem.at[0], recv_sem=st_sem.at[1],
            device_id=offset_device(dy, dz), device_id_type=MESH,
        )

    def res_copy(dy, dz):
        return pltpu.make_async_remote_copy(
            src_ref=res_recv.at[me], dst_ref=res_recv.at[me],
            send_sem=st_sem.at[2], recv_sem=st_sem.at[3],
            device_id=offset_device(dy, dz), device_id_type=MESH,
        )

    def all_copies(ref, first):
        others = ref.at[pl.ds(0, OWNERS - 1)]
        return pltpu.make_async_remote_copy(
            src_ref=others, dst_ref=others, send_sem=st_sem.at[first], recv_sem=st_sem.at[first + 1],
            device_id=sibling, device_id_type=MESH,
        )

    def leave(first):
        for n in range(first, first + 4):
            t_max, t_sum, s_max, s_sum, cross = joined([stat[n, b] for b in range(BATCHES)])
            whole = jnp.concatenate([t_max, t_sum, s_max, s_sum, cross, cross, cross, cross], axis=0)
            for y in range(NYL):
                stat_send[y * NZ + n, 0] = whole[:, y * ROWS:(y + 1) * ROWS]
            four = jnp.concatenate([whole[0:4, :ROWS], whole[0:4, ROWS:]], axis=0)
            for y in range(NYL):
                stat_send[y * NZ + (n + 4) % NZ, 1] = four

    large = 3 * NZ
    size = 4 * OWN

    def large_product(i, raw):
        product((2 + 4 * div(i, NZ), 4), rem(i, NZ), raw)

    def large_weights(i, raw):
        b = div(i, NZ)
        weights(1 + b, pl.multiple_of(2 * OWN + b * size, 2 * OWN), rem(i, NZ), raw, size)

    from_sibling(1)
    large_product(0, raw_a)

    def score_step(j, carry):
        @pl.when(j == 1)
        def _():
            far_across()

        @pl.when(j == 3)
        def _():
            from_sibling(2)

        @pl.when(j == 6)
        def _():
            sides_to_sibling(1)

        @pl.when(j == 7)
        def _():
            from_sibling(3)

        @pl.when(j == 10)
        def _():
            far_from_across()

        large_product(2 * j + 1, raw_b)
        large_weights(2 * j, raw_a)
        large_product(jnp.minimum(2 * j + 2, large - 1), raw_a)
        large_weights(2 * j + 1, raw_b)
        return carry

    lax.fori_loop(0, large // 2, score_step, 0)
    from_sibling(4)
    for first in (0, 4):
        small_scores(4, first)
        leave(first)
    for offset in offsets:
        stat_copy(*offset).start()
    stat_recv[0] = stat_send[me]
    turn()
    spread_wait()
    all_copies(stat_recv, 0).wait_recv()
    def totals(parts):
        t_max, t_sum, s_max, s_sum, cross = joined(parts)
        t_in, s_in = factor / t_sum, factor / s_sum
        result = jnp.concatenate([t_max, t_in, s_max, s_in, t_in, t_in, t_in, t_in], axis=0)
        return result, (t_max, t_sum, s_max, s_sum, cross)

    result, (t_max, t_sum, s_max, s_sum, cross) = totals([stat_recv[m, 0] for m in range(OWNERS)])
    res_recv[me] = result
    for offset in offsets:
        res_copy(*offset).start()
    far = []
    for y in range(NYL):
        parts = [stat_recv[m, 1, 4 * y:4 * y + 4] for m in range(OWNERS)]
        far.append(totals([jnp.concatenate([p, p], axis=0) for p in parts])[0])
    far = jnp.concatenate(far, axis=1)

    def group(away):
        return rem(z + NZ + away, NZ)

    def sequence(i):
        size = 4 - div(i + 1, 2)
        return group(size * (2 * rem(i, 2) - 1))

    def lanes(n):
        return pl.ds(pl.multiple_of(n * GROUP, GROUP), GROUP)

    def form(i, res=None):
        n = sequence(i)
        if res is None:
            res = jnp.concatenate([res_recv[n], res_recv[NZ + n]], axis=1)
        for b, (first, count) in enumerate(BATCH_SLOTS):
            st = stat[n, b]
            t_in = jnp.exp2(st[0:1] - res[0:1]) * res[1:2]
            s_in = jnp.exp2(st[2:3] - res[2:3]) * res[3:4]
            rows = pl.ds(first * OWN, count * OWN)
            grad = (sw[n, rows] * s_in - tw[n, rows] * t_in).astype(BF16)
            half = count * OWN // 2
            rows = pl.ds(first * OWN // 2, half)
            gt[0, rows, lanes(n)] = grad[:half]
            gt[1, rows, lanes(n)] = grad[half:]

    def pair_copy(i):
        return pltpu.make_async_remote_copy(
            src_ref=y_pair_send.at[i], dst_ref=y_pair_recv.at[i],
            send_sem=ring_sem.at[3], recv_sem=yp_recv_sem.at[i],
            device_id=y_mate, device_id_type=MESH,
        )

    def query_part(i):
        n = sequence(i)
        total = nn(spt[...], gt[:, :, lanes(n)].reshape(NCORE * PLACES * OWN, GROUP))
        gq[n, 0] = total[:, :ROWS]
        gq[n, 1] = total[:, ROWS:]
        y_pair_send[i] = gq[n, 1 - yl, ZF:].astype(BF16)

    ORDER = (4, 3, -3, 2, -2, 1, -1, 0)

    rings = (z_send.at[0], z_recv.at[0]), (z_send.at[1], z_recv.at[1]), (y_send, y_recv)

    def part(chain, away):
        n = group(away)
        if chain < 2:
            return gq[n, chain, :ZF]
        return gq[n, yl, ZF:] + y_pair_recv[ORDER.index(away)].astype(F32)

    def pair_arrived(away):
        pair_copy(ORDER.index(away)).wait_recv()

    def ring_message(chain, way, step, rows):
        sends, recvs = rings[chain]
        return message(
            lambda: (sends.at[4 * way + step, rows], recvs.at[4 * way + step, rows]), ("ring", chain, way, step),
            down if way else up, ring_sem.at[chain],
        )

    def rows_of(chain, way, step):
        if chain == 2 and step == 0:
            return pl.ds(way * (YF // 2), YF // 2)
        return pl.ds(0, ZF)

    def come(chain, way, step):
        rows = rows_of(chain, way, step)
        ring_message(chain, way, step, rows).wait_recv()
        return rings[chain][1][4 * way + step, rows].astype(F32)

    def ring_start(chain, way):
        rows = rows_of(chain, way, 0)
        rings[chain][0][4 * way, rows] = part(chain, 4)[rows.start:rows.start + rows.size].astype(BF16)
        ring_message(chain, way, 0, rows).start()

    def ring_step(chain, way, step):
        total = part(chain, 4 - step if way == 0 else step - 4)
        to = rings[chain][0]
        if step == 1 and chain == 2:
            h = YF // 2
            halves = [total[:h], total[h:]]
            halves[way] = halves[way] + come(chain, way, 0)
            to[4 * way + step, :h] = halves[0].astype(BF16)
            to[4 * way + step, h:] = halves[1].astype(BF16)
        else:
            if step > 1 or chain == way:
                total = total + come(chain, way, step - 1)
            to[4 * way + step] = total.astype(BF16)
        ring_message(chain, way, step, pl.ds(0, ZF)).start()

    def ring_steps(chains, step):
        for chain in chains:
            for way in (0, 1):
                ring_step(chain, way, step)

    def ring_total(chain):
        return part(chain, 0) + come(chain, 0, 3) + come(chain, 1, 3)

    def passage_part(core, to):
        to[...] = jnp.zeros_like(to)

        def body(n, carry):
            term = nn(gt[core, :, lanes(n)], sq[n].reshape(GROUP, DS))
            to[...] = to[...] + term.reshape(PLACES, OWN, DS)
            return carry

        lax.fori_loop(0, NZ, body, 0)

    def gp_of(h, where):
        return gp[place(h, where)]

    def gp_first():
        received(gps_recv, "gp sibling")
        gp[...] = gp[...] + gps_recv[...].astype(F32)
        for h in range(NYH):
            gp1_send[h] = gp_of(h, FAR).astype(BF16)
        send(lambda: (gp1_send.at[0], gp1_recv.at[0]), ("gp", RIGHT, 1), right)
        send(lambda: (gp1_send.at[1], gp1_recv.at[1]), ("gp", LEFT, 1), left)

    def gp_second():
        received(gp1_recv.at[0], ("gp", RIGHT, 1))
        gp2_send[0, 0] = (gp_of(0, RIGHT) + gp1_recv[0].astype(F32)).astype(BF16)
        gp2_send[0, 1] = gp_of(1, RIGHT).astype(BF16)
        send(lambda: (gp2_send.at[0], gp2_recv.at[0]), ("gp", RIGHT, 2), right)
        received(gp1_recv.at[1], ("gp", LEFT, 1))
        gp2_send[1, 0] = gp_of(0, LEFT).astype(BF16)
        gp2_send[1, 1] = (gp_of(1, LEFT) + gp1_recv[1].astype(F32)).astype(BF16)
        send(lambda: (gp2_send.at[1], gp2_recv.at[1]), ("gp", LEFT, 2), left)

    def gp_third():
        received(gp2_recv.at[0], ("gp", RIGHT, 2))
        received(gp2_recv.at[1], ("gp", LEFT, 2))
        gp3_send[...] = x_total(1).astype(BF16)
        send(lambda: (gp3_send, gp3_recv), "gp across", across)

    def x_total(h):
        return gp_of(h, SELF) + gp2_recv[0, h].astype(F32) + gp2_recv[1, h].astype(F32)

    form(0, far)
    query_part(0)
    ring_start(0, 0)
    ring_start(1, 1)
    pair_copy(0).start()
    div_out[...] = cross * LN2 / t_sum - (t_max * LN2 + jnp.log(t_sum)) + (s_max * LN2 + jnp.log(s_sum))
    all_copies(stat_send, 0).wait_send()
    all_copies(res_recv, 2).wait_recv()
    form(1)

    def gradient_step(i, carry):
        query_part(i)
        form(i + 1)

        @pl.when(i == 1)
        def _():
            ring_step(1, 0, 1)

        @pl.when(i == 2)
        def _():
            ring_step(0, 1, 1)
            ring_step(0, 0, 1)
            ring_step(1, 1, 1)

        pair_copy(i).start()

        @pl.when(i == 3)
        def _():
            pair_arrived(4)
            ring_start(2, 0)
            ring_start(2, 1)

        @pl.when(i == 6)
        def _():
            pair_arrived(3)
            pair_arrived(-3)
            ring_steps((2,), 1)

        return carry

    lax.fori_loop(1, NZ - 1, gradient_step, 0)
    query_part(NZ - 1)
    pair_copy(NZ - 1).start()
    ring_steps((0, 1), 2)
    passage_part(1, gp)
    gps_send[...] = gp[...].astype(BF16)
    send(lambda: (gps_send, gps_recv), "gp sibling", sibling)
    pair_arrived(2)
    pair_arrived(-2)
    ring_steps((2,), 2)
    passage_part(0, gp)
    gp_first()
    ring_steps((0, 1), 3)
    pair_arrived(1)
    pair_arrived(-1)
    ring_steps((2,), 3)
    gp_second()
    all_copies(res_recv, 2).wait_send()
    for y in range(NYL):
        gq[z, y, :ZF] = ring_total(y)
    z_pair_send[...] = gq[z, 1 - yl, :ZF].astype(BF16)
    send(lambda: (z_pair_send, z_pair_recv), "z pair", y_mate)
    gp_third()
    pair_arrived(0)
    gq_out[:, ZF:] = ring_total(2).T
    for i, ref in enumerate((z_send.at[0, pl.ds(0, 7)], z_send.at[1, pl.ds(0, 7)], y_send.at[pl.ds(0, 7)], y_pair_send)):
        message(lambda: (ref, ref), "ring", sibling, ring_sem.at[i]).wait_send()
    flush()
    received(z_pair_recv, "z pair")
    gq_out[:, :ZF] = (gq[z, yl, :ZF] + z_pair_recv[...].astype(F32)).T
    received(gp3_recv, "gp across")
    gp_out[...] = x_total(0) + gp3_recv[...].astype(F32)


def deliver(gq_in, gp_in, div_in, gq_out, gp_out, div_out, gq, gp, div, in_sem, out_sem):
    parts = ((gq_in, gq, gq_out), (gp_in, gp, gp_out), (div_in, div, div_out))
    ins = [pltpu.make_async_copy(src, mid, in_sem.at[i]) for i, (src, mid, _) in enumerate(parts)]
    outs = [pltpu.make_async_copy(mid, dst, out_sem.at[i]) for i, (_, mid, dst) in enumerate(parts)]
    for copy in ins:
        copy.start()
    for arrive, leave in zip(ins, outs):
        arrive.wait()
        leave.start()
    for copy in outs:
        copy.wait()


def local(teacher_query, student_query, teacher_passages, student_passages):
    blocks = NYL, NZ, NCORE, ROWS
    hbm = pl.BlockSpec(memory_space=pl.ANY)
    vmem = pl.BlockSpec(memory_space=pltpu.VMEM)
    outs = (
        jax.ShapeDtypeStruct((ROWS, DS), F32),
        jax.ShapeDtypeStruct((OWN, DS), F32),
        jax.ShapeDtypeStruct((1, ROWS), F32),
    )
    results = pl.pallas_call(
        kernel,
        out_shape=outs,
        in_specs=[hbm] * 4,
        out_specs=(vmem,) * 3,
        scratch_shapes=[
            pltpu.VMEM((NZ, NYL, ROWS, DT), BF16),
            pltpu.VMEM((NZ, NYL, ROWS, DS), BF16),
            pltpu.VMEM((SLOTS, OWN, DT + DS), BF16),
            pltpu.VMEM((DS, SLOTS * OWN), BF16),
            pltpu.VMEM((NZ, SLOTS * OWN, GROUP), F32),
            pltpu.VMEM((NZ, SLOTS * OWN, GROUP), F32),
            pltpu.VMEM((2, BATCH, GROUP), F32),
            pltpu.VMEM((2, BATCH, GROUP), F32),
            pltpu.VMEM((NCORE, PLACES * OWN, NZ * GROUP), BF16),
            pltpu.VMEM((NZ, BATCHES, 8, GROUP), F32),
            pltpu.VMEM((NZ, NYL, DS, ROWS), F32),
            pltpu.VMEM((OWNERS, 2, 8, ROWS), F32),
            pltpu.VMEM((OWNERS, 2, 8, ROWS), F32),
            pltpu.VMEM((OWNERS, 8, ROWS), F32),
            pltpu.VMEM((2, 8, ZF, ROWS), BF16),
            pltpu.VMEM((2, 8, ZF, ROWS), BF16),
            pltpu.VMEM((ZF, ROWS), BF16),
            pltpu.VMEM((ZF, ROWS), BF16),
            pltpu.VMEM((NZ, YF, ROWS), BF16),
            pltpu.VMEM((NZ, YF, ROWS), BF16),
            pltpu.VMEM((8, YF, ROWS), BF16),
            pltpu.VMEM((8, YF, ROWS), BF16),
            pltpu.VMEM((PLACES, OWN, DS), F32),
            pltpu.VMEM((PLACES, OWN, DS), BF16),
            pltpu.VMEM((PLACES, OWN, DS), BF16),
            pltpu.VMEM((NYH, OWN, DS), BF16),
            pltpu.VMEM((NYH, OWN, DS), BF16),
            pltpu.VMEM((2, NYH, OWN, DS), BF16),
            pltpu.VMEM((2, NYH, OWN, DS), BF16),
            pltpu.VMEM((OWN, DS), BF16),
            pltpu.VMEM((OWN, DS), BF16),
            pltpu.SemaphoreType.DMA((6,)),
            pltpu.SemaphoreType.REGULAR((4,)),
            pltpu.SemaphoreType.DMA,
            pltpu.SemaphoreType.DMA((4,)),
            pltpu.SemaphoreType.DMA((MESSAGES,)),
            pltpu.SemaphoreType.DMA((MESSAGES,)),
            pltpu.SemaphoreType.DMA((NZ,)),
            pltpu.SemaphoreType.DMA((4,)),
        ],
        compiler_params=pltpu.CompilerParams(
            collective_id=0, has_side_effects=True, vmem_limit_bytes=VMEM_BYTES
        ),
    )(
        teacher_query.reshape(*blocks, DT),
        student_query.reshape(*blocks, DS),
        teacher_passages,
        student_passages,
    )
    grad_query, grad_passage, divergence = pl.pallas_call(
        deliver,
        out_shape=outs,
        in_specs=[hbm] * 3,
        out_specs=(hbm,) * 3,
        scratch_shapes=[
            *(pltpu.VMEM(out.shape, out.dtype) for out in outs),
            pltpu.SemaphoreType.DMA((3,)),
            pltpu.SemaphoreType.DMA((3,)),
        ],
        compiler_params=pltpu.CompilerParams(vmem_limit_bytes=VMEM_BYTES),
    )(*results)
    return divergence.reshape(ROWS), grad_query, grad_passage


def solution(mesh):
    return jax.shard_map(
        local,
        mesh=mesh,
        in_specs=(
            P("query", None),
            P("query", None),
            P(("query", "corpus"), None),
            P(("query", "corpus"), None),
        ),
        out_specs=(
            P(("query", "corpus")),
            P(("query", "corpus"), None),
            P(("query", "corpus"), None),
        ),
        check_vma=False,
    )
```

```python
import functools
import math

import jax
import jax.numpy as jnp
from jax import lax
from jax.experimental import pallas as pl
from jax.experimental.pallas import tpu as pltpu
from jax.sharding import PartitionSpec as P

NX, NYH, NYL, NZ, NCORE = 4, 2, 2, 8, 2
OWN = 64
ROWS = 128
DT, DS = 1024, 384
BATCH = 256
GROUP = NYL * ROWS
OWNERS = NYL * NZ
HALF = OWN // 2
ZF = 192
YF = DS - ZF
LOG2E = math.log2(math.e)
LN2 = math.log(2.0)
F32, BF16 = jnp.float32, jnp.bfloat16
MESH = pl.DeviceIdType.MESH

SELF, LEFT, RIGHT, FAR = 0, 1, 2, 3


BATCH_SLOTS = (0, 2), (2, 4), (6, 4), (10, 4), (14, 2)
BATCHES = len(BATCH_SLOTS)
SLOTS = 16
PLACES = 8


def place(h, where):
    if h == 0:
        return {SELF: 0, LEFT: 1, RIGHT: 2, FAR: 4}[where]
    return {SELF: 3, LEFT: 5, RIGHT: 6, FAR: 7}[where]


def slot_of(h, where, core):
    p = place(h, where)
    for first, count in BATCH_SLOTS:
        if p < count // 2:
            return first + p + core * (count // 2)
        p -= count // 2


def div(a, b):
    return lax.div(a, jnp.int32(b))


def rem(a, b):
    return lax.rem(a, jnp.int32(b))


def nt(a, b):
    return lax.dot_general(a, b, (((1,), (1,)), ((), ())), preferred_element_type=F32)


def nn(a, b):
    return lax.dot_general(a, b, (((1,), (0,)), ((), ())), preferred_element_type=F32)


class Messages:
    def __init__(self):
        self.numbers = {}

    def __call__(self, name):
        return self.numbers.setdefault(name, len(self.numbers))


MESSAGES = 80
VMEM_BYTES = 60 * 1024 * 1024


def kernel(
    tq_hbm, sq_hbm, tp_hbm, sp_hbm,
    gq_out, gp_out, div_out,
    tq, sq, pbuf, spt, tw, sw, raw_a, raw_b, gt, stat, gq,
    stat_send, stat_recv, res_recv,
    z_send, z_recv_r, z_recv_l, z_pair_send, z_pair_recv,
    y_pair_send, y_pair_recv, y_send, y_recv_r, y_recv_l,
    gp, gps_send, gps_recv, gp1_send, gp1_recv, gp2_send, gp2_recv, gp3_send, gp3_recv,
    load_sem, known_sem, gather_sem, ring_sem, send_sem, recv_sem, yp_recv_sem, st_sem,
):
    t_scale = DT ** (-0.5) * LOG2E
    s_scale = DS ** (-0.5) * LOG2E
    factor = DS ** (-0.5)
    q = lax.axis_index("query")
    c = lax.axis_index("corpus")
    x, yh = div(q, NYH), rem(q, NYH)
    yl, z, k = div(c, NZ * NCORE), rem(div(c, NCORE), NZ), rem(c, NCORE)
    me = yl * NZ + z

    def at(x_, yh_, yl_, z_, k_):
        return (x_ * NYH + yh_, (yl_ * NZ + z_) * NCORE + k_)

    right, left = at(rem(x + 1, NX), yh, yl, z, k), at(rem(x + NX - 1, NX), yh, yl, z, k)
    across = at(x, 1 - yh, 1 - yl, z, k)
    sibling = at(x, yh, yl, z, 1 - k)
    up, down = at(x, yh, yl, rem(z + 1, NZ), k), at(x, yh, yl, rem(z + NZ - 1, NZ), k)
    y_mate = at(x, yh, 1 - yl, z, k)

    offsets = [(dy, dz) for dy in range(NYL) for dz in range(NZ) if (dy, dz) != (0, 0)]
    y_of = [yl, 1 - yl]
    z_of = [rem(z + dz, NZ) for dz in range(NZ)]

    def offset_device(dy, dz):
        return at(x, yh, y_of[dy], z_of[dz], k)

    def slot(h, where, core, half=None):
        i = slot_of(h, where, core)
        if half is None:
            return pbuf.at[i]
        return pbuf.at[i, pl.ds(half * HALF, HALF)]

    def both(b, core):
        first, count = BATCH_SLOTS[b]
        return pbuf.at[pl.ds(first + core * (count // 2), count // 2)]

    loads = [
        pltpu.make_async_copy(tp_hbm, pbuf.at[0, :, pl.ds(0, DT)], load_sem.at[0]),
        pltpu.make_async_copy(sp_hbm, pbuf.at[0, :, pl.ds(DT, DS)], load_sem.at[1]),
    ]
    for y in range(NYL):
        loads.append(pltpu.make_async_copy(tq_hbm.at[y, :, k], tq.at[:, y], load_sem.at[2 + y]))
        loads.append(pltpu.make_async_copy(sq_hbm.at[y, :, k], sq.at[:, y], load_sem.at[4 + y]))
    for load in loads:
        load.start()

    barrier = pltpu.get_barrier_semaphore()
    for device in (right, left, across, sibling, up, down, y_mate):
        pl.semaphore_signal(barrier, inc=1, device_id=device, device_id_type=MESH)
    pl.semaphore_wait(barrier, 7)
    loads[0].wait()
    loads[1].wait()

    number = Messages()
    sent = []

    def message(refs, name, device, out=None):
        i = number(name)
        src, dst = refs()
        return pltpu.make_async_remote_copy(
            src_ref=src, dst_ref=dst, send_sem=send_sem.at[i] if out is None else out, recv_sem=recv_sem.at[i],
            device_id=device, device_id_type=MESH,
        )

    def send(refs, name, device):
        message(refs, name, device).start()
        sent.append((refs, name, device))

    def flush():
        for args in sent:
            message(*args).wait_send()
        sent.clear()

    def received(ref, name):
        message(lambda: (ref, ref), name, sibling).wait_recv()

    def spread(refs, name, device):
        message(refs, name, device, gather_sem).start()

    def spread_wait():
        everything = pbuf.at[pl.ds(0, SLOTS - 1)]
        message(lambda: (everything, everything), "gather", sibling, gather_sem).wait_send()

    def half_to(where, half, device):
        spread(lambda: (slot(0, SELF, 0, half), slot(0, where, 0, half)), ("p", where, half), device)

    def sides_to_sibling(h):
        if h == 0:
            received(slot(0, LEFT, 0, 1), ("p", LEFT, 1))
            received(slot(0, RIGHT, 0, 0), ("p", RIGHT, 0))
        else:
            received(slot(1, LEFT, 0), ("p1", LEFT))
            received(slot(1, RIGHT, 0), ("p1", RIGHT))
        to_sibling(3 if h else 1)

    def to_sibling(b):
        spread(lambda: (both(b, 0), both(b, 1)), ("sib", b), sibling)

    def from_sibling(b):
        received(both(b, 1), ("sib", b))

    def far_on():
        received(slot(0, LEFT, 0, 0), ("p", LEFT, 0))
        spread(lambda: (slot(0, LEFT, 0, 0), slot(0, FAR, 0, 0)), ("far",), right)
        received(slot(0, RIGHT, 0, 1), ("p", RIGHT, 1))
        spread(lambda: (slot(0, RIGHT, 0, 1), slot(0, FAR, 0, 1)), ("far",), left)

    def across_on(half):
        received(slot(1, SELF, 0, half), ("across", half))
        spread(lambda: (slot(1, SELF, 0, half), slot(1, LEFT, 0, half)), ("p1", LEFT), right)
        spread(lambda: (slot(1, SELF, 0, half), slot(1, RIGHT, 0, half)), ("p1", RIGHT), left)

    def far_across():
        received(slot(0, FAR, 0), ("far",))
        spread(lambda: (slot(0, FAR, 0), slot(1, FAR, 0)), ("far across",), across)
        to_sibling(2)

    def far_from_across():
        received(slot(1, FAR, 0), ("far across",))
        to_sibling(4)

    half_to(LEFT, 0, right)
    half_to(RIGHT, 1, left)
    spread(lambda: (slot(0, SELF, 0, 0), slot(1, SELF, 0, 0)), ("across", 0), across)
    half_to(LEFT, 1, right)
    half_to(RIGHT, 0, left)
    spread(lambda: (slot(0, SELF, 0, 1), slot(1, SELF, 0, 1)), ("across", 1), across)
    to_sibling(0)

    def product(slots, n, raw):
        first, count = slots
        batch = pbuf[pl.ds(first, count)].reshape(count * OWN, DT + DS)
        raw[0] = nt(batch[:, :DT], tq[n].reshape(GROUP, DT))
        raw[1] = nt(batch[:, DT:], sq[n].reshape(GROUP, DS))

    def weights(b, row, n, raw, size):
        t = raw[0] * t_scale
        s = raw[1] * s_scale
        t_max = jnp.max(t, axis=0, keepdims=True)
        s_max = jnp.max(s, axis=0, keepdims=True)
        t_weight = jnp.exp2(t - t_max)
        s_weight = jnp.exp2(s - s_max)
        tw[n, pl.ds(row, size)] = t_weight
        sw[n, pl.ds(row, size)] = s_weight
        t_sum = jnp.sum(t_weight, axis=0, keepdims=True)
        s_sum = jnp.sum(s_weight, axis=0, keepdims=True)
        cross = jnp.sum(t_weight * (t - s), axis=0, keepdims=True)
        stat[n, b] = jnp.concatenate([t_max, t_sum, s_max, s_sum, cross, cross, cross, cross], axis=0)

    def small_scores(b, first):
        slots = BATCH_SLOTS[b]
        row, size = slots[0] * OWN, slots[1] * OWN
        half_a, half_b = raw_a.at[:, pl.ds(0, size)], raw_b.at[:, pl.ds(0, size)]

        def body(i, carry):
            n = first + 2 * i
            product(slots, n, half_a)
            product(slots, n + 1, half_b)
            weights(b, row, n, half_a, size)
            weights(b, row, n + 1, half_b, size)
            return carry

        lax.fori_loop(0, 2, body, 0)

    def turn():
        for core in range(NCORE):
            rows = [
                pbuf[first + core * (count // 2):first + (core + 1) * (count // 2)].reshape(-1, DT + DS)[:, DT:]
                for first, count in BATCH_SLOTS
            ]
            size = PLACES * OWN
            spt[:, core * size:(core + 1) * size] = jnp.concatenate(rows, axis=0).T

    def know(i):
        for device in (up, down, y_mate):
            pl.semaphore_signal(known_sem.at[i], inc=1, device_id=device, device_id_type=MESH)
        pl.semaphore_wait(known_sem.at[i], 3)

    know(0)
    for load in loads[2:]:
        load.wait()
    from_sibling(0)
    small_scores(0, 0)
    far_on()
    across_on(0)
    know(1)
    small_scores(0, 4)
    across_on(1)
    sides_to_sibling(0)
    know(2)
    know(3)

    def joined(parts):
        t_max = functools.reduce(jnp.maximum, [p[0:1] for p in parts])
        s_max = functools.reduce(jnp.maximum, [p[2:3] for p in parts])
        t_in = [jnp.exp2(p[0:1] - t_max) for p in parts]
        s_in = [jnp.exp2(p[2:3] - s_max) for p in parts]
        t_sum = functools.reduce(jnp.add, [p[1:2] * w for p, w in zip(parts, t_in)])
        s_sum = functools.reduce(jnp.add, [p[3:4] * w for p, w in zip(parts, s_in)])
        cross = functools.reduce(jnp.add, [p[4:5] * w for p, w in zip(parts, t_in)])
        return t_max, t_sum, s_max, s_sum, cross

    def stat_copy(dy, dz):
        return pltpu.make_async_remote_copy(
            src_ref=stat_send.at[y_of[dy] * NZ + z_of[dz]], dst_ref=stat_recv.at[dy * NZ + (NZ - dz) % NZ],
            send_sem=st_sem.at[0], recv_sem=st_sem.at[1],
            device_id=offset_device(dy, dz), device_id_type=MESH,
        )

    def res_copy(dy, dz):
        return pltpu.make_async_remote_copy(
            src_ref=res_recv.at[me], dst_ref=res_recv.at[me],
            send_sem=st_sem.at[2], recv_sem=st_sem.at[3],
            device_id=offset_device(dy, dz), device_id_type=MESH,
        )

    def all_copies(ref, first):
        others = ref.at[pl.ds(0, OWNERS - 1)]
        return pltpu.make_async_remote_copy(
            src_ref=others, dst_ref=others, send_sem=st_sem.at[first], recv_sem=st_sem.at[first + 1],
            device_id=sibling, device_id_type=MESH,
        )

    def leave(first):
        for n in range(first, first + 4):
            t_max, t_sum, s_max, s_sum, cross = joined([stat[n, b] for b in range(BATCHES)])
            whole = jnp.concatenate([t_max, t_sum, s_max, s_sum, cross, cross, cross, cross], axis=0)
            for y in range(NYL):
                stat_send[y * NZ + n, 0] = whole[:, y * ROWS:(y + 1) * ROWS]
            four = jnp.concatenate([whole[0:4, :ROWS], whole[0:4, ROWS:]], axis=0)
            for y in range(NYL):
                stat_send[y * NZ + (n + 4) % NZ, 1] = four

    large = 3 * NZ
    size = 4 * OWN

    def large_product(i, raw):
        product((2 + 4 * div(i, NZ), 4), rem(i, NZ), raw)

    def large_weights(i, raw):
        b = div(i, NZ)
        weights(1 + b, pl.multiple_of(2 * OWN + b * size, 2 * OWN), rem(i, NZ), raw, size)

    from_sibling(1)
    large_product(0, raw_a)

    def score_step(j, carry):
        @pl.when(j == 1)
        def _():
            far_across()

        @pl.when(j == 3)
        def _():
            from_sibling(2)

        @pl.when(j == 6)
        def _():
            sides_to_sibling(1)

        @pl.when(j == 7)
        def _():
            from_sibling(3)

        @pl.when(j == 10)
        def _():
            far_from_across()

        large_product(2 * j + 1, raw_b)
        large_weights(2 * j, raw_a)
        large_product(jnp.minimum(2 * j + 2, large - 1), raw_a)
        large_weights(2 * j + 1, raw_b)
        return carry

    lax.fori_loop(0, large // 2, score_step, 0)
    from_sibling(4)
    for first in (0, 4):
        small_scores(4, first)
        leave(first)
    for offset in offsets:
        stat_copy(*offset).start()
    stat_recv[0] = stat_send[me]
    turn()
    spread_wait()
    all_copies(stat_recv, 0).wait_recv()
    def totals(parts):
        t_max, t_sum, s_max, s_sum, cross = joined(parts)
        t_in, s_in = factor / t_sum, factor / s_sum
        result = jnp.concatenate([t_max, t_in, s_max, s_in, t_in, t_in, t_in, t_in], axis=0)
        return result, (t_max, t_sum, s_max, s_sum, cross)

    result, (t_max, t_sum, s_max, s_sum, cross) = totals([stat_recv[m, 0] for m in range(OWNERS)])
    res_recv[me] = result
    for offset in offsets:
        res_copy(*offset).start()
    far = []
    for y in range(NYL):
        parts = [stat_recv[m, 1, 4 * y:4 * y + 4] for m in range(OWNERS)]
        far.append(totals([jnp.concatenate([p, p], axis=0) for p in parts])[0])
    far = jnp.concatenate(far, axis=1)

    def group(away):
        return rem(z + NZ + away, NZ)

    def sequence(i):
        size = 4 - div(i + 1, 2)
        return group(size * (2 * rem(i, 2) - 1))

    def lanes(n):
        return pl.ds(pl.multiple_of(n * GROUP, GROUP), GROUP)

    def form(i, res=None):
        n = sequence(i)
        if res is None:
            res = jnp.concatenate([res_recv[n], res_recv[NZ + n]], axis=1)
        for b, (first, count) in enumerate(BATCH_SLOTS):
            st = stat[n, b]
            t_in = jnp.exp2(st[0:1] - res[0:1]) * res[1:2]
            s_in = jnp.exp2(st[2:3] - res[2:3]) * res[3:4]
            rows = pl.ds(first * OWN, count * OWN)
            grad = (sw[n, rows] * s_in - tw[n, rows] * t_in).astype(BF16)
            half = count * OWN // 2
            rows = pl.ds(first * OWN // 2, half)
            gt[0, rows, lanes(n)] = grad[:half]
            gt[1, rows, lanes(n)] = grad[half:]

    def pair_copy(i):
        return pltpu.make_async_remote_copy(
            src_ref=y_pair_send.at[i], dst_ref=y_pair_recv.at[i],
            send_sem=ring_sem.at[2], recv_sem=yp_recv_sem.at[i],
            device_id=y_mate, device_id_type=MESH,
        )

    def query_part(i):
        n = sequence(i)
        total = nn(spt[...], gt[:, :, lanes(n)].reshape(NCORE * PLACES * OWN, GROUP))
        gq[n, 0] = total[:, :ROWS]
        gq[n, 1] = total[:, ROWS:]
        y_pair_send[i] = gq[n, 1 - yl, ZF:].astype(BF16)

    def z_part(away):
        return gq[group(away), :, :ZF]

    def y_part(away):
        i = (4, 3, -3, 2, -2, 1, -1, 0).index(away)
        pair_copy(i).wait_recv()
        return gq[group(away), yl, ZF:] + y_pair_recv[i].astype(F32)

    ZH, YH = ZF // 2, YF // 2

    def z_start():
        far = z_part(4).astype(BF16)
        z_send[0] = far
        message(lambda: (z_send.at[0, :, pl.ds(0, ZH)], z_recv_r.at[0, :, pl.ds(0, ZH)]), ("zr", 0), up, ring_sem.at[0]).start()
        message(lambda: (z_send.at[0, :, pl.ds(ZH, ZH)], z_recv_l.at[0, :, pl.ds(ZH, ZH)]), ("zl", 0), down, ring_sem.at[0]).start()

    def y_start():
        y_send[0] = y_part(4).astype(BF16)
        message(lambda: (y_send.at[0, pl.ds(0, YH)], y_recv_r.at[0, pl.ds(0, YH)]), ("yr", 0), up, ring_sem.at[1]).start()
        message(lambda: (y_send.at[0, pl.ds(YH, YH)], y_recv_l.at[0, pl.ds(YH, YH)]), ("yl", 0), down, ring_sem.at[1]).start()

    def z_step(step):
        if step == 1:
            mine = z_part(3)
            received(z_recv_r.at[0, :, pl.ds(0, ZH)], ("zr", 0))
            z_send[1, :, :ZH] = (mine[:, :ZH] + z_recv_r[0, :, :ZH].astype(F32)).astype(BF16)
            z_send[1, :, ZH:] = mine[:, ZH:].astype(BF16)
        else:
            received(z_recv_r.at[step - 1], ("zr", step - 1))
            z_send[step] = (z_part(4 - step) + z_recv_r[step - 1].astype(F32)).astype(BF16)
        message(lambda step=step: (z_send.at[step], z_recv_r.at[step]), ("zr", step), up, ring_sem.at[0]).start()
        if step == 1:
            mine = z_part(-3)
            received(z_recv_l.at[0, :, pl.ds(ZH, ZH)], ("zl", 0))
            z_send[5, :, :ZH] = mine[:, :ZH].astype(BF16)
            z_send[5, :, ZH:] = (mine[:, ZH:] + z_recv_l[0, :, ZH:].astype(F32)).astype(BF16)
        else:
            received(z_recv_l.at[step - 1], ("zl", step - 1))
            z_send[4 + step] = (z_part(step - 4) + z_recv_l[step - 1].astype(F32)).astype(BF16)
        message(lambda step=step: (z_send.at[4 + step], z_recv_l.at[step]), ("zl", step), down, ring_sem.at[0]).start()

    def y_step(step):
        mine = y_part(4 - step)
        if step == 1:
            received(y_recv_r.at[0, pl.ds(0, YH)], ("yr", 0))
            y_send[1, :YH] = (mine[:YH] + y_recv_r[0, :YH].astype(F32)).astype(BF16)
            y_send[1, YH:] = mine[YH:].astype(BF16)
        else:
            received(y_recv_r.at[step - 1], ("yr", step - 1))
            y_send[step] = (mine + y_recv_r[step - 1].astype(F32)).astype(BF16)
        message(lambda step=step: (y_send.at[step], y_recv_r.at[step]), ("yr", step), up, ring_sem.at[1]).start()
        mine = y_part(step - 4)
        if step == 1:
            received(y_recv_l.at[0, pl.ds(YH, YH)], ("yl", 0))
            y_send[5, :YH] = mine[:YH].astype(BF16)
            y_send[5, YH:] = (mine[YH:] + y_recv_l[0, YH:].astype(F32)).astype(BF16)
        else:
            received(y_recv_l.at[step - 1], ("yl", step - 1))
            y_send[4 + step] = (mine + y_recv_l[step - 1].astype(F32)).astype(BF16)
        message(lambda step=step: (y_send.at[4 + step], y_recv_l.at[step]), ("yl", step), down, ring_sem.at[1]).start()

    def passage_add(core, i):
        n = sequence(i)
        term = nn(gt[core, :, lanes(n)], sq[n].reshape(GROUP, DS))
        gp[...] = gp[...] + term.reshape(PLACES, OWN, DS)

    def passage_part(core, first, count):
        def body(i, carry):
            passage_add(core, i)
            return carry

        lax.fori_loop(first, first + count, body, 0)

    def gp_of(h, where):
        return gp[place(h, where)]

    def gp_first():
        received(gps_recv, "gp sibling")
        gp[...] = gp[...] + gps_recv[...].astype(F32)
        for h in range(NYH):
            gp1_send[h] = gp_of(h, FAR).astype(BF16)
        send(lambda: (gp1_send.at[0], gp1_recv.at[0]), ("gp", RIGHT, 1), right)
        send(lambda: (gp1_send.at[1], gp1_recv.at[1]), ("gp", LEFT, 1), left)

    def gp_second():
        received(gp1_recv.at[0], ("gp", RIGHT, 1))
        gp2_send[0, 0] = (gp_of(0, RIGHT) + gp1_recv[0].astype(F32)).astype(BF16)
        gp2_send[0, 1] = gp_of(1, RIGHT).astype(BF16)
        send(lambda: (gp2_send.at[0], gp2_recv.at[0]), ("gp", RIGHT, 2), right)
        received(gp1_recv.at[1], ("gp", LEFT, 1))
        gp2_send[1, 0] = gp_of(0, LEFT).astype(BF16)
        gp2_send[1, 1] = (gp_of(1, LEFT) + gp1_recv[1].astype(F32)).astype(BF16)
        send(lambda: (gp2_send.at[1], gp2_recv.at[1]), ("gp", LEFT, 2), left)

    def gp_third():
        received(gp2_recv.at[0], ("gp", RIGHT, 2))
        received(gp2_recv.at[1], ("gp", LEFT, 2))
        gp3_send[...] = x_total(1).astype(BF16)
        send(lambda: (gp3_send, gp3_recv), "gp across", across)

    def x_total(h):
        return gp_of(h, SELF) + gp2_recv[0, h].astype(F32) + gp2_recv[1, h].astype(F32)

    def z_last():
        received(z_recv_r.at[3], ("zr", 3))
        received(z_recv_l.at[3], ("zl", 3))
        for y in range(NYL):
            gq[z, y, :ZF] = gq[z, y, :ZF] + z_recv_r[3, y].astype(F32) + z_recv_l[3, y].astype(F32)
        z_pair_send[...] = gq[z, 1 - yl, :ZF].astype(BF16)
        send(lambda: (z_pair_send, z_pair_recv), "z pair", y_mate)

    form(0, far)
    query_part(0)
    pair_copy(0).start()
    z_start()
    div_out[...] = cross * LN2 / t_sum - (t_max * LN2 + jnp.log(t_sum)) + (s_max * LN2 + jnp.log(s_sum))
    all_copies(stat_send, 0).wait_send()
    all_copies(res_recv, 2).wait_recv()
    form(1)

    def near_step(i, carry):
        query_part(i)
        form(i + 1)
        pair_copy(i).start()
        return carry

    lax.fori_loop(1, 3, near_step, 0)
    z_step(1)
    y_start()
    gp[...] = jnp.zeros_like(gp)

    def form_step(i, carry):
        passage_add(1, i - 3)
        form(i + 1)
        return carry

    lax.fori_loop(3, NZ - 1, form_step, 0)
    passage_part(1, 4, 4)
    gps_send[...] = gp[...].astype(BF16)
    send(lambda: (gps_send, gps_recv), "gp sibling", sibling)
    gp[...] = jnp.zeros_like(gp)

    def query_step(i, carry):
        query_part(i)
        pair_copy(i).start()
        passage_add(0, i - 3)
        return carry

    lax.fori_loop(3, 5, query_step, 0)
    z_step(2)
    lax.fori_loop(5, NZ, query_step, 0)
    passage_part(0, 5, 3)
    gp_first()
    y_step(1)
    z_step(3)
    gp_second()
    y_step(2)
    all_copies(res_recv, 2).wait_send()
    gp_third()
    z_last()
    y_step(3)
    for i, ref in enumerate((z_send.at[pl.ds(0, 7)], y_send.at[pl.ds(0, 7)], y_pair_send)):
        message(lambda: (ref, ref), "ring", sibling, ring_sem.at[i]).wait_send()
    flush()

    mine = y_part(0)
    received(y_recv_r.at[3], ("yr", 3))
    received(y_recv_l.at[3], ("yl", 3))
    gq_out[:, ZF:] = (mine + y_recv_r[3].astype(F32) + y_recv_l[3].astype(F32)).T
    received(z_pair_recv, "z pair")
    gq_out[:, :ZF] = (gq[z, yl, :ZF] + z_pair_recv[...].astype(F32)).T
    received(gp3_recv, "gp across")
    gp_out[...] = x_total(0) + gp3_recv[...].astype(F32)


def deliver(gq_in, gp_in, div_in, gq_out, gp_out, div_out, gq, gp, div, in_sem, out_sem):
    parts = ((gq_in, gq, gq_out), (gp_in, gp, gp_out), (div_in, div, div_out))
    ins = [pltpu.make_async_copy(src, mid, in_sem.at[i]) for i, (src, mid, _) in enumerate(parts)]
    outs = [pltpu.make_async_copy(mid, dst, out_sem.at[i]) for i, (_, mid, dst) in enumerate(parts)]
    for copy in ins:
        copy.start()
    for arrive, leave in zip(ins, outs):
        arrive.wait()
        leave.start()
    for copy in outs:
        copy.wait()


def local(teacher_query, student_query, teacher_passages, student_passages):
    blocks = NYL, NZ, NCORE, ROWS
    hbm = pl.BlockSpec(memory_space=pl.ANY)
    vmem = pl.BlockSpec(memory_space=pltpu.VMEM)
    outs = (
        jax.ShapeDtypeStruct((ROWS, DS), F32),
        jax.ShapeDtypeStruct((OWN, DS), F32),
        jax.ShapeDtypeStruct((1, ROWS), F32),
    )
    results = pl.pallas_call(
        kernel,
        out_shape=outs,
        in_specs=[hbm] * 4,
        out_specs=(vmem,) * 3,
        scratch_shapes=[
            pltpu.VMEM((NZ, NYL, ROWS, DT), BF16),
            pltpu.VMEM((NZ, NYL, ROWS, DS), BF16),
            pltpu.VMEM((SLOTS, OWN, DT + DS), BF16),
            pltpu.VMEM((DS, SLOTS * OWN), BF16),
            pltpu.VMEM((NZ, SLOTS * OWN, GROUP), F32),
            pltpu.VMEM((NZ, SLOTS * OWN, GROUP), F32),
            pltpu.VMEM((2, BATCH, GROUP), F32),
            pltpu.VMEM((2, BATCH, GROUP), F32),
            pltpu.VMEM((NCORE, PLACES * OWN, NZ * GROUP), BF16),
            pltpu.VMEM((NZ, BATCHES, 8, GROUP), F32),
            pltpu.VMEM((NZ, NYL, DS, ROWS), F32),
            pltpu.VMEM((OWNERS, 2, 8, ROWS), F32),
            pltpu.VMEM((OWNERS, 2, 8, ROWS), F32),
            pltpu.VMEM((OWNERS, 8, ROWS), F32),
            pltpu.VMEM((8, NYL, ZF, ROWS), BF16),
            pltpu.VMEM((4, NYL, ZF, ROWS), BF16),
            pltpu.VMEM((4, NYL, ZF, ROWS), BF16),
            pltpu.VMEM((ZF, ROWS), BF16),
            pltpu.VMEM((ZF, ROWS), BF16),
            pltpu.VMEM((NZ, YF, ROWS), BF16),
            pltpu.VMEM((NZ, YF, ROWS), BF16),
            pltpu.VMEM((8, YF, ROWS), BF16),
            pltpu.VMEM((4, YF, ROWS), BF16),
            pltpu.VMEM((4, YF, ROWS), BF16),
            pltpu.VMEM((PLACES, OWN, DS), F32),
            pltpu.VMEM((PLACES, OWN, DS), BF16),
            pltpu.VMEM((PLACES, OWN, DS), BF16),
            pltpu.VMEM((NYH, OWN, DS), BF16),
            pltpu.VMEM((NYH, OWN, DS), BF16),
            pltpu.VMEM((2, NYH, OWN, DS), BF16),
            pltpu.VMEM((2, NYH, OWN, DS), BF16),
            pltpu.VMEM((OWN, DS), BF16),
            pltpu.VMEM((OWN, DS), BF16),
            pltpu.SemaphoreType.DMA((6,)),
            pltpu.SemaphoreType.REGULAR((4,)),
            pltpu.SemaphoreType.DMA,
            pltpu.SemaphoreType.DMA((3,)),
            pltpu.SemaphoreType.DMA((MESSAGES,)),
            pltpu.SemaphoreType.DMA((MESSAGES,)),
            pltpu.SemaphoreType.DMA((NZ,)),
            pltpu.SemaphoreType.DMA((4,)),
        ],
        compiler_params=pltpu.CompilerParams(
            collective_id=0, has_side_effects=True, vmem_limit_bytes=VMEM_BYTES
        ),
    )(
        teacher_query.reshape(*blocks, DT),
        student_query.reshape(*blocks, DS),
        teacher_passages,
        student_passages,
    )
    grad_query, grad_passage, divergence = pl.pallas_call(
        deliver,
        out_shape=outs,
        in_specs=[hbm] * 3,
        out_specs=(hbm,) * 3,
        scratch_shapes=[
            *(pltpu.VMEM(out.shape, out.dtype) for out in outs),
            pltpu.SemaphoreType.DMA((3,)),
            pltpu.SemaphoreType.DMA((3,)),
        ],
        compiler_params=pltpu.CompilerParams(vmem_limit_bytes=VMEM_BYTES),
    )(*results)
    return divergence.reshape(ROWS), grad_query, grad_passage


def solution(mesh):
    return jax.shard_map(
        local,
        mesh=mesh,
        in_specs=(
            P("query", None),
            P("query", None),
            P(("query", "corpus"), None),
            P(("query", "corpus"), None),
        ),
        out_specs=(
            P(("query", "corpus")),
            P(("query", "corpus"), None),
            P(("query", "corpus"), None),
        ),
        check_vma=False,
    )
```

```python
import functools
import math

import jax
import jax.numpy as jnp
from jax import lax
from jax.experimental import pallas as pl
from jax.experimental.pallas import tpu as pltpu
from jax.sharding import PartitionSpec as P

NX, NYH, NYL, NZ, NCORE = 4, 2, 2, 8, 2
OWN = 64
ROWS = 128
DT, DS = 1024, 384
BATCHES = 4
SLOTS = 4
BATCH = 256
GROUP = NYL * ROWS
OWNERS = NYL * NZ
HALF = OWN // 2
ZF = 128
YF = DS - ZF
LOG2E = math.log2(math.e)
LN2 = math.log(2.0)
F32, BF16 = jnp.float32, jnp.bfloat16
MESH = pl.DeviceIdType.MESH

SELF, LEFT, RIGHT, FAR = 0, 1, 2, 3


def place(h, where, core):
    if where == SELF:
        return 1, core * 2 + h
    if where == FAR:
        return 3, core * 2 + h
    return 2 * h, core * 2 + (where - LEFT)


def div(a, b):
    return lax.div(a, jnp.int32(b))


def rem(a, b):
    return lax.rem(a, jnp.int32(b))


def nt(a, b):
    return lax.dot_general(a, b, (((1,), (1,)), ((), ())), preferred_element_type=F32)


def nn(a, b):
    return lax.dot_general(a, b, (((1,), (0,)), ((), ())), preferred_element_type=F32)


class Messages:
    def __init__(self):
        self.numbers = {}

    def __call__(self, name):
        return self.numbers.setdefault(name, len(self.numbers))


MESSAGES = 80
VMEM_BYTES = 60 * 1024 * 1024


def kernel(
    tq_hbm, sq_hbm, tp_hbm, sp_hbm,
    gq_out, gp_out, div_out,
    tq, sq, pbuf, spt, tw, sw, raw_a, raw_b, gt, stat, gq,
    stat_send, stat_recv, res_recv,
    z_send, z_recv_r, z_recv_l, z_pair_send, z_pair_recv,
    y_pair_send, y_pair_recv, y_send, y_recv_r, y_recv_l,
    gp, gps_send, gps_recv, gp1_send, gp1_recv, gp2_send, gp2_recv, gp3_send, gp3_recv,
    load_sem, known_sem, gather_sem, ring_sem, send_sem, recv_sem, yp_recv_sem, st_sem,
):
    t_scale = DT ** (-0.5) * LOG2E
    s_scale = DS ** (-0.5) * LOG2E
    factor = DS ** (-0.5)
    q = lax.axis_index("query")
    c = lax.axis_index("corpus")
    x, yh = div(q, NYH), rem(q, NYH)
    yl, z, k = div(c, NZ * NCORE), rem(div(c, NCORE), NZ), rem(c, NCORE)
    me = yl * NZ + z

    def at(x_, yh_, yl_, z_, k_):
        return (x_ * NYH + yh_, (yl_ * NZ + z_) * NCORE + k_)

    right, left = at(rem(x + 1, NX), yh, yl, z, k), at(rem(x + NX - 1, NX), yh, yl, z, k)
    across = at(x, 1 - yh, 1 - yl, z, k)
    sibling = at(x, yh, yl, z, 1 - k)
    up, down = at(x, yh, yl, rem(z + 1, NZ), k), at(x, yh, yl, rem(z + NZ - 1, NZ), k)
    y_mate = at(x, yh, 1 - yl, z, k)

    offsets = [(dy, dz) for dy in range(NYL) for dz in range(NZ) if (dy, dz) != (0, 0)]
    y_of = [yl, 1 - yl]
    z_of = [rem(z + dz, NZ) for dz in range(NZ)]

    def offset_device(dy, dz):
        return at(x, yh, y_of[dy], z_of[dz], k)

    def slot(h, where, core, half=None):
        b, s = place(h, where, core)
        if half is None:
            return pbuf.at[b * SLOTS + s]
        return pbuf.at[b * SLOTS + s, pl.ds(half * HALF, HALF)]

    def both(b, core):
        return pbuf.at[pl.ds(b * SLOTS + core * 2, 2)]

    loads = [
        pltpu.make_async_copy(tp_hbm, pbuf.at[SLOTS, :, pl.ds(0, DT)], load_sem.at[0]),
        pltpu.make_async_copy(sp_hbm, pbuf.at[SLOTS, :, pl.ds(DT, DS)], load_sem.at[1]),
    ]
    for y in range(NYL):
        loads.append(pltpu.make_async_copy(tq_hbm.at[y, :, k], tq.at[:, y], load_sem.at[2 + y]))
        loads.append(pltpu.make_async_copy(sq_hbm.at[y, :, k], sq.at[:, y], load_sem.at[4 + y]))
    for load in loads:
        load.start()

    barrier = pltpu.get_barrier_semaphore()
    for device in (right, left, across, sibling, up, down, y_mate):
        pl.semaphore_signal(barrier, inc=1, device_id=device, device_id_type=MESH)
    pl.semaphore_wait(barrier, 7)
    loads[0].wait()
    loads[1].wait()

    number = Messages()
    sent = []

    def message(refs, name, device, out=None):
        i = number(name)
        src, dst = refs()
        return pltpu.make_async_remote_copy(
            src_ref=src, dst_ref=dst, send_sem=send_sem.at[i] if out is None else out, recv_sem=recv_sem.at[i],
            device_id=device, device_id_type=MESH,
        )

    def send(refs, name, device):
        message(refs, name, device).start()
        sent.append((refs, name, device))

    def flush():
        for args in sent:
            message(*args).wait_send()
        sent.clear()

    def received(ref, name):
        message(lambda: (ref, ref), name, sibling).wait_recv()

    def spread(refs, name, device):
        message(refs, name, device, gather_sem).start()

    def spread_wait():
        everything = pbuf.at[pl.ds(0, BATCHES * SLOTS - 1)]
        message(lambda: (everything, everything), "gather", sibling, gather_sem).wait_send()

    def half_to(where, half, device):
        spread(lambda: (slot(0, SELF, 0, half), slot(0, where, 0, half)), ("p", where, half), device)

    def sides_to_sibling(h):
        if h == 0:
            received(slot(0, LEFT, 0, 1), ("p", LEFT, 1))
            received(slot(0, RIGHT, 0, 0), ("p", RIGHT, 0))
        else:
            received(slot(1, LEFT, 0), ("p1", LEFT))
            received(slot(1, RIGHT, 0), ("p1", RIGHT))
        to_sibling(2 * h)

    def to_sibling(b):
        spread(lambda: (both(b, 0), both(b, 1)), ("sib", b), sibling)

    def from_sibling(b):
        received(both(b, 1), ("sib", b))

    def far_on():
        received(slot(0, LEFT, 0, 0), ("p", LEFT, 0))
        spread(lambda: (slot(0, LEFT, 0, 0), slot(0, FAR, 0, 0)), ("far",), right)
        received(slot(0, RIGHT, 0, 1), ("p", RIGHT, 1))
        spread(lambda: (slot(0, RIGHT, 0, 1), slot(0, FAR, 0, 1)), ("far",), left)

    def across_on(half):
        received(slot(1, SELF, 0, half), ("across", half))
        spread(lambda: (slot(1, SELF, 0, half), slot(1, LEFT, 0, half)), ("p1", LEFT), right)
        spread(lambda: (slot(1, SELF, 0, half), slot(1, RIGHT, 0, half)), ("p1", RIGHT), left)

    def far_across():
        received(slot(0, FAR, 0), ("far",))
        spread(lambda: (slot(0, FAR, 0), slot(1, FAR, 0)), ("far across",), across)

    def far_from_across():
        received(slot(1, FAR, 0), ("far across",))
        to_sibling(3)

    half_to(LEFT, 0, right)
    half_to(RIGHT, 1, left)
    spread(lambda: (slot(0, SELF, 0, 0), slot(1, SELF, 0, 0)), ("across", 0), across)
    half_to(LEFT, 1, right)
    half_to(RIGHT, 0, left)
    spread(lambda: (slot(0, SELF, 0, 1), slot(1, SELF, 0, 1)), ("across", 1), across)

    def product(i, raw):
        b, n = div(i, NZ), rem(i, NZ)
        batch = pbuf[pl.ds(b * SLOTS, SLOTS)].reshape(BATCH, DT + DS)
        raw[0] = nt(batch[:, :DT], tq[n].reshape(GROUP, DT))
        raw[1] = nt(batch[:, DT:], sq[n].reshape(GROUP, DS))

    def weights(i, raw):
        b, n = div(i, NZ), rem(i, NZ)
        t = raw[0] * t_scale
        s = raw[1] * s_scale
        t_max = jnp.max(t, axis=0, keepdims=True)
        s_max = jnp.max(s, axis=0, keepdims=True)
        t_weight = jnp.exp2(t - t_max)
        s_weight = jnp.exp2(s - s_max)
        tw[n, b] = t_weight
        sw[n, b] = s_weight
        t_sum = jnp.sum(t_weight, axis=0, keepdims=True)
        s_sum = jnp.sum(s_weight, axis=0, keepdims=True)
        cross = jnp.sum(t_weight * (t - s), axis=0, keepdims=True)
        stat[n, b] = jnp.concatenate([t_max, t_sum, s_max, s_sum, cross, cross, cross, cross], axis=0)

    def turn(b):
        turned = pbuf[b * SLOTS:(b + 1) * SLOTS].reshape(BATCH, DT + DS)[:, DT:].T
        part = BATCH // NCORE
        for core in range(NCORE):
            start = (core * BATCHES + b) * part
            spt[:, start:start + part] = turned[:, core * part:(core + 1) * part]

    def know(i):
        for device in (up, down, y_mate):
            pl.semaphore_signal(known_sem.at[i], inc=1, device_id=device, device_id_type=MESH)
        pl.semaphore_wait(known_sem.at[i], 3)

    know(0)
    far_on()
    across_on(0)
    across_on(1)
    to_sibling(1)
    know(1)
    sides_to_sibling(0)
    know(2)
    far_across()
    know(3)
    for load in loads[2:]:
        load.wait()

    def joined(parts):
        t_max = functools.reduce(jnp.maximum, [p[0:1] for p in parts])
        s_max = functools.reduce(jnp.maximum, [p[2:3] for p in parts])
        t_in = [jnp.exp2(p[0:1] - t_max) for p in parts]
        s_in = [jnp.exp2(p[2:3] - s_max) for p in parts]
        t_sum = functools.reduce(jnp.add, [p[1:2] * w for p, w in zip(parts, t_in)])
        s_sum = functools.reduce(jnp.add, [p[3:4] * w for p, w in zip(parts, s_in)])
        cross = functools.reduce(jnp.add, [p[4:5] * w for p, w in zip(parts, t_in)])
        return t_max, t_sum, s_max, s_sum, cross

    def stat_copy(dy, dz):
        return pltpu.make_async_remote_copy(
            src_ref=stat_send.at[y_of[dy] * NZ + z_of[dz]], dst_ref=stat_recv.at[dy * NZ + (NZ - dz) % NZ],
            send_sem=st_sem.at[0], recv_sem=st_sem.at[1],
            device_id=offset_device(dy, dz), device_id_type=MESH,
        )

    def res_copy(dy, dz):
        return pltpu.make_async_remote_copy(
            src_ref=res_recv.at[me], dst_ref=res_recv.at[me],
            send_sem=st_sem.at[2], recv_sem=st_sem.at[3],
            device_id=offset_device(dy, dz), device_id_type=MESH,
        )

    def all_copies(ref, first):
        others = ref.at[pl.ds(0, OWNERS - 1)]
        return pltpu.make_async_remote_copy(
            src_ref=others, dst_ref=others, send_sem=st_sem.at[first], recv_sem=st_sem.at[first + 1],
            device_id=sibling, device_id_type=MESH,
        )

    def leave(first):
        for n in range(first, first + 4):
            t_max, t_sum, s_max, s_sum, cross = joined([stat[n, b] for b in range(BATCHES)])
            whole = jnp.concatenate([t_max, t_sum, s_max, s_sum, cross, cross, cross, cross], axis=0)
            for y in range(NYL):
                stat_send[y * NZ + n, 0] = whole[:, y * ROWS:(y + 1) * ROWS]
            four = jnp.concatenate([whole[0:4, :ROWS], whole[0:4, ROWS:]], axis=0)
            for y in range(NYL):
                stat_send[y * NZ + (n + 4) % NZ, 1] = four

    from_sibling(0)
    product(0, raw_a)

    def score_step(j, carry):
        @pl.when(j == 3)
        def _():
            from_sibling(1)

        @pl.when(j == 5)
        def _():
            sides_to_sibling(1)

        @pl.when(j == 7)
        def _():
            far_from_across()
            from_sibling(2)

        @pl.when(j == 11)
        def _():
            from_sibling(3)

        @pl.when(j == 14)
        def _():
            leave(0)

        product(2 * j + 1, raw_b)
        weights(2 * j, raw_a)
        product(jnp.minimum(2 * j + 2, BATCHES * NZ - 1), raw_a)
        weights(2 * j + 1, raw_b)
        return carry

    lax.fori_loop(0, BATCHES * NZ // 2, score_step, 0)
    leave(4)
    for offset in offsets:
        stat_copy(*offset).start()
    stat_recv[0] = stat_send[me]
    for b in range(BATCHES):
        turn(b)
    spread_wait()
    all_copies(stat_recv, 0).wait_recv()
    def totals(parts):
        t_max, t_sum, s_max, s_sum, cross = joined(parts)
        t_in, s_in = factor / t_sum, factor / s_sum
        result = jnp.concatenate([t_max, t_in, s_max, s_in, t_in, t_in, t_in, t_in], axis=0)
        return result, (t_max, t_sum, s_max, s_sum, cross)

    result, (t_max, t_sum, s_max, s_sum, cross) = totals([stat_recv[m, 0] for m in range(OWNERS)])
    res_recv[me] = result
    for offset in offsets:
        res_copy(*offset).start()
    far = []
    for y in range(NYL):
        parts = [stat_recv[m, 1, 4 * y:4 * y + 4] for m in range(OWNERS)]
        far.append(totals([jnp.concatenate([p, p], axis=0) for p in parts])[0])
    far = jnp.concatenate(far, axis=1)

    def group(away):
        return rem(z + NZ + away, NZ)

    def sequence(i):
        size = 4 - div(i + 1, 2)
        return group(size * (2 * rem(i, 2) - 1))

    def lanes(n):
        return pl.ds(pl.multiple_of(n * GROUP, GROUP), GROUP)

    def form(i, res=None):
        n = sequence(i)
        if res is None:
            res = jnp.concatenate([res_recv[n], res_recv[NZ + n]], axis=1)
        for b in range(BATCHES):
            st = stat[n, b]
            t_in = jnp.exp2(st[0:1] - res[0:1]) * res[1:2]
            s_in = jnp.exp2(st[2:3] - res[2:3]) * res[3:4]
            grad = (sw[n, b] * s_in - tw[n, b] * t_in).astype(BF16)
            gt[0, b, :, lanes(n)] = grad[:BATCH // 2]
            gt[1, b, :, lanes(n)] = grad[BATCH // 2:]

    def pair_copy(i):
        return pltpu.make_async_remote_copy(
            src_ref=y_pair_send.at[i], dst_ref=y_pair_recv.at[i],
            send_sem=ring_sem.at[2], recv_sem=yp_recv_sem.at[i],
            device_id=y_mate, device_id_type=MESH,
        )

    def query_part(i):
        n = sequence(i)
        total = nn(spt[...], gt[:, :, :, lanes(n)].reshape(NCORE * BATCHES * BATCH // 2, GROUP))
        gq[n, 0] = total[:, :ROWS]
        gq[n, 1] = total[:, ROWS:]
        y_pair_send[i] = gq[n, 1 - yl, ZF:].astype(BF16)

    def z_part(away):
        return gq[group(away), :, :ZF]

    def y_part(away):
        i = (4, 3, -3, 2, -2, 1, -1, 0).index(away)
        pair_copy(i).wait_recv()
        return gq[group(away), yl, ZF:] + y_pair_recv[i].astype(F32)

    ZH, YH = ZF // 2, YF // 2

    def z_start():
        far = z_part(4).astype(BF16)
        z_send[0] = far
        message(lambda: (z_send.at[0, :, pl.ds(0, ZH)], z_recv_r.at[0, :, pl.ds(0, ZH)]), ("zr", 0), up, ring_sem.at[0]).start()
        message(lambda: (z_send.at[0, :, pl.ds(ZH, ZH)], z_recv_l.at[0, :, pl.ds(ZH, ZH)]), ("zl", 0), down, ring_sem.at[0]).start()

    def y_start():
        y_send[0] = y_part(4).astype(BF16)
        message(lambda: (y_send.at[0, pl.ds(0, YH)], y_recv_r.at[0, pl.ds(0, YH)]), ("yr", 0), up, ring_sem.at[1]).start()
        message(lambda: (y_send.at[0, pl.ds(YH, YH)], y_recv_l.at[0, pl.ds(YH, YH)]), ("yl", 0), down, ring_sem.at[1]).start()

    def z_step(step):
        if step == 1:
            mine = z_part(3)
            received(z_recv_r.at[0, :, pl.ds(0, ZH)], ("zr", 0))
            z_send[1, :, :ZH] = (mine[:, :ZH] + z_recv_r[0, :, :ZH].astype(F32)).astype(BF16)
            z_send[1, :, ZH:] = mine[:, ZH:].astype(BF16)
        else:
            received(z_recv_r.at[step - 1], ("zr", step - 1))
            z_send[step] = (z_part(4 - step) + z_recv_r[step - 1].astype(F32)).astype(BF16)
        message(lambda step=step: (z_send.at[step], z_recv_r.at[step]), ("zr", step), up, ring_sem.at[0]).start()
        if step == 1:
            mine = z_part(-3)
            received(z_recv_l.at[0, :, pl.ds(ZH, ZH)], ("zl", 0))
            z_send[5, :, :ZH] = mine[:, :ZH].astype(BF16)
            z_send[5, :, ZH:] = (mine[:, ZH:] + z_recv_l[0, :, ZH:].astype(F32)).astype(BF16)
        else:
            received(z_recv_l.at[step - 1], ("zl", step - 1))
            z_send[4 + step] = (z_part(step - 4) + z_recv_l[step - 1].astype(F32)).astype(BF16)
        message(lambda step=step: (z_send.at[4 + step], z_recv_l.at[step]), ("zl", step), down, ring_sem.at[0]).start()

    def y_step(step):
        mine = y_part(4 - step)
        if step == 1:
            received(y_recv_r.at[0, pl.ds(0, YH)], ("yr", 0))
            y_send[1, :YH] = (mine[:YH] + y_recv_r[0, :YH].astype(F32)).astype(BF16)
            y_send[1, YH:] = mine[YH:].astype(BF16)
        else:
            received(y_recv_r.at[step - 1], ("yr", step - 1))
            y_send[step] = (mine + y_recv_r[step - 1].astype(F32)).astype(BF16)
        message(lambda step=step: (y_send.at[step], y_recv_r.at[step]), ("yr", step), up, ring_sem.at[1]).start()
        mine = y_part(step - 4)
        if step == 1:
            received(y_recv_l.at[0, pl.ds(YH, YH)], ("yl", 0))
            y_send[5, :YH] = mine[:YH].astype(BF16)
            y_send[5, YH:] = (mine[YH:] + y_recv_l[0, YH:].astype(F32)).astype(BF16)
        else:
            received(y_recv_l.at[step - 1], ("yl", step - 1))
            y_send[4 + step] = (mine + y_recv_l[step - 1].astype(F32)).astype(BF16)
        message(lambda step=step: (y_send.at[4 + step], y_recv_l.at[step]), ("yl", step), down, ring_sem.at[1]).start()

    def passage_part(core, to):
        def term(i):
            wide = pl.ds(pl.multiple_of(i * 2 * GROUP, 2 * GROUP), 2 * GROUP)
            grads = gt[core, :, :, wide].reshape(BATCHES * BATCH // 2, 2 * GROUP)
            queries = sq[pl.ds(2 * i, 2)].reshape(2 * GROUP, DS)
            return nn(grads, queries).reshape(BATCHES, 2, OWN, DS)

        to[...] = term(0)

        def body(i, carry):
            to[...] = to[...] + term(i)
            return carry

        lax.fori_loop(1, NZ // 2, body, 0)

    def gp_of(h, where):
        b, s = place(h, where, 0)
        return gp[b, s]

    def gp_first():
        received(gps_recv, "gp sibling")
        gp[...] = gp[...] + gps_recv[...].astype(F32)
        for h in range(NYH):
            gp1_send[h] = gp_of(h, FAR).astype(BF16)
        send(lambda: (gp1_send.at[0], gp1_recv.at[0]), ("gp", RIGHT, 1), right)
        send(lambda: (gp1_send.at[1], gp1_recv.at[1]), ("gp", LEFT, 1), left)

    def gp_second():
        received(gp1_recv.at[0], ("gp", RIGHT, 1))
        gp2_send[0, 0] = (gp_of(0, RIGHT) + gp1_recv[0].astype(F32)).astype(BF16)
        gp2_send[0, 1] = gp_of(1, RIGHT).astype(BF16)
        send(lambda: (gp2_send.at[0], gp2_recv.at[0]), ("gp", RIGHT, 2), right)
        received(gp1_recv.at[1], ("gp", LEFT, 1))
        gp2_send[1, 0] = gp_of(0, LEFT).astype(BF16)
        gp2_send[1, 1] = (gp_of(1, LEFT) + gp1_recv[1].astype(F32)).astype(BF16)
        send(lambda: (gp2_send.at[1], gp2_recv.at[1]), ("gp", LEFT, 2), left)

    def gp_third():
        received(gp2_recv.at[0], ("gp", RIGHT, 2))
        received(gp2_recv.at[1], ("gp", LEFT, 2))
        gp3_send[...] = x_total(1).astype(BF16)
        send(lambda: (gp3_send, gp3_recv), "gp across", across)

    def x_total(h):
        return gp_of(h, SELF) + gp2_recv[0, h].astype(F32) + gp2_recv[1, h].astype(F32)

    def z_last():
        received(z_recv_r.at[3], ("zr", 3))
        received(z_recv_l.at[3], ("zl", 3))
        for y in range(NYL):
            gq[z, y, :ZF] = gq[z, y, :ZF] + z_recv_r[3, y].astype(F32) + z_recv_l[3, y].astype(F32)
        z_pair_send[...] = gq[z, 1 - yl, :ZF].astype(BF16)
        send(lambda: (z_pair_send, z_pair_recv), "z pair", y_mate)

    form(0, far)
    query_part(0)
    z_start()
    pair_copy(0).start()
    div_out[...] = cross * LN2 / t_sum - (t_max * LN2 + jnp.log(t_sum)) + (s_max * LN2 + jnp.log(s_sum))
    all_copies(stat_send, 0).wait_send()
    all_copies(res_recv, 2).wait_recv()
    form(1)

    def gradient_step(i, carry):
        query_part(i)
        form(i + 1)

        @pl.when(i == 2)
        def _():
            z_step(1)

        pair_copy(i).start()

        @pl.when(i == 4)
        def _():
            y_start()

        return carry

    lax.fori_loop(1, NZ - 1, gradient_step, 0)
    query_part(NZ - 1)
    pair_copy(NZ - 1).start()
    passage_part(1, gp)
    gps_send[...] = gp[...].astype(BF16)
    send(lambda: (gps_send, gps_recv), "gp sibling", sibling)
    z_step(2)
    y_step(1)
    passage_part(0, gp)
    gp_first()
    z_step(3)
    y_step(2)
    gp_second()
    all_copies(res_recv, 2).wait_send()
    z_last()
    y_step(3)
    gp_third()
    for i, ref in enumerate((z_send.at[pl.ds(0, 7)], y_send.at[pl.ds(0, 7)], y_pair_send)):
        message(lambda: (ref, ref), "ring", sibling, ring_sem.at[i]).wait_send()
    flush()

    mine = y_part(0)
    received(y_recv_r.at[3], ("yr", 3))
    received(y_recv_l.at[3], ("yl", 3))
    gq_out[:, ZF:] = (mine + y_recv_r[3].astype(F32) + y_recv_l[3].astype(F32)).T
    received(z_pair_recv, "z pair")
    gq_out[:, :ZF] = (gq[z, yl, :ZF] + z_pair_recv[...].astype(F32)).T
    received(gp3_recv, "gp across")
    gp_out[...] = x_total(0) + gp3_recv[...].astype(F32)


def deliver(gq_in, gp_in, div_in, gq_out, gp_out, div_out, gq, gp, div, in_sem, out_sem):
    parts = ((gq_in, gq, gq_out), (gp_in, gp, gp_out), (div_in, div, div_out))
    ins = [pltpu.make_async_copy(src, mid, in_sem.at[i]) for i, (src, mid, _) in enumerate(parts)]
    outs = [pltpu.make_async_copy(mid, dst, out_sem.at[i]) for i, (_, mid, dst) in enumerate(parts)]
    for copy in ins:
        copy.start()
    for arrive, leave in zip(ins, outs):
        arrive.wait()
        leave.start()
    for copy in outs:
        copy.wait()


def local(teacher_query, student_query, teacher_passages, student_passages):
    blocks = NYL, NZ, NCORE, ROWS
    hbm = pl.BlockSpec(memory_space=pl.ANY)
    vmem = pl.BlockSpec(memory_space=pltpu.VMEM)
    outs = (
        jax.ShapeDtypeStruct((ROWS, DS), F32),
        jax.ShapeDtypeStruct((OWN, DS), F32),
        jax.ShapeDtypeStruct((1, ROWS), F32),
    )
    results = pl.pallas_call(
        kernel,
        out_shape=outs,
        in_specs=[hbm] * 4,
        out_specs=(vmem,) * 3,
        scratch_shapes=[
            pltpu.VMEM((NZ, NYL, ROWS, DT), BF16),
            pltpu.VMEM((NZ, NYL, ROWS, DS), BF16),
            pltpu.VMEM((BATCHES * SLOTS, OWN, DT + DS), BF16),
            pltpu.VMEM((DS, BATCHES * BATCH), BF16),
            pltpu.VMEM((NZ, BATCHES, BATCH, GROUP), F32),
            pltpu.VMEM((NZ, BATCHES, BATCH, GROUP), F32),
            pltpu.VMEM((2, BATCH, GROUP), F32),
            pltpu.VMEM((2, BATCH, GROUP), F32),
            pltpu.VMEM((NCORE, BATCHES, BATCH // 2, NZ * GROUP), BF16),
            pltpu.VMEM((NZ, BATCHES, 8, GROUP), F32),
            pltpu.VMEM((NZ, NYL, DS, ROWS), F32),
            pltpu.VMEM((OWNERS, 2, 8, ROWS), F32),
            pltpu.VMEM((OWNERS, 2, 8, ROWS), F32),
            pltpu.VMEM((OWNERS, 8, ROWS), F32),
            pltpu.VMEM((8, NYL, ZF, ROWS), BF16),
            pltpu.VMEM((4, NYL, ZF, ROWS), BF16),
            pltpu.VMEM((4, NYL, ZF, ROWS), BF16),
            pltpu.VMEM((ZF, ROWS), BF16),
            pltpu.VMEM((ZF, ROWS), BF16),
            pltpu.VMEM((NZ, YF, ROWS), BF16),
            pltpu.VMEM((NZ, YF, ROWS), BF16),
            pltpu.VMEM((8, YF, ROWS), BF16),
            pltpu.VMEM((4, YF, ROWS), BF16),
            pltpu.VMEM((4, YF, ROWS), BF16),
            pltpu.VMEM((BATCHES, 2, OWN, DS), F32),
            pltpu.VMEM((BATCHES, 2, OWN, DS), BF16),
            pltpu.VMEM((BATCHES, 2, OWN, DS), BF16),
            pltpu.VMEM((NYH, OWN, DS), BF16),
            pltpu.VMEM((NYH, OWN, DS), BF16),
            pltpu.VMEM((2, NYH, OWN, DS), BF16),
            pltpu.VMEM((2, NYH, OWN, DS), BF16),
            pltpu.VMEM((OWN, DS), BF16),
            pltpu.VMEM((OWN, DS), BF16),
            pltpu.SemaphoreType.DMA((6,)),
            pltpu.SemaphoreType.REGULAR((4,)),
            pltpu.SemaphoreType.DMA,
            pltpu.SemaphoreType.DMA((3,)),
            pltpu.SemaphoreType.DMA((MESSAGES,)),
            pltpu.SemaphoreType.DMA((MESSAGES,)),
            pltpu.SemaphoreType.DMA((NZ,)),
            pltpu.SemaphoreType.DMA((4,)),
        ],
        compiler_params=pltpu.CompilerParams(
            collective_id=0, has_side_effects=True, vmem_limit_bytes=VMEM_BYTES
        ),
    )(
        teacher_query.reshape(*blocks, DT),
        student_query.reshape(*blocks, DS),
        teacher_passages,
        student_passages,
    )
    grad_query, grad_passage, divergence = pl.pallas_call(
        deliver,
        out_shape=outs,
        in_specs=[hbm] * 3,
        out_specs=(hbm,) * 3,
        scratch_shapes=[
            *(pltpu.VMEM(out.shape, out.dtype) for out in outs),
            pltpu.SemaphoreType.DMA((3,)),
            pltpu.SemaphoreType.DMA((3,)),
        ],
        compiler_params=pltpu.CompilerParams(vmem_limit_bytes=VMEM_BYTES),
    )(*results)
    return divergence.reshape(ROWS), grad_query, grad_passage


def solution(mesh):
    return jax.shard_map(
        local,
        mesh=mesh,
        in_specs=(
            P("query", None),
            P("query", None),
            P(("query", "corpus"), None),
            P(("query", "corpus"), None),
        ),
        out_specs=(
            P(("query", "corpus")),
            P(("query", "corpus"), None),
            P(("query", "corpus"), None),
        ),
        check_vma=False,
    )
```

```python
import functools
import math

import jax
import jax.numpy as jnp
from jax import lax
from jax.experimental import pallas as pl
from jax.experimental.pallas import tpu as pltpu
from jax.sharding import PartitionSpec as P

NX, NYH, NYL, NZ, NCORE = 4, 2, 2, 8, 2
OWN = 64
ROWS = 128
DT, DS = 1024, 384
BATCHES = 4
SLOTS = 4
WIDE = 2
BATCH = 256
GROUP = NYL * ROWS
OWNERS = NYL * NZ
HALF = OWN // 2
ZF = 128
YF = DS - ZF
LOG2E = math.log2(math.e)
LN2 = math.log(2.0)
F32, BF16 = jnp.float32, jnp.bfloat16
MESH = pl.DeviceIdType.MESH

SELF, LEFT, RIGHT, FAR = 0, 1, 2, 3


def place(h, where, core):
    if where == SELF:
        return 1, core * 2 + h
    if where == FAR:
        return 3, core * 2 + h
    return 2 * h, core * 2 + (where - LEFT)


def div(a, b):
    return lax.div(a, jnp.int32(b))


def rem(a, b):
    return lax.rem(a, jnp.int32(b))


def nt(a, b):
    return lax.dot_general(a, b, (((1,), (1,)), ((), ())), preferred_element_type=F32)


def nn(a, b):
    return lax.dot_general(a, b, (((1,), (0,)), ((), ())), preferred_element_type=F32)


class Messages:
    def __init__(self):
        self.numbers = {}

    def __call__(self, name):
        return self.numbers.setdefault(name, len(self.numbers))


MESSAGES = 80
VMEM_BYTES = 60 * 1024 * 1024


def kernel(
    tq_hbm, sq_hbm, tp_hbm, sp_hbm,
    gq_out, gp_out, div_out,
    tq, sq, pbuf, spt, tw, sw, raw_a, raw_b, gt, stat, gq,
    stat_send, stat_recv, res_recv,
    z_send, z_recv_r, z_recv_l, z_pair_send, z_pair_recv,
    y_pair_send, y_pair_recv, y_send, y_recv_r, y_recv_l,
    gp2, gps_send, gps_recv, gp1_send, gp1_recv, gp2_send, gp2_recv, gp3_send, gp3_recv,
    load_sem, known_sem, gather_sem, ring_sem, send_sem, recv_sem, yp_recv_sem, st_sem,
):
    t_scale = DT ** (-0.5) * LOG2E
    s_scale = DS ** (-0.5) * LOG2E
    factor = DS ** (-0.5)
    q = lax.axis_index("query")
    c = lax.axis_index("corpus")
    x, yh = div(q, NYH), rem(q, NYH)
    yl, z, k = div(c, NZ * NCORE), rem(div(c, NCORE), NZ), rem(c, NCORE)
    me = yl * NZ + z

    def at(x_, yh_, yl_, z_, k_):
        return (x_ * NYH + yh_, (yl_ * NZ + z_) * NCORE + k_)

    right, left = at(rem(x + 1, NX), yh, yl, z, k), at(rem(x + NX - 1, NX), yh, yl, z, k)
    across = at(x, 1 - yh, 1 - yl, z, k)
    sibling = at(x, yh, yl, z, 1 - k)
    up, down = at(x, yh, yl, rem(z + 1, NZ), k), at(x, yh, yl, rem(z + NZ - 1, NZ), k)
    y_mate = at(x, yh, 1 - yl, z, k)

    offsets = [(dy, dz) for dy in range(NYL) for dz in range(NZ) if (dy, dz) != (0, 0)]
    y_of = [yl, 1 - yl]
    z_of = [rem(z + dz, NZ) for dz in range(NZ)]

    def offset_device(dy, dz):
        return at(x, yh, y_of[dy], z_of[dz], k)

    def slot(h, where, core, half=None):
        b, s = place(h, where, core)
        if half is None:
            return pbuf.at[b * SLOTS + s]
        return pbuf.at[b * SLOTS + s, pl.ds(half * HALF, HALF)]

    def both(b, core):
        return pbuf.at[pl.ds(b * SLOTS + core * 2, 2)]

    loads = [
        pltpu.make_async_copy(tp_hbm, pbuf.at[SLOTS, :, pl.ds(0, DT)], load_sem.at[0]),
        pltpu.make_async_copy(sp_hbm, pbuf.at[SLOTS, :, pl.ds(DT, DS)], load_sem.at[1]),
    ]
    for y in range(NYL):
        loads.append(pltpu.make_async_copy(tq_hbm.at[y, :, k], tq.at[:, y], load_sem.at[2 + y]))
        loads.append(pltpu.make_async_copy(sq_hbm.at[y, :, k], sq.at[:, y], load_sem.at[4 + y]))
    for load in loads:
        load.start()

    barrier = pltpu.get_barrier_semaphore()
    for device in (right, left, across, sibling, up, down, y_mate):
        pl.semaphore_signal(barrier, inc=1, device_id=device, device_id_type=MESH)
    pl.semaphore_wait(barrier, 7)
    loads[0].wait()
    loads[1].wait()

    number = Messages()
    sent = []

    def message(refs, name, device, out=None):
        i = number(name)
        src, dst = refs()
        return pltpu.make_async_remote_copy(
            src_ref=src, dst_ref=dst, send_sem=send_sem.at[i] if out is None else out, recv_sem=recv_sem.at[i],
            device_id=device, device_id_type=MESH,
        )

    def send(refs, name, device):
        message(refs, name, device).start()
        sent.append((refs, name, device))

    def flush():
        for args in sent:
            message(*args).wait_send()
        sent.clear()

    def received(ref, name):
        message(lambda: (ref, ref), name, sibling).wait_recv()

    def spread(refs, name, device):
        message(refs, name, device, gather_sem).start()

    def spread_wait():
        everything = pbuf.at[pl.ds(0, BATCHES * SLOTS - 1)]
        message(lambda: (everything, everything), "gather", sibling, gather_sem).wait_send()

    def half_to(where, half, device):
        spread(lambda: (slot(0, SELF, 0, half), slot(0, where, 0, half)), ("p", where, half), device)

    def sides_to_sibling(h):
        if h == 0:
            received(slot(0, LEFT, 0, 1), ("p", LEFT, 1))
            received(slot(0, RIGHT, 0, 0), ("p", RIGHT, 0))
        else:
            received(slot(1, LEFT, 0), ("p1", LEFT))
            received(slot(1, RIGHT, 0), ("p1", RIGHT))
        to_sibling(2 * h)

    def to_sibling(b):
        spread(lambda: (both(b, 0), both(b, 1)), ("sib", b), sibling)

    def from_sibling(b):
        received(both(b, 1), ("sib", b))

    def far_on():
        received(slot(0, LEFT, 0, 0), ("p", LEFT, 0))
        spread(lambda: (slot(0, LEFT, 0, 0), slot(0, FAR, 0, 0)), ("far",), right)
        received(slot(0, RIGHT, 0, 1), ("p", RIGHT, 1))
        spread(lambda: (slot(0, RIGHT, 0, 1), slot(0, FAR, 0, 1)), ("far",), left)

    def across_on(half):
        received(slot(1, SELF, 0, half), ("across", half))
        spread(lambda: (slot(1, SELF, 0, half), slot(1, LEFT, 0, half)), ("p1", LEFT), right)
        spread(lambda: (slot(1, SELF, 0, half), slot(1, RIGHT, 0, half)), ("p1", RIGHT), left)

    def far_across():
        received(slot(0, FAR, 0), ("far",))
        spread(lambda: (slot(0, FAR, 0), slot(1, FAR, 0)), ("far across",), across)

    def far_from_across():
        received(slot(1, FAR, 0), ("far across",))
        to_sibling(3)

    half_to(LEFT, 0, right)
    half_to(RIGHT, 1, left)
    spread(lambda: (slot(0, SELF, 0, 0), slot(1, SELF, 0, 0)), ("across", 0), across)
    half_to(LEFT, 1, right)
    half_to(RIGHT, 0, left)
    spread(lambda: (slot(0, SELF, 0, 1), slot(1, SELF, 0, 1)), ("across", 1), across)

    def product(i, raw):
        b, n = div(i, NZ), rem(i, NZ)
        batch = pbuf[pl.ds(b * WIDE * SLOTS, WIDE * SLOTS)].reshape(WIDE * BATCH, DT + DS)
        raw[0] = nt(batch[:, :DT], tq[n].reshape(GROUP, DT))
        raw[1] = nt(batch[:, DT:], sq[n].reshape(GROUP, DS))

    def weights(i, raw):
        b, n = div(i, NZ), rem(i, NZ)
        t = raw[0] * t_scale
        s = raw[1] * s_scale
        t_max = jnp.max(t, axis=0, keepdims=True)
        s_max = jnp.max(s, axis=0, keepdims=True)
        t_weight = jnp.exp2(t - t_max)
        s_weight = jnp.exp2(s - s_max)
        tw[n, b] = t_weight.reshape(WIDE, BATCH, GROUP)
        sw[n, b] = s_weight.reshape(WIDE, BATCH, GROUP)
        t_sum = jnp.sum(t_weight, axis=0, keepdims=True)
        s_sum = jnp.sum(s_weight, axis=0, keepdims=True)
        cross = jnp.sum(t_weight * (t - s), axis=0, keepdims=True)
        stat[n, b] = jnp.concatenate([t_max, t_sum, s_max, s_sum, cross, cross, cross, cross], axis=0)

    def turn(b):
        turned = pbuf[b * SLOTS:(b + 1) * SLOTS].reshape(BATCH, DT + DS)[:, DT:].T
        part = BATCH // NCORE
        for core in range(NCORE):
            start = (core * BATCHES + b) * part
            spt[:, start:start + part] = turned[:, core * part:(core + 1) * part]

    def know(i):
        for device in (up, down, y_mate):
            pl.semaphore_signal(known_sem.at[i], inc=1, device_id=device, device_id_type=MESH)
        pl.semaphore_wait(known_sem.at[i], 3)

    know(0)
    far_on()
    across_on(0)
    across_on(1)
    to_sibling(1)
    know(1)
    sides_to_sibling(0)
    know(2)
    far_across()
    know(3)
    for load in loads[2:]:
        load.wait()

    def joined(parts):
        t_max = functools.reduce(jnp.maximum, [p[0:1] for p in parts])
        s_max = functools.reduce(jnp.maximum, [p[2:3] for p in parts])
        t_in = [jnp.exp2(p[0:1] - t_max) for p in parts]
        s_in = [jnp.exp2(p[2:3] - s_max) for p in parts]
        t_sum = functools.reduce(jnp.add, [p[1:2] * w for p, w in zip(parts, t_in)])
        s_sum = functools.reduce(jnp.add, [p[3:4] * w for p, w in zip(parts, s_in)])
        cross = functools.reduce(jnp.add, [p[4:5] * w for p, w in zip(parts, t_in)])
        return t_max, t_sum, s_max, s_sum, cross

    def stat_copy(dy, dz):
        return pltpu.make_async_remote_copy(
            src_ref=stat_send.at[y_of[dy] * NZ + z_of[dz]], dst_ref=stat_recv.at[dy * NZ + (NZ - dz) % NZ],
            send_sem=st_sem.at[0], recv_sem=st_sem.at[1],
            device_id=offset_device(dy, dz), device_id_type=MESH,
        )

    def res_copy(dy, dz):
        return pltpu.make_async_remote_copy(
            src_ref=res_recv.at[me], dst_ref=res_recv.at[me],
            send_sem=st_sem.at[2], recv_sem=st_sem.at[3],
            device_id=offset_device(dy, dz), device_id_type=MESH,
        )

    def all_copies(ref, first):
        others = ref.at[pl.ds(0, OWNERS - 1)]
        return pltpu.make_async_remote_copy(
            src_ref=others, dst_ref=others, send_sem=st_sem.at[first], recv_sem=st_sem.at[first + 1],
            device_id=sibling, device_id_type=MESH,
        )

    def leave(first):
        for n in range(first, first + 4):
            t_max, t_sum, s_max, s_sum, cross = joined([stat[n, b] for b in range(BATCHES // WIDE)])
            whole = jnp.concatenate([t_max, t_sum, s_max, s_sum, cross, cross, cross, cross], axis=0)
            for y in range(NYL):
                stat_send[y * NZ + n, 0] = whole[:, y * ROWS:(y + 1) * ROWS]
            four = jnp.concatenate([whole[0:4, :ROWS], whole[0:4, ROWS:]], axis=0)
            for y in range(NYL):
                stat_send[y * NZ + (n + 4) % NZ, 1] = four

    tiles = BATCHES // WIDE * NZ
    from_sibling(0)
    from_sibling(1)
    product(0, raw_a)

    def score_step(j, carry):
        @pl.when(j == 2)
        def _():
            sides_to_sibling(1)

        @pl.when(j == 3)
        def _():
            far_from_across()
            from_sibling(2)
            from_sibling(3)

        @pl.when(j == 6)
        def _():
            leave(0)

        product(2 * j + 1, raw_b)
        weights(2 * j, raw_a)
        product(jnp.minimum(2 * j + 2, tiles - 1), raw_a)
        weights(2 * j + 1, raw_b)
        return carry

    lax.fori_loop(0, tiles // 2, score_step, 0)
    leave(4)
    for offset in offsets:
        stat_copy(*offset).start()
    stat_recv[0] = stat_send[me]
    for b in range(BATCHES):
        turn(b)
    spread_wait()
    all_copies(stat_recv, 0).wait_recv()
    def totals(parts):
        t_max, t_sum, s_max, s_sum, cross = joined(parts)
        t_in, s_in = factor / t_sum, factor / s_sum
        result = jnp.concatenate([t_max, t_in, s_max, s_in, t_in, t_in, t_in, t_in], axis=0)
        return result, (t_max, t_sum, s_max, s_sum, cross)

    result, (t_max, t_sum, s_max, s_sum, cross) = totals([stat_recv[m, 0] for m in range(OWNERS)])
    res_recv[me] = result
    for offset in offsets:
        res_copy(*offset).start()
    far = []
    for y in range(NYL):
        parts = [stat_recv[m, 1, 4 * y:4 * y + 4] for m in range(OWNERS)]
        far.append(totals([jnp.concatenate([p, p], axis=0) for p in parts])[0])
    far = jnp.concatenate(far, axis=1)

    def group(away):
        return rem(z + NZ + away, NZ)

    def sequence(i):
        size = 4 - div(i + 1, 2)
        return group(size * (2 * rem(i, 2) - 1))

    def lanes(n):
        return pl.ds(pl.multiple_of(n * GROUP, GROUP), GROUP)

    def form(i, res=None):
        n = sequence(i)
        if res is None:
            res = jnp.concatenate([res_recv[n], res_recv[NZ + n]], axis=1)
        for b in range(BATCHES):
            st = stat[n, b // WIDE]
            t_in = jnp.exp2(st[0:1] - res[0:1]) * res[1:2]
            s_in = jnp.exp2(st[2:3] - res[2:3]) * res[3:4]
            grad = (sw[n, b // WIDE, b % WIDE] * s_in - tw[n, b // WIDE, b % WIDE] * t_in).astype(BF16)
            gt[0, b, :, lanes(n)] = grad[:BATCH // 2]
            gt[1, b, :, lanes(n)] = grad[BATCH // 2:]

    def pair_copy(i):
        return pltpu.make_async_remote_copy(
            src_ref=y_pair_send.at[i], dst_ref=y_pair_recv.at[i],
            send_sem=ring_sem.at[2], recv_sem=yp_recv_sem.at[i],
            device_id=y_mate, device_id_type=MESH,
        )

    def query_part(i):
        n = sequence(i)
        total = nn(spt[...], gt[:, :, :, lanes(n)].reshape(NCORE * BATCHES * BATCH // 2, GROUP))
        gq[n, 0] = total[:, :ROWS]
        gq[n, 1] = total[:, ROWS:]
        y_pair_send[i] = gq[n, 1 - yl, ZF:].astype(BF16)

    def z_part(away):
        return gq[group(away), :, :ZF]

    def y_part(away):
        i = (4, 3, -3, 2, -2, 1, -1, 0).index(away)
        pair_copy(i).wait_recv()
        return gq[group(away), yl, ZF:] + y_pair_recv[i].astype(F32)

    ZH, YH = ZF // 2, YF // 2

    def z_start():
        far = z_part(4).astype(BF16)
        z_send[0] = far
        message(lambda: (z_send.at[0, :, pl.ds(0, ZH)], z_recv_r.at[0, :, pl.ds(0, ZH)]), ("zr", 0), up, ring_sem.at[0]).start()
        message(lambda: (z_send.at[0, :, pl.ds(ZH, ZH)], z_recv_l.at[0, :, pl.ds(ZH, ZH)]), ("zl", 0), down, ring_sem.at[0]).start()

    def y_start():
        y_send[0] = y_part(4).astype(BF16)
        message(lambda: (y_send.at[0, pl.ds(0, YH)], y_recv_r.at[0, pl.ds(0, YH)]), ("yr", 0), up, ring_sem.at[1]).start()
        message(lambda: (y_send.at[0, pl.ds(YH, YH)], y_recv_l.at[0, pl.ds(YH, YH)]), ("yl", 0), down, ring_sem.at[1]).start()

    def z_step(step):
        if step == 1:
            mine = z_part(3)
            received(z_recv_r.at[0, :, pl.ds(0, ZH)], ("zr", 0))
            z_send[1, :, :ZH] = (mine[:, :ZH] + z_recv_r[0, :, :ZH].astype(F32)).astype(BF16)
            z_send[1, :, ZH:] = mine[:, ZH:].astype(BF16)
        else:
            received(z_recv_r.at[step - 1], ("zr", step - 1))
            z_send[step] = (z_part(4 - step) + z_recv_r[step - 1].astype(F32)).astype(BF16)
        message(lambda step=step: (z_send.at[step], z_recv_r.at[step]), ("zr", step), up, ring_sem.at[0]).start()
        if step == 1:
            mine = z_part(-3)
            received(z_recv_l.at[0, :, pl.ds(ZH, ZH)], ("zl", 0))
            z_send[5, :, :ZH] = mine[:, :ZH].astype(BF16)
            z_send[5, :, ZH:] = (mine[:, ZH:] + z_recv_l[0, :, ZH:].astype(F32)).astype(BF16)
        else:
            received(z_recv_l.at[step - 1], ("zl", step - 1))
            z_send[4 + step] = (z_part(step - 4) + z_recv_l[step - 1].astype(F32)).astype(BF16)
        message(lambda step=step: (z_send.at[4 + step], z_recv_l.at[step]), ("zl", step), down, ring_sem.at[0]).start()

    def y_step(step):
        mine = y_part(4 - step)
        if step == 1:
            received(y_recv_r.at[0, pl.ds(0, YH)], ("yr", 0))
            y_send[1, :YH] = (mine[:YH] + y_recv_r[0, :YH].astype(F32)).astype(BF16)
            y_send[1, YH:] = mine[YH:].astype(BF16)
        else:
            received(y_recv_r.at[step - 1], ("yr", step - 1))
            y_send[step] = (mine + y_recv_r[step - 1].astype(F32)).astype(BF16)
        message(lambda step=step: (y_send.at[step], y_recv_r.at[step]), ("yr", step), up, ring_sem.at[1]).start()
        mine = y_part(step - 4)
        if step == 1:
            received(y_recv_l.at[0, pl.ds(YH, YH)], ("yl", 0))
            y_send[5, :YH] = mine[:YH].astype(BF16)
            y_send[5, YH:] = (mine[YH:] + y_recv_l[0, YH:].astype(F32)).astype(BF16)
        else:
            received(y_recv_l.at[step - 1], ("yl", step - 1))
            y_send[4 + step] = (mine + y_recv_l[step - 1].astype(F32)).astype(BF16)
        message(lambda step=step: (y_send.at[4 + step], y_recv_l.at[step]), ("yl", step), down, ring_sem.at[1]).start()

    def passage_products():
        def term(i):
            wide = pl.ds(pl.multiple_of(i * 2 * GROUP, 2 * GROUP), 2 * GROUP)
            grads = gt[:, :, :, wide].reshape(BATCHES * BATCH, 2 * GROUP)
            queries = sq[pl.ds(2 * i, 2)].reshape(2 * GROUP, DS)
            return nn(grads, queries).reshape(NCORE, BATCHES, 2, OWN, DS)

        gp2[...] = term(0)

        def body(i, carry):
            gp2[...] = gp2[...] + term(i)
            return carry

        lax.fori_loop(1, NZ // 2, body, 0)

    gp = gp2.at[0]

    def gp_of(h, where):
        b, s = place(h, where, 0)
        return gp[b, s]

    def gp_first():
        received(gps_recv, "gp sibling")
        gp[...] = gp[...] + gps_recv[...].astype(F32)
        for h in range(NYH):
            gp1_send[h] = gp_of(h, FAR).astype(BF16)
        send(lambda: (gp1_send.at[0], gp1_recv.at[0]), ("gp", RIGHT, 1), right)
        send(lambda: (gp1_send.at[1], gp1_recv.at[1]), ("gp", LEFT, 1), left)

    def gp_second():
        received(gp1_recv.at[0], ("gp", RIGHT, 1))
        gp2_send[0, 0] = (gp_of(0, RIGHT) + gp1_recv[0].astype(F32)).astype(BF16)
        gp2_send[0, 1] = gp_of(1, RIGHT).astype(BF16)
        send(lambda: (gp2_send.at[0], gp2_recv.at[0]), ("gp", RIGHT, 2), right)
        received(gp1_recv.at[1], ("gp", LEFT, 1))
        gp2_send[1, 0] = gp_of(0, LEFT).astype(BF16)
        gp2_send[1, 1] = (gp_of(1, LEFT) + gp1_recv[1].astype(F32)).astype(BF16)
        send(lambda: (gp2_send.at[1], gp2_recv.at[1]), ("gp", LEFT, 2), left)

    def gp_third():
        received(gp2_recv.at[0], ("gp", RIGHT, 2))
        received(gp2_recv.at[1], ("gp", LEFT, 2))
        gp3_send[...] = x_total(1).astype(BF16)
        send(lambda: (gp3_send, gp3_recv), "gp across", across)

    def x_total(h):
        return gp_of(h, SELF) + gp2_recv[0, h].astype(F32) + gp2_recv[1, h].astype(F32)

    def z_last():
        received(z_recv_r.at[3], ("zr", 3))
        received(z_recv_l.at[3], ("zl", 3))
        for y in range(NYL):
            gq[z, y, :ZF] = gq[z, y, :ZF] + z_recv_r[3, y].astype(F32) + z_recv_l[3, y].astype(F32)
        z_pair_send[...] = gq[z, 1 - yl, :ZF].astype(BF16)
        send(lambda: (z_pair_send, z_pair_recv), "z pair", y_mate)

    form(0, far)
    query_part(0)
    z_start()
    pair_copy(0).start()
    div_out[...] = cross * LN2 / t_sum - (t_max * LN2 + jnp.log(t_sum)) + (s_max * LN2 + jnp.log(s_sum))
    all_copies(stat_send, 0).wait_send()
    all_copies(res_recv, 2).wait_recv()
    form(1)

    def gradient_step(i, carry):
        query_part(i)
        form(i + 1)

        @pl.when(i == 2)
        def _():
            z_step(1)

        pair_copy(i).start()

        @pl.when(i == 4)
        def _():
            y_start()

        return carry

    lax.fori_loop(1, NZ - 1, gradient_step, 0)
    query_part(NZ - 1)
    pair_copy(NZ - 1).start()
    passage_products()
    gps_send[...] = gp2[1].astype(BF16)
    send(lambda: (gps_send, gps_recv), "gp sibling", sibling)
    z_step(2)
    y_step(1)
    gp_first()
    z_step(3)
    y_step(2)
    gp_second()
    all_copies(res_recv, 2).wait_send()
    z_last()
    y_step(3)
    gp_third()
    for i, ref in enumerate((z_send.at[pl.ds(0, 7)], y_send.at[pl.ds(0, 7)], y_pair_send)):
        message(lambda: (ref, ref), "ring", sibling, ring_sem.at[i]).wait_send()
    flush()

    mine = y_part(0)
    received(y_recv_r.at[3], ("yr", 3))
    received(y_recv_l.at[3], ("yl", 3))
    gq_out[:, ZF:] = (mine + y_recv_r[3].astype(F32) + y_recv_l[3].astype(F32)).T
    received(z_pair_recv, "z pair")
    gq_out[:, :ZF] = (gq[z, yl, :ZF] + z_pair_recv[...].astype(F32)).T
    received(gp3_recv, "gp across")
    gp_out[...] = x_total(0) + gp3_recv[...].astype(F32)


def deliver(gq_in, gp_in, div_in, gq_out, gp_out, div_out, gq, gp, div, in_sem, out_sem):
    parts = ((gq_in, gq, gq_out), (gp_in, gp, gp_out), (div_in, div, div_out))
    ins = [pltpu.make_async_copy(src, mid, in_sem.at[i]) for i, (src, mid, _) in enumerate(parts)]
    outs = [pltpu.make_async_copy(mid, dst, out_sem.at[i]) for i, (_, mid, dst) in enumerate(parts)]
    for copy in ins:
        copy.start()
    for arrive, leave in zip(ins, outs):
        arrive.wait()
        leave.start()
    for copy in outs:
        copy.wait()


def local(teacher_query, student_query, teacher_passages, student_passages):
    blocks = NYL, NZ, NCORE, ROWS
    hbm = pl.BlockSpec(memory_space=pl.ANY)
    vmem = pl.BlockSpec(memory_space=pltpu.VMEM)
    outs = (
        jax.ShapeDtypeStruct((ROWS, DS), F32),
        jax.ShapeDtypeStruct((OWN, DS), F32),
        jax.ShapeDtypeStruct((1, ROWS), F32),
    )
    results = pl.pallas_call(
        kernel,
        out_shape=outs,
        in_specs=[hbm] * 4,
        out_specs=(vmem,) * 3,
        scratch_shapes=[
            pltpu.VMEM((NZ, NYL, ROWS, DT), BF16),
            pltpu.VMEM((NZ, NYL, ROWS, DS), BF16),
            pltpu.VMEM((BATCHES * SLOTS, OWN, DT + DS), BF16),
            pltpu.VMEM((DS, BATCHES * BATCH), BF16),
            pltpu.VMEM((NZ, BATCHES // WIDE, WIDE, BATCH, GROUP), F32),
            pltpu.VMEM((NZ, BATCHES // WIDE, WIDE, BATCH, GROUP), F32),
            pltpu.VMEM((2, WIDE * BATCH, GROUP), F32),
            pltpu.VMEM((2, WIDE * BATCH, GROUP), F32),
            pltpu.VMEM((NCORE, BATCHES, BATCH // 2, NZ * GROUP), BF16),
            pltpu.VMEM((NZ, BATCHES // WIDE, 8, GROUP), F32),
            pltpu.VMEM((NZ, NYL, DS, ROWS), F32),
            pltpu.VMEM((OWNERS, 2, 8, ROWS), F32),
            pltpu.VMEM((OWNERS, 2, 8, ROWS), F32),
            pltpu.VMEM((OWNERS, 8, ROWS), F32),
            pltpu.VMEM((8, NYL, ZF, ROWS), BF16),
            pltpu.VMEM((4, NYL, ZF, ROWS), BF16),
            pltpu.VMEM((4, NYL, ZF, ROWS), BF16),
            pltpu.VMEM((ZF, ROWS), BF16),
            pltpu.VMEM((ZF, ROWS), BF16),
            pltpu.VMEM((NZ, YF, ROWS), BF16),
            pltpu.VMEM((NZ, YF, ROWS), BF16),
            pltpu.VMEM((8, YF, ROWS), BF16),
            pltpu.VMEM((4, YF, ROWS), BF16),
            pltpu.VMEM((4, YF, ROWS), BF16),
            pltpu.VMEM((NCORE, BATCHES, 2, OWN, DS), F32),
            pltpu.VMEM((BATCHES, 2, OWN, DS), BF16),
            pltpu.VMEM((BATCHES, 2, OWN, DS), BF16),
            pltpu.VMEM((NYH, OWN, DS), BF16),
            pltpu.VMEM((NYH, OWN, DS), BF16),
            pltpu.VMEM((2, NYH, OWN, DS), BF16),
            pltpu.VMEM((2, NYH, OWN, DS), BF16),
            pltpu.VMEM((OWN, DS), BF16),
            pltpu.VMEM((OWN, DS), BF16),
            pltpu.SemaphoreType.DMA((6,)),
            pltpu.SemaphoreType.REGULAR((4,)),
            pltpu.SemaphoreType.DMA,
            pltpu.SemaphoreType.DMA((3,)),
            pltpu.SemaphoreType.DMA((MESSAGES,)),
            pltpu.SemaphoreType.DMA((MESSAGES,)),
            pltpu.SemaphoreType.DMA((NZ,)),
            pltpu.SemaphoreType.DMA((4,)),
        ],
        compiler_params=pltpu.CompilerParams(
            collective_id=0, has_side_effects=True, vmem_limit_bytes=VMEM_BYTES
        ),
    )(
        teacher_query.reshape(*blocks, DT),
        student_query.reshape(*blocks, DS),
        teacher_passages,
        student_passages,
    )
    grad_query, grad_passage, divergence = pl.pallas_call(
        deliver,
        out_shape=outs,
        in_specs=[hbm] * 3,
        out_specs=(hbm,) * 3,
        scratch_shapes=[
            *(pltpu.VMEM(out.shape, out.dtype) for out in outs),
            pltpu.SemaphoreType.DMA((3,)),
            pltpu.SemaphoreType.DMA((3,)),
        ],
        compiler_params=pltpu.CompilerParams(vmem_limit_bytes=VMEM_BYTES),
    )(*results)
    return divergence.reshape(ROWS), grad_query, grad_passage


def solution(mesh):
    return jax.shard_map(
        local,
        mesh=mesh,
        in_specs=(
            P("query", None),
            P("query", None),
            P(("query", "corpus"), None),
            P(("query", "corpus"), None),
        ),
        out_specs=(
            P(("query", "corpus")),
            P(("query", "corpus"), None),
            P(("query", "corpus"), None),
        ),
        check_vma=False,
    )
```

```python
import functools
import math

import jax
import jax.numpy as jnp
from jax import lax
from jax.experimental import pallas as pl
from jax.experimental.pallas import tpu as pltpu
from jax.sharding import PartitionSpec as P

NX, NYH, NYL, NZ, NCORE = 4, 2, 2, 8, 2
OWN = 64
ROWS = 128
DT, DS = 1024, 384
BATCH = 256
GROUP = NYL * ROWS
OWNERS = NYL * NZ
HALF = OWN // 2
ZF = 128
YF = DS - ZF
LOG2E = math.log2(math.e)
LN2 = math.log(2.0)
F32, BF16 = jnp.float32, jnp.bfloat16
MESH = pl.DeviceIdType.MESH

SELF, LEFT, RIGHT, FAR = 0, 1, 2, 3


BATCH_SLOTS = (0, 2), (2, 4), (6, 4), (10, 4), (14, 2)
BATCHES = len(BATCH_SLOTS)
SLOTS = 16
PLACES = 8


def place(h, where):
    if h == 0:
        return {SELF: 0, LEFT: 1, RIGHT: 2, FAR: 4}[where]
    return {SELF: 3, LEFT: 5, RIGHT: 6, FAR: 7}[where]


def slot_of(h, where, core):
    p = place(h, where)
    for first, count in BATCH_SLOTS:
        if p < count // 2:
            return first + p + core * (count // 2)
        p -= count // 2


def div(a, b):
    return lax.div(a, jnp.int32(b))


def rem(a, b):
    return lax.rem(a, jnp.int32(b))


def nt(a, b):
    return lax.dot_general(a, b, (((1,), (1,)), ((), ())), preferred_element_type=F32)


def nn(a, b):
    return lax.dot_general(a, b, (((1,), (0,)), ((), ())), preferred_element_type=F32)


class Messages:
    def __init__(self):
        self.numbers = {}

    def __call__(self, name):
        return self.numbers.setdefault(name, len(self.numbers))


MESSAGES = 80
VMEM_BYTES = 60 * 1024 * 1024


def kernel(
    tq_hbm, sq_hbm, tp_hbm, sp_hbm,
    gq_out, gp_out, div_out,
    tq, sq, pbuf, spt, tw, sw, raw_a, raw_b, gt, stat, gq,
    stat_send, stat_recv, res_recv,
    z_send, z_recv_r, z_recv_l, z_pair_send, z_pair_recv,
    y_pair_send, y_pair_recv, y_send, y_recv_r, y_recv_l,
    gp, gps_send, gps_recv, gp1_send, gp1_recv, gp2_send, gp2_recv, gp3_send, gp3_recv,
    load_sem, known_sem, gather_sem, ring_sem, send_sem, recv_sem, yp_recv_sem, st_sem,
):
    t_scale = DT ** (-0.5) * LOG2E
    s_scale = DS ** (-0.5) * LOG2E
    factor = DS ** (-0.5)
    q = lax.axis_index("query")
    c = lax.axis_index("corpus")
    x, yh = div(q, NYH), rem(q, NYH)
    yl, z, k = div(c, NZ * NCORE), rem(div(c, NCORE), NZ), rem(c, NCORE)
    me = yl * NZ + z

    def at(x_, yh_, yl_, z_, k_):
        return (x_ * NYH + yh_, (yl_ * NZ + z_) * NCORE + k_)

    right, left = at(rem(x + 1, NX), yh, yl, z, k), at(rem(x + NX - 1, NX), yh, yl, z, k)
    across = at(x, 1 - yh, 1 - yl, z, k)
    sibling = at(x, yh, yl, z, 1 - k)
    up, down = at(x, yh, yl, rem(z + 1, NZ), k), at(x, yh, yl, rem(z + NZ - 1, NZ), k)
    y_mate = at(x, yh, 1 - yl, z, k)

    offsets = [(dy, dz) for dy in range(NYL) for dz in range(NZ) if (dy, dz) != (0, 0)]
    y_of = [yl, 1 - yl]
    z_of = [rem(z + dz, NZ) for dz in range(NZ)]

    def offset_device(dy, dz):
        return at(x, yh, y_of[dy], z_of[dz], k)

    def slot(h, where, core, half=None):
        i = slot_of(h, where, core)
        if half is None:
            return pbuf.at[i]
        return pbuf.at[i, pl.ds(half * HALF, HALF)]

    def both(b, core):
        first, count = BATCH_SLOTS[b]
        return pbuf.at[pl.ds(first + core * (count // 2), count // 2)]

    loads = [
        pltpu.make_async_copy(tp_hbm, pbuf.at[0, :, pl.ds(0, DT)], load_sem.at[0]),
        pltpu.make_async_copy(sp_hbm, pbuf.at[0, :, pl.ds(DT, DS)], load_sem.at[1]),
    ]
    for y in range(NYL):
        loads.append(pltpu.make_async_copy(tq_hbm.at[y, :, k], tq.at[:, y], load_sem.at[2 + y]))
        loads.append(pltpu.make_async_copy(sq_hbm.at[y, :, k], sq.at[:, y], load_sem.at[4 + y]))
    for load in loads:
        load.start()

    barrier = pltpu.get_barrier_semaphore()
    for device in (right, left, across, sibling, up, down, y_mate):
        pl.semaphore_signal(barrier, inc=1, device_id=device, device_id_type=MESH)
    pl.semaphore_wait(barrier, 7)
    loads[0].wait()
    loads[1].wait()

    number = Messages()
    sent = []

    def message(refs, name, device, out=None):
        i = number(name)
        src, dst = refs()
        return pltpu.make_async_remote_copy(
            src_ref=src, dst_ref=dst, send_sem=send_sem.at[i] if out is None else out, recv_sem=recv_sem.at[i],
            device_id=device, device_id_type=MESH,
        )

    def send(refs, name, device):
        message(refs, name, device).start()
        sent.append((refs, name, device))

    def flush():
        for args in sent:
            message(*args).wait_send()
        sent.clear()

    def received(ref, name):
        message(lambda: (ref, ref), name, sibling).wait_recv()

    def spread(refs, name, device):
        message(refs, name, device, gather_sem).start()

    def spread_wait():
        everything = pbuf.at[pl.ds(0, SLOTS - 1)]
        message(lambda: (everything, everything), "gather", sibling, gather_sem).wait_send()

    def half_to(where, half, device):
        spread(lambda: (slot(0, SELF, 0, half), slot(0, where, 0, half)), ("p", where, half), device)

    def sides_to_sibling(h):
        if h == 0:
            received(slot(0, LEFT, 0, 1), ("p", LEFT, 1))
            received(slot(0, RIGHT, 0, 0), ("p", RIGHT, 0))
        else:
            received(slot(1, LEFT, 0), ("p1", LEFT))
            received(slot(1, RIGHT, 0), ("p1", RIGHT))
        to_sibling(3 if h else 1)

    def to_sibling(b):
        spread(lambda: (both(b, 0), both(b, 1)), ("sib", b), sibling)

    def from_sibling(b):
        received(both(b, 1), ("sib", b))

    def far_on():
        received(slot(0, LEFT, 0, 0), ("p", LEFT, 0))
        spread(lambda: (slot(0, LEFT, 0, 0), slot(0, FAR, 0, 0)), ("far",), right)
        received(slot(0, RIGHT, 0, 1), ("p", RIGHT, 1))
        spread(lambda: (slot(0, RIGHT, 0, 1), slot(0, FAR, 0, 1)), ("far",), left)

    def across_on(half):
        received(slot(1, SELF, 0, half), ("across", half))
        spread(lambda: (slot(1, SELF, 0, half), slot(1, LEFT, 0, half)), ("p1", LEFT), right)
        spread(lambda: (slot(1, SELF, 0, half), slot(1, RIGHT, 0, half)), ("p1", RIGHT), left)

    def far_across():
        received(slot(0, FAR, 0), ("far",))
        spread(lambda: (slot(0, FAR, 0), slot(1, FAR, 0)), ("far across",), across)
        to_sibling(2)

    def far_from_across():
        received(slot(1, FAR, 0), ("far across",))
        to_sibling(4)

    half_to(LEFT, 0, right)
    half_to(RIGHT, 1, left)
    spread(lambda: (slot(0, SELF, 0, 0), slot(1, SELF, 0, 0)), ("across", 0), across)
    half_to(LEFT, 1, right)
    half_to(RIGHT, 0, left)
    spread(lambda: (slot(0, SELF, 0, 1), slot(1, SELF, 0, 1)), ("across", 1), across)
    to_sibling(0)

    def product(slots, n, raw):
        first, count = slots
        batch = pbuf[pl.ds(first, count)].reshape(count * OWN, DT + DS)
        raw[0] = nt(batch[:, :DT], tq[n].reshape(GROUP, DT))
        raw[1] = nt(batch[:, DT:], sq[n].reshape(GROUP, DS))

    def weights(b, row, n, raw, size):
        t = raw[0] * t_scale
        s = raw[1] * s_scale
        t_max = jnp.max(t, axis=0, keepdims=True)
        s_max = jnp.max(s, axis=0, keepdims=True)
        t_weight = jnp.exp2(t - t_max)
        s_weight = jnp.exp2(s - s_max)
        tw[n, pl.ds(row, size)] = t_weight
        sw[n, pl.ds(row, size)] = s_weight
        t_sum = jnp.sum(t_weight, axis=0, keepdims=True)
        s_sum = jnp.sum(s_weight, axis=0, keepdims=True)
        cross = jnp.sum(t_weight * (t - s), axis=0, keepdims=True)
        stat[n, b] = jnp.concatenate([t_max, t_sum, s_max, s_sum, cross, cross, cross, cross], axis=0)

    def small_scores(b, first):
        slots = BATCH_SLOTS[b]
        row, size = slots[0] * OWN, slots[1] * OWN
        half_a, half_b = raw_a.at[:, pl.ds(0, size)], raw_b.at[:, pl.ds(0, size)]

        def body(i, carry):
            n = first + 2 * i
            product(slots, n, half_a)
            product(slots, n + 1, half_b)
            weights(b, row, n, half_a, size)
            weights(b, row, n + 1, half_b, size)
            return carry

        lax.fori_loop(0, 2, body, 0)

    def turn():
        for core in range(NCORE):
            rows = [
                pbuf[first + core * (count // 2):first + (core + 1) * (count // 2)].reshape(-1, DT + DS)[:, DT:]
                for first, count in BATCH_SLOTS
            ]
            size = PLACES * OWN
            spt[:, core * size:(core + 1) * size] = jnp.concatenate(rows, axis=0).T

    def know(i):
        for device in (up, down, y_mate):
            pl.semaphore_signal(known_sem.at[i], inc=1, device_id=device, device_id_type=MESH)
        pl.semaphore_wait(known_sem.at[i], 3)

    know(0)
    far_on()
    across_on(0)
    know(1)
    for load in loads[2:]:
        load.wait()
    from_sibling(0)
    small_scores(0, 0)
    across_on(1)
    know(2)
    small_scores(0, 4)
    sides_to_sibling(0)
    know(3)

    def joined(parts):
        t_max = functools.reduce(jnp.maximum, [p[0:1] for p in parts])
        s_max = functools.reduce(jnp.maximum, [p[2:3] for p in parts])
        t_in = [jnp.exp2(p[0:1] - t_max) for p in parts]
        s_in = [jnp.exp2(p[2:3] - s_max) for p in parts]
        t_sum = functools.reduce(jnp.add, [p[1:2] * w for p, w in zip(parts, t_in)])
        s_sum = functools.reduce(jnp.add, [p[3:4] * w for p, w in zip(parts, s_in)])
        cross = functools.reduce(jnp.add, [p[4:5] * w for p, w in zip(parts, t_in)])
        return t_max, t_sum, s_max, s_sum, cross

    def stat_copy(dy, dz):
        return pltpu.make_async_remote_copy(
            src_ref=stat_send.at[y_of[dy] * NZ + z_of[dz]], dst_ref=stat_recv.at[dy * NZ + (NZ - dz) % NZ],
            send_sem=st_sem.at[0], recv_sem=st_sem.at[1],
            device_id=offset_device(dy, dz), device_id_type=MESH,
        )

    def res_copy(dy, dz):
        return pltpu.make_async_remote_copy(
            src_ref=res_recv.at[me], dst_ref=res_recv.at[me],
            send_sem=st_sem.at[2], recv_sem=st_sem.at[3],
            device_id=offset_device(dy, dz), device_id_type=MESH,
        )

    def all_copies(ref, first):
        others = ref.at[pl.ds(0, OWNERS - 1)]
        return pltpu.make_async_remote_copy(
            src_ref=others, dst_ref=others, send_sem=st_sem.at[first], recv_sem=st_sem.at[first + 1],
            device_id=sibling, device_id_type=MESH,
        )

    def leave(first):
        for n in range(first, first + 4):
            t_max, t_sum, s_max, s_sum, cross = joined([stat[n, b] for b in range(BATCHES)])
            whole = jnp.concatenate([t_max, t_sum, s_max, s_sum, cross, cross, cross, cross], axis=0)
            for y in range(NYL):
                stat_send[y * NZ + n, 0] = whole[:, y * ROWS:(y + 1) * ROWS]
            four = jnp.concatenate([whole[0:4, :ROWS], whole[0:4, ROWS:]], axis=0)
            for y in range(NYL):
                stat_send[y * NZ + (n + 4) % NZ, 1] = four

    large = 3 * NZ
    size = 4 * OWN

    def large_product(i, raw):
        product((2 + 4 * div(i, NZ), 4), rem(i, NZ), raw)

    def large_weights(i, raw):
        b = div(i, NZ)
        weights(1 + b, pl.multiple_of(2 * OWN + b * size, 2 * OWN), rem(i, NZ), raw, size)

    from_sibling(1)
    large_product(0, raw_a)

    def score_step(j, carry):
        @pl.when(j == 1)
        def _():
            far_across()

        @pl.when(j == 3)
        def _():
            from_sibling(2)

        @pl.when(j == 5)
        def _():
            sides_to_sibling(1)

        @pl.when(j == 7)
        def _():
            from_sibling(3)

        @pl.when(j == 9)
        def _():
            far_from_across()

        large_product(2 * j + 1, raw_b)
        large_weights(2 * j, raw_a)
        large_product(jnp.minimum(2 * j + 2, large - 1), raw_a)
        large_weights(2 * j + 1, raw_b)
        return carry

    lax.fori_loop(0, large // 2, score_step, 0)
    from_sibling(4)
    for first in (0, 4):
        small_scores(4, first)
        leave(first)
    for offset in offsets:
        stat_copy(*offset).start()
    stat_recv[0] = stat_send[me]
    turn()
    spread_wait()
    all_copies(stat_recv, 0).wait_recv()
    def totals(parts):
        t_max, t_sum, s_max, s_sum, cross = joined(parts)
        t_in, s_in = factor / t_sum, factor / s_sum
        result = jnp.concatenate([t_max, t_in, s_max, s_in, t_in, t_in, t_in, t_in], axis=0)
        return result, (t_max, t_sum, s_max, s_sum, cross)

    result, (t_max, t_sum, s_max, s_sum, cross) = totals([stat_recv[m, 0] for m in range(OWNERS)])
    res_recv[me] = result
    for offset in offsets:
        res_copy(*offset).start()
    far = []
    for y in range(NYL):
        parts = [stat_recv[m, 1, 4 * y:4 * y + 4] for m in range(OWNERS)]
        far.append(totals([jnp.concatenate([p, p], axis=0) for p in parts])[0])
    far = jnp.concatenate(far, axis=1)

    def group(away):
        return rem(z + NZ + away, NZ)

    def sequence(i):
        size = 4 - div(i + 1, 2)
        return group(size * (2 * rem(i, 2) - 1))

    def lanes(n):
        return pl.ds(pl.multiple_of(n * GROUP, GROUP), GROUP)

    def form(i, res=None):
        n = sequence(i)
        if res is None:
            res = jnp.concatenate([res_recv[n], res_recv[NZ + n]], axis=1)
        for b, (first, count) in enumerate(BATCH_SLOTS):
            st = stat[n, b]
            t_in = jnp.exp2(st[0:1] - res[0:1]) * res[1:2]
            s_in = jnp.exp2(st[2:3] - res[2:3]) * res[3:4]
            rows = pl.ds(first * OWN, count * OWN)
            grad = (sw[n, rows] * s_in - tw[n, rows] * t_in).astype(BF16)
            half = count * OWN // 2
            rows = pl.ds(first * OWN // 2, half)
            gt[0, rows, lanes(n)] = grad[:half]
            gt[1, rows, lanes(n)] = grad[half:]

    def pair_copy(i):
        return pltpu.make_async_remote_copy(
            src_ref=y_pair_send.at[i], dst_ref=y_pair_recv.at[i],
            send_sem=ring_sem.at[2], recv_sem=yp_recv_sem.at[i],
            device_id=y_mate, device_id_type=MESH,
        )

    def query_part(i):
        n = sequence(i)
        total = nn(spt[...], gt[:, :, lanes(n)].reshape(NCORE * PLACES * OWN, GROUP))
        gq[n, 0] = total[:, :ROWS]
        gq[n, 1] = total[:, ROWS:]
        y_pair_send[i] = gq[n, 1 - yl, ZF:].astype(BF16)

    def z_part(away):
        return gq[group(away), :, :ZF]

    def y_part(away):
        i = (4, 3, -3, 2, -2, 1, -1, 0).index(away)
        pair_copy(i).wait_recv()
        return gq[group(away), yl, ZF:] + y_pair_recv[i].astype(F32)

    ZH, YH = ZF // 2, YF // 2

    def z_start():
        far = z_part(4).astype(BF16)
        z_send[0] = far
        message(lambda: (z_send.at[0, :, pl.ds(0, ZH)], z_recv_r.at[0, :, pl.ds(0, ZH)]), ("zr", 0), up, ring_sem.at[0]).start()
        message(lambda: (z_send.at[0, :, pl.ds(ZH, ZH)], z_recv_l.at[0, :, pl.ds(ZH, ZH)]), ("zl", 0), down, ring_sem.at[0]).start()

    def y_start():
        y_send[0] = y_part(4).astype(BF16)
        message(lambda: (y_send.at[0, pl.ds(0, YH)], y_recv_r.at[0, pl.ds(0, YH)]), ("yr", 0), up, ring_sem.at[1]).start()
        message(lambda: (y_send.at[0, pl.ds(YH, YH)], y_recv_l.at[0, pl.ds(YH, YH)]), ("yl", 0), down, ring_sem.at[1]).start()

    def z_step(step):
        if step == 1:
            mine = z_part(3)
            received(z_recv_r.at[0, :, pl.ds(0, ZH)], ("zr", 0))
            z_send[1, :, :ZH] = (mine[:, :ZH] + z_recv_r[0, :, :ZH].astype(F32)).astype(BF16)
            z_send[1, :, ZH:] = mine[:, ZH:].astype(BF16)
        else:
            received(z_recv_r.at[step - 1], ("zr", step - 1))
            z_send[step] = (z_part(4 - step) + z_recv_r[step - 1].astype(F32)).astype(BF16)
        message(lambda step=step: (z_send.at[step], z_recv_r.at[step]), ("zr", step), up, ring_sem.at[0]).start()
        if step == 1:
            mine = z_part(-3)
            received(z_recv_l.at[0, :, pl.ds(ZH, ZH)], ("zl", 0))
            z_send[5, :, :ZH] = mine[:, :ZH].astype(BF16)
            z_send[5, :, ZH:] = (mine[:, ZH:] + z_recv_l[0, :, ZH:].astype(F32)).astype(BF16)
        else:
            received(z_recv_l.at[step - 1], ("zl", step - 1))
            z_send[4 + step] = (z_part(step - 4) + z_recv_l[step - 1].astype(F32)).astype(BF16)
        message(lambda step=step: (z_send.at[4 + step], z_recv_l.at[step]), ("zl", step), down, ring_sem.at[0]).start()

    def y_step(step):
        mine = y_part(4 - step)
        if step == 1:
            received(y_recv_r.at[0, pl.ds(0, YH)], ("yr", 0))
            y_send[1, :YH] = (mine[:YH] + y_recv_r[0, :YH].astype(F32)).astype(BF16)
            y_send[1, YH:] = mine[YH:].astype(BF16)
        else:
            received(y_recv_r.at[step - 1], ("yr", step - 1))
            y_send[step] = (mine + y_recv_r[step - 1].astype(F32)).astype(BF16)
        message(lambda step=step: (y_send.at[step], y_recv_r.at[step]), ("yr", step), up, ring_sem.at[1]).start()
        mine = y_part(step - 4)
        if step == 1:
            received(y_recv_l.at[0, pl.ds(YH, YH)], ("yl", 0))
            y_send[5, :YH] = mine[:YH].astype(BF16)
            y_send[5, YH:] = (mine[YH:] + y_recv_l[0, YH:].astype(F32)).astype(BF16)
        else:
            received(y_recv_l.at[step - 1], ("yl", step - 1))
            y_send[4 + step] = (mine + y_recv_l[step - 1].astype(F32)).astype(BF16)
        message(lambda step=step: (y_send.at[4 + step], y_recv_l.at[step]), ("yl", step), down, ring_sem.at[1]).start()

    def passage_part(core, to):
        def term(i):
            wide = pl.ds(pl.multiple_of(i * 2 * GROUP, 2 * GROUP), 2 * GROUP)
            queries = sq[pl.ds(2 * i, 2)].reshape(2 * GROUP, DS)
            return nn(gt[core, :, wide], queries).reshape(PLACES, OWN, DS)

        to[...] = term(0)

        def body(i, carry):
            to[...] = to[...] + term(i)
            return carry

        lax.fori_loop(1, NZ // 2, body, 0)

    def gp_of(h, where):
        return gp[place(h, where)]

    def gp_first():
        received(gps_recv, "gp sibling")
        gp[...] = gp[...] + gps_recv[...].astype(F32)
        for h in range(NYH):
            gp1_send[h] = gp_of(h, FAR).astype(BF16)
        send(lambda: (gp1_send.at[0], gp1_recv.at[0]), ("gp", RIGHT, 1), right)
        send(lambda: (gp1_send.at[1], gp1_recv.at[1]), ("gp", LEFT, 1), left)

    def gp_second():
        received(gp1_recv.at[0], ("gp", RIGHT, 1))
        gp2_send[0, 0] = (gp_of(0, RIGHT) + gp1_recv[0].astype(F32)).astype(BF16)
        gp2_send[0, 1] = gp_of(1, RIGHT).astype(BF16)
        send(lambda: (gp2_send.at[0], gp2_recv.at[0]), ("gp", RIGHT, 2), right)
        received(gp1_recv.at[1], ("gp", LEFT, 1))
        gp2_send[1, 0] = gp_of(0, LEFT).astype(BF16)
        gp2_send[1, 1] = (gp_of(1, LEFT) + gp1_recv[1].astype(F32)).astype(BF16)
        send(lambda: (gp2_send.at[1], gp2_recv.at[1]), ("gp", LEFT, 2), left)

    def gp_third():
        received(gp2_recv.at[0], ("gp", RIGHT, 2))
        received(gp2_recv.at[1], ("gp", LEFT, 2))
        gp3_send[...] = x_total(1).astype(BF16)
        send(lambda: (gp3_send, gp3_recv), "gp across", across)

    def x_total(h):
        return gp_of(h, SELF) + gp2_recv[0, h].astype(F32) + gp2_recv[1, h].astype(F32)

    def z_last():
        received(z_recv_r.at[3], ("zr", 3))
        received(z_recv_l.at[3], ("zl", 3))
        for y in range(NYL):
            gq[z, y, :ZF] = gq[z, y, :ZF] + z_recv_r[3, y].astype(F32) + z_recv_l[3, y].astype(F32)
        z_pair_send[...] = gq[z, 1 - yl, :ZF].astype(BF16)
        send(lambda: (z_pair_send, z_pair_recv), "z pair", y_mate)

    form(0, far)
    query_part(0)
    z_start()
    pair_copy(0).start()
    div_out[...] = cross * LN2 / t_sum - (t_max * LN2 + jnp.log(t_sum)) + (s_max * LN2 + jnp.log(s_sum))
    all_copies(stat_send, 0).wait_send()
    all_copies(res_recv, 2).wait_recv()
    form(1)

    def gradient_step(i, carry):
        query_part(i)
        form(i + 1)

        @pl.when(i == 2)
        def _():
            z_step(1)

        pair_copy(i).start()

        @pl.when(i == 4)
        def _():
            y_start()

        return carry

    lax.fori_loop(1, NZ - 1, gradient_step, 0)
    query_part(NZ - 1)
    pair_copy(NZ - 1).start()
    passage_part(1, gp)
    gps_send[...] = gp[...].astype(BF16)
    send(lambda: (gps_send, gps_recv), "gp sibling", sibling)
    z_step(2)
    y_step(1)
    passage_part(0, gp)
    gp_first()
    z_step(3)
    y_step(2)
    gp_second()
    all_copies(res_recv, 2).wait_send()
    z_last()
    y_step(3)
    gp_third()
    for i, ref in enumerate((z_send.at[pl.ds(0, 7)], y_send.at[pl.ds(0, 7)], y_pair_send)):
        message(lambda: (ref, ref), "ring", sibling, ring_sem.at[i]).wait_send()
    flush()

    mine = y_part(0)
    received(y_recv_r.at[3], ("yr", 3))
    received(y_recv_l.at[3], ("yl", 3))
    gq_out[:, ZF:] = (mine + y_recv_r[3].astype(F32) + y_recv_l[3].astype(F32)).T
    received(z_pair_recv, "z pair")
    gq_out[:, :ZF] = (gq[z, yl, :ZF] + z_pair_recv[...].astype(F32)).T
    received(gp3_recv, "gp across")
    gp_out[...] = x_total(0) + gp3_recv[...].astype(F32)


def deliver(gq_in, gp_in, div_in, gq_out, gp_out, div_out, gq, gp, div, in_sem, out_sem):
    parts = ((gq_in, gq, gq_out), (gp_in, gp, gp_out), (div_in, div, div_out))
    ins = [pltpu.make_async_copy(src, mid, in_sem.at[i]) for i, (src, mid, _) in enumerate(parts)]
    outs = [pltpu.make_async_copy(mid, dst, out_sem.at[i]) for i, (_, mid, dst) in enumerate(parts)]
    for copy in ins:
        copy.start()
    for arrive, leave in zip(ins, outs):
        arrive.wait()
        leave.start()
    for copy in outs:
        copy.wait()


def local(teacher_query, student_query, teacher_passages, student_passages):
    blocks = NYL, NZ, NCORE, ROWS
    hbm = pl.BlockSpec(memory_space=pl.ANY)
    vmem = pl.BlockSpec(memory_space=pltpu.VMEM)
    outs = (
        jax.ShapeDtypeStruct((ROWS, DS), F32),
        jax.ShapeDtypeStruct((OWN, DS), F32),
        jax.ShapeDtypeStruct((1, ROWS), F32),
    )
    results = pl.pallas_call(
        kernel,
        out_shape=outs,
        in_specs=[hbm] * 4,
        out_specs=(vmem,) * 3,
        scratch_shapes=[
            pltpu.VMEM((NZ, NYL, ROWS, DT), BF16),
            pltpu.VMEM((NZ, NYL, ROWS, DS), BF16),
            pltpu.VMEM((SLOTS, OWN, DT + DS), BF16),
            pltpu.VMEM((DS, SLOTS * OWN), BF16),
            pltpu.VMEM((NZ, SLOTS * OWN, GROUP), F32),
            pltpu.VMEM((NZ, SLOTS * OWN, GROUP), F32),
            pltpu.VMEM((2, BATCH, GROUP), F32),
            pltpu.VMEM((2, BATCH, GROUP), F32),
            pltpu.VMEM((NCORE, PLACES * OWN, NZ * GROUP), BF16),
            pltpu.VMEM((NZ, BATCHES, 8, GROUP), F32),
            pltpu.VMEM((NZ, NYL, DS, ROWS), F32),
            pltpu.VMEM((OWNERS, 2, 8, ROWS), F32),
            pltpu.VMEM((OWNERS, 2, 8, ROWS), F32),
            pltpu.VMEM((OWNERS, 8, ROWS), F32),
            pltpu.VMEM((8, NYL, ZF, ROWS), BF16),
            pltpu.VMEM((4, NYL, ZF, ROWS), BF16),
            pltpu.VMEM((4, NYL, ZF, ROWS), BF16),
            pltpu.VMEM((ZF, ROWS), BF16),
            pltpu.VMEM((ZF, ROWS), BF16),
            pltpu.VMEM((NZ, YF, ROWS), BF16),
            pltpu.VMEM((NZ, YF, ROWS), BF16),
            pltpu.VMEM((8, YF, ROWS), BF16),
            pltpu.VMEM((4, YF, ROWS), BF16),
            pltpu.VMEM((4, YF, ROWS), BF16),
            pltpu.VMEM((PLACES, OWN, DS), F32),
            pltpu.VMEM((PLACES, OWN, DS), BF16),
            pltpu.VMEM((PLACES, OWN, DS), BF16),
            pltpu.VMEM((NYH, OWN, DS), BF16),
            pltpu.VMEM((NYH, OWN, DS), BF16),
            pltpu.VMEM((2, NYH, OWN, DS), BF16),
            pltpu.VMEM((2, NYH, OWN, DS), BF16),
            pltpu.VMEM((OWN, DS), BF16),
            pltpu.VMEM((OWN, DS), BF16),
            pltpu.SemaphoreType.DMA((6,)),
            pltpu.SemaphoreType.REGULAR((4,)),
            pltpu.SemaphoreType.DMA,
            pltpu.SemaphoreType.DMA((3,)),
            pltpu.SemaphoreType.DMA((MESSAGES,)),
            pltpu.SemaphoreType.DMA((MESSAGES,)),
            pltpu.SemaphoreType.DMA((NZ,)),
            pltpu.SemaphoreType.DMA((4,)),
        ],
        compiler_params=pltpu.CompilerParams(
            collective_id=0, has_side_effects=True, vmem_limit_bytes=VMEM_BYTES
        ),
    )(
        teacher_query.reshape(*blocks, DT),
        student_query.reshape(*blocks, DS),
        teacher_passages,
        student_passages,
    )
    grad_query, grad_passage, divergence = pl.pallas_call(
        deliver,
        out_shape=outs,
        in_specs=[hbm] * 3,
        out_specs=(hbm,) * 3,
        scratch_shapes=[
            *(pltpu.VMEM(out.shape, out.dtype) for out in outs),
            pltpu.SemaphoreType.DMA((3,)),
            pltpu.SemaphoreType.DMA((3,)),
        ],
        compiler_params=pltpu.CompilerParams(vmem_limit_bytes=VMEM_BYTES),
    )(*results)
    return divergence.reshape(ROWS), grad_query, grad_passage


def solution(mesh):
    return jax.shard_map(
        local,
        mesh=mesh,
        in_specs=(
            P("query", None),
            P("query", None),
            P(("query", "corpus"), None),
            P(("query", "corpus"), None),
        ),
        out_specs=(
            P(("query", "corpus")),
            P(("query", "corpus"), None),
            P(("query", "corpus"), None),
        ),
        check_vma=False,
    )
```

```python
import functools
import math

import jax
import jax.numpy as jnp
from jax import lax
from jax.experimental import pallas as pl
from jax.experimental.pallas import tpu as pltpu
from jax.sharding import PartitionSpec as P

NX, NYH, NYL, NZ, NCORE = 4, 2, 2, 8, 2
OWN = 64
ROWS = 128
DT, DS = 1024, 384
BATCHES = 4
SLOTS = 4
BATCH = 256
GROUP = NYL * ROWS
OWNERS = NYL * NZ
HALF = OWN // 2
ZF = 128
YF = DS - ZF
LOG2E = math.log2(math.e)
LN2 = math.log(2.0)
F32, BF16 = jnp.float32, jnp.bfloat16
MESH = pl.DeviceIdType.MESH

SELF, LEFT, RIGHT, FAR = 0, 1, 2, 3


def place(h, where, core):
    if where == SELF:
        return 1, core * 2 + h
    if where == FAR:
        return 3, core * 2 + h
    return 2 * h, core * 2 + (where - LEFT)


def div(a, b):
    return lax.div(a, jnp.int32(b))


def rem(a, b):
    return lax.rem(a, jnp.int32(b))


def nt(a, b):
    return lax.dot_general(a, b, (((1,), (1,)), ((), ())), preferred_element_type=F32)


def nn(a, b):
    return lax.dot_general(a, b, (((1,), (0,)), ((), ())), preferred_element_type=F32)


class Messages:
    def __init__(self):
        self.numbers = {}

    def __call__(self, name):
        return self.numbers.setdefault(name, len(self.numbers))


MESSAGES = 80
VMEM_BYTES = 60 * 1024 * 1024


def kernel(
    tq_hbm, sq_hbm, tp_hbm, sp_hbm,
    gq_out, gp_out, div_out,
    tq, sq, pbuf, spt, tw, sw, gt, stat, gq,
    stat_send, stat_recv, res_recv,
    z_send, z_recv_r, z_recv_l, z_pair_send, z_pair_recv,
    y_pair_send, y_pair_recv, y_send, y_recv_r, y_recv_l,
    gp, gps_send, gps_recv, gp1_send, gp1_recv, gp2_send, gp2_recv, gp3_send, gp3_recv,
    load_sem, known_sem, gather_sem, ring_sem, send_sem, recv_sem, yp_recv_sem, st_sem,
):
    t_scale = DT ** (-0.5) * LOG2E
    s_scale = DS ** (-0.5) * LOG2E
    factor = DS ** (-0.5)
    q = lax.axis_index("query")
    c = lax.axis_index("corpus")
    x, yh = div(q, NYH), rem(q, NYH)
    yl, z, k = div(c, NZ * NCORE), rem(div(c, NCORE), NZ), rem(c, NCORE)
    me = yl * NZ + z

    def at(x_, yh_, yl_, z_, k_):
        return (x_ * NYH + yh_, (yl_ * NZ + z_) * NCORE + k_)

    right, left = at(rem(x + 1, NX), yh, yl, z, k), at(rem(x + NX - 1, NX), yh, yl, z, k)
    across = at(x, 1 - yh, 1 - yl, z, k)
    sibling = at(x, yh, yl, z, 1 - k)
    up, down = at(x, yh, yl, rem(z + 1, NZ), k), at(x, yh, yl, rem(z + NZ - 1, NZ), k)
    y_mate = at(x, yh, 1 - yl, z, k)

    offsets = [(dy, dz) for dy in range(NYL) for dz in range(NZ) if (dy, dz) != (0, 0)]
    y_of = [yl, 1 - yl]
    z_of = [rem(z + dz, NZ) for dz in range(NZ)]

    def offset_device(dy, dz):
        return at(x, yh, y_of[dy], z_of[dz], k)

    def slot(h, where, core, half=None):
        b, s = place(h, where, core)
        if half is None:
            return pbuf.at[b * SLOTS + s]
        return pbuf.at[b * SLOTS + s, pl.ds(half * HALF, HALF)]

    def both(b, core):
        return pbuf.at[pl.ds(b * SLOTS + core * 2, 2)]

    loads = [
        pltpu.make_async_copy(tp_hbm, pbuf.at[SLOTS, :, pl.ds(0, DT)], load_sem.at[0]),
        pltpu.make_async_copy(sp_hbm, pbuf.at[SLOTS, :, pl.ds(DT, DS)], load_sem.at[1]),
    ]
    for y in range(NYL):
        loads.append(pltpu.make_async_copy(tq_hbm.at[y, :, k], tq.at[:, y], load_sem.at[2 + y]))
        loads.append(pltpu.make_async_copy(sq_hbm.at[y, :, k], sq.at[:, y], load_sem.at[4 + y]))
    for load in loads:
        load.start()

    barrier = pltpu.get_barrier_semaphore()
    for device in (right, left, across, sibling, up, down, y_mate):
        pl.semaphore_signal(barrier, inc=1, device_id=device, device_id_type=MESH)
    pl.semaphore_wait(barrier, 7)
    loads[0].wait()
    loads[1].wait()

    number = Messages()
    sent = []

    def message(refs, name, device, out=None):
        i = number(name)
        src, dst = refs()
        return pltpu.make_async_remote_copy(
            src_ref=src, dst_ref=dst, send_sem=send_sem.at[i] if out is None else out, recv_sem=recv_sem.at[i],
            device_id=device, device_id_type=MESH,
        )

    def send(refs, name, device):
        message(refs, name, device).start()
        sent.append((refs, name, device))

    def flush():
        for args in sent:
            message(*args).wait_send()
        sent.clear()

    def received(ref, name):
        message(lambda: (ref, ref), name, sibling).wait_recv()

    def spread(refs, name, device):
        message(refs, name, device, gather_sem).start()

    def spread_wait():
        everything = pbuf.at[pl.ds(0, BATCHES * SLOTS - 1)]
        message(lambda: (everything, everything), "gather", sibling, gather_sem).wait_send()

    def half_to(where, half, device):
        spread(lambda: (slot(0, SELF, 0, half), slot(0, where, 0, half)), ("p", where, half), device)

    def sides_to_sibling(h):
        if h == 0:
            received(slot(0, LEFT, 0, 1), ("p", LEFT, 1))
            received(slot(0, RIGHT, 0, 0), ("p", RIGHT, 0))
        else:
            received(slot(1, LEFT, 0), ("p1", LEFT))
            received(slot(1, RIGHT, 0), ("p1", RIGHT))
        to_sibling(2 * h)

    def to_sibling(b):
        spread(lambda: (both(b, 0), both(b, 1)), ("sib", b), sibling)

    def from_sibling(b):
        received(both(b, 1), ("sib", b))

    def far_on():
        received(slot(0, LEFT, 0, 0), ("p", LEFT, 0))
        spread(lambda: (slot(0, LEFT, 0, 0), slot(0, FAR, 0, 0)), ("far",), right)
        received(slot(0, RIGHT, 0, 1), ("p", RIGHT, 1))
        spread(lambda: (slot(0, RIGHT, 0, 1), slot(0, FAR, 0, 1)), ("far",), left)

    def across_on(half):
        received(slot(1, SELF, 0, half), ("across", half))
        spread(lambda: (slot(1, SELF, 0, half), slot(1, LEFT, 0, half)), ("p1", LEFT), right)
        spread(lambda: (slot(1, SELF, 0, half), slot(1, RIGHT, 0, half)), ("p1", RIGHT), left)

    def far_across():
        received(slot(0, FAR, 0), ("far",))
        spread(lambda: (slot(0, FAR, 0), slot(1, FAR, 0)), ("far across",), across)

    def far_from_across():
        received(slot(1, FAR, 0), ("far across",))
        to_sibling(3)

    half_to(LEFT, 0, right)
    half_to(RIGHT, 1, left)
    spread(lambda: (slot(0, SELF, 0, 0), slot(1, SELF, 0, 0)), ("across", 0), across)
    half_to(LEFT, 1, right)
    half_to(RIGHT, 0, left)
    spread(lambda: (slot(0, SELF, 0, 1), slot(1, SELF, 0, 1)), ("across", 1), across)

    def scores(i):
        b, n = div(i, NZ), rem(i, NZ)
        batch = pbuf[pl.ds(b * SLOTS, SLOTS)].reshape(BATCH, DT + DS)
        t = nt(batch[:, :DT], tq[n].reshape(GROUP, DT)) * t_scale
        s = nt(batch[:, DT:], sq[n].reshape(GROUP, DS)) * s_scale
        t_max = jnp.max(t, axis=0, keepdims=True)
        s_max = jnp.max(s, axis=0, keepdims=True)
        t_weight = jnp.exp2(t - t_max)
        s_weight = jnp.exp2(s - s_max)
        tw[n, b] = t_weight
        sw[n, b] = s_weight
        t_sum = jnp.sum(t_weight, axis=0, keepdims=True)
        s_sum = jnp.sum(s_weight, axis=0, keepdims=True)
        cross = jnp.sum(t_weight * (t - s), axis=0, keepdims=True)
        stat[n, b] = jnp.concatenate([t_max, t_sum, s_max, s_sum, cross, cross, cross, cross], axis=0)

    def turn(b):
        turned = pbuf[b * SLOTS:(b + 1) * SLOTS].reshape(BATCH, DT + DS)[:, DT:].T
        part = BATCH // NCORE
        for core in range(NCORE):
            start = (core * BATCHES + b) * part
            spt[:, start:start + part] = turned[:, core * part:(core + 1) * part]

    def know(i):
        for device in (up, down, y_mate):
            pl.semaphore_signal(known_sem.at[i], inc=1, device_id=device, device_id_type=MESH)
        pl.semaphore_wait(known_sem.at[i], 3)

    know(0)
    far_on()
    across_on(0)
    across_on(1)
    to_sibling(1)
    know(1)
    sides_to_sibling(0)
    know(2)
    far_across()
    know(3)
    for load in loads[2:]:
        load.wait()

    def joined(parts):
        t_max = functools.reduce(jnp.maximum, [p[0:1] for p in parts])
        s_max = functools.reduce(jnp.maximum, [p[2:3] for p in parts])
        t_in = [jnp.exp2(p[0:1] - t_max) for p in parts]
        s_in = [jnp.exp2(p[2:3] - s_max) for p in parts]
        t_sum = functools.reduce(jnp.add, [p[1:2] * w for p, w in zip(parts, t_in)])
        s_sum = functools.reduce(jnp.add, [p[3:4] * w for p, w in zip(parts, s_in)])
        cross = functools.reduce(jnp.add, [p[4:5] * w for p, w in zip(parts, t_in)])
        return t_max, t_sum, s_max, s_sum, cross

    def stat_copy(dy, dz):
        return pltpu.make_async_remote_copy(
            src_ref=stat_send.at[y_of[dy] * NZ + z_of[dz]], dst_ref=stat_recv.at[dy * NZ + (NZ - dz) % NZ],
            send_sem=st_sem.at[0], recv_sem=st_sem.at[1],
            device_id=offset_device(dy, dz), device_id_type=MESH,
        )

    def res_copy(dy, dz):
        return pltpu.make_async_remote_copy(
            src_ref=res_recv.at[me], dst_ref=res_recv.at[me],
            send_sem=st_sem.at[2], recv_sem=st_sem.at[3],
            device_id=offset_device(dy, dz), device_id_type=MESH,
        )

    def all_copies(ref, first):
        others = ref.at[pl.ds(0, OWNERS - 1)]
        return pltpu.make_async_remote_copy(
            src_ref=others, dst_ref=others, send_sem=st_sem.at[first], recv_sem=st_sem.at[first + 1],
            device_id=sibling, device_id_type=MESH,
        )

    def gather_stats(n, carry):
        t_max, t_sum, s_max, s_sum, cross = joined([stat[n, b] for b in range(BATCHES)])
        whole = jnp.concatenate([t_max, t_sum, s_max, s_sum, cross, cross, cross, cross], axis=0)
        for y in range(NYL):
            stat_send[y * NZ + n, 0] = whole[:, y * ROWS:(y + 1) * ROWS]
        four = jnp.concatenate([whole[0:4, :ROWS], whole[0:4, ROWS:]], axis=0)
        for y in range(NYL):
            stat_send[y * NZ + rem(n + 4, NZ), 1] = four
        return carry

    from_sibling(0)

    def score_step(i, carry):
        @pl.when(i == 8)
        def _():
            from_sibling(1)

        @pl.when(i == 11)
        def _():
            sides_to_sibling(1)

        @pl.when(i == 15)
        def _():
            far_from_across()

        @pl.when(i == 16)
        def _():
            from_sibling(2)

        @pl.when(i == 24)
        def _():
            from_sibling(3)

        scores(i)
        return carry

    lax.fori_loop(0, BATCHES * NZ, score_step, 0)
    lax.fori_loop(0, NZ, gather_stats, 0, unroll=2)
    for offset in offsets:
        stat_copy(*offset).start()
    stat_recv[0] = stat_send[me]
    for b in range(BATCHES):
        turn(b)
    spread_wait()
    all_copies(stat_recv, 0).wait_recv()
    def totals(parts):
        t_max, t_sum, s_max, s_sum, cross = joined(parts)
        t_in, s_in = factor / t_sum, factor / s_sum
        result = jnp.concatenate([t_max, t_in, s_max, s_in, t_in, t_in, t_in, t_in], axis=0)
        return result, (t_max, t_sum, s_max, s_sum, cross)

    result, (t_max, t_sum, s_max, s_sum, cross) = totals([stat_recv[m, 0] for m in range(OWNERS)])
    res_recv[me] = result
    for offset in offsets:
        res_copy(*offset).start()
    far = []
    for y in range(NYL):
        parts = [stat_recv[m, 1, 4 * y:4 * y + 4] for m in range(OWNERS)]
        far.append(totals([jnp.concatenate([p, p], axis=0) for p in parts])[0])
    far = jnp.concatenate(far, axis=1)

    def group(away):
        return rem(z + NZ + away, NZ)

    def sequence(i):
        size = 4 - div(i + 1, 2)
        return group(size * (2 * rem(i, 2) - 1))

    def lanes(n):
        return pl.ds(pl.multiple_of(n * GROUP, GROUP), GROUP)

    def form(i, res=None):
        n = sequence(i)
        if res is None:
            res = jnp.concatenate([res_recv[n], res_recv[NZ + n]], axis=1)
        for b in range(BATCHES):
            st = stat[n, b]
            t_in = jnp.exp2(st[0:1] - res[0:1]) * res[1:2]
            s_in = jnp.exp2(st[2:3] - res[2:3]) * res[3:4]
            grad = (sw[n, b] * s_in - tw[n, b] * t_in).astype(BF16)
            gt[0, b, :, lanes(n)] = grad[:BATCH // 2]
            gt[1, b, :, lanes(n)] = grad[BATCH // 2:]

    def pair_copy(i):
        return pltpu.make_async_remote_copy(
            src_ref=y_pair_send.at[i], dst_ref=y_pair_recv.at[i],
            send_sem=ring_sem.at[2], recv_sem=yp_recv_sem.at[i],
            device_id=y_mate, device_id_type=MESH,
        )

    def query_part(i):
        n = sequence(i)
        total = nn(spt[...], gt[:, :, :, lanes(n)].reshape(NCORE * BATCHES * BATCH // 2, GROUP))
        gq[n, 0] = total[:, :ROWS]
        gq[n, 1] = total[:, ROWS:]
        y_pair_send[i] = gq[n, 1 - yl, ZF:].astype(BF16)

    def z_part(away):
        return gq[group(away), :, :ZF]

    def y_part(away):
        i = (4, 3, -3, 2, -2, 1, -1, 0).index(away)
        pair_copy(i).wait_recv()
        return gq[group(away), yl, ZF:] + y_pair_recv[i].astype(F32)

    ZH, YH = ZF // 2, YF // 2

    def z_start():
        far = z_part(4).astype(BF16)
        z_send[0] = far
        message(lambda: (z_send.at[0, :, pl.ds(0, ZH)], z_recv_r.at[0, :, pl.ds(0, ZH)]), ("zr", 0), up, ring_sem.at[0]).start()
        message(lambda: (z_send.at[0, :, pl.ds(ZH, ZH)], z_recv_l.at[0, :, pl.ds(ZH, ZH)]), ("zl", 0), down, ring_sem.at[0]).start()

    def y_start():
        y_send[0] = y_part(4).astype(BF16)
        message(lambda: (y_send.at[0, pl.ds(0, YH)], y_recv_r.at[0, pl.ds(0, YH)]), ("yr", 0), up, ring_sem.at[1]).start()
        message(lambda: (y_send.at[0, pl.ds(YH, YH)], y_recv_l.at[0, pl.ds(YH, YH)]), ("yl", 0), down, ring_sem.at[1]).start()

    def z_step(step):
        if step == 1:
            mine = z_part(3)
            received(z_recv_r.at[0, :, pl.ds(0, ZH)], ("zr", 0))
            z_send[1, :, :ZH] = (mine[:, :ZH] + z_recv_r[0, :, :ZH].astype(F32)).astype(BF16)
            z_send[1, :, ZH:] = mine[:, ZH:].astype(BF16)
        else:
            received(z_recv_r.at[step - 1], ("zr", step - 1))
            z_send[step] = (z_part(4 - step) + z_recv_r[step - 1].astype(F32)).astype(BF16)
        message(lambda step=step: (z_send.at[step], z_recv_r.at[step]), ("zr", step), up, ring_sem.at[0]).start()
        if step == 1:
            mine = z_part(-3)
            received(z_recv_l.at[0, :, pl.ds(ZH, ZH)], ("zl", 0))
            z_send[5, :, :ZH] = mine[:, :ZH].astype(BF16)
            z_send[5, :, ZH:] = (mine[:, ZH:] + z_recv_l[0, :, ZH:].astype(F32)).astype(BF16)
        else:
            received(z_recv_l.at[step - 1], ("zl", step - 1))
            z_send[4 + step] = (z_part(step - 4) + z_recv_l[step - 1].astype(F32)).astype(BF16)
        message(lambda step=step: (z_send.at[4 + step], z_recv_l.at[step]), ("zl", step), down, ring_sem.at[0]).start()

    def y_step(step):
        mine = y_part(4 - step)
        if step == 1:
            received(y_recv_r.at[0, pl.ds(0, YH)], ("yr", 0))
            y_send[1, :YH] = (mine[:YH] + y_recv_r[0, :YH].astype(F32)).astype(BF16)
            y_send[1, YH:] = mine[YH:].astype(BF16)
        else:
            received(y_recv_r.at[step - 1], ("yr", step - 1))
            y_send[step] = (mine + y_recv_r[step - 1].astype(F32)).astype(BF16)
        message(lambda step=step: (y_send.at[step], y_recv_r.at[step]), ("yr", step), up, ring_sem.at[1]).start()
        mine = y_part(step - 4)
        if step == 1:
            received(y_recv_l.at[0, pl.ds(YH, YH)], ("yl", 0))
            y_send[5, :YH] = mine[:YH].astype(BF16)
            y_send[5, YH:] = (mine[YH:] + y_recv_l[0, YH:].astype(F32)).astype(BF16)
        else:
            received(y_recv_l.at[step - 1], ("yl", step - 1))
            y_send[4 + step] = (mine + y_recv_l[step - 1].astype(F32)).astype(BF16)
        message(lambda step=step: (y_send.at[4 + step], y_recv_l.at[step]), ("yl", step), down, ring_sem.at[1]).start()

    def passage_part(core):
        gp[...] = jnp.zeros_like(gp)

        def body(n, carry):
            grads = gt[core, :, :, lanes(n)].reshape(BATCHES * BATCH // 2, GROUP)
            term = nn(grads, sq[n].reshape(GROUP, DS))
            gp[...] = gp[...] + term.reshape(BATCHES, 2, OWN, DS)
            return carry

        lax.fori_loop(0, NZ, body, 0)

    def gp_of(h, where):
        b, s = place(h, where, 0)
        return gp[b, s]

    def gp_first():
        received(gps_recv, "gp sibling")
        gp[...] = gp[...] + gps_recv[...].astype(F32)
        for h in range(NYH):
            gp1_send[h] = gp_of(h, FAR).astype(BF16)
        send(lambda: (gp1_send.at[0], gp1_recv.at[0]), ("gp", RIGHT, 1), right)
        send(lambda: (gp1_send.at[1], gp1_recv.at[1]), ("gp", LEFT, 1), left)

    def gp_second():
        received(gp1_recv.at[0], ("gp", RIGHT, 1))
        gp2_send[0, 0] = (gp_of(0, RIGHT) + gp1_recv[0].astype(F32)).astype(BF16)
        gp2_send[0, 1] = gp_of(1, RIGHT).astype(BF16)
        send(lambda: (gp2_send.at[0], gp2_recv.at[0]), ("gp", RIGHT, 2), right)
        received(gp1_recv.at[1], ("gp", LEFT, 1))
        gp2_send[1, 0] = gp_of(0, LEFT).astype(BF16)
        gp2_send[1, 1] = (gp_of(1, LEFT) + gp1_recv[1].astype(F32)).astype(BF16)
        send(lambda: (gp2_send.at[1], gp2_recv.at[1]), ("gp", LEFT, 2), left)

    def gp_third():
        received(gp2_recv.at[0], ("gp", RIGHT, 2))
        received(gp2_recv.at[1], ("gp", LEFT, 2))
        gp3_send[...] = x_total(1).astype(BF16)
        send(lambda: (gp3_send, gp3_recv), "gp across", across)

    def x_total(h):
        return gp_of(h, SELF) + gp2_recv[0, h].astype(F32) + gp2_recv[1, h].astype(F32)

    def z_last():
        received(z_recv_r.at[3], ("zr", 3))
        received(z_recv_l.at[3], ("zl", 3))
        for y in range(NYL):
            gq[z, y, :ZF] = gq[z, y, :ZF] + z_recv_r[3, y].astype(F32) + z_recv_l[3, y].astype(F32)
        z_pair_send[...] = gq[z, 1 - yl, :ZF].astype(BF16)
        send(lambda: (z_pair_send, z_pair_recv), "z pair", y_mate)

    form(0, far)
    query_part(0)
    z_start()
    pair_copy(0).start()
    div_out[...] = cross * LN2 / t_sum - (t_max * LN2 + jnp.log(t_sum)) + (s_max * LN2 + jnp.log(s_sum))
    all_copies(stat_send, 0).wait_send()
    all_copies(res_recv, 2).wait_recv()
    form(1)

    def gradient_step(i, carry):
        query_part(i)
        form(i + 1)

        @pl.when(i == 2)
        def _():
            z_step(1)

        pair_copy(i).start()

        @pl.when(i == 4)
        def _():
            y_start()

        return carry

    lax.fori_loop(1, NZ - 1, gradient_step, 0)
    query_part(NZ - 1)
    pair_copy(NZ - 1).start()

    def passage_step(i, carry):
        passage_part(1 - i)

        @pl.when(i == 0)
        def _():
            gps_send[...] = gp[...].astype(BF16)
            send(lambda: (gps_send, gps_recv), "gp sibling", sibling)
            z_step(2)
            y_step(1)

        return carry

    lax.fori_loop(0, 2, passage_step, 0)
    gp_first()
    z_step(3)
    y_step(2)
    gp_second()
    all_copies(res_recv, 2).wait_send()
    z_last()
    y_step(3)
    gp_third()
    for i, ref in enumerate((z_send.at[pl.ds(0, 7)], y_send.at[pl.ds(0, 7)], y_pair_send)):
        message(lambda: (ref, ref), "ring", sibling, ring_sem.at[i]).wait_send()
    flush()

    mine = y_part(0)
    received(y_recv_r.at[3], ("yr", 3))
    received(y_recv_l.at[3], ("yl", 3))
    gq_out[:, ZF:] = (mine + y_recv_r[3].astype(F32) + y_recv_l[3].astype(F32)).T
    received(z_pair_recv, "z pair")
    gq_out[:, :ZF] = (gq[z, yl, :ZF] + z_pair_recv[...].astype(F32)).T
    received(gp3_recv, "gp across")
    gp_out[...] = x_total(0) + gp3_recv[...].astype(F32)


def deliver(gq_in, gp_in, div_in, gq_out, gp_out, div_out, gq, gp, div, in_sem, out_sem):
    parts = ((gq_in, gq, gq_out), (gp_in, gp, gp_out), (div_in, div, div_out))
    ins = [pltpu.make_async_copy(src, mid, in_sem.at[i]) for i, (src, mid, _) in enumerate(parts)]
    outs = [pltpu.make_async_copy(mid, dst, out_sem.at[i]) for i, (_, mid, dst) in enumerate(parts)]
    for copy in ins:
        copy.start()
    for arrive, leave in zip(ins, outs):
        arrive.wait()
        leave.start()
    for copy in outs:
        copy.wait()


def local(teacher_query, student_query, teacher_passages, student_passages):
    blocks = NYL, NZ, NCORE, ROWS
    hbm = pl.BlockSpec(memory_space=pl.ANY)
    vmem = pl.BlockSpec(memory_space=pltpu.VMEM)
    outs = (
        jax.ShapeDtypeStruct((ROWS, DS), F32),
        jax.ShapeDtypeStruct((OWN, DS), F32),
        jax.ShapeDtypeStruct((1, ROWS), F32),
    )
    results = pl.pallas_call(
        kernel,
        out_shape=outs,
        in_specs=[hbm] * 4,
        out_specs=(vmem,) * 3,
        scratch_shapes=[
            pltpu.VMEM((NZ, NYL, ROWS, DT), BF16),
            pltpu.VMEM((NZ, NYL, ROWS, DS), BF16),
            pltpu.VMEM((BATCHES * SLOTS, OWN, DT + DS), BF16),
            pltpu.VMEM((DS, BATCHES * BATCH), BF16),
            pltpu.VMEM((NZ, BATCHES, BATCH, GROUP), F32),
            pltpu.VMEM((NZ, BATCHES, BATCH, GROUP), F32),
            pltpu.VMEM((NCORE, BATCHES, BATCH // 2, NZ * GROUP), BF16),
            pltpu.VMEM((NZ, BATCHES, 8, GROUP), F32),
            pltpu.VMEM((NZ, NYL, DS, ROWS), F32),
            pltpu.VMEM((OWNERS, 2, 8, ROWS), F32),
            pltpu.VMEM((OWNERS, 2, 8, ROWS), F32),
            pltpu.VMEM((OWNERS, 8, ROWS), F32),
            pltpu.VMEM((8, NYL, ZF, ROWS), BF16),
            pltpu.VMEM((4, NYL, ZF, ROWS), BF16),
            pltpu.VMEM((4, NYL, ZF, ROWS), BF16),
            pltpu.VMEM((ZF, ROWS), BF16),
            pltpu.VMEM((ZF, ROWS), BF16),
            pltpu.VMEM((NZ, YF, ROWS), BF16),
            pltpu.VMEM((NZ, YF, ROWS), BF16),
            pltpu.VMEM((8, YF, ROWS), BF16),
            pltpu.VMEM((4, YF, ROWS), BF16),
            pltpu.VMEM((4, YF, ROWS), BF16),
            pltpu.VMEM((BATCHES, 2, OWN, DS), F32),
            pltpu.VMEM((BATCHES, 2, OWN, DS), BF16),
            pltpu.VMEM((BATCHES, 2, OWN, DS), BF16),
            pltpu.VMEM((NYH, OWN, DS), BF16),
            pltpu.VMEM((NYH, OWN, DS), BF16),
            pltpu.VMEM((2, NYH, OWN, DS), BF16),
            pltpu.VMEM((2, NYH, OWN, DS), BF16),
            pltpu.VMEM((OWN, DS), BF16),
            pltpu.VMEM((OWN, DS), BF16),
            pltpu.SemaphoreType.DMA((6,)),
            pltpu.SemaphoreType.REGULAR((4,)),
            pltpu.SemaphoreType.DMA,
            pltpu.SemaphoreType.DMA((3,)),
            pltpu.SemaphoreType.DMA((MESSAGES,)),
            pltpu.SemaphoreType.DMA((MESSAGES,)),
            pltpu.SemaphoreType.DMA((NZ,)),
            pltpu.SemaphoreType.DMA((4,)),
        ],
        compiler_params=pltpu.CompilerParams(
            collective_id=0, has_side_effects=True, vmem_limit_bytes=VMEM_BYTES
        ),
    )(
        teacher_query.reshape(*blocks, DT),
        student_query.reshape(*blocks, DS),
        teacher_passages,
        student_passages,
    )
    grad_query, grad_passage, divergence = pl.pallas_call(
        deliver,
        out_shape=outs,
        in_specs=[hbm] * 3,
        out_specs=(hbm,) * 3,
        scratch_shapes=[
            *(pltpu.VMEM(out.shape, out.dtype) for out in outs),
            pltpu.SemaphoreType.DMA((3,)),
            pltpu.SemaphoreType.DMA((3,)),
        ],
        compiler_params=pltpu.CompilerParams(vmem_limit_bytes=VMEM_BYTES),
    )(*results)
    return divergence.reshape(ROWS), grad_query, grad_passage


def solution(mesh):
    return jax.shard_map(
        local,
        mesh=mesh,
        in_specs=(
            P("query", None),
            P("query", None),
            P(("query", "corpus"), None),
            P(("query", "corpus"), None),
        ),
        out_specs=(
            P(("query", "corpus")),
            P(("query", "corpus"), None),
            P(("query", "corpus"), None),
        ),
        check_vma=False,
    )
```

```python
import functools
import math

import jax
import jax.numpy as jnp
from jax import lax
from jax.experimental import pallas as pl
from jax.experimental.pallas import tpu as pltpu
from jax.sharding import PartitionSpec as P

NX, NYH, NYL, NZ, NCORE = 4, 2, 2, 8, 2
OWN = 64
ROWS = 128
DT, DS = 1024, 384
BATCHES = 4
SLOTS = 4
BATCH = 256
GROUP = NYL * ROWS
OWNERS = NYL * NZ
HALF = OWN // 2
ZF = 128
YF = DS - ZF
LOG2E = math.log2(math.e)
LN2 = math.log(2.0)
F32, BF16 = jnp.float32, jnp.bfloat16
MESH = pl.DeviceIdType.MESH

SELF, LEFT, RIGHT, FAR = 0, 1, 2, 3


def place(h, where, core):
    if where == SELF:
        return 1, core * 2 + h
    if where == FAR:
        return 3, core * 2 + h
    return 2 * h, core * 2 + (where - LEFT)


def div(a, b):
    return lax.div(a, jnp.int32(b))


def rem(a, b):
    return lax.rem(a, jnp.int32(b))


def nt(a, b):
    return lax.dot_general(a, b, (((1,), (1,)), ((), ())), preferred_element_type=F32)


def nn(a, b):
    return lax.dot_general(a, b, (((1,), (0,)), ((), ())), preferred_element_type=F32)


class Messages:
    def __init__(self):
        self.numbers = {}

    def __call__(self, name):
        return self.numbers.setdefault(name, len(self.numbers))


MESSAGES = 80
VMEM_BYTES = 60 * 1024 * 1024


def kernel(
    tq_hbm, sq_hbm, tp_hbm, sp_hbm,
    gq_out, gp_out, div_out,
    tq, sq, pbuf, spt, tw, sw, raw_a, raw_b, top_a, top_b, gt_a, gt_b, stat, gq,
    stat_send, stat_recv, res_recv,
    z_send, z_recv_r, z_recv_l, z_pair_send, z_pair_recv,
    y_pair_send, y_pair_recv, y_send, y_recv_r, y_recv_l,
    gp, gps_send, gps_recv, gp1_send, gp1_recv, gp2_send, gp2_recv, gp3_send, gp3_recv,
    load_sem, known_sem, gather_sem, ring_sem, send_sem, recv_sem, yp_recv_sem, st_sem,
):
    t_scale = DT ** (-0.5) * LOG2E
    s_scale = DS ** (-0.5) * LOG2E
    factor = DS ** (-0.5)
    q = lax.axis_index("query")
    c = lax.axis_index("corpus")
    x, yh = div(q, NYH), rem(q, NYH)
    yl, z, k = div(c, NZ * NCORE), rem(div(c, NCORE), NZ), rem(c, NCORE)
    me = yl * NZ + z

    def at(x_, yh_, yl_, z_, k_):
        return (x_ * NYH + yh_, (yl_ * NZ + z_) * NCORE + k_)

    right, left = at(rem(x + 1, NX), yh, yl, z, k), at(rem(x + NX - 1, NX), yh, yl, z, k)
    across = at(x, 1 - yh, 1 - yl, z, k)
    sibling = at(x, yh, yl, z, 1 - k)
    up, down = at(x, yh, yl, rem(z + 1, NZ), k), at(x, yh, yl, rem(z + NZ - 1, NZ), k)
    y_mate = at(x, yh, 1 - yl, z, k)

    offsets = [(dy, dz) for dy in range(NYL) for dz in range(NZ) if (dy, dz) != (0, 0)]
    y_of = [yl, 1 - yl]
    z_of = [rem(z + dz, NZ) for dz in range(NZ)]

    def offset_device(dy, dz):
        return at(x, yh, y_of[dy], z_of[dz], k)

    def slot(h, where, core, half=None):
        b, s = place(h, where, core)
        if half is None:
            return pbuf.at[b * SLOTS + s]
        return pbuf.at[b * SLOTS + s, pl.ds(half * HALF, HALF)]

    def both(b, core):
        return pbuf.at[pl.ds(b * SLOTS + core * 2, 2)]

    loads = [
        pltpu.make_async_copy(tp_hbm, pbuf.at[SLOTS, :, pl.ds(0, DT)], load_sem.at[0]),
        pltpu.make_async_copy(sp_hbm, pbuf.at[SLOTS, :, pl.ds(DT, DS)], load_sem.at[1]),
    ]
    for y in range(NYL):
        loads.append(pltpu.make_async_copy(tq_hbm.at[y, :, k], tq.at[:, y], load_sem.at[2 + y]))
        loads.append(pltpu.make_async_copy(sq_hbm.at[y, :, k], sq.at[:, y], load_sem.at[4 + y]))
    for load in loads:
        load.start()

    barrier = pltpu.get_barrier_semaphore()
    for device in (right, left, across, sibling, up, down, y_mate):
        pl.semaphore_signal(barrier, inc=1, device_id=device, device_id_type=MESH)
    pl.semaphore_wait(barrier, 7)
    loads[0].wait()
    loads[1].wait()

    number = Messages()
    sent = []

    def message(refs, name, device, out=None):
        i = number(name)
        src, dst = refs()
        return pltpu.make_async_remote_copy(
            src_ref=src, dst_ref=dst, send_sem=send_sem.at[i] if out is None else out, recv_sem=recv_sem.at[i],
            device_id=device, device_id_type=MESH,
        )

    def send(refs, name, device):
        message(refs, name, device).start()
        sent.append((refs, name, device))

    def flush():
        for args in sent:
            message(*args).wait_send()
        sent.clear()

    def received(ref, name):
        message(lambda: (ref, ref), name, sibling).wait_recv()

    def spread(refs, name, device):
        message(refs, name, device, gather_sem).start()

    def spread_wait():
        everything = pbuf.at[pl.ds(0, BATCHES * SLOTS - 1)]
        message(lambda: (everything, everything), "gather", sibling, gather_sem).wait_send()

    def half_to(where, half, device):
        spread(lambda: (slot(0, SELF, 0, half), slot(0, where, 0, half)), ("p", where, half), device)

    def sides_to_sibling(h):
        if h == 0:
            received(slot(0, LEFT, 0, 1), ("p", LEFT, 1))
            received(slot(0, RIGHT, 0, 0), ("p", RIGHT, 0))
        else:
            received(slot(1, LEFT, 0), ("p1", LEFT))
            received(slot(1, RIGHT, 0), ("p1", RIGHT))
        to_sibling(2 * h)

    def to_sibling(b):
        spread(lambda: (both(b, 0), both(b, 1)), ("sib", b), sibling)

    def from_sibling(b):
        received(both(b, 1), ("sib", b))

    def far_on():
        received(slot(0, LEFT, 0, 0), ("p", LEFT, 0))
        spread(lambda: (slot(0, LEFT, 0, 0), slot(0, FAR, 0, 0)), ("far",), right)
        received(slot(0, RIGHT, 0, 1), ("p", RIGHT, 1))
        spread(lambda: (slot(0, RIGHT, 0, 1), slot(0, FAR, 0, 1)), ("far",), left)

    def across_on(half):
        received(slot(1, SELF, 0, half), ("across", half))
        spread(lambda: (slot(1, SELF, 0, half), slot(1, LEFT, 0, half)), ("p1", LEFT), right)
        spread(lambda: (slot(1, SELF, 0, half), slot(1, RIGHT, 0, half)), ("p1", RIGHT), left)

    def far_across():
        received(slot(0, FAR, 0), ("far",))
        spread(lambda: (slot(0, FAR, 0), slot(1, FAR, 0)), ("far across",), across)

    def far_from_across():
        received(slot(1, FAR, 0), ("far across",))
        to_sibling(3)

    half_to(LEFT, 0, right)
    half_to(RIGHT, 1, left)
    spread(lambda: (slot(0, SELF, 0, 0), slot(1, SELF, 0, 0)), ("across", 0), across)
    half_to(LEFT, 1, right)
    half_to(RIGHT, 0, left)
    spread(lambda: (slot(0, SELF, 0, 1), slot(1, SELF, 0, 1)), ("across", 1), across)

    def product(i, raw, top):
        b, n = div(i, NZ), rem(i, NZ)
        batch = pbuf[pl.ds(b * SLOTS, SLOTS)].reshape(BATCH, DT + DS)
        t = nt(batch[:, :DT], tq[n].reshape(GROUP, DT)) * t_scale
        raw[0] = t
        top[0:1] = jnp.max(t, axis=0, keepdims=True)
        s = nt(batch[:, DT:], sq[n].reshape(GROUP, DS)) * s_scale
        raw[1] = s
        top[1:2] = jnp.max(s, axis=0, keepdims=True)

    def weights(i, raw, top):
        b, n = div(i, NZ), rem(i, NZ)
        t, s = raw[0], raw[1]
        t_max, s_max = top[0:1], top[1:2]
        t_weight = jnp.exp2(t - t_max)
        s_weight = jnp.exp2(s - s_max)
        tw[n, b] = t_weight
        sw[n, b] = s_weight
        t_sum = jnp.sum(t_weight, axis=0, keepdims=True)
        s_sum = jnp.sum(s_weight, axis=0, keepdims=True)
        cross = jnp.sum(t_weight * (t - s), axis=0, keepdims=True)
        stat[n, b] = jnp.concatenate([t_max, t_sum, s_max, s_sum, cross, cross, cross, cross], axis=0)

    def turn(b):
        turned = pbuf[b * SLOTS:(b + 1) * SLOTS].reshape(BATCH, DT + DS)[:, DT:].T
        part = BATCH // NCORE
        for core in range(NCORE):
            start = (core * BATCHES + b) * part
            spt[:, start:start + part] = turned[:, core * part:(core + 1) * part]

    def know(i):
        for device in (up, down, y_mate):
            pl.semaphore_signal(known_sem.at[i], inc=1, device_id=device, device_id_type=MESH)
        pl.semaphore_wait(known_sem.at[i], 3)

    know(0)
    far_on()
    across_on(0)
    across_on(1)
    to_sibling(1)
    know(1)
    sides_to_sibling(0)
    know(2)
    far_across()
    know(3)
    for load in loads[2:]:
        load.wait()

    def joined(parts):
        t_max = functools.reduce(jnp.maximum, [p[0:1] for p in parts])
        s_max = functools.reduce(jnp.maximum, [p[2:3] for p in parts])
        t_in = [jnp.exp2(p[0:1] - t_max) for p in parts]
        s_in = [jnp.exp2(p[2:3] - s_max) for p in parts]
        t_sum = functools.reduce(jnp.add, [p[1:2] * w for p, w in zip(parts, t_in)])
        s_sum = functools.reduce(jnp.add, [p[3:4] * w for p, w in zip(parts, s_in)])
        cross = functools.reduce(jnp.add, [p[4:5] * w for p, w in zip(parts, t_in)])
        return t_max, t_sum, s_max, s_sum, cross

    def stat_copy(dy, dz):
        return pltpu.make_async_remote_copy(
            src_ref=stat_send.at[y_of[dy] * NZ + z_of[dz]], dst_ref=stat_recv.at[dy * NZ + (NZ - dz) % NZ],
            send_sem=st_sem.at[0], recv_sem=st_sem.at[1],
            device_id=offset_device(dy, dz), device_id_type=MESH,
        )

    def res_copy(dy, dz):
        return pltpu.make_async_remote_copy(
            src_ref=res_recv.at[me], dst_ref=res_recv.at[me],
            send_sem=st_sem.at[2], recv_sem=st_sem.at[3],
            device_id=offset_device(dy, dz), device_id_type=MESH,
        )

    def all_copies(ref, first):
        others = ref.at[pl.ds(0, OWNERS - 1)]
        return pltpu.make_async_remote_copy(
            src_ref=others, dst_ref=others, send_sem=st_sem.at[first], recv_sem=st_sem.at[first + 1],
            device_id=sibling, device_id_type=MESH,
        )

    def leave(first):
        for n in range(first, first + 4):
            t_max, t_sum, s_max, s_sum, cross = joined([stat[n, b] for b in range(BATCHES)])
            whole = jnp.concatenate([t_max, t_sum, s_max, s_sum, cross, cross, cross, cross], axis=0)
            for y in range(NYL):
                stat_send[y * NZ + n, 0] = whole[:, y * ROWS:(y + 1) * ROWS]
            four = jnp.concatenate([whole[0:4, :ROWS], whole[0:4, ROWS:]], axis=0)
            for y in range(NYL):
                stat_send[y * NZ + (n + 4) % NZ, 1] = four

    from_sibling(0)
    product(0, raw_a, top_a)

    def score_step(j, carry):
        @pl.when(j == 3)
        def _():
            from_sibling(1)

        @pl.when(j == 5)
        def _():
            sides_to_sibling(1)

        @pl.when(j == 7)
        def _():
            far_from_across()
            from_sibling(2)

        @pl.when(j == 11)
        def _():
            from_sibling(3)

        @pl.when(j == 14)
        def _():
            leave(0)

        product(2 * j + 1, raw_b, top_b)
        weights(2 * j, raw_a, top_a)
        product(jnp.minimum(2 * j + 2, BATCHES * NZ - 1), raw_a, top_a)
        weights(2 * j + 1, raw_b, top_b)
        return carry

    lax.fori_loop(0, BATCHES * NZ // 2, score_step, 0)
    leave(4)
    for offset in offsets:
        stat_copy(*offset).start()
    stat_recv[0] = stat_send[me]
    for b in range(BATCHES):
        turn(b)
    spread_wait()
    all_copies(stat_recv, 0).wait_recv()
    def totals(parts):
        t_max, t_sum, s_max, s_sum, cross = joined(parts)
        t_in, s_in = factor / t_sum, factor / s_sum
        result = jnp.concatenate([t_max, t_in, s_max, s_in, t_in, t_in, t_in, t_in], axis=0)
        return result, (t_max, t_sum, s_max, s_sum, cross)

    result, (t_max, t_sum, s_max, s_sum, cross) = totals([stat_recv[m, 0] for m in range(OWNERS)])
    res_recv[me] = result
    for offset in offsets:
        res_copy(*offset).start()
    far = []
    for y in range(NYL):
        parts = [stat_recv[m, 1, 4 * y:4 * y + 4] for m in range(OWNERS)]
        far.append(totals([jnp.concatenate([p, p], axis=0) for p in parts])[0])
    far = jnp.concatenate(far, axis=1)

    def group(away):
        return rem(z + NZ + away, NZ)

    def sequence(i):
        size = 4 - div(i + 1, 2)
        return group(size * (2 * rem(i, 2) - 1))

    def lanes(n):
        return pl.ds(pl.multiple_of(n * GROUP, GROUP), GROUP)

    def form(i, gt, p, res=None):
        n = sequence(i)
        if res is None:
            res = jnp.concatenate([res_recv[n], res_recv[NZ + n]], axis=1)
        for b in range(BATCHES):
            st = stat[n, b]
            t_in = jnp.exp2(st[0:1] - res[0:1]) * res[1:2]
            s_in = jnp.exp2(st[2:3] - res[2:3]) * res[3:4]
            grad = (sw[n, b] * s_in - tw[n, b] * t_in).astype(BF16)
            gt[0, b, :, lanes(p)] = grad[:BATCH // 2]
            gt[1, b, :, lanes(p)] = grad[BATCH // 2:]

    def pair_copy(i):
        return pltpu.make_async_remote_copy(
            src_ref=y_pair_send.at[i], dst_ref=y_pair_recv.at[i],
            send_sem=ring_sem.at[2], recv_sem=yp_recv_sem.at[i],
            device_id=y_mate, device_id_type=MESH,
        )

    def query_part(i, gt, p):
        n = sequence(i)
        total = nn(spt[...], gt[:, :, :, lanes(p)].reshape(NCORE * BATCHES * BATCH // 2, GROUP))
        gq[n, 0] = total[:, :ROWS]
        gq[n, 1] = total[:, ROWS:]
        y_pair_send[i] = gq[n, 1 - yl, ZF:].astype(BF16)

    def z_part(away):
        return gq[group(away), :, :ZF]

    def y_part(away):
        i = (4, 3, -3, 2, -2, 1, -1, 0).index(away)
        pair_copy(i).wait_recv()
        return gq[group(away), yl, ZF:] + y_pair_recv[i].astype(F32)

    ZH, YH = ZF // 2, YF // 2

    def z_start():
        far = z_part(4).astype(BF16)
        z_send[0] = far
        message(lambda: (z_send.at[0, :, pl.ds(0, ZH)], z_recv_r.at[0, :, pl.ds(0, ZH)]), ("zr", 0), up, ring_sem.at[0]).start()
        message(lambda: (z_send.at[0, :, pl.ds(ZH, ZH)], z_recv_l.at[0, :, pl.ds(ZH, ZH)]), ("zl", 0), down, ring_sem.at[0]).start()

    def y_start():
        y_send[0] = y_part(4).astype(BF16)
        message(lambda: (y_send.at[0, pl.ds(0, YH)], y_recv_r.at[0, pl.ds(0, YH)]), ("yr", 0), up, ring_sem.at[1]).start()
        message(lambda: (y_send.at[0, pl.ds(YH, YH)], y_recv_l.at[0, pl.ds(YH, YH)]), ("yl", 0), down, ring_sem.at[1]).start()

    def z_step(step):
        if step == 1:
            mine = z_part(3)
            received(z_recv_r.at[0, :, pl.ds(0, ZH)], ("zr", 0))
            z_send[1, :, :ZH] = (mine[:, :ZH] + z_recv_r[0, :, :ZH].astype(F32)).astype(BF16)
            z_send[1, :, ZH:] = mine[:, ZH:].astype(BF16)
        else:
            received(z_recv_r.at[step - 1], ("zr", step - 1))
            z_send[step] = (z_part(4 - step) + z_recv_r[step - 1].astype(F32)).astype(BF16)
        message(lambda step=step: (z_send.at[step], z_recv_r.at[step]), ("zr", step), up, ring_sem.at[0]).start()
        if step == 1:
            mine = z_part(-3)
            received(z_recv_l.at[0, :, pl.ds(ZH, ZH)], ("zl", 0))
            z_send[5, :, :ZH] = mine[:, :ZH].astype(BF16)
            z_send[5, :, ZH:] = (mine[:, ZH:] + z_recv_l[0, :, ZH:].astype(F32)).astype(BF16)
        else:
            received(z_recv_l.at[step - 1], ("zl", step - 1))
            z_send[4 + step] = (z_part(step - 4) + z_recv_l[step - 1].astype(F32)).astype(BF16)
        message(lambda step=step: (z_send.at[4 + step], z_recv_l.at[step]), ("zl", step), down, ring_sem.at[0]).start()

    def y_step(step):
        mine = y_part(4 - step)
        if step == 1:
            received(y_recv_r.at[0, pl.ds(0, YH)], ("yr", 0))
            y_send[1, :YH] = (mine[:YH] + y_recv_r[0, :YH].astype(F32)).astype(BF16)
            y_send[1, YH:] = mine[YH:].astype(BF16)
        else:
            received(y_recv_r.at[step - 1], ("yr", step - 1))
            y_send[step] = (mine + y_recv_r[step - 1].astype(F32)).astype(BF16)
        message(lambda step=step: (y_send.at[step], y_recv_r.at[step]), ("yr", step), up, ring_sem.at[1]).start()
        mine = y_part(step - 4)
        if step == 1:
            received(y_recv_l.at[0, pl.ds(YH, YH)], ("yl", 0))
            y_send[5, :YH] = mine[:YH].astype(BF16)
            y_send[5, YH:] = (mine[YH:] + y_recv_l[0, YH:].astype(F32)).astype(BF16)
        else:
            received(y_recv_l.at[step - 1], ("yl", step - 1))
            y_send[4 + step] = (mine + y_recv_l[step - 1].astype(F32)).astype(BF16)
        message(lambda step=step: (y_send.at[4 + step], y_recv_l.at[step]), ("yl", step), down, ring_sem.at[1]).start()

    def passage_part(core, to):
        def term(p):
            grads = [gt[core, :, :, lanes(p)].reshape(BATCHES * BATCH // 2, GROUP) for gt in (gt_a, gt_b)]
            queries = [sq[sequence(2 * p + i)].reshape(GROUP, DS) for i in (0, 1)]
            return (nn(grads[0], queries[0]) + nn(grads[1], queries[1])).reshape(BATCHES, 2, OWN, DS)

        to[...] = term(0)

        def body(p, carry):
            to[...] = to[...] + term(p)
            return carry

        lax.fori_loop(1, NZ // 2, body, 0)

    def gp_of(h, where):
        b, s = place(h, where, 0)
        return gp[b, s]

    def gp_first():
        received(gps_recv, "gp sibling")
        gp[...] = gp[...] + gps_recv[...].astype(F32)
        for h in range(NYH):
            gp1_send[h] = gp_of(h, FAR).astype(BF16)
        send(lambda: (gp1_send.at[0], gp1_recv.at[0]), ("gp", RIGHT, 1), right)
        send(lambda: (gp1_send.at[1], gp1_recv.at[1]), ("gp", LEFT, 1), left)

    def gp_second():
        received(gp1_recv.at[0], ("gp", RIGHT, 1))
        gp2_send[0, 0] = (gp_of(0, RIGHT) + gp1_recv[0].astype(F32)).astype(BF16)
        gp2_send[0, 1] = gp_of(1, RIGHT).astype(BF16)
        send(lambda: (gp2_send.at[0], gp2_recv.at[0]), ("gp", RIGHT, 2), right)
        received(gp1_recv.at[1], ("gp", LEFT, 1))
        gp2_send[1, 0] = gp_of(0, LEFT).astype(BF16)
        gp2_send[1, 1] = (gp_of(1, LEFT) + gp1_recv[1].astype(F32)).astype(BF16)
        send(lambda: (gp2_send.at[1], gp2_recv.at[1]), ("gp", LEFT, 2), left)

    def gp_third():
        received(gp2_recv.at[0], ("gp", RIGHT, 2))
        received(gp2_recv.at[1], ("gp", LEFT, 2))
        gp3_send[...] = x_total(1).astype(BF16)
        send(lambda: (gp3_send, gp3_recv), "gp across", across)

    def x_total(h):
        return gp_of(h, SELF) + gp2_recv[0, h].astype(F32) + gp2_recv[1, h].astype(F32)

    def z_last():
        received(z_recv_r.at[3], ("zr", 3))
        received(z_recv_l.at[3], ("zl", 3))
        for y in range(NYL):
            gq[z, y, :ZF] = gq[z, y, :ZF] + z_recv_r[3, y].astype(F32) + z_recv_l[3, y].astype(F32)
        z_pair_send[...] = gq[z, 1 - yl, :ZF].astype(BF16)
        send(lambda: (z_pair_send, z_pair_recv), "z pair", y_mate)

    form(0, gt_a, 0, far)
    query_part(0, gt_a, 0)
    z_start()
    pair_copy(0).start()
    div_out[...] = cross * LN2 / t_sum - (t_max * LN2 + jnp.log(t_sum)) + (s_max * LN2 + jnp.log(s_sum))
    all_copies(stat_send, 0).wait_send()
    all_copies(res_recv, 2).wait_recv()
    form(1, gt_b, 0)

    def gradient_step(p, carry):
        query_part(2 * p + 1, gt_b, p)
        form(2 * p + 2, gt_a, p + 1)
        pair_copy(2 * p + 1).start()
        query_part(2 * p + 2, gt_a, p + 1)
        form(2 * p + 3, gt_b, p + 1)

        @pl.when(p == 0)
        def _():
            z_step(1)

        @pl.when(p == 1)
        def _():
            y_start()

        pair_copy(2 * p + 2).start()
        return carry

    lax.fori_loop(0, NZ // 2 - 1, gradient_step, 0)
    query_part(NZ - 1, gt_b, NZ // 2 - 1)
    pair_copy(NZ - 1).start()
    passage_part(1, gp)
    gps_send[...] = gp[...].astype(BF16)
    send(lambda: (gps_send, gps_recv), "gp sibling", sibling)
    z_step(2)
    y_step(1)
    passage_part(0, gp)
    gp_first()
    z_step(3)
    y_step(2)
    gp_second()
    all_copies(res_recv, 2).wait_send()
    z_last()
    y_step(3)
    gp_third()
    for i, ref in enumerate((z_send.at[pl.ds(0, 7)], y_send.at[pl.ds(0, 7)], y_pair_send)):
        message(lambda: (ref, ref), "ring", sibling, ring_sem.at[i]).wait_send()
    flush()

    mine = y_part(0)
    received(y_recv_r.at[3], ("yr", 3))
    received(y_recv_l.at[3], ("yl", 3))
    gq_out[:, ZF:] = (mine + y_recv_r[3].astype(F32) + y_recv_l[3].astype(F32)).T
    received(z_pair_recv, "z pair")
    gq_out[:, :ZF] = (gq[z, yl, :ZF] + z_pair_recv[...].astype(F32)).T
    received(gp3_recv, "gp across")
    gp_out[...] = x_total(0) + gp3_recv[...].astype(F32)


def deliver(gq_in, gp_in, div_in, gq_out, gp_out, div_out, gq, gp, div, in_sem, out_sem):
    parts = ((gq_in, gq, gq_out), (gp_in, gp, gp_out), (div_in, div, div_out))
    ins = [pltpu.make_async_copy(src, mid, in_sem.at[i]) for i, (src, mid, _) in enumerate(parts)]
    outs = [pltpu.make_async_copy(mid, dst, out_sem.at[i]) for i, (_, mid, dst) in enumerate(parts)]
    for copy in ins:
        copy.start()
    for arrive, leave in zip(ins, outs):
        arrive.wait()
        leave.start()
    for copy in outs:
        copy.wait()


def local(teacher_query, student_query, teacher_passages, student_passages):
    blocks = NYL, NZ, NCORE, ROWS
    hbm = pl.BlockSpec(memory_space=pl.ANY)
    vmem = pl.BlockSpec(memory_space=pltpu.VMEM)
    outs = (
        jax.ShapeDtypeStruct((ROWS, DS), F32),
        jax.ShapeDtypeStruct((OWN, DS), F32),
        jax.ShapeDtypeStruct((1, ROWS), F32),
    )
    results = pl.pallas_call(
        kernel,
        out_shape=outs,
        in_specs=[hbm] * 4,
        out_specs=(vmem,) * 3,
        scratch_shapes=[
            pltpu.VMEM((NZ, NYL, ROWS, DT), BF16),
            pltpu.VMEM((NZ, NYL, ROWS, DS), BF16),
            pltpu.VMEM((BATCHES * SLOTS, OWN, DT + DS), BF16),
            pltpu.VMEM((DS, BATCHES * BATCH), BF16),
            pltpu.VMEM((NZ, BATCHES, BATCH, GROUP), F32),
            pltpu.VMEM((NZ, BATCHES, BATCH, GROUP), F32),
            pltpu.VMEM((2, BATCH, GROUP), F32),
            pltpu.VMEM((2, BATCH, GROUP), F32),
            pltpu.VMEM((8, GROUP), F32),
            pltpu.VMEM((8, GROUP), F32),
            pltpu.VMEM((NCORE, BATCHES, BATCH // 2, NZ // 2 * GROUP), BF16),
            pltpu.VMEM((NCORE, BATCHES, BATCH // 2, NZ // 2 * GROUP), BF16),
            pltpu.VMEM((NZ, BATCHES, 8, GROUP), F32),
            pltpu.VMEM((NZ, NYL, DS, ROWS), F32),
            pltpu.VMEM((OWNERS, 2, 8, ROWS), F32),
            pltpu.VMEM((OWNERS, 2, 8, ROWS), F32),
            pltpu.VMEM((OWNERS, 8, ROWS), F32),
            pltpu.VMEM((8, NYL, ZF, ROWS), BF16),
            pltpu.VMEM((4, NYL, ZF, ROWS), BF16),
            pltpu.VMEM((4, NYL, ZF, ROWS), BF16),
            pltpu.VMEM((ZF, ROWS), BF16),
            pltpu.VMEM((ZF, ROWS), BF16),
            pltpu.VMEM((NZ, YF, ROWS), BF16),
            pltpu.VMEM((NZ, YF, ROWS), BF16),
            pltpu.VMEM((8, YF, ROWS), BF16),
            pltpu.VMEM((4, YF, ROWS), BF16),
            pltpu.VMEM((4, YF, ROWS), BF16),
            pltpu.VMEM((BATCHES, 2, OWN, DS), F32),
            pltpu.VMEM((BATCHES, 2, OWN, DS), BF16),
            pltpu.VMEM((BATCHES, 2, OWN, DS), BF16),
            pltpu.VMEM((NYH, OWN, DS), BF16),
            pltpu.VMEM((NYH, OWN, DS), BF16),
            pltpu.VMEM((2, NYH, OWN, DS), BF16),
            pltpu.VMEM((2, NYH, OWN, DS), BF16),
            pltpu.VMEM((OWN, DS), BF16),
            pltpu.VMEM((OWN, DS), BF16),
            pltpu.SemaphoreType.DMA((6,)),
            pltpu.SemaphoreType.REGULAR((4,)),
            pltpu.SemaphoreType.DMA,
            pltpu.SemaphoreType.DMA((3,)),
            pltpu.SemaphoreType.DMA((MESSAGES,)),
            pltpu.SemaphoreType.DMA((MESSAGES,)),
            pltpu.SemaphoreType.DMA((NZ,)),
            pltpu.SemaphoreType.DMA((4,)),
        ],
        compiler_params=pltpu.CompilerParams(
            collective_id=0, has_side_effects=True, vmem_limit_bytes=VMEM_BYTES
        ),
    )(
        teacher_query.reshape(*blocks, DT),
        student_query.reshape(*blocks, DS),
        teacher_passages,
        student_passages,
    )
    grad_query, grad_passage, divergence = pl.pallas_call(
        deliver,
        out_shape=outs,
        in_specs=[hbm] * 3,
        out_specs=(hbm,) * 3,
        scratch_shapes=[
            *(pltpu.VMEM(out.shape, out.dtype) for out in outs),
            pltpu.SemaphoreType.DMA((3,)),
            pltpu.SemaphoreType.DMA((3,)),
        ],
        compiler_params=pltpu.CompilerParams(vmem_limit_bytes=VMEM_BYTES),
    )(*results)
    return divergence.reshape(ROWS), grad_query, grad_passage


def solution(mesh):
    return jax.shard_map(
        local,
        mesh=mesh,
        in_specs=(
            P("query", None),
            P("query", None),
            P(("query", "corpus"), None),
            P(("query", "corpus"), None),
        ),
        out_specs=(
            P(("query", "corpus")),
            P(("query", "corpus"), None),
            P(("query", "corpus"), None),
        ),
        check_vma=False,
    )
```

```python
import functools
import math

import jax
import jax.numpy as jnp
from jax import lax
from jax.experimental import pallas as pl
from jax.experimental.pallas import tpu as pltpu
from jax.sharding import PartitionSpec as P

NX, NYH, NYL, NZ, NCORE = 4, 2, 2, 8, 2
OWN = 64
ROWS = 128
DT, DS = 1024, 384
BATCHES = 4
SLOTS = 4
BATCH = 256
GROUP = NYL * ROWS
OWNERS = NYL * NZ
HALF = OWN // 2
ZF = 128
YF = DS - ZF
LOG2E = math.log2(math.e)
LN2 = math.log(2.0)
F32, BF16 = jnp.float32, jnp.bfloat16
MESH = pl.DeviceIdType.MESH

SELF, LEFT, RIGHT, FAR = 0, 1, 2, 3


def place(h, where, core):
    if where == SELF:
        return 1, core * 2 + h
    if where == FAR:
        return 3, core * 2 + h
    return 2 * h, core * 2 + (where - LEFT)


def div(a, b):
    return lax.div(a, jnp.int32(b))


def rem(a, b):
    return lax.rem(a, jnp.int32(b))


def nt(a, b):
    return lax.dot_general(a, b, (((1,), (1,)), ((), ())), preferred_element_type=F32)


def nn(a, b):
    return lax.dot_general(a, b, (((1,), (0,)), ((), ())), preferred_element_type=F32)


class Messages:
    def __init__(self):
        self.numbers = {}

    def __call__(self, name):
        return self.numbers.setdefault(name, len(self.numbers))


MESSAGES = 80
VMEM_BYTES = 60 * 1024 * 1024


def kernel(
    tq_hbm, sq_hbm, tp_hbm, sp_hbm,
    gq_out, gp_out, div_out,
    tq, sq, pbuf, spt, tw, sw, raw_a, raw_b, gt, stat, gq,
    stat_send, stat_recv, res_recv,
    z_send, z_recv_r, z_recv_l, z_pair_send, z_pair_recv,
    y_pair_send, y_pair_recv, y_send, y_recv_r, y_recv_l,
    gp, gps_send, gps_recv, gp1_send, gp1_recv, gp2_send, gp2_recv, gp3_send, gp3_recv,
    load_sem, known_sem, gather_sem, ring_sem, send_sem, recv_sem, yp_recv_sem, st_sem,
):
    t_scale = DT ** (-0.5) * LOG2E
    s_scale = DS ** (-0.5) * LOG2E
    factor = DS ** (-0.5)
    q = lax.axis_index("query")
    c = lax.axis_index("corpus")
    x, yh = div(q, NYH), rem(q, NYH)
    yl, z, k = div(c, NZ * NCORE), rem(div(c, NCORE), NZ), rem(c, NCORE)
    me = yl * NZ + z

    def at(x_, yh_, yl_, z_, k_):
        return (x_ * NYH + yh_, (yl_ * NZ + z_) * NCORE + k_)

    right, left = at(rem(x + 1, NX), yh, yl, z, k), at(rem(x + NX - 1, NX), yh, yl, z, k)
    across = at(x, 1 - yh, 1 - yl, z, k)
    sibling = at(x, yh, yl, z, 1 - k)
    up, down = at(x, yh, yl, rem(z + 1, NZ), k), at(x, yh, yl, rem(z + NZ - 1, NZ), k)
    y_mate = at(x, yh, 1 - yl, z, k)

    offsets = [(dy, dz) for dz in (4, 3, 5, 2, 6, 1, 7, 0) for dy in (1, 0) if (dy, dz) != (0, 0)]
    results_to = [offset for offset in offsets if offset[1] != 4]
    y_of = [yl, 1 - yl]
    z_of = [rem(z + dz, NZ) for dz in range(NZ)]

    def offset_device(dy, dz):
        return at(x, yh, y_of[dy], z_of[dz], k)

    def slot(h, where, core, half=None):
        b, s = place(h, where, core)
        if half is None:
            return pbuf.at[b * SLOTS + s]
        return pbuf.at[b * SLOTS + s, pl.ds(half * HALF, HALF)]

    def both(b, core):
        return pbuf.at[pl.ds(b * SLOTS + core * 2, 2)]

    loads = [
        pltpu.make_async_copy(tp_hbm, pbuf.at[SLOTS, :, pl.ds(0, DT)], load_sem.at[0]),
        pltpu.make_async_copy(sp_hbm, pbuf.at[SLOTS, :, pl.ds(DT, DS)], load_sem.at[1]),
    ]
    for y in range(NYL):
        loads.append(pltpu.make_async_copy(tq_hbm.at[y, :, k], tq.at[:, y], load_sem.at[2 + y]))
        loads.append(pltpu.make_async_copy(sq_hbm.at[y, :, k], sq.at[:, y], load_sem.at[4 + y]))
    for load in loads:
        load.start()

    barrier = pltpu.get_barrier_semaphore()
    for device in (right, left, across, sibling, up, down, y_mate):
        pl.semaphore_signal(barrier, inc=1, device_id=device, device_id_type=MESH)
    pl.semaphore_wait(barrier, 7)
    loads[0].wait()
    loads[1].wait()

    number = Messages()
    sent = []

    def message(refs, name, device, out=None):
        i = number(name)
        src, dst = refs()
        return pltpu.make_async_remote_copy(
            src_ref=src, dst_ref=dst, send_sem=send_sem.at[i] if out is None else out, recv_sem=recv_sem.at[i],
            device_id=device, device_id_type=MESH,
        )

    def send(refs, name, device):
        message(refs, name, device).start()
        sent.append((refs, name, device))

    def flush():
        for args in sent:
            message(*args).wait_send()
        sent.clear()

    def received(ref, name):
        message(lambda: (ref, ref), name, sibling).wait_recv()

    def spread(refs, name, device):
        message(refs, name, device, gather_sem).start()

    def spread_wait():
        everything = pbuf.at[pl.ds(0, BATCHES * SLOTS - 1)]
        message(lambda: (everything, everything), "gather", sibling, gather_sem).wait_send()

    def half_to(where, half, device):
        spread(lambda: (slot(0, SELF, 0, half), slot(0, where, 0, half)), ("p", where, half), device)

    def sides_to_sibling(h):
        if h == 0:
            received(slot(0, LEFT, 0, 1), ("p", LEFT, 1))
            received(slot(0, RIGHT, 0, 0), ("p", RIGHT, 0))
        else:
            received(slot(1, LEFT, 0), ("p1", LEFT))
            received(slot(1, RIGHT, 0), ("p1", RIGHT))
        to_sibling(2 * h)

    def to_sibling(b):
        spread(lambda: (both(b, 0), both(b, 1)), ("sib", b), sibling)

    def from_sibling(b):
        received(both(b, 1), ("sib", b))

    def far_on():
        received(slot(0, LEFT, 0, 0), ("p", LEFT, 0))
        spread(lambda: (slot(0, LEFT, 0, 0), slot(0, FAR, 0, 0)), ("far",), right)
        received(slot(0, RIGHT, 0, 1), ("p", RIGHT, 1))
        spread(lambda: (slot(0, RIGHT, 0, 1), slot(0, FAR, 0, 1)), ("far",), left)

    def across_on(half):
        received(slot(1, SELF, 0, half), ("across", half))
        spread(lambda: (slot(1, SELF, 0, half), slot(1, LEFT, 0, half)), ("p1", LEFT), right)
        spread(lambda: (slot(1, SELF, 0, half), slot(1, RIGHT, 0, half)), ("p1", RIGHT), left)

    def far_across():
        received(slot(0, FAR, 0), ("far",))
        spread(lambda: (slot(0, FAR, 0), slot(1, FAR, 0)), ("far across",), across)

    def far_from_across():
        received(slot(1, FAR, 0), ("far across",))
        to_sibling(3)

    half_to(LEFT, 0, right)
    half_to(RIGHT, 1, left)
    spread(lambda: (slot(0, SELF, 0, 0), slot(1, SELF, 0, 0)), ("across", 0), across)
    half_to(LEFT, 1, right)
    half_to(RIGHT, 0, left)
    spread(lambda: (slot(0, SELF, 0, 1), slot(1, SELF, 0, 1)), ("across", 1), across)

    def product(i, raw):
        b, n = div(i, NZ), rem(i, NZ)
        batch = pbuf[pl.ds(b * SLOTS, SLOTS)].reshape(BATCH, DT + DS)
        raw[0] = nt(batch[:, :DT], tq[n].reshape(GROUP, DT))
        raw[1] = nt(batch[:, DT:], sq[n].reshape(GROUP, DS))

    def weights(i, raw):
        b, n = div(i, NZ), rem(i, NZ)
        t = raw[0] * t_scale
        s = raw[1] * s_scale
        t_max = jnp.max(t, axis=0, keepdims=True)
        s_max = jnp.max(s, axis=0, keepdims=True)
        t_weight = jnp.exp2(t - t_max)
        s_weight = jnp.exp2(s - s_max)
        tw[n, b] = t_weight
        sw[n, b] = s_weight
        t_sum = jnp.sum(t_weight, axis=0, keepdims=True)
        s_sum = jnp.sum(s_weight, axis=0, keepdims=True)
        cross = jnp.sum(t_weight * (t - s), axis=0, keepdims=True)
        stat[n, b] = jnp.concatenate([t_max, t_sum, s_max, s_sum, cross, cross, cross, cross], axis=0)

    def turn(b):
        turned = pbuf[b * SLOTS:(b + 1) * SLOTS].reshape(BATCH, DT + DS)[:, DT:].T
        part = BATCH // NCORE
        for core in range(NCORE):
            start = (core * BATCHES + b) * part
            spt[:, start:start + part] = turned[:, core * part:(core + 1) * part]

    def know(i):
        for device in (up, down, y_mate):
            pl.semaphore_signal(known_sem.at[i], inc=1, device_id=device, device_id_type=MESH)
        pl.semaphore_wait(known_sem.at[i], 3)

    know(0)
    far_on()
    across_on(0)
    across_on(1)
    to_sibling(1)
    know(1)
    sides_to_sibling(0)
    know(2)
    far_across()
    know(3)
    for load in loads[2:]:
        load.wait()

    def joined(parts):
        t_max = functools.reduce(jnp.maximum, [p[0:1] for p in parts])
        s_max = functools.reduce(jnp.maximum, [p[2:3] for p in parts])
        t_in = [jnp.exp2(p[0:1] - t_max) for p in parts]
        s_in = [jnp.exp2(p[2:3] - s_max) for p in parts]
        t_sum = functools.reduce(jnp.add, [p[1:2] * w for p, w in zip(parts, t_in)])
        s_sum = functools.reduce(jnp.add, [p[3:4] * w for p, w in zip(parts, s_in)])
        cross = functools.reduce(jnp.add, [p[4:5] * w for p, w in zip(parts, t_in)])
        return t_max, t_sum, s_max, s_sum, cross

    def stat_copy(dy, dz):
        return pltpu.make_async_remote_copy(
            src_ref=stat_send.at[y_of[dy] * NZ + z_of[dz]], dst_ref=stat_recv.at[dy * NZ + (NZ - dz) % NZ],
            send_sem=st_sem.at[0], recv_sem=st_sem.at[1],
            device_id=offset_device(dy, dz), device_id_type=MESH,
        )

    def res_copy(dy, dz):
        return pltpu.make_async_remote_copy(
            src_ref=res_recv.at[me], dst_ref=res_recv.at[me],
            send_sem=st_sem.at[2], recv_sem=st_sem.at[3],
            device_id=offset_device(dy, dz), device_id_type=MESH,
        )

    def all_copies(ref, first):
        others = ref.at[pl.ds(0, len(offsets) if first == 0 else len(results_to))]
        return pltpu.make_async_remote_copy(
            src_ref=others, dst_ref=others, send_sem=st_sem.at[first], recv_sem=st_sem.at[first + 1],
            device_id=sibling, device_id_type=MESH,
        )

    def leave(first):
        for n in range(first, first + 4):
            t_max, t_sum, s_max, s_sum, cross = joined([stat[n, b] for b in range(BATCHES)])
            whole = jnp.concatenate([t_max, t_sum, s_max, s_sum, cross, cross, cross, cross], axis=0)
            for y in range(NYL):
                stat_send[y * NZ + n, 0] = whole[:, y * ROWS:(y + 1) * ROWS]
            four = jnp.concatenate([whole[0:4, :ROWS], whole[0:4, ROWS:]], axis=0)
            for y in range(NYL):
                stat_send[y * NZ + (n + 4) % NZ, 1] = four

    from_sibling(0)
    product(0, raw_a)

    def score_step(j, carry):
        @pl.when(j == 3)
        def _():
            from_sibling(1)

        @pl.when(j == 5)
        def _():
            sides_to_sibling(1)

        @pl.when(j == 7)
        def _():
            far_from_across()
            from_sibling(2)

        @pl.when(j == 11)
        def _():
            from_sibling(3)

        @pl.when(j == 14)
        def _():
            leave(0)

        product(2 * j + 1, raw_b)
        weights(2 * j, raw_a)
        product(jnp.minimum(2 * j + 2, BATCHES * NZ - 1), raw_a)
        weights(2 * j + 1, raw_b)
        return carry

    lax.fori_loop(0, BATCHES * NZ // 2, score_step, 0)
    leave(4)
    for offset in offsets:
        stat_copy(*offset).start()
    stat_recv[0] = stat_send[me]
    for b in range(BATCHES):
        turn(b)
    spread_wait()
    all_copies(stat_recv, 0).wait_recv()
    def totals(parts):
        t_max, t_sum, s_max, s_sum, cross = joined(parts)
        t_in, s_in = factor / t_sum, factor / s_sum
        result = jnp.concatenate([t_max, t_in, s_max, s_in, t_in, t_in, t_in, t_in], axis=0)
        return result, (t_max, t_sum, s_max, s_sum, cross)

    result, (t_max, t_sum, s_max, s_sum, cross) = totals([stat_recv[m, 0] for m in range(OWNERS)])
    res_recv[me] = result
    for offset in results_to:
        res_copy(*offset).start()
    far = []
    for y in range(NYL):
        parts = [stat_recv[m, 1, 4 * y:4 * y + 4] for m in range(OWNERS)]
        far.append(totals([jnp.concatenate([p, p], axis=0) for p in parts])[0])
    far = jnp.concatenate(far, axis=1)

    def group(away):
        return rem(z + NZ + away, NZ)

    def sequence(i):
        size = 4 - div(i + 1, 2)
        return group(size * (2 * rem(i, 2) - 1))

    def lanes(n):
        return pl.ds(pl.multiple_of(n * GROUP, GROUP), GROUP)

    def form(i, res=None):
        n = sequence(i)
        if res is None:
            res = jnp.concatenate([res_recv[n], res_recv[NZ + n]], axis=1)
        for b in range(BATCHES):
            st = stat[n, b]
            t_in = jnp.exp2(st[0:1] - res[0:1]) * res[1:2]
            s_in = jnp.exp2(st[2:3] - res[2:3]) * res[3:4]
            grad = (sw[n, b] * s_in - tw[n, b] * t_in).astype(BF16)
            gt[0, b, :, lanes(n)] = grad[:BATCH // 2]
            gt[1, b, :, lanes(n)] = grad[BATCH // 2:]

    def pair_copy(i):
        return pltpu.make_async_remote_copy(
            src_ref=y_pair_send.at[i], dst_ref=y_pair_recv.at[i],
            send_sem=ring_sem.at[2], recv_sem=yp_recv_sem.at[i],
            device_id=y_mate, device_id_type=MESH,
        )

    def query_part(i):
        n = sequence(i)
        total = nn(spt[...], gt[:, :, :, lanes(n)].reshape(NCORE * BATCHES * BATCH // 2, GROUP))
        gq[n, 0] = total[:, :ROWS]
        gq[n, 1] = total[:, ROWS:]
        y_pair_send[i] = gq[n, 1 - yl, ZF:].astype(BF16)

    def z_part(away):
        return gq[group(away), :, :ZF]

    def y_part(away):
        i = (4, 3, -3, 2, -2, 1, -1, 0).index(away)
        pair_copy(i).wait_recv()
        return gq[group(away), yl, ZF:] + y_pair_recv[i].astype(F32)

    ZH, YH = ZF // 2, YF // 2

    def z_start():
        far = z_part(4).astype(BF16)
        z_send[0] = far
        message(lambda: (z_send.at[0, :, pl.ds(0, ZH)], z_recv_r.at[0, :, pl.ds(0, ZH)]), ("zr", 0), up, ring_sem.at[0]).start()
        message(lambda: (z_send.at[0, :, pl.ds(ZH, ZH)], z_recv_l.at[0, :, pl.ds(ZH, ZH)]), ("zl", 0), down, ring_sem.at[0]).start()

    def y_start():
        y_send[0] = y_part(4).astype(BF16)
        message(lambda: (y_send.at[0, pl.ds(0, YH)], y_recv_r.at[0, pl.ds(0, YH)]), ("yr", 0), up, ring_sem.at[1]).start()
        message(lambda: (y_send.at[0, pl.ds(YH, YH)], y_recv_l.at[0, pl.ds(YH, YH)]), ("yl", 0), down, ring_sem.at[1]).start()

    def z_step(step):
        if step == 1:
            mine = z_part(3)
            received(z_recv_r.at[0, :, pl.ds(0, ZH)], ("zr", 0))
            z_send[1, :, :ZH] = (mine[:, :ZH] + z_recv_r[0, :, :ZH].astype(F32)).astype(BF16)
            z_send[1, :, ZH:] = mine[:, ZH:].astype(BF16)
        else:
            received(z_recv_r.at[step - 1], ("zr", step - 1))
            z_send[step] = (z_part(4 - step) + z_recv_r[step - 1].astype(F32)).astype(BF16)
        message(lambda step=step: (z_send.at[step], z_recv_r.at[step]), ("zr", step), up, ring_sem.at[0]).start()
        if step == 1:
            mine = z_part(-3)
            received(z_recv_l.at[0, :, pl.ds(ZH, ZH)], ("zl", 0))
            z_send[5, :, :ZH] = mine[:, :ZH].astype(BF16)
            z_send[5, :, ZH:] = (mine[:, ZH:] + z_recv_l[0, :, ZH:].astype(F32)).astype(BF16)
        else:
            received(z_recv_l.at[step - 1], ("zl", step - 1))
            z_send[4 + step] = (z_part(step - 4) + z_recv_l[step - 1].astype(F32)).astype(BF16)
        message(lambda step=step: (z_send.at[4 + step], z_recv_l.at[step]), ("zl", step), down, ring_sem.at[0]).start()

    def y_step(step):
        mine = y_part(4 - step)
        if step == 1:
            received(y_recv_r.at[0, pl.ds(0, YH)], ("yr", 0))
            y_send[1, :YH] = (mine[:YH] + y_recv_r[0, :YH].astype(F32)).astype(BF16)
            y_send[1, YH:] = mine[YH:].astype(BF16)
        else:
            received(y_recv_r.at[step - 1], ("yr", step - 1))
            y_send[step] = (mine + y_recv_r[step - 1].astype(F32)).astype(BF16)
        message(lambda step=step: (y_send.at[step], y_recv_r.at[step]), ("yr", step), up, ring_sem.at[1]).start()
        mine = y_part(step - 4)
        if step == 1:
            received(y_recv_l.at[0, pl.ds(YH, YH)], ("yl", 0))
            y_send[5, :YH] = mine[:YH].astype(BF16)
            y_send[5, YH:] = (mine[YH:] + y_recv_l[0, YH:].astype(F32)).astype(BF16)
        else:
            received(y_recv_l.at[step - 1], ("yl", step - 1))
            y_send[4 + step] = (mine + y_recv_l[step - 1].astype(F32)).astype(BF16)
        message(lambda step=step: (y_send.at[4 + step], y_recv_l.at[step]), ("yl", step), down, ring_sem.at[1]).start()

    def passage_part(core, to):
        def term(i):
            wide = pl.ds(pl.multiple_of(i * 2 * GROUP, 2 * GROUP), 2 * GROUP)
            grads = gt[core, :, :, wide].reshape(BATCHES * BATCH // 2, 2 * GROUP)
            queries = sq[pl.ds(2 * i, 2)].reshape(2 * GROUP, DS)
            return nn(grads, queries).reshape(BATCHES, 2, OWN, DS)

        to[...] = term(0)

        def body(i, carry):
            to[...] = to[...] + term(i)
            return carry

        lax.fori_loop(1, NZ // 2, body, 0)

    def gp_of(h, where):
        b, s = place(h, where, 0)
        return gp[b, s]

    def gp_first():
        received(gps_recv, "gp sibling")
        gp[...] = gp[...] + gps_recv[...].astype(F32)
        for h in range(NYH):
            gp1_send[h] = gp_of(h, FAR).astype(BF16)
        send(lambda: (gp1_send.at[0], gp1_recv.at[0]), ("gp", RIGHT, 1), right)
        send(lambda: (gp1_send.at[1], gp1_recv.at[1]), ("gp", LEFT, 1), left)

    def gp_second():
        received(gp1_recv.at[0], ("gp", RIGHT, 1))
        gp2_send[0, 0] = (gp_of(0, RIGHT) + gp1_recv[0].astype(F32)).astype(BF16)
        gp2_send[0, 1] = gp_of(1, RIGHT).astype(BF16)
        send(lambda: (gp2_send.at[0], gp2_recv.at[0]), ("gp", RIGHT, 2), right)
        received(gp1_recv.at[1], ("gp", LEFT, 1))
        gp2_send[1, 0] = gp_of(0, LEFT).astype(BF16)
        gp2_send[1, 1] = (gp_of(1, LEFT) + gp1_recv[1].astype(F32)).astype(BF16)
        send(lambda: (gp2_send.at[1], gp2_recv.at[1]), ("gp", LEFT, 2), left)

    def gp_third():
        received(gp2_recv.at[0], ("gp", RIGHT, 2))
        received(gp2_recv.at[1], ("gp", LEFT, 2))
        gp3_send[...] = x_total(1).astype(BF16)
        send(lambda: (gp3_send, gp3_recv), "gp across", across)

    def x_total(h):
        return gp_of(h, SELF) + gp2_recv[0, h].astype(F32) + gp2_recv[1, h].astype(F32)

    def z_last():
        received(z_recv_r.at[3], ("zr", 3))
        received(z_recv_l.at[3], ("zl", 3))
        for y in range(NYL):
            gq[z, y, :ZF] = gq[z, y, :ZF] + z_recv_r[3, y].astype(F32) + z_recv_l[3, y].astype(F32)
        z_pair_send[...] = gq[z, 1 - yl, :ZF].astype(BF16)
        send(lambda: (z_pair_send, z_pair_recv), "z pair", y_mate)

    form(0, far)
    query_part(0)
    z_start()
    pair_copy(0).start()
    div_out[...] = cross * LN2 / t_sum - (t_max * LN2 + jnp.log(t_sum)) + (s_max * LN2 + jnp.log(s_sum))
    all_copies(stat_send, 0).wait_send()
    all_copies(res_recv, 2).wait_recv()
    form(1)

    def gradient_step(i, carry):
        query_part(i)
        form(i + 1)

        @pl.when(i == 2)
        def _():
            z_step(1)

        pair_copy(i).start()

        @pl.when(i == 4)
        def _():
            y_start()

        return carry

    lax.fori_loop(1, NZ - 1, gradient_step, 0)
    query_part(NZ - 1)
    pair_copy(NZ - 1).start()
    passage_part(1, gp)
    gps_send[...] = gp[...].astype(BF16)
    send(lambda: (gps_send, gps_recv), "gp sibling", sibling)
    z_step(2)
    y_step(1)
    passage_part(0, gp)
    gp_first()
    z_step(3)
    y_step(2)
    gp_second()
    all_copies(res_recv, 2).wait_send()
    z_last()
    y_step(3)
    gp_third()
    for i, ref in enumerate((z_send.at[pl.ds(0, 7)], y_send.at[pl.ds(0, 7)], y_pair_send)):
        message(lambda: (ref, ref), "ring", sibling, ring_sem.at[i]).wait_send()
    flush()

    mine = y_part(0)
    received(y_recv_r.at[3], ("yr", 3))
    received(y_recv_l.at[3], ("yl", 3))
    gq_out[:, ZF:] = (mine + y_recv_r[3].astype(F32) + y_recv_l[3].astype(F32)).T
    received(z_pair_recv, "z pair")
    gq_out[:, :ZF] = (gq[z, yl, :ZF] + z_pair_recv[...].astype(F32)).T
    received(gp3_recv, "gp across")
    gp_out[...] = x_total(0) + gp3_recv[...].astype(F32)


def deliver(gq_in, gp_in, div_in, gq_out, gp_out, div_out, gq, gp, div, in_sem, out_sem):
    parts = ((gq_in, gq, gq_out), (gp_in, gp, gp_out), (div_in, div, div_out))
    ins = [pltpu.make_async_copy(src, mid, in_sem.at[i]) for i, (src, mid, _) in enumerate(parts)]
    outs = [pltpu.make_async_copy(mid, dst, out_sem.at[i]) for i, (_, mid, dst) in enumerate(parts)]
    for copy in ins:
        copy.start()
    for arrive, leave in zip(ins, outs):
        arrive.wait()
        leave.start()
    for copy in outs:
        copy.wait()


def local(teacher_query, student_query, teacher_passages, student_passages):
    blocks = NYL, NZ, NCORE, ROWS
    hbm = pl.BlockSpec(memory_space=pl.ANY)
    vmem = pl.BlockSpec(memory_space=pltpu.VMEM)
    outs = (
        jax.ShapeDtypeStruct((ROWS, DS), F32),
        jax.ShapeDtypeStruct((OWN, DS), F32),
        jax.ShapeDtypeStruct((1, ROWS), F32),
    )
    results = pl.pallas_call(
        kernel,
        out_shape=outs,
        in_specs=[hbm] * 4,
        out_specs=(vmem,) * 3,
        scratch_shapes=[
            pltpu.VMEM((NZ, NYL, ROWS, DT), BF16),
            pltpu.VMEM((NZ, NYL, ROWS, DS), BF16),
            pltpu.VMEM((BATCHES * SLOTS, OWN, DT + DS), BF16),
            pltpu.VMEM((DS, BATCHES * BATCH), BF16),
            pltpu.VMEM((NZ, BATCHES, BATCH, GROUP), F32),
            pltpu.VMEM((NZ, BATCHES, BATCH, GROUP), F32),
            pltpu.VMEM((2, BATCH, GROUP), F32),
            pltpu.VMEM((2, BATCH, GROUP), F32),
            pltpu.VMEM((NCORE, BATCHES, BATCH // 2, NZ * GROUP), BF16),
            pltpu.VMEM((NZ, BATCHES, 8, GROUP), F32),
            pltpu.VMEM((NZ, NYL, DS, ROWS), F32),
            pltpu.VMEM((OWNERS, 2, 8, ROWS), F32),
            pltpu.VMEM((OWNERS, 2, 8, ROWS), F32),
            pltpu.VMEM((OWNERS, 8, ROWS), F32),
            pltpu.VMEM((8, NYL, ZF, ROWS), BF16),
            pltpu.VMEM((4, NYL, ZF, ROWS), BF16),
            pltpu.VMEM((4, NYL, ZF, ROWS), BF16),
            pltpu.VMEM((ZF, ROWS), BF16),
            pltpu.VMEM((ZF, ROWS), BF16),
            pltpu.VMEM((NZ, YF, ROWS), BF16),
            pltpu.VMEM((NZ, YF, ROWS), BF16),
            pltpu.VMEM((8, YF, ROWS), BF16),
            pltpu.VMEM((4, YF, ROWS), BF16),
            pltpu.VMEM((4, YF, ROWS), BF16),
            pltpu.VMEM((BATCHES, 2, OWN, DS), F32),
            pltpu.VMEM((BATCHES, 2, OWN, DS), BF16),
            pltpu.VMEM((BATCHES, 2, OWN, DS), BF16),
            pltpu.VMEM((NYH, OWN, DS), BF16),
            pltpu.VMEM((NYH, OWN, DS), BF16),
            pltpu.VMEM((2, NYH, OWN, DS), BF16),
            pltpu.VMEM((2, NYH, OWN, DS), BF16),
            pltpu.VMEM((OWN, DS), BF16),
            pltpu.VMEM((OWN, DS), BF16),
            pltpu.SemaphoreType.DMA((6,)),
            pltpu.SemaphoreType.REGULAR((4,)),
            pltpu.SemaphoreType.DMA,
            pltpu.SemaphoreType.DMA((3,)),
            pltpu.SemaphoreType.DMA((MESSAGES,)),
            pltpu.SemaphoreType.DMA((MESSAGES,)),
            pltpu.SemaphoreType.DMA((NZ,)),
            pltpu.SemaphoreType.DMA((4,)),
        ],
        compiler_params=pltpu.CompilerParams(
            collective_id=0, has_side_effects=True, vmem_limit_bytes=VMEM_BYTES
        ),
    )(
        teacher_query.reshape(*blocks, DT),
        student_query.reshape(*blocks, DS),
        teacher_passages,
        student_passages,
    )
    grad_query, grad_passage, divergence = pl.pallas_call(
        deliver,
        out_shape=outs,
        in_specs=[hbm] * 3,
        out_specs=(hbm,) * 3,
        scratch_shapes=[
            *(pltpu.VMEM(out.shape, out.dtype) for out in outs),
            pltpu.SemaphoreType.DMA((3,)),
            pltpu.SemaphoreType.DMA((3,)),
        ],
        compiler_params=pltpu.CompilerParams(vmem_limit_bytes=VMEM_BYTES),
    )(*results)
    return divergence.reshape(ROWS), grad_query, grad_passage


def solution(mesh):
    return jax.shard_map(
        local,
        mesh=mesh,
        in_specs=(
            P("query", None),
            P("query", None),
            P(("query", "corpus"), None),
            P(("query", "corpus"), None),
        ),
        out_specs=(
            P(("query", "corpus")),
            P(("query", "corpus"), None),
            P(("query", "corpus"), None),
        ),
        check_vma=False,
    )
```

```python
import functools
import math

import jax
import jax.numpy as jnp
from jax import lax
from jax.experimental import pallas as pl
from jax.experimental.pallas import tpu as pltpu
from jax.sharding import PartitionSpec as P

NX, NYH, NYL, NZ, NCORE = 4, 2, 2, 8, 2
OWN = 64
ROWS = 128
DT, DS = 1024, 384
BATCHES = 4
SLOTS = 4
BATCH = 256
GROUP = NYL * ROWS
OWNERS = NYL * NZ
HALF = OWN // 2
ZF = 128
YF = DS - ZF
LOG2E = math.log2(math.e)
LN2 = math.log(2.0)
F32, BF16 = jnp.float32, jnp.bfloat16
MESH = pl.DeviceIdType.MESH

SELF, LEFT, RIGHT, FAR = 0, 1, 2, 3


def place(h, where, core):
    if where == SELF:
        return 1, core * 2 + h
    if where == FAR:
        return 3, core * 2 + h
    return 2 * h, core * 2 + (where - LEFT)


def div(a, b):
    return lax.div(a, jnp.int32(b))


def rem(a, b):
    return lax.rem(a, jnp.int32(b))


def nt(a, b):
    return lax.dot_general(a, b, (((1,), (1,)), ((), ())), preferred_element_type=F32)


def nn(a, b):
    return lax.dot_general(a, b, (((1,), (0,)), ((), ())), preferred_element_type=F32)


class Messages:
    def __init__(self):
        self.numbers = {}

    def __call__(self, name):
        return self.numbers.setdefault(name, len(self.numbers))


MESSAGES = 80
VMEM_BYTES = 60 * 1024 * 1024


def kernel(
    tq_hbm, sq_hbm, tp_hbm, sp_hbm,
    gq_out, gp_out, div_out,
    tq, sq, pbuf, spt, tw, sw, raw_a, raw_b, gt, stat, gq,
    stat_send, stat_recv, res_recv,
    z_send, z_recv_r, z_recv_l, z_pair_send, z_pair_recv,
    y_pair_send, y_pair_recv, y_send, y_recv_r, y_recv_l,
    gp, gps_send, gps_recv, gp1_send, gp1_recv, gp2_send, gp2_recv, gp3_send, gp3_recv,
    load_sem, known_sem, gather_sem, ring_sem, send_sem, recv_sem, yp_recv_sem, st_sem,
):
    t_scale = DT ** (-0.5) * LOG2E
    s_scale = DS ** (-0.5) * LOG2E
    factor = DS ** (-0.5)
    q = lax.axis_index("query")
    c = lax.axis_index("corpus")
    x, yh = div(q, NYH), rem(q, NYH)
    yl, z, k = div(c, NZ * NCORE), rem(div(c, NCORE), NZ), rem(c, NCORE)
    me = yl * NZ + z

    def at(x_, yh_, yl_, z_, k_):
        return (x_ * NYH + yh_, (yl_ * NZ + z_) * NCORE + k_)

    right, left = at(rem(x + 1, NX), yh, yl, z, k), at(rem(x + NX - 1, NX), yh, yl, z, k)
    across = at(x, 1 - yh, 1 - yl, z, k)
    sibling = at(x, yh, yl, z, 1 - k)
    up, down = at(x, yh, yl, rem(z + 1, NZ), k), at(x, yh, yl, rem(z + NZ - 1, NZ), k)
    y_mate = at(x, yh, 1 - yl, z, k)

    offsets = [(dy, dz) for dz in (4, 3, 5, 2, 6, 1, 7, 0) for dy in (1, 0) if (dy, dz) != (0, 0)]
    results_to = [offset for offset in offsets if offset[1] != 4]
    y_of = [yl, 1 - yl]
    z_of = [rem(z + dz, NZ) for dz in range(NZ)]

    def offset_device(dy, dz):
        return at(x, yh, y_of[dy], z_of[dz], k)

    def slot(h, where, core, half=None):
        b, s = place(h, where, core)
        if half is None:
            return pbuf.at[b * SLOTS + s]
        return pbuf.at[b * SLOTS + s, pl.ds(half * HALF, HALF)]

    def both(b, core):
        return pbuf.at[pl.ds(b * SLOTS + core * 2, 2)]

    loads = [
        pltpu.make_async_copy(tp_hbm, pbuf.at[SLOTS, :, pl.ds(0, DT)], load_sem.at[0]),
        pltpu.make_async_copy(sp_hbm, pbuf.at[SLOTS, :, pl.ds(DT, DS)], load_sem.at[1]),
    ]
    for y in range(NYL):
        loads.append(pltpu.make_async_copy(tq_hbm.at[y, :, k], tq.at[:, y], load_sem.at[2 + y]))
        loads.append(pltpu.make_async_copy(sq_hbm.at[y, :, k], sq.at[:, y], load_sem.at[4 + y]))
    for load in loads:
        load.start()

    barrier = pltpu.get_barrier_semaphore()
    for device in (right, left, across, sibling, up, down, y_mate):
        pl.semaphore_signal(barrier, inc=1, device_id=device, device_id_type=MESH)
    pl.semaphore_wait(barrier, 7)
    loads[0].wait()
    loads[1].wait()

    number = Messages()
    sent = []

    def message(refs, name, device, out=None):
        i = number(name)
        src, dst = refs()
        return pltpu.make_async_remote_copy(
            src_ref=src, dst_ref=dst, send_sem=send_sem.at[i] if out is None else out, recv_sem=recv_sem.at[i],
            device_id=device, device_id_type=MESH,
        )

    def send(refs, name, device):
        message(refs, name, device).start()
        sent.append((refs, name, device))

    def flush():
        for args in sent:
            message(*args).wait_send()
        sent.clear()

    def received(ref, name):
        message(lambda: (ref, ref), name, sibling).wait_recv()

    def spread(refs, name, device):
        message(refs, name, device, gather_sem).start()

    def spread_wait():
        everything = pbuf.at[pl.ds(0, BATCHES * SLOTS - 1)]
        message(lambda: (everything, everything), "gather", sibling, gather_sem).wait_send()

    def half_to(where, half, device):
        spread(lambda: (slot(0, SELF, 0, half), slot(0, where, 0, half)), ("p", where, half), device)

    def sides_to_sibling(h):
        if h == 0:
            received(slot(0, LEFT, 0, 1), ("p", LEFT, 1))
            received(slot(0, RIGHT, 0, 0), ("p", RIGHT, 0))
        else:
            received(slot(1, LEFT, 0), ("p1", LEFT))
            received(slot(1, RIGHT, 0), ("p1", RIGHT))
        to_sibling(2 * h)

    def to_sibling(b):
        spread(lambda: (both(b, 0), both(b, 1)), ("sib", b), sibling)

    def from_sibling(b):
        received(both(b, 1), ("sib", b))

    def far_on():
        received(slot(0, LEFT, 0, 0), ("p", LEFT, 0))
        spread(lambda: (slot(0, LEFT, 0, 0), slot(0, FAR, 0, 0)), ("far",), right)
        received(slot(0, RIGHT, 0, 1), ("p", RIGHT, 1))
        spread(lambda: (slot(0, RIGHT, 0, 1), slot(0, FAR, 0, 1)), ("far",), left)

    def across_on(half):
        received(slot(1, SELF, 0, half), ("across", half))
        spread(lambda: (slot(1, SELF, 0, half), slot(1, LEFT, 0, half)), ("p1", LEFT), right)
        spread(lambda: (slot(1, SELF, 0, half), slot(1, RIGHT, 0, half)), ("p1", RIGHT), left)

    def far_across():
        received(slot(0, FAR, 0), ("far",))
        spread(lambda: (slot(0, FAR, 0), slot(1, FAR, 0)), ("far across",), across)

    def far_from_across():
        received(slot(1, FAR, 0), ("far across",))
        to_sibling(3)

    half_to(LEFT, 0, right)
    half_to(RIGHT, 1, left)
    spread(lambda: (slot(0, SELF, 0, 0), slot(1, SELF, 0, 0)), ("across", 0), across)
    half_to(LEFT, 1, right)
    half_to(RIGHT, 0, left)
    spread(lambda: (slot(0, SELF, 0, 1), slot(1, SELF, 0, 1)), ("across", 1), across)

    def group_of(i):
        return rem(i, 2) * 4 + div(rem(i, NZ), 2)

    def product(i, raw):
        b, n = div(i, NZ), group_of(i)
        batch = pbuf[pl.ds(b * SLOTS, SLOTS)].reshape(BATCH, DT + DS)
        raw[0] = nt(batch[:, :DT], tq[n].reshape(GROUP, DT))
        raw[1] = nt(batch[:, DT:], sq[n].reshape(GROUP, DS))

    def weights(i, raw):
        b, n = div(i, NZ), group_of(i)
        t = raw[0] * t_scale
        s = raw[1] * s_scale
        t_max = jnp.max(t, axis=0, keepdims=True)
        s_max = jnp.max(s, axis=0, keepdims=True)
        t_weight = jnp.exp2(t - t_max)
        s_weight = jnp.exp2(s - s_max)
        tw[n, b] = t_weight
        sw[n, b] = s_weight
        t_sum = jnp.sum(t_weight, axis=0, keepdims=True)
        s_sum = jnp.sum(s_weight, axis=0, keepdims=True)
        cross = jnp.sum(t_weight * (t - s), axis=0, keepdims=True)
        stat[n, b] = jnp.concatenate([t_max, t_sum, s_max, s_sum, cross, cross, cross, cross], axis=0)

    def turn(b):
        turned = pbuf[b * SLOTS:(b + 1) * SLOTS].reshape(BATCH, DT + DS)[:, DT:].T
        part = BATCH // NCORE
        for core in range(NCORE):
            start = (core * BATCHES + b) * part
            spt[:, start:start + part] = turned[:, core * part:(core + 1) * part]

    def know(i):
        for device in (up, down, y_mate):
            pl.semaphore_signal(known_sem.at[i], inc=1, device_id=device, device_id_type=MESH)
        pl.semaphore_wait(known_sem.at[i], 3)

    know(0)
    far_on()
    across_on(0)
    across_on(1)
    to_sibling(1)
    know(1)
    sides_to_sibling(0)
    know(2)
    far_across()
    know(3)
    for load in loads[2:]:
        load.wait()

    def joined(parts):
        t_max = functools.reduce(jnp.maximum, [p[0:1] for p in parts])
        s_max = functools.reduce(jnp.maximum, [p[2:3] for p in parts])
        t_in = [jnp.exp2(p[0:1] - t_max) for p in parts]
        s_in = [jnp.exp2(p[2:3] - s_max) for p in parts]
        t_sum = functools.reduce(jnp.add, [p[1:2] * w for p, w in zip(parts, t_in)])
        s_sum = functools.reduce(jnp.add, [p[3:4] * w for p, w in zip(parts, s_in)])
        cross = functools.reduce(jnp.add, [p[4:5] * w for p, w in zip(parts, t_in)])
        return t_max, t_sum, s_max, s_sum, cross

    def stat_copy(dy, dz):
        return pltpu.make_async_remote_copy(
            src_ref=stat_send.at[y_of[dy] * NZ + z_of[dz]], dst_ref=stat_recv.at[dy * NZ + (NZ - dz) % NZ],
            send_sem=st_sem.at[0], recv_sem=st_sem.at[1],
            device_id=offset_device(dy, dz), device_id_type=MESH,
        )

    def res_copy(dy, dz):
        return pltpu.make_async_remote_copy(
            src_ref=res_recv.at[me], dst_ref=res_recv.at[me],
            send_sem=st_sem.at[2], recv_sem=st_sem.at[3 if dz in (3, 5) else 4],
            device_id=offset_device(dy, dz), device_id_type=MESH,
        )

    def all_copies(ref, count, out, into):
        others = ref.at[pl.ds(0, count)]
        return pltpu.make_async_remote_copy(
            src_ref=others, dst_ref=others, send_sem=st_sem.at[out], recv_sem=st_sem.at[into],
            device_id=sibling, device_id_type=MESH,
        )

    def leave(first):
        for n in (first, first + 4, first + 1, first + 5):
            t_max, t_sum, s_max, s_sum, cross = joined([stat[n, b] for b in range(BATCHES)])
            whole = jnp.concatenate([t_max, t_sum, s_max, s_sum, cross, cross, cross, cross], axis=0)
            for y in range(NYL):
                stat_send[y * NZ + n, 0] = whole[:, y * ROWS:(y + 1) * ROWS]
            four = jnp.concatenate([whole[0:4, :ROWS], whole[0:4, ROWS:]], axis=0)
            for y in range(NYL):
                stat_send[y * NZ + (n + 4) % NZ, 1] = four

        for offset in offsets:
            @pl.when(div(rem(z_of[offset[1]], 4), 2) == first // 2)
            def _():
                stat_copy(*offset).start()

    from_sibling(0)
    product(0, raw_a)

    def score_step(j, carry):
        @pl.when(j == 3)
        def _():
            from_sibling(1)

        @pl.when(j == 5)
        def _():
            sides_to_sibling(1)

        @pl.when(j == 7)
        def _():
            far_from_across()
            from_sibling(2)

        @pl.when(j == 11)
        def _():
            from_sibling(3)

        @pl.when(j == 14)
        def _():
            leave(0)

        product(2 * j + 1, raw_b)
        weights(2 * j, raw_a)
        product(jnp.minimum(2 * j + 2, BATCHES * NZ - 1), raw_a)
        weights(2 * j + 1, raw_b)
        return carry

    lax.fori_loop(0, BATCHES * NZ // 2, score_step, 0)
    leave(2)
    stat_recv[0] = stat_send[me]
    for b in range(BATCHES):
        turn(b)
    spread_wait()
    all_copies(stat_recv, 15, 0, 1).wait_recv()
    def totals(parts):
        t_max, t_sum, s_max, s_sum, cross = joined(parts)
        t_in, s_in = factor / t_sum, factor / s_sum
        result = jnp.concatenate([t_max, t_in, s_max, s_in, t_in, t_in, t_in, t_in], axis=0)
        return result, (t_max, t_sum, s_max, s_sum, cross)

    result, (t_max, t_sum, s_max, s_sum, cross) = totals([stat_recv[m, 0] for m in range(OWNERS)])
    res_recv[me] = result
    for offset in results_to:
        res_copy(*offset).start()
    far = []
    for y in range(NYL):
        parts = [stat_recv[m, 1, 4 * y:4 * y + 4] for m in range(OWNERS)]
        far.append(totals([jnp.concatenate([p, p], axis=0) for p in parts])[0])
    far = jnp.concatenate(far, axis=1)

    def group(away):
        return rem(z + NZ + away, NZ)

    def sequence(i):
        size = 4 - div(i + 1, 2)
        return group(size * (2 * rem(i, 2) - 1))

    def lanes(n):
        return pl.ds(pl.multiple_of(n * GROUP, GROUP), GROUP)

    def form(i, res=None):
        n = sequence(i)
        if res is None:
            res = jnp.concatenate([res_recv[n], res_recv[NZ + n]], axis=1)
        for b in range(BATCHES):
            st = stat[n, b]
            t_in = jnp.exp2(st[0:1] - res[0:1]) * res[1:2]
            s_in = jnp.exp2(st[2:3] - res[2:3]) * res[3:4]
            grad = (sw[n, b] * s_in - tw[n, b] * t_in).astype(BF16)
            gt[0, b, :, lanes(n)] = grad[:BATCH // 2]
            gt[1, b, :, lanes(n)] = grad[BATCH // 2:]

    def pair_copy(i, count):
        slots = pl.ds(i, count)
        return pltpu.make_async_remote_copy(
            src_ref=y_pair_send.at[slots], dst_ref=y_pair_recv.at[slots],
            send_sem=ring_sem.at[2], recv_sem=yp_recv_sem.at[div(i + 1, 2)],
            device_id=y_mate, device_id_type=MESH,
        )

    def query_part(i):
        n = sequence(i)
        total = nn(spt[...], gt[:, :, :, lanes(n)].reshape(NCORE * BATCHES * BATCH // 2, GROUP))
        gq[n, 0] = total[:, :ROWS]
        gq[n, 1] = total[:, ROWS:]
        y_pair_send[i] = gq[n, 1 - yl, ZF:].astype(BF16)

    def z_part(away):
        return gq[group(away), :, :ZF]

    def y_part(away):
        i = (4, 3, -3, 2, -2, 1, -1, 0).index(away)
        if away >= 0:
            pair_copy(i, 1 if away in (4, 0) else 2).wait_recv()
        return gq[group(away), yl, ZF:] + y_pair_recv[i].astype(F32)

    ZH, YH = ZF // 2, YF // 2

    def z_start():
        far = z_part(4).astype(BF16)
        z_send[0] = far
        message(lambda: (z_send.at[0, :, pl.ds(0, ZH)], z_recv_r.at[0, :, pl.ds(0, ZH)]), ("zr", 0), up, ring_sem.at[0]).start()
        message(lambda: (z_send.at[0, :, pl.ds(ZH, ZH)], z_recv_l.at[0, :, pl.ds(ZH, ZH)]), ("zl", 0), down, ring_sem.at[0]).start()

    def y_start():
        y_send[0] = y_part(4).astype(BF16)
        message(lambda: (y_send.at[0, pl.ds(0, YH)], y_recv_r.at[0, pl.ds(0, YH)]), ("yr", 0), up, ring_sem.at[1]).start()
        message(lambda: (y_send.at[0, pl.ds(YH, YH)], y_recv_l.at[0, pl.ds(YH, YH)]), ("yl", 0), down, ring_sem.at[1]).start()

    def z_step(step):
        if step == 1:
            mine = z_part(3)
            received(z_recv_r.at[0, :, pl.ds(0, ZH)], ("zr", 0))
            z_send[1, :, :ZH] = (mine[:, :ZH] + z_recv_r[0, :, :ZH].astype(F32)).astype(BF16)
            z_send[1, :, ZH:] = mine[:, ZH:].astype(BF16)
        else:
            received(z_recv_r.at[step - 1], ("zr", step - 1))
            z_send[step] = (z_part(4 - step) + z_recv_r[step - 1].astype(F32)).astype(BF16)
        message(lambda step=step: (z_send.at[step], z_recv_r.at[step]), ("zr", step), up, ring_sem.at[0]).start()
        if step == 1:
            mine = z_part(-3)
            received(z_recv_l.at[0, :, pl.ds(ZH, ZH)], ("zl", 0))
            z_send[5, :, :ZH] = mine[:, :ZH].astype(BF16)
            z_send[5, :, ZH:] = (mine[:, ZH:] + z_recv_l[0, :, ZH:].astype(F32)).astype(BF16)
        else:
            received(z_recv_l.at[step - 1], ("zl", step - 1))
            z_send[4 + step] = (z_part(step - 4) + z_recv_l[step - 1].astype(F32)).astype(BF16)
        message(lambda step=step: (z_send.at[4 + step], z_recv_l.at[step]), ("zl", step), down, ring_sem.at[0]).start()

    def y_step(step):
        mine = y_part(4 - step)
        if step == 1:
            received(y_recv_r.at[0, pl.ds(0, YH)], ("yr", 0))
            y_send[1, :YH] = (mine[:YH] + y_recv_r[0, :YH].astype(F32)).astype(BF16)
            y_send[1, YH:] = mine[YH:].astype(BF16)
        else:
            received(y_recv_r.at[step - 1], ("yr", step - 1))
            y_send[step] = (mine + y_recv_r[step - 1].astype(F32)).astype(BF16)
        message(lambda step=step: (y_send.at[step], y_recv_r.at[step]), ("yr", step), up, ring_sem.at[1]).start()
        mine = y_part(step - 4)
        if step == 1:
            received(y_recv_l.at[0, pl.ds(YH, YH)], ("yl", 0))
            y_send[5, :YH] = mine[:YH].astype(BF16)
            y_send[5, YH:] = (mine[YH:] + y_recv_l[0, YH:].astype(F32)).astype(BF16)
        else:
            received(y_recv_l.at[step - 1], ("yl", step - 1))
            y_send[4 + step] = (mine + y_recv_l[step - 1].astype(F32)).astype(BF16)
        message(lambda step=step: (y_send.at[4 + step], y_recv_l.at[step]), ("yl", step), down, ring_sem.at[1]).start()

    def passage_part(core, to):
        def term(i):
            wide = pl.ds(pl.multiple_of(i * 2 * GROUP, 2 * GROUP), 2 * GROUP)
            grads = gt[core, :, :, wide].reshape(BATCHES * BATCH // 2, 2 * GROUP)
            queries = sq[pl.ds(2 * i, 2)].reshape(2 * GROUP, DS)
            return nn(grads, queries).reshape(BATCHES, 2, OWN, DS)

        to[...] = term(0)

        def body(i, carry):
            to[...] = to[...] + term(i)
            return carry

        lax.fori_loop(1, NZ // 2, body, 0)

    def gp_of(h, where):
        b, s = place(h, where, 0)
        return gp[b, s]

    def gp_first():
        received(gps_recv, "gp sibling")
        gp[...] = gp[...] + gps_recv[...].astype(F32)
        for h in range(NYH):
            gp1_send[h] = gp_of(h, FAR).astype(BF16)
        send(lambda: (gp1_send.at[0], gp1_recv.at[0]), ("gp", RIGHT, 1), right)
        send(lambda: (gp1_send.at[1], gp1_recv.at[1]), ("gp", LEFT, 1), left)

    def gp_second():
        received(gp1_recv.at[0], ("gp", RIGHT, 1))
        gp2_send[0, 0] = (gp_of(0, RIGHT) + gp1_recv[0].astype(F32)).astype(BF16)
        gp2_send[0, 1] = gp_of(1, RIGHT).astype(BF16)
        send(lambda: (gp2_send.at[0], gp2_recv.at[0]), ("gp", RIGHT, 2), right)
        received(gp1_recv.at[1], ("gp", LEFT, 1))
        gp2_send[1, 0] = gp_of(0, LEFT).astype(BF16)
        gp2_send[1, 1] = (gp_of(1, LEFT) + gp1_recv[1].astype(F32)).astype(BF16)
        send(lambda: (gp2_send.at[1], gp2_recv.at[1]), ("gp", LEFT, 2), left)

    def gp_third():
        received(gp2_recv.at[0], ("gp", RIGHT, 2))
        received(gp2_recv.at[1], ("gp", LEFT, 2))
        gp3_send[...] = x_total(1).astype(BF16)
        send(lambda: (gp3_send, gp3_recv), "gp across", across)

    def x_total(h):
        return gp_of(h, SELF) + gp2_recv[0, h].astype(F32) + gp2_recv[1, h].astype(F32)

    def z_last():
        received(z_recv_r.at[3], ("zr", 3))
        received(z_recv_l.at[3], ("zl", 3))
        for y in range(NYL):
            gq[z, y, :ZF] = gq[z, y, :ZF] + z_recv_r[3, y].astype(F32) + z_recv_l[3, y].astype(F32)
        z_pair_send[...] = gq[z, 1 - yl, :ZF].astype(BF16)
        send(lambda: (z_pair_send, z_pair_recv), "z pair", y_mate)

    form(0, far)
    query_part(0)
    z_start()
    pair_copy(0, 1).start()
    div_out[...] = cross * LN2 / t_sum - (t_max * LN2 + jnp.log(t_sum)) + (s_max * LN2 + jnp.log(s_sum))
    all_copies(stat_send, 15, 0, 1).wait_send()
    all_copies(res_recv, 4, 2, 3).wait_recv()
    form(1)

    def gradient_step(i, carry):
        @pl.when(i == 2)
        def _():
            all_copies(res_recv, 9, 2, 4).wait_recv()

        query_part(i)
        form(i + 1)

        @pl.when(i == 2)
        def _():
            z_step(1)

        @pl.when(rem(i, 2) == 0)
        def _():
            pair_copy(i - 1, 2).start()


        @pl.when(i == 4)
        def _():
            y_start()

        return carry

    lax.fori_loop(1, NZ - 1, gradient_step, 0)
    query_part(NZ - 1)
    pair_copy(NZ - 1, 1).start()
    passage_part(1, gp)
    gps_send[...] = gp[...].astype(BF16)
    send(lambda: (gps_send, gps_recv), "gp sibling", sibling)
    z_step(2)
    y_step(1)
    passage_part(0, gp)
    gp_first()
    z_step(3)
    y_step(2)
    gp_second()
    all_copies(res_recv, 13, 2, 3).wait_send()
    z_last()
    y_step(3)
    gp_third()
    for i, ref in enumerate((z_send.at[pl.ds(0, 7)], y_send.at[pl.ds(0, 7)], y_pair_send)):
        message(lambda: (ref, ref), "ring", sibling, ring_sem.at[i]).wait_send()
    flush()

    mine = y_part(0)
    received(y_recv_r.at[3], ("yr", 3))
    received(y_recv_l.at[3], ("yl", 3))
    gq_out[:, ZF:] = (mine + y_recv_r[3].astype(F32) + y_recv_l[3].astype(F32)).T
    received(z_pair_recv, "z pair")
    gq_out[:, :ZF] = (gq[z, yl, :ZF] + z_pair_recv[...].astype(F32)).T
    received(gp3_recv, "gp across")
    gp_out[...] = x_total(0) + gp3_recv[...].astype(F32)


def deliver(gq_in, gp_in, div_in, gq_out, gp_out, div_out, gq, gp, div, in_sem, out_sem):
    parts = ((gq_in, gq, gq_out), (gp_in, gp, gp_out), (div_in, div, div_out))
    ins = [pltpu.make_async_copy(src, mid, in_sem.at[i]) for i, (src, mid, _) in enumerate(parts)]
    outs = [pltpu.make_async_copy(mid, dst, out_sem.at[i]) for i, (_, mid, dst) in enumerate(parts)]
    for copy in ins:
        copy.start()
    for arrive, leave in zip(ins, outs):
        arrive.wait()
        leave.start()
    for copy in outs:
        copy.wait()


def local(teacher_query, student_query, teacher_passages, student_passages):
    blocks = NYL, NZ, NCORE, ROWS
    hbm = pl.BlockSpec(memory_space=pl.ANY)
    vmem = pl.BlockSpec(memory_space=pltpu.VMEM)
    outs = (
        jax.ShapeDtypeStruct((ROWS, DS), F32),
        jax.ShapeDtypeStruct((OWN, DS), F32),
        jax.ShapeDtypeStruct((1, ROWS), F32),
    )
    results = pl.pallas_call(
        kernel,
        out_shape=outs,
        in_specs=[hbm] * 4,
        out_specs=(vmem,) * 3,
        scratch_shapes=[
            pltpu.VMEM((NZ, NYL, ROWS, DT), BF16),
            pltpu.VMEM((NZ, NYL, ROWS, DS), BF16),
            pltpu.VMEM((BATCHES * SLOTS, OWN, DT + DS), BF16),
            pltpu.VMEM((DS, BATCHES * BATCH), BF16),
            pltpu.VMEM((NZ, BATCHES, BATCH, GROUP), F32),
            pltpu.VMEM((NZ, BATCHES, BATCH, GROUP), F32),
            pltpu.VMEM((2, BATCH, GROUP), F32),
            pltpu.VMEM((2, BATCH, GROUP), F32),
            pltpu.VMEM((NCORE, BATCHES, BATCH // 2, NZ * GROUP), BF16),
            pltpu.VMEM((NZ, BATCHES, 8, GROUP), F32),
            pltpu.VMEM((NZ, NYL, DS, ROWS), F32),
            pltpu.VMEM((OWNERS, 2, 8, ROWS), F32),
            pltpu.VMEM((OWNERS, 2, 8, ROWS), F32),
            pltpu.VMEM((OWNERS, 8, ROWS), F32),
            pltpu.VMEM((8, NYL, ZF, ROWS), BF16),
            pltpu.VMEM((4, NYL, ZF, ROWS), BF16),
            pltpu.VMEM((4, NYL, ZF, ROWS), BF16),
            pltpu.VMEM((ZF, ROWS), BF16),
            pltpu.VMEM((ZF, ROWS), BF16),
            pltpu.VMEM((NZ, YF, ROWS), BF16),
            pltpu.VMEM((NZ, YF, ROWS), BF16),
            pltpu.VMEM((8, YF, ROWS), BF16),
            pltpu.VMEM((4, YF, ROWS), BF16),
            pltpu.VMEM((4, YF, ROWS), BF16),
            pltpu.VMEM((BATCHES, 2, OWN, DS), F32),
            pltpu.VMEM((BATCHES, 2, OWN, DS), BF16),
            pltpu.VMEM((BATCHES, 2, OWN, DS), BF16),
            pltpu.VMEM((NYH, OWN, DS), BF16),
            pltpu.VMEM((NYH, OWN, DS), BF16),
            pltpu.VMEM((2, NYH, OWN, DS), BF16),
            pltpu.VMEM((2, NYH, OWN, DS), BF16),
            pltpu.VMEM((OWN, DS), BF16),
            pltpu.VMEM((OWN, DS), BF16),
            pltpu.SemaphoreType.DMA((6,)),
            pltpu.SemaphoreType.REGULAR((4,)),
            pltpu.SemaphoreType.DMA,
            pltpu.SemaphoreType.DMA((3,)),
            pltpu.SemaphoreType.DMA((MESSAGES,)),
            pltpu.SemaphoreType.DMA((MESSAGES,)),
            pltpu.SemaphoreType.DMA((NZ,)),
            pltpu.SemaphoreType.DMA((5,)),
        ],
        compiler_params=pltpu.CompilerParams(
            collective_id=0, has_side_effects=True, vmem_limit_bytes=VMEM_BYTES
        ),
    )(
        teacher_query.reshape(*blocks, DT),
        student_query.reshape(*blocks, DS),
        teacher_passages,
        student_passages,
    )
    grad_query, grad_passage, divergence = pl.pallas_call(
        deliver,
        out_shape=outs,
        in_specs=[hbm] * 3,
        out_specs=(hbm,) * 3,
        scratch_shapes=[
            *(pltpu.VMEM(out.shape, out.dtype) for out in outs),
            pltpu.SemaphoreType.DMA((3,)),
            pltpu.SemaphoreType.DMA((3,)),
        ],
        compiler_params=pltpu.CompilerParams(vmem_limit_bytes=VMEM_BYTES),
    )(*results)
    return divergence.reshape(ROWS), grad_query, grad_passage


def solution(mesh):
    return jax.shard_map(
        local,
        mesh=mesh,
        in_specs=(
            P("query", None),
            P("query", None),
            P(("query", "corpus"), None),
            P(("query", "corpus"), None),
        ),
        out_specs=(
            P(("query", "corpus")),
            P(("query", "corpus"), None),
            P(("query", "corpus"), None),
        ),
        check_vma=False,
    )
```

```python
import functools
import math

import jax
import jax.numpy as jnp
from jax import lax
from jax.experimental import pallas as pl
from jax.experimental.pallas import tpu as pltpu
from jax.sharding import PartitionSpec as P

NX, NYH, NYL, NZ, NCORE = 4, 2, 2, 8, 2
OWN = 64
ROWS = 128
DT, DS = 1024, 384
BATCHES = 4
SLOTS = 4
BATCH = 256
GROUP = NYL * ROWS
OWNERS = NYL * NZ
HALF = OWN // 2
ZF = 128
YF = DS - ZF
LOG2E = math.log2(math.e)
LN2 = math.log(2.0)
F32, BF16 = jnp.float32, jnp.bfloat16
MESH = pl.DeviceIdType.MESH

SELF, LEFT, RIGHT, FAR = 0, 1, 2, 3


def place(h, where, core):
    if where == SELF:
        return 1, core * 2 + h
    if where == FAR:
        return 3, core * 2 + h
    return 2 * h, core * 2 + (where - LEFT)


def div(a, b):
    return lax.div(a, jnp.int32(b))


def rem(a, b):
    return lax.rem(a, jnp.int32(b))


def nt(a, b):
    return lax.dot_general(a, b, (((1,), (1,)), ((), ())), preferred_element_type=F32)


def nn(a, b):
    return lax.dot_general(a, b, (((1,), (0,)), ((), ())), preferred_element_type=F32)


class Messages:
    def __init__(self):
        self.numbers = {}

    def __call__(self, name):
        return self.numbers.setdefault(name, len(self.numbers))


MESSAGES = 80
VMEM_BYTES = 60 * 1024 * 1024


def kernel(
    tq_hbm, sq_hbm, tp_hbm, sp_hbm,
    gq_out, gp_out, div_out,
    tq, sq, pbuf, spt, tw, sw, raw_a, raw_b, gt, stat, gq,
    stat_send, stat_recv, res_recv,
    z_send, z_recv_r, z_recv_l, z_pair_send, z_pair_recv,
    y_pair_send, y_pair_recv, y_send, y_recv_r, y_recv_l,
    gp, gps_send, gps_recv, gp1_send, gp1_recv, gp2_send, gp2_recv, gp3_send, gp3_recv,
    load_sem, known_sem, gather_sem, ring_sem, send_sem, recv_sem, yp_recv_sem, st_sem,
):
    t_scale = DT ** (-0.5) * LOG2E
    s_scale = DS ** (-0.5) * LOG2E
    factor = DS ** (-0.5)
    q = lax.axis_index("query")
    c = lax.axis_index("corpus")
    x, yh = div(q, NYH), rem(q, NYH)
    yl, z, k = div(c, NZ * NCORE), rem(div(c, NCORE), NZ), rem(c, NCORE)
    me = yl * NZ + z

    def at(x_, yh_, yl_, z_, k_):
        return (x_ * NYH + yh_, (yl_ * NZ + z_) * NCORE + k_)

    right, left = at(rem(x + 1, NX), yh, yl, z, k), at(rem(x + NX - 1, NX), yh, yl, z, k)
    across = at(x, 1 - yh, 1 - yl, z, k)
    sibling = at(x, yh, yl, z, 1 - k)
    up, down = at(x, yh, yl, rem(z + 1, NZ), k), at(x, yh, yl, rem(z + NZ - 1, NZ), k)
    y_mate = at(x, yh, 1 - yl, z, k)

    offsets = [(dy, dz) for dz in (4, 3, 5, 2, 6, 1, 7, 0) for dy in (1, 0) if (dy, dz) != (0, 0)]
    results_to = [offset for offset in offsets if offset[1] != 4]
    y_of = [yl, 1 - yl]
    z_of = [rem(z + dz, NZ) for dz in range(NZ)]

    def offset_device(dy, dz):
        return at(x, yh, y_of[dy], z_of[dz], k)

    def slot(h, where, core, half=None):
        b, s = place(h, where, core)
        if half is None:
            return pbuf.at[b * SLOTS + s]
        return pbuf.at[b * SLOTS + s, pl.ds(half * HALF, HALF)]

    def both(b, core):
        return pbuf.at[pl.ds(b * SLOTS + core * 2, 2)]

    loads = [
        pltpu.make_async_copy(tp_hbm, pbuf.at[SLOTS, :, pl.ds(0, DT)], load_sem.at[0]),
        pltpu.make_async_copy(sp_hbm, pbuf.at[SLOTS, :, pl.ds(DT, DS)], load_sem.at[1]),
    ]
    for y in range(NYL):
        loads.append(pltpu.make_async_copy(tq_hbm.at[y, :, k], tq.at[:, y], load_sem.at[2 + y]))
        loads.append(pltpu.make_async_copy(sq_hbm.at[y, :, k], sq.at[:, y], load_sem.at[4 + y]))
    for load in loads:
        load.start()

    barrier = pltpu.get_barrier_semaphore()
    for device in (right, left, across, sibling, up, down, y_mate):
        pl.semaphore_signal(barrier, inc=1, device_id=device, device_id_type=MESH)
    pl.semaphore_wait(barrier, 7)
    loads[0].wait()
    loads[1].wait()

    number = Messages()
    sent = []

    def message(refs, name, device, out=None):
        i = number(name)
        src, dst = refs()
        return pltpu.make_async_remote_copy(
            src_ref=src, dst_ref=dst, send_sem=send_sem.at[i] if out is None else out, recv_sem=recv_sem.at[i],
            device_id=device, device_id_type=MESH,
        )

    def send(refs, name, device):
        message(refs, name, device).start()
        sent.append((refs, name, device))

    def flush():
        for args in sent:
            message(*args).wait_send()
        sent.clear()

    def received(ref, name):
        message(lambda: (ref, ref), name, sibling).wait_recv()

    def spread(refs, name, device):
        message(refs, name, device, gather_sem).start()

    def spread_wait():
        everything = pbuf.at[pl.ds(0, BATCHES * SLOTS - 1)]
        message(lambda: (everything, everything), "gather", sibling, gather_sem).wait_send()

    def half_to(where, half, device):
        spread(lambda: (slot(0, SELF, 0, half), slot(0, where, 0, half)), ("p", where, half), device)

    def sides_to_sibling(h):
        if h == 0:
            received(slot(0, LEFT, 0, 1), ("p", LEFT, 1))
            received(slot(0, RIGHT, 0, 0), ("p", RIGHT, 0))
        else:
            received(slot(1, LEFT, 0), ("p1", LEFT))
            received(slot(1, RIGHT, 0), ("p1", RIGHT))
        to_sibling(2 * h)

    def to_sibling(b):
        spread(lambda: (both(b, 0), both(b, 1)), ("sib", b), sibling)

    def from_sibling(b):
        received(both(b, 1), ("sib", b))

    def far_on():
        received(slot(0, LEFT, 0, 0), ("p", LEFT, 0))
        spread(lambda: (slot(0, LEFT, 0, 0), slot(0, FAR, 0, 0)), ("far",), right)
        received(slot(0, RIGHT, 0, 1), ("p", RIGHT, 1))
        spread(lambda: (slot(0, RIGHT, 0, 1), slot(0, FAR, 0, 1)), ("far",), left)

    def across_on(half):
        received(slot(1, SELF, 0, half), ("across", half))
        spread(lambda: (slot(1, SELF, 0, half), slot(1, LEFT, 0, half)), ("p1", LEFT), right)
        spread(lambda: (slot(1, SELF, 0, half), slot(1, RIGHT, 0, half)), ("p1", RIGHT), left)

    def far_across():
        received(slot(0, FAR, 0), ("far",))
        spread(lambda: (slot(0, FAR, 0), slot(1, FAR, 0)), ("far across",), across)

    def far_from_across():
        received(slot(1, FAR, 0), ("far across",))
        to_sibling(3)

    half_to(LEFT, 0, right)
    half_to(RIGHT, 1, left)
    spread(lambda: (slot(0, SELF, 0, 0), slot(1, SELF, 0, 0)), ("across", 0), across)
    half_to(LEFT, 1, right)
    half_to(RIGHT, 0, left)
    spread(lambda: (slot(0, SELF, 0, 1), slot(1, SELF, 0, 1)), ("across", 1), across)

    def group_of(i):
        return rem(i, 2) * 4 + div(rem(i, NZ), 2)

    def product(i, raw):
        b, n = div(i, NZ), group_of(i)
        batch = pbuf[pl.ds(b * SLOTS, SLOTS)].reshape(BATCH, DT + DS)
        raw[0] = nt(batch[:, :DT], tq[n].reshape(GROUP, DT))
        raw[1] = nt(batch[:, DT:], sq[n].reshape(GROUP, DS))

    def weights(i, raw):
        b, n = div(i, NZ), group_of(i)
        t = raw[0] * t_scale
        s = raw[1] * s_scale
        t_max = jnp.max(t, axis=0, keepdims=True)
        s_max = jnp.max(s, axis=0, keepdims=True)
        t_weight = jnp.exp2(t - t_max)
        s_weight = jnp.exp2(s - s_max)
        tw[n, b] = t_weight
        sw[n, b] = s_weight
        t_sum = jnp.sum(t_weight, axis=0, keepdims=True)
        s_sum = jnp.sum(s_weight, axis=0, keepdims=True)
        cross = jnp.sum(t_weight * (t - s), axis=0, keepdims=True)
        stat[n, b] = jnp.concatenate([t_max, t_sum, s_max, s_sum, cross, cross, cross, cross], axis=0)

    def turn(b):
        turned = pbuf[b * SLOTS:(b + 1) * SLOTS].reshape(BATCH, DT + DS)[:, DT:].T
        part = BATCH // NCORE
        for core in range(NCORE):
            start = (core * BATCHES + b) * part
            spt[:, start:start + part] = turned[:, core * part:(core + 1) * part]

    def know(i):
        for device in (up, down, y_mate):
            pl.semaphore_signal(known_sem.at[i], inc=1, device_id=device, device_id_type=MESH)
        pl.semaphore_wait(known_sem.at[i], 3)

    know(0)
    far_on()
    across_on(0)
    across_on(1)
    to_sibling(1)
    know(1)
    sides_to_sibling(0)
    know(2)
    know(3)
    for load in loads[2:]:
        load.wait()

    def joined(parts):
        t_max = functools.reduce(jnp.maximum, [p[0:1] for p in parts])
        s_max = functools.reduce(jnp.maximum, [p[2:3] for p in parts])
        t_in = [jnp.exp2(p[0:1] - t_max) for p in parts]
        s_in = [jnp.exp2(p[2:3] - s_max) for p in parts]
        t_sum = functools.reduce(jnp.add, [p[1:2] * w for p, w in zip(parts, t_in)])
        s_sum = functools.reduce(jnp.add, [p[3:4] * w for p, w in zip(parts, s_in)])
        cross = functools.reduce(jnp.add, [p[4:5] * w for p, w in zip(parts, t_in)])
        return t_max, t_sum, s_max, s_sum, cross

    def stat_copy(dy, dz):
        return pltpu.make_async_remote_copy(
            src_ref=stat_send.at[y_of[dy] * NZ + z_of[dz]], dst_ref=stat_recv.at[dy * NZ + (NZ - dz) % NZ],
            send_sem=st_sem.at[0], recv_sem=st_sem.at[1],
            device_id=offset_device(dy, dz), device_id_type=MESH,
        )

    def res_copy(dy, dz):
        return pltpu.make_async_remote_copy(
            src_ref=res_recv.at[me], dst_ref=res_recv.at[me],
            send_sem=st_sem.at[2], recv_sem=st_sem.at[3 if dz in (3, 5) else 4],
            device_id=offset_device(dy, dz), device_id_type=MESH,
        )

    def all_copies(ref, count, out, into):
        others = ref.at[pl.ds(0, count)]
        return pltpu.make_async_remote_copy(
            src_ref=others, dst_ref=others, send_sem=st_sem.at[out], recv_sem=st_sem.at[into],
            device_id=sibling, device_id_type=MESH,
        )

    def leave(first):
        for n in (first, first + 4, first + 1, first + 5):
            t_max, t_sum, s_max, s_sum, cross = joined([stat[n, b] for b in range(BATCHES)])
            whole = jnp.concatenate([t_max, t_sum, s_max, s_sum, cross, cross, cross, cross], axis=0)
            for y in range(NYL):
                stat_send[y * NZ + n, 0] = whole[:, y * ROWS:(y + 1) * ROWS]
            four = jnp.concatenate([whole[0:4, :ROWS], whole[0:4, ROWS:]], axis=0)
            for y in range(NYL):
                stat_send[y * NZ + (n + 4) % NZ, 1] = four

        for offset in offsets:
            @pl.when(div(rem(z_of[offset[1]], 4), 2) == first // 2)
            def _():
                stat_copy(*offset).start()

    from_sibling(0)
    product(0, raw_a)

    def score_step(j, carry):
        @pl.when(j == 1)
        def _():
            far_across()

        @pl.when(j == 3)
        def _():
            from_sibling(1)

        @pl.when(j == 5)
        def _():
            sides_to_sibling(1)

        @pl.when(j == 7)
        def _():
            from_sibling(2)

        @pl.when(j == 8)
        def _():
            far_from_across()

        @pl.when(j == 11)
        def _():
            from_sibling(3)

        @pl.when(j == 14)
        def _():
            leave(0)

        product(2 * j + 1, raw_b)
        weights(2 * j, raw_a)
        product(jnp.minimum(2 * j + 2, BATCHES * NZ - 1), raw_a)
        weights(2 * j + 1, raw_b)
        return carry

    lax.fori_loop(0, BATCHES * NZ // 2, score_step, 0)
    leave(2)
    stat_recv[0] = stat_send[me]
    for b in range(BATCHES):
        turn(b)
    spread_wait()
    all_copies(stat_recv, 15, 0, 1).wait_recv()
    def totals(parts):
        t_max, t_sum, s_max, s_sum, cross = joined(parts)
        t_in, s_in = factor / t_sum, factor / s_sum
        result = jnp.concatenate([t_max, t_in, s_max, s_in, t_in, t_in, t_in, t_in], axis=0)
        return result, (t_max, t_sum, s_max, s_sum, cross)

    result, (t_max, t_sum, s_max, s_sum, cross) = totals([stat_recv[m, 0] for m in range(OWNERS)])
    res_recv[me] = result
    for offset in results_to:
        res_copy(*offset).start()
    far = []
    for y in range(NYL):
        parts = [stat_recv[m, 1, 4 * y:4 * y + 4] for m in range(OWNERS)]
        far.append(totals([jnp.concatenate([p, p], axis=0) for p in parts])[0])
    far = jnp.concatenate(far, axis=1)

    def group(away):
        return rem(z + NZ + away, NZ)

    def sequence(i):
        size = 4 - div(i + 1, 2)
        return group(size * (2 * rem(i, 2) - 1))

    def lanes(n):
        return pl.ds(pl.multiple_of(n * GROUP, GROUP), GROUP)

    def form(i, res=None):
        n = sequence(i)
        if res is None:
            res = jnp.concatenate([res_recv[n], res_recv[NZ + n]], axis=1)
        for b in range(BATCHES):
            st = stat[n, b]
            t_in = jnp.exp2(st[0:1] - res[0:1]) * res[1:2]
            s_in = jnp.exp2(st[2:3] - res[2:3]) * res[3:4]
            grad = (sw[n, b] * s_in - tw[n, b] * t_in).astype(BF16)
            gt[0, b, :, lanes(n)] = grad[:BATCH // 2]
            gt[1, b, :, lanes(n)] = grad[BATCH // 2:]

    def pair_copy(i, count):
        slots = pl.ds(i, count)
        return pltpu.make_async_remote_copy(
            src_ref=y_pair_send.at[slots], dst_ref=y_pair_recv.at[slots],
            send_sem=ring_sem.at[2], recv_sem=yp_recv_sem.at[div(i + 1, 2)],
            device_id=y_mate, device_id_type=MESH,
        )

    def query_part(i):
        n = sequence(i)
        total = nn(spt[...], gt[:, :, :, lanes(n)].reshape(NCORE * BATCHES * BATCH // 2, GROUP))
        gq[n, 0] = total[:, :ROWS]
        gq[n, 1] = total[:, ROWS:]
        y_pair_send[i] = gq[n, 1 - yl, ZF:].astype(BF16)

    def z_part(away):
        return gq[group(away), :, :ZF]

    def y_part(away):
        i = (4, 3, -3, 2, -2, 1, -1, 0).index(away)
        if away >= 0:
            pair_copy(i, 1 if away in (4, 0) else 2).wait_recv()
        return gq[group(away), yl, ZF:] + y_pair_recv[i].astype(F32)

    ZH, YH = ZF // 2, YF // 2

    def z_start():
        far = z_part(4).astype(BF16)
        z_send[0] = far
        message(lambda: (z_send.at[0, :, pl.ds(0, ZH)], z_recv_r.at[0, :, pl.ds(0, ZH)]), ("zr", 0), up, ring_sem.at[0]).start()
        message(lambda: (z_send.at[0, :, pl.ds(ZH, ZH)], z_recv_l.at[0, :, pl.ds(ZH, ZH)]), ("zl", 0), down, ring_sem.at[0]).start()

    def y_start():
        y_send[0] = y_part(4).astype(BF16)
        message(lambda: (y_send.at[0, pl.ds(0, YH)], y_recv_r.at[0, pl.ds(0, YH)]), ("yr", 0), up, ring_sem.at[1]).start()
        message(lambda: (y_send.at[0, pl.ds(YH, YH)], y_recv_l.at[0, pl.ds(YH, YH)]), ("yl", 0), down, ring_sem.at[1]).start()

    def z_step(step):
        if step == 1:
            mine = z_part(3)
            received(z_recv_r.at[0, :, pl.ds(0, ZH)], ("zr", 0))
            z_send[1, :, :ZH] = (mine[:, :ZH] + z_recv_r[0, :, :ZH].astype(F32)).astype(BF16)
            z_send[1, :, ZH:] = mine[:, ZH:].astype(BF16)
        else:
            received(z_recv_r.at[step - 1], ("zr", step - 1))
            z_send[step] = (z_part(4 - step) + z_recv_r[step - 1].astype(F32)).astype(BF16)
        message(lambda step=step: (z_send.at[step], z_recv_r.at[step]), ("zr", step), up, ring_sem.at[0]).start()
        if step == 1:
            mine = z_part(-3)
            received(z_recv_l.at[0, :, pl.ds(ZH, ZH)], ("zl", 0))
            z_send[5, :, :ZH] = mine[:, :ZH].astype(BF16)
            z_send[5, :, ZH:] = (mine[:, ZH:] + z_recv_l[0, :, ZH:].astype(F32)).astype(BF16)
        else:
            received(z_recv_l.at[step - 1], ("zl", step - 1))
            z_send[4 + step] = (z_part(step - 4) + z_recv_l[step - 1].astype(F32)).astype(BF16)
        message(lambda step=step: (z_send.at[4 + step], z_recv_l.at[step]), ("zl", step), down, ring_sem.at[0]).start()

    def y_step(step):
        mine = y_part(4 - step)
        if step == 1:
            received(y_recv_r.at[0, pl.ds(0, YH)], ("yr", 0))
            y_send[1, :YH] = (mine[:YH] + y_recv_r[0, :YH].astype(F32)).astype(BF16)
            y_send[1, YH:] = mine[YH:].astype(BF16)
        else:
            received(y_recv_r.at[step - 1], ("yr", step - 1))
            y_send[step] = (mine + y_recv_r[step - 1].astype(F32)).astype(BF16)
        message(lambda step=step: (y_send.at[step], y_recv_r.at[step]), ("yr", step), up, ring_sem.at[1]).start()
        mine = y_part(step - 4)
        if step == 1:
            received(y_recv_l.at[0, pl.ds(YH, YH)], ("yl", 0))
            y_send[5, :YH] = mine[:YH].astype(BF16)
            y_send[5, YH:] = (mine[YH:] + y_recv_l[0, YH:].astype(F32)).astype(BF16)
        else:
            received(y_recv_l.at[step - 1], ("yl", step - 1))
            y_send[4 + step] = (mine + y_recv_l[step - 1].astype(F32)).astype(BF16)
        message(lambda step=step: (y_send.at[4 + step], y_recv_l.at[step]), ("yl", step), down, ring_sem.at[1]).start()

    def passage_part(core, to):
        def term(i):
            wide = pl.ds(pl.multiple_of(i * 2 * GROUP, 2 * GROUP), 2 * GROUP)
            grads = gt[core, :, :, wide].reshape(BATCHES * BATCH // 2, 2 * GROUP)
            queries = sq[pl.ds(2 * i, 2)].reshape(2 * GROUP, DS)
            return nn(grads, queries).reshape(BATCHES, 2, OWN, DS)

        to[...] = term(0)

        def body(i, carry):
            to[...] = to[...] + term(i)
            return carry

        lax.fori_loop(1, NZ // 2, body, 0)

    def gp_of(h, where):
        b, s = place(h, where, 0)
        return gp[b, s]

    def gp_first():
        received(gps_recv, "gp sibling")
        gp[...] = gp[...] + gps_recv[...].astype(F32)
        for h in range(NYH):
            gp1_send[h] = gp_of(h, FAR).astype(BF16)
        send(lambda: (gp1_send.at[0], gp1_recv.at[0]), ("gp", RIGHT, 1), right)
        send(lambda: (gp1_send.at[1], gp1_recv.at[1]), ("gp", LEFT, 1), left)

    def gp_second():
        received(gp1_recv.at[0], ("gp", RIGHT, 1))
        gp2_send[0, 0] = (gp_of(0, RIGHT) + gp1_recv[0].astype(F32)).astype(BF16)
        gp2_send[0, 1] = gp_of(1, RIGHT).astype(BF16)
        send(lambda: (gp2_send.at[0], gp2_recv.at[0]), ("gp", RIGHT, 2), right)
        received(gp1_recv.at[1], ("gp", LEFT, 1))
        gp2_send[1, 0] = gp_of(0, LEFT).astype(BF16)
        gp2_send[1, 1] = (gp_of(1, LEFT) + gp1_recv[1].astype(F32)).astype(BF16)
        send(lambda: (gp2_send.at[1], gp2_recv.at[1]), ("gp", LEFT, 2), left)

    def gp_third():
        received(gp2_recv.at[0], ("gp", RIGHT, 2))
        received(gp2_recv.at[1], ("gp", LEFT, 2))
        gp3_send[...] = x_total(1).astype(BF16)
        send(lambda: (gp3_send, gp3_recv), "gp across", across)

    def x_total(h):
        return gp_of(h, SELF) + gp2_recv[0, h].astype(F32) + gp2_recv[1, h].astype(F32)

    def z_last():
        received(z_recv_r.at[3], ("zr", 3))
        received(z_recv_l.at[3], ("zl", 3))
        for y in range(NYL):
            gq[z, y, :ZF] = gq[z, y, :ZF] + z_recv_r[3, y].astype(F32) + z_recv_l[3, y].astype(F32)
        z_pair_send[...] = gq[z, 1 - yl, :ZF].astype(BF16)
        send(lambda: (z_pair_send, z_pair_recv), "z pair", y_mate)

    form(0, far)
    query_part(0)
    z_start()
    pair_copy(0, 1).start()
    div_out[...] = cross * LN2 / t_sum - (t_max * LN2 + jnp.log(t_sum)) + (s_max * LN2 + jnp.log(s_sum))
    all_copies(stat_send, 15, 0, 1).wait_send()
    all_copies(res_recv, 4, 2, 3).wait_recv()
    form(1)

    def gradient_step(i, carry):
        @pl.when(i == 2)
        def _():
            all_copies(res_recv, 9, 2, 4).wait_recv()

        query_part(i)
        form(i + 1)

        @pl.when(i == 2)
        def _():
            z_step(1)

        @pl.when(rem(i, 2) == 0)
        def _():
            pair_copy(i - 1, 2).start()


        @pl.when(i == 4)
        def _():
            y_start()

        return carry

    lax.fori_loop(1, NZ - 1, gradient_step, 0)
    query_part(NZ - 1)
    pair_copy(NZ - 1, 1).start()
    passage_part(1, gp)
    gps_send[...] = gp[...].astype(BF16)
    send(lambda: (gps_send, gps_recv), "gp sibling", sibling)
    z_step(2)
    y_step(1)
    passage_part(0, gp)
    gp_first()
    z_step(3)
    y_step(2)
    gp_second()
    all_copies(res_recv, 13, 2, 3).wait_send()
    z_last()
    y_step(3)
    gp_third()
    for i, ref in enumerate((z_send.at[pl.ds(0, 7)], y_send.at[pl.ds(0, 7)], y_pair_send)):
        message(lambda: (ref, ref), "ring", sibling, ring_sem.at[i]).wait_send()
    flush()

    mine = y_part(0)
    received(y_recv_r.at[3], ("yr", 3))
    received(y_recv_l.at[3], ("yl", 3))
    gq_out[:, ZF:] = (mine + y_recv_r[3].astype(F32) + y_recv_l[3].astype(F32)).T
    received(z_pair_recv, "z pair")
    gq_out[:, :ZF] = (gq[z, yl, :ZF] + z_pair_recv[...].astype(F32)).T
    received(gp3_recv, "gp across")
    gp_out[...] = x_total(0) + gp3_recv[...].astype(F32)


def deliver(gq_in, gp_in, div_in, gq_out, gp_out, div_out, gq, gp, div, in_sem, out_sem):
    parts = ((gq_in, gq, gq_out), (gp_in, gp, gp_out), (div_in, div, div_out))
    ins = [pltpu.make_async_copy(src, mid, in_sem.at[i]) for i, (src, mid, _) in enumerate(parts)]
    outs = [pltpu.make_async_copy(mid, dst, out_sem.at[i]) for i, (_, mid, dst) in enumerate(parts)]
    for copy in ins:
        copy.start()
    for arrive, leave in zip(ins, outs):
        arrive.wait()
        leave.start()
    for copy in outs:
        copy.wait()


def local(teacher_query, student_query, teacher_passages, student_passages):
    blocks = NYL, NZ, NCORE, ROWS
    hbm = pl.BlockSpec(memory_space=pl.ANY)
    vmem = pl.BlockSpec(memory_space=pltpu.VMEM)
    outs = (
        jax.ShapeDtypeStruct((ROWS, DS), F32),
        jax.ShapeDtypeStruct((OWN, DS), F32),
        jax.ShapeDtypeStruct((1, ROWS), F32),
    )
    results = pl.pallas_call(
        kernel,
        out_shape=outs,
        in_specs=[hbm] * 4,
        out_specs=(vmem,) * 3,
        scratch_shapes=[
            pltpu.VMEM((NZ, NYL, ROWS, DT), BF16),
            pltpu.VMEM((NZ, NYL, ROWS, DS), BF16),
            pltpu.VMEM((BATCHES * SLOTS, OWN, DT + DS), BF16),
            pltpu.VMEM((DS, BATCHES * BATCH), BF16),
            pltpu.VMEM((NZ, BATCHES, BATCH, GROUP), F32),
            pltpu.VMEM((NZ, BATCHES, BATCH, GROUP), F32),
            pltpu.VMEM((2, BATCH, GROUP), F32),
            pltpu.VMEM((2, BATCH, GROUP), F32),
            pltpu.VMEM((NCORE, BATCHES, BATCH // 2, NZ * GROUP), BF16),
            pltpu.VMEM((NZ, BATCHES, 8, GROUP), F32),
            pltpu.VMEM((NZ, NYL, DS, ROWS), F32),
            pltpu.VMEM((OWNERS, 2, 8, ROWS), F32),
            pltpu.VMEM((OWNERS, 2, 8, ROWS), F32),
            pltpu.VMEM((OWNERS, 8, ROWS), F32),
            pltpu.VMEM((8, NYL, ZF, ROWS), BF16),
            pltpu.VMEM((4, NYL, ZF, ROWS), BF16),
            pltpu.VMEM((4, NYL, ZF, ROWS), BF16),
            pltpu.VMEM((ZF, ROWS), BF16),
            pltpu.VMEM((ZF, ROWS), BF16),
            pltpu.VMEM((NZ, YF, ROWS), BF16),
            pltpu.VMEM((NZ, YF, ROWS), BF16),
            pltpu.VMEM((8, YF, ROWS), BF16),
            pltpu.VMEM((4, YF, ROWS), BF16),
            pltpu.VMEM((4, YF, ROWS), BF16),
            pltpu.VMEM((BATCHES, 2, OWN, DS), F32),
            pltpu.VMEM((BATCHES, 2, OWN, DS), BF16),
            pltpu.VMEM((BATCHES, 2, OWN, DS), BF16),
            pltpu.VMEM((NYH, OWN, DS), BF16),
            pltpu.VMEM((NYH, OWN, DS), BF16),
            pltpu.VMEM((2, NYH, OWN, DS), BF16),
            pltpu.VMEM((2, NYH, OWN, DS), BF16),
            pltpu.VMEM((OWN, DS), BF16),
            pltpu.VMEM((OWN, DS), BF16),
            pltpu.SemaphoreType.DMA((6,)),
            pltpu.SemaphoreType.REGULAR((4,)),
            pltpu.SemaphoreType.DMA,
            pltpu.SemaphoreType.DMA((3,)),
            pltpu.SemaphoreType.DMA((MESSAGES,)),
            pltpu.SemaphoreType.DMA((MESSAGES,)),
            pltpu.SemaphoreType.DMA((NZ,)),
            pltpu.SemaphoreType.DMA((5,)),
        ],
        compiler_params=pltpu.CompilerParams(
            collective_id=0, has_side_effects=True, vmem_limit_bytes=VMEM_BYTES
        ),
    )(
        teacher_query.reshape(*blocks, DT),
        student_query.reshape(*blocks, DS),
        teacher_passages,
        student_passages,
    )
    grad_query, grad_passage, divergence = pl.pallas_call(
        deliver,
        out_shape=outs,
        in_specs=[hbm] * 3,
        out_specs=(hbm,) * 3,
        scratch_shapes=[
            *(pltpu.VMEM(out.shape, out.dtype) for out in outs),
            pltpu.SemaphoreType.DMA((3,)),
            pltpu.SemaphoreType.DMA((3,)),
        ],
        compiler_params=pltpu.CompilerParams(vmem_limit_bytes=VMEM_BYTES),
    )(*results)
    return divergence.reshape(ROWS), grad_query, grad_passage


def solution(mesh):
    return jax.shard_map(
        local,
        mesh=mesh,
        in_specs=(
            P("query", None),
            P("query", None),
            P(("query", "corpus"), None),
            P(("query", "corpus"), None),
        ),
        out_specs=(
            P(("query", "corpus")),
            P(("query", "corpus"), None),
            P(("query", "corpus"), None),
        ),
        check_vma=False,
    )
```
